32 devices in a mesh: seq: 16 (over z, y, x), head: 2 (over core).
Axes of the slice: x: 2, y: 2, z: 4, core: 2. Of those that a mesh axis runs over, the one named last changes fastest.
Arguments:
- hidden_in: float32 [4096, 2048], P('seq'), may hold values from -6 to 6
- grad_out: float32 [4096, 2048], P('seq'), may hold values from -6 to 6
- doc_starts: int32 [8], replicated, may hold values from 0 to 4095, as said below
- norm_mixer: float32 [2048], P('seq'), may hold values from 0.5 to 1.5
- norm_ffn: float32 [2048], P('seq'), may hold values from 0.5 to 1.5
- mamba_z: float32 [2048, 3072], P('seq', 'head'), may hold values from -0.125 to 0.125
- mamba_x: float32 [2048, 3072], P('seq', 'head'), may hold values from -0.125 to 0.125
- mamba_bc: float32 [2048, 512], P('seq'), may hold values from -0.015625 to 0.015625
- mamba_dt: float32 [2048, 48], P('seq', 'head'), may hold values from -0.125 to 0.125
- conv_x: float32 [4, 3072], P(None, 'head'), may hold values from -0.5 to 0.5
- conv_bc: float32 [4, 512], replicated, may hold values from -0.5 to 0.5
- a_log: float32 [48], P('head'), may hold values from -16 to -3
- dt_bias: float32 [48], P('head'), may hold values from -1 to 1
- skip_gain: float32 [48], P('head'), may hold values from 0.5 to 1.5
- mamba_out: float32 [3072, 2048], P('head', 'seq'), may hold values from -0.109375 to 0.109375
- attn_query: float32 [2048, 1024], P('seq', 'head'), may hold values from -0.125 to 0.125
- attn_key: float32 [2048, 256], P('seq', 'head'), may hold values from -0.125 to 0.125
- attn_value: float32 [2048, 256], P('seq', 'head'), may hold values from -0.125 to 0.125
- attn_out: float32 [1024, 2048], P('head', 'seq'), may hold values from -0.75 to 0.75
- ffn_gate: float32 [2048, 4096], P('seq', 'head'), may hold values from -0.125 to 0.125
- ffn_up: float32 [2048, 4096], P('seq', 'head'), may hold values from -0.125 to 0.125
- ffn_down: float32 [4096, 2048], P('head', 'seq'), may hold values from -0.09375 to 0.09375
Outputs:
- block_out: float32 [4096, 2048], P('seq')
- grad_in: float32 [4096, 2048], P('seq')
- grad_norm_mixer: float32 [2048], P('seq')
- grad_norm_ffn: float32 [2048], P('seq')
- grad_mamba_z: float32 [2048, 3072], P('seq', 'head')
- grad_mamba_x: float32 [2048, 3072], P('seq', 'head')
- grad_mamba_bc: float32 [2048, 512], P('seq')
- grad_mamba_dt: float32 [2048, 48], P('seq', 'head')
- grad_conv_x: float32 [4, 3072], P(None, 'head')
- grad_conv_bc: float32 [4, 512], replicated
- grad_a_log: float32 [48], P('head')
- grad_dt_bias: float32 [48], P('head')
- grad_skip_gain: float32 [48], P('head')
- grad_mamba_out: float32 [3072, 2048], P('head', 'seq')
- grad_attn_query: float32 [2048, 1024], P('seq', 'head')
- grad_attn_key: float32 [2048, 256], P('seq', 'head')
- grad_attn_value: float32 [2048, 256], P('seq', 'head')
- grad_attn_out: float32 [1024, 2048], P('head', 'seq')
- grad_ffn_gate: float32 [2048, 4096], P('seq', 'head')
- grad_ffn_up: float32 [2048, 4096], P('seq', 'head')
- grad_ffn_down: float32 [4096, 2048], P('head', 'seq')
The draws below stay inside these ranges and needn't reach their ends.
Inputs may be any that keep to these rules, and one draw needn't show every extreme that they name: `doc_starts`: strictly increasing, the first 0 and the last 4095; 3 of the others lie below 256 and the remaining 3 above 3840.
All inputs are finite; a program needn't handle non-finite values.
Results may differ from the reference program's by a relative error of at most 0.019.
The reference program's roundings to bfloat16 on the way count: a program that leaves them out, or rounds other values in their place, can miss the bound.
Values may be sent and summed in bfloat16 or wider, within the bound.
A program may use at most 512 MiB of HBM per device.

```python
import math
import jax
import jax.numpy as jnp
from jax import lax

D = 2048
MHEADS = 48
MHDIM = 64
NSTATE = 256
CONV = 4
QHEADS = 8
KVHEADS = 2
HDIM = 128
FF = 4096
TOK_DEV = 256
SPAN = 128
NDOCS = 8
TOKENS = 4096


def draw_doc_starts(key, part):
    key = jax.random.fold_in(key, 17)
    key_early, key_late = jax.random.split(key)
    half_count = NDOCS // 2
    early_starts = jax.random.permutation(key_early, TOK_DEV - 1)[:half_count - 1] + 1
    late_starts = jax.random.permutation(key_late, TOK_DEV - 2)[:half_count - 1] + (TOKENS - TOK_DEV + 1)
    return jnp.concatenate([jnp.zeros((1,), jnp.int32), jnp.sort(early_starts).astype(jnp.int32), jnp.sort(late_starts).astype(jnp.int32), jnp.full((1,), TOKENS - 1, jnp.int32)])


def draw_a_log(key, part):
    key = jax.random.fold_in(key, 29)
    key_pick, key_slow, key_fast = jax.random.split(key, 3)
    slow_share = 0.5
    slow_heads = jax.random.uniform(key_pick, (MHEADS,), jnp.float32) < slow_share
    slow_logs = jax.random.uniform(key_slow, (MHEADS,), jnp.float32, minval=math.log(0.3 / TOKENS), maxval=math.log(2.0 / TOKENS))
    fast_logs = jax.random.uniform(key_fast, (MHEADS,), jnp.float32, minval=math.log(0.01), maxval=math.log(0.045))
    return jnp.where(slow_heads, slow_logs, fast_logs).astype(jnp.float32)


def block_levels(stream_key, extent, cuts, low, high):
    level, own = 1.0, jax.random.fold_in(stream_key, 6)
    for axis_at, parts in cuts:
        draws = jnp.exp(jax.random.uniform(jax.random.fold_in(own, axis_at), (parts,), jnp.float32, low / len(cuts), high / len(cuts)))
        level = level * jnp.repeat(draws, extent[axis_at] // parts).reshape([-1 if axis == axis_at else 1 for axis in range(len(extent))])
    return level


def gaussian(stream_key, shape, spread, bound, cuts=(), kind=jnp.bfloat16):
    level = block_levels(stream_key, shape, cuts, -0.22, 0.18) if cuts else 1.0
    drawn = jax.random.normal(stream_key, shape, jnp.float32) * spread * level
    return jnp.minimum(jnp.maximum(drawn, -bound), bound).astype(kind)


def setup_inputs(seed: int = 0) -> dict:
    key_of = jax.random.split(jax.random.key(seed), 23)
    return {
        "hidden_in": gaussian(key_of[0], (TOKENS, D), 1.0, 6.0, ((0, 16),), jnp.float32),
        "grad_out": gaussian(key_of[1], (TOKENS, D), 1.0, 6.0, ((0, 16),), jnp.float32),
        "doc_starts": draw_doc_starts(jax.random.fold_in(key_of[22], 71), 0),
        "norm_mixer": jnp.clip(1.0 + 0.1 * jax.random.normal(key_of[3], (D,), jnp.float32), 0.5, 1.5),
        "norm_ffn": jnp.clip(1.0 + 0.1 * jax.random.normal(key_of[4], (D,), jnp.float32), 0.5, 1.5),
        "mamba_z": gaussian(key_of[5], (D, MHEADS * MHDIM), D ** -0.5, 0.125, ((0, 16), (1, 2)), jnp.float32),
        "mamba_x": gaussian(key_of[6], (D, MHEADS * MHDIM), D ** -0.5, 0.125, ((0, 16), (1, 2)), jnp.float32),
        "mamba_bc": gaussian(key_of[7], (D, 2 * NSTATE), (64 * D) ** -0.5, 0.015625, ((0, 16),), jnp.float32),
        "mamba_dt": gaussian(key_of[8], (D, MHEADS), D ** -0.5, 0.125, ((0, 16), (1, 2)), jnp.float32),
        "conv_x": jnp.clip(jax.random.uniform(key_of[9], (CONV, MHEADS * MHDIM), jnp.float32, -0.5, 0.5) * block_levels(key_of[9], (CONV, MHEADS * MHDIM), ((1, 2),), -0.4, 0.0), -0.5, 0.5),
        "conv_bc": jnp.clip(jax.random.uniform(key_of[10], (CONV, 2 * NSTATE), jnp.float32, -0.5, 0.5), -0.5, 0.5),
        "a_log": draw_a_log(jax.random.fold_in(key_of[22], 71), 0),
        "dt_bias": jnp.clip(jax.random.uniform(key_of[12], (MHEADS,), jnp.float32, -1.0, 1.0) * block_levels(key_of[12], (MHEADS,), ((0, 2),), -0.4, 0.0), -1.0, 1.0),
        "skip_gain": jnp.clip(0.5 + 1.0 * jax.random.uniform(key_of[13], (MHEADS,), jnp.float32) ** block_levels(key_of[13], (MHEADS,), ((0, 2),), -0.2, 0.2), 0.5, 1.5),
        "mamba_out": gaussian(key_of[14], (MHEADS * MHDIM, D), (MHEADS * MHDIM) ** -0.5, 0.109375, ((0, 2), (1, 16)), jnp.float32),
        "attn_query": gaussian(key_of[15], (D, QHEADS * HDIM), D ** -0.5, 0.125, ((0, 16), (1, 2)), jnp.float32),
        "attn_key": gaussian(key_of[16], (D, KVHEADS * HDIM), D ** -0.5, 0.125, ((0, 16), (1, 2)), jnp.float32),
        "attn_value": gaussian(key_of[17], (D, KVHEADS * HDIM), D ** -0.5, 0.125, ((0, 16), (1, 2)), jnp.float32),
        "attn_out": gaussian(key_of[18], (QHEADS * HDIM, D), (QHEADS * HDIM // 16) ** -0.5, 0.75, ((0, 2), (1, 16)), jnp.float32),
        "ffn_gate": gaussian(key_of[19], (D, FF), D ** -0.5, 0.125, ((0, 16), (1, 2)), jnp.float32),
        "ffn_up": gaussian(key_of[20], (D, FF), D ** -0.5, 0.125, ((0, 16), (1, 2)), jnp.float32),
        "ffn_down": gaussian(key_of[21], (FF, D), FF ** -0.5, 0.09375, ((0, 2), (1, 16)), jnp.float32),
    }


eps_norm = 1e-05
rope_base = 100000000000.0
neg_large = -1e+30
top_prec = lax.Precision.HIGHEST

@jax.custom_vjp
def low(v):
    return lax.optimization_barrier(v.astype(jnp.bfloat16)).astype(jnp.float32)

@jax.custom_vjp
def low_back(v):
    return v

def low_keep(v):
    return (low(v), None)

def low_pass(kept, grad):
    return (grad,)

def back_keep(v):
    return (v, None)

def back_low(kept, grad):
    return (low(grad),)
low.defvjp(low_keep, low_pass)
low_back.defvjp(back_keep, back_low)

def matmul(left, right):
    return jnp.dot(left, right, precision=top_prec)

def rms_scale(rows, gain):
    return rows * lax.rsqrt(lax.optimization_barrier(jnp.mean(rows * rows, axis=1, keepdims=True)) + eps_norm) * gain[None, :]

def doc_ids(positions, doc_starts):
    return lax.optimization_barrier(jnp.sum((doc_starts[None, :] <= positions[:, None]).astype(jnp.int32), axis=1)) - 1

def rope_tables(positions, head_dim):
    half_dim = head_dim // 2
    freqs = rope_base ** (-2.0 * jnp.arange(half_dim, dtype=jnp.float32) / head_dim)
    angles = positions.astype(jnp.float32)[:, None] * freqs[None, :]
    return (jnp.cos(angles)[:, None, :], jnp.sin(angles)[:, None, :])

def rotate(values, positions):
    half_dim = values.shape[-1] // 2
    cosine, sine = rope_tables(positions, values.shape[-1])
    first_half, second_half = (values[..., :half_dim], values[..., half_dim:])
    return jnp.concatenate([first_half * cosine - second_half * sine, second_half * cosine + first_half * sine], axis=-1)

def convolve(extended, weights, ext_docs, tok_count):
    edge_rows = weights.shape[0] - 1
    summed = jnp.zeros((tok_count, extended.shape[1]), jnp.float32)
    for tap_index in range(weights.shape[0]):
        begin_row = edge_rows - tap_index
        same_doc = (ext_docs[begin_row:begin_row + tok_count] == ext_docs[edge_rows:])[:, None]
        summed = summed + jnp.where(same_doc, extended[begin_row:begin_row + tok_count], 0.0) * weights[tap_index][None, :]
    return summed

def span_ssd(start_state, inputs_x, inputs_b, inputs_c, step_sizes, log_decay, span_docs, before_doc):
    length = inputs_x.shape[0]
    cumulative = jnp.cumsum(log_decay, axis=0)
    order = jnp.arange(length)
    linked = (span_docs[:, None] == span_docs[None, :]) & (order[:, None] >= order[None, :])
    gaps = jnp.where(linked[:, :, None], cumulative[:, None, :] - cumulative[None, :, :], neg_large)
    inner = jnp.dot(inputs_c, inputs_b.T, precision=top_prec)
    pair_weights = jnp.exp(gaps) * inner[:, :, None] * step_sizes[None, :, :]
    y_inner = jnp.einsum('tsh,shp->thp', pair_weights, inputs_x, precision=top_prec)
    carried = span_docs == before_doc
    entry_decay = jnp.where(carried[:, None], jnp.exp(cumulative), 0.0)
    y_state = jnp.einsum('tn,hpn->thp', inputs_c, start_state, precision=top_prec) * entry_decay[:, :, None]
    tail = jnp.where((span_docs == span_docs[-1])[:, None], jnp.exp(cumulative[-1][None, :] - cumulative), 0.0) * step_sizes
    new_state = jnp.einsum('sh,shp,sn->hpn', tail, inputs_x, inputs_b, precision=top_prec) + entry_decay[-1][:, None, None] * start_state
    return (y_inner + y_state, new_state)

def layer(hidden_in, norm_mixer, norm_ffn, mamba_z, mamba_x, mamba_bc, mamba_dt, conv_x, conv_bc, a_log, dt_bias, skip_gain, mamba_out, attn_query, attn_key, attn_value, attn_out, ffn_gate, ffn_up, ffn_down, doc_starts):
    positions = jnp.arange(TOKENS, dtype=jnp.int32)
    docs = doc_ids(positions, doc_starts)
    edge_rows = CONV - 1
    ext_docs = doc_ids(jnp.arange(-edge_rows, TOKENS, dtype=jnp.int32), doc_starts)
    normed_one = low(rms_scale(hidden_in, low(norm_mixer)))
    gate_z = low_back(matmul(normed_one, low(mamba_z)))
    x_pre = low(low_back(matmul(normed_one, low(mamba_x))))
    bc_pre = low(low_back(matmul(normed_one, low(mamba_bc))))
    dt_raw = low_back(matmul(normed_one, low(mamba_dt)))
    x_ssm = low(jax.nn.silu(convolve(jnp.pad(x_pre, ((edge_rows, 0), (0, 0))), conv_x, ext_docs, TOKENS)))
    bc_ssm = low(jax.nn.silu(convolve(jnp.pad(bc_pre, ((edge_rows, 0), (0, 0))), conv_bc, ext_docs, TOKENS)))
    dt_val = jax.nn.softplus(dt_raw + dt_bias[None, :])
    log_decay = -jnp.exp(a_log)[None, :] * dt_val
    x_heads = x_ssm.reshape(TOKENS, MHEADS, MHDIM)
    b_mat = bc_ssm[:, :NSTATE]
    c_mat = bc_ssm[:, NSTATE:]
    nchunk = TOKENS // SPAN
    span_prev = jnp.concatenate([jnp.full((1,), -1, jnp.int32), docs[SPAN - 1::SPAN][:-1].astype(jnp.int32)])

    def spanned(values):
        return values.reshape((nchunk, SPAN) + values.shape[1:])

    def ssd_step(state_in, inputs):
        xs_c, b_c, c_c, dt_c, la_c, docs_c, before = inputs
        y_c, state_out = span_ssd(state_in, xs_c, b_c, c_c, dt_c, la_c, docs_c, before)
        return (state_out, y_c)
    final_state, y_spans = lax.scan(jax.checkpoint(ssd_step), jnp.zeros((MHEADS, MHDIM, NSTATE), jnp.float32), (spanned(x_heads), spanned(b_mat), spanned(c_mat), spanned(dt_val), spanned(log_decay), spanned(docs), span_prev))
    y_ssd = y_spans.reshape(TOKENS, MHEADS, MHDIM) + skip_gain[None, :, None] * x_heads
    gated = low(y_ssd.reshape(TOKENS, MHEADS * MHDIM) * jax.nn.silu(gate_z))
    mixer_branch = low_back(matmul(gated, low(mamba_out)))
    queries = low(rotate(low_back(matmul(normed_one, low(attn_query))).reshape(TOKENS, QHEADS, HDIM), positions))
    keys = low(rotate(low_back(matmul(normed_one, low(attn_key))).reshape(TOKENS, KVHEADS, HDIM), positions))
    values = low(low_back(matmul(normed_one, low(attn_value)))).reshape(TOKENS, KVHEADS, HDIM)
    group_size = QHEADS // KVHEADS
    block_rows = math.gcd(TOKENS, 512)
    query_blocks = queries.reshape(TOKENS // block_rows, block_rows, KVHEADS, group_size, HDIM)
    block_firsts = jnp.arange(TOKENS // block_rows, dtype=jnp.int32) * block_rows

    def attend(inputs):
        query_blk, block_first = inputs
        query_pos = block_first + jnp.arange(block_rows, dtype=jnp.int32)
        visible = ((query_pos[:, None] >= positions[None, :]) & (doc_ids(query_pos, doc_starts)[:, None] == docs[None, :]))[:, None, None, :]
        scores = low_back(jnp.einsum('qgrd,kgd->qgrk', query_blk, keys, precision=top_prec) * HDIM ** (-0.5))
        masked = jnp.where(visible, scores, neg_large)
        row_max = lax.optimization_barrier(jnp.max(masked, axis=3, keepdims=True))
        log_total = row_max + jnp.log(lax.optimization_barrier(jnp.sum(jnp.exp(masked - row_max), axis=3, keepdims=True)))
        probabilities = jnp.where(visible, jnp.exp(masked - log_total), 0.0)
        return jnp.einsum('qgrk,kgd->qgrd', low(probabilities), values, precision=top_prec)
    attended = lax.map(jax.checkpoint(attend), (query_blocks, block_firsts))
    attn_low = low(low_back(attended.reshape(TOKENS, QHEADS * HDIM)))
    attn_branch = low_back(matmul(attn_low, low(attn_out)))
    mid = hidden_in + mixer_branch + attn_branch
    normed_two = low(rms_scale(mid, low(norm_ffn)))
    gate_val = low_back(matmul(normed_two, low(ffn_gate)))
    up_val = low_back(matmul(normed_two, low(ffn_up)))
    activated = low(jax.nn.silu(gate_val) * up_val)
    return mid + low_back(matmul(activated, low(ffn_down)))

def reference(hidden_in, grad_out, doc_starts, norm_mixer, norm_ffn, mamba_z, mamba_x, mamba_bc, mamba_dt, conv_x, conv_bc, a_log, dt_bias, skip_gain, mamba_out, attn_query, attn_key, attn_value, attn_out, ffn_gate, ffn_up, ffn_down):

    def forward(hidden_one, gain_one, gain_two, weight_z, weight_x, weight_bc, weight_dt, taps_x, taps_bc, rates_log, bias_dt, gain_skip, weight_mout, weight_query, weight_key, weight_value, weight_aout, weight_gate, weight_up, weight_down):
        return layer(hidden_one, gain_one, gain_two, weight_z, weight_x, weight_bc, weight_dt, taps_x, taps_bc, rates_log, bias_dt, gain_skip, weight_mout, weight_query, weight_key, weight_value, weight_aout, weight_gate, weight_up, weight_down, doc_starts)
    block_out, pullback = jax.vjp(forward, hidden_in.astype(jnp.float32), norm_mixer, norm_ffn, mamba_z, mamba_x, mamba_bc, mamba_dt, conv_x, conv_bc, a_log, dt_bias, skip_gain, mamba_out, attn_query, attn_key, attn_value, attn_out, ffn_gate, ffn_up, ffn_down)
    grads = pullback(grad_out.astype(jnp.float32))
    return (block_out, grads[0], grads[1], grads[2], grads[3], grads[4], grads[5], grads[6], grads[7], grads[8], grads[9], grads[10], grads[11], grads[12], grads[13], grads[14], grads[15], grads[16], grads[17], grads[18], grads[19])
```

```python
import math

import jax
import jax.numpy as jnp
import numpy as np
from jax import lax
from jax.sharding import Mesh
from jax.sharding import PartitionSpec as P

MHDIM = 64
NSTATE = 256
HDIM = 128
SPAN = 128

eps_norm = 1e-05
rope_base = 100000000000.0
neg_large = -1e30
top_prec = lax.Precision.HIGHEST
bf16 = jnp.bfloat16
f32 = jnp.float32


def doc_ids(positions, doc_starts):
    return jnp.sum((doc_starts[None, :] <= positions[:, None]).astype(jnp.int32), axis=1) - 1


def product(left, right):
    return jnp.dot(left, right, preferred_element_type=f32)


def product_t(left, right):
    return lax.dot_general(left, right, (((0,), (0,)), ((), ())), preferred_element_type=f32)


def product_nt(left, right):
    return lax.dot_general(left, right, (((1,), (1,)), ((), ())), preferred_element_type=f32)


def norm_rows(rows, gain):
    row_scale = lax.rsqrt(jnp.mean(rows * rows, axis=1, keepdims=True) + eps_norm)
    return (row_scale, (rows * row_scale * gain.astype(f32)[None, :]).astype(bf16))


def norm_back(rows, row_scale, gain, d_normed):
    weighted = d_normed * gain.astype(f32)[None, :]
    grad_gain = jnp.sum(d_normed * rows * row_scale, axis=0)
    d_rows = row_scale * weighted - rows * row_scale**3 * jnp.mean(
        weighted * rows, axis=1, keepdims=True
    )
    return (d_rows, grad_gain)


def silu_slope(values):
    sigma_val = jax.nn.sigmoid(values)
    return sigma_val * (1.0 + values * (1.0 - sigma_val))


def link_states(earlier, later):
    return (earlier[0] * later[0], later[0][:, None, None] * earlier[1] + later[1])


def carried_in(value, axis, join, neutral, backward):
    count, mine = (lax.axis_size(axis), lax.axis_index(axis))
    pieces = jax.tree.map(lambda part: lax.all_gather(part, axis), value)
    if backward:
        pieces = jax.tree.map(lambda part: part[::-1], pieces)
        mine = count - 1 - mine
    running = jax.tree.map(
        lambda part, zero: jnp.full_like(part, 0) + jnp.asarray(zero, part.dtype), value, neutral
    )

    def turn(position, running):
        longer = join(running, jax.tree.map(lambda part: part[position], pieces))
        return jax.tree.map(lambda new, old: jnp.where(position < mine, new, old), longer, running)

    return lax.fori_loop(0, count - 1, turn, running)


def passed_along(block, axis, distance):
    devices = range(lax.axis_size(axis))
    route = [(i - distance, i) for i in devices if i - distance in devices]
    return lax.ppermute(block, axis, route)


def convolve(extended, weights, ext_docs, tok_count):
    edge_rows = weights.shape[0] - 1
    summed = jnp.zeros((tok_count, extended.shape[1]), f32)
    for tap_index in range(weights.shape[0]):
        begin_row = edge_rows - tap_index
        same_doc = (ext_docs[begin_row : begin_row + tok_count] == ext_docs[edge_rows:])[:, None]
        summed = (
            summed
            + jnp.where(same_doc, extended[begin_row : begin_row + tok_count].astype(f32), 0.0)
            * weights[tap_index][None, :]
        )
    return summed


def convolve_back(d_conv, extended, weights, ext_docs, tok_count):
    edge_rows = weights.shape[0] - 1
    d_extended = jnp.zeros((tok_count + edge_rows, d_conv.shape[1]), f32)
    tap_grads = []
    for tap_index in range(weights.shape[0]):
        begin_row = edge_rows - tap_index
        same_doc = (ext_docs[begin_row : begin_row + tok_count] == ext_docs[edge_rows:])[:, None]
        masked_grad = jnp.where(same_doc, d_conv, 0.0)
        tap_grads.append(
            jnp.sum(
                masked_grad * extended[begin_row : begin_row + tok_count].astype(f32), axis=0
            )
        )
        d_extended = d_extended + jnp.pad(
            masked_grad * weights[tap_index][None, :], ((begin_row, edge_rows - begin_row), (0, 0))
        )
    return (d_extended, jnp.stack(tap_grads))


def span_ssd(
    start_state, inputs_x, inputs_b, inputs_c, step_sizes, log_decay, span_docs, before_doc
):
    length = inputs_x.shape[0]
    cumulative = jnp.cumsum(log_decay, axis=0)
    order = jnp.arange(length)
    linked = (span_docs[:, None] == span_docs[None, :]) & (order[:, None] >= order[None, :])
    gaps = jnp.where(linked[:, :, None], cumulative[:, None, :] - cumulative[None, :, :], neg_large)
    inner = jnp.dot(inputs_c, inputs_b.T, precision=top_prec)
    pair_weights = jnp.exp(gaps) * inner[:, :, None] * step_sizes[None, :, :]
    y_inner = jnp.einsum("tsh,shp->thp", pair_weights, inputs_x, precision=top_prec)
    carried = span_docs == before_doc
    entry_decay = jnp.where(carried[:, None], jnp.exp(cumulative), 0.0)
    y_state = (
        jnp.einsum("tn,hpn->thp", inputs_c, start_state, precision=top_prec)
        * entry_decay[:, :, None]
    )
    tail = (
        jnp.where(
            (span_docs == span_docs[-1])[:, None],
            jnp.exp(cumulative[-1][None, :] - cumulative),
            0.0,
        )
        * step_sizes
    )
    new_state = (
        jnp.einsum("sh,shp,sn->hpn", tail, inputs_x, inputs_b, precision=top_prec)
        + entry_decay[-1][:, None, None] * start_state
    )
    return (y_inner + y_state, new_state)


def rope_tables(positions, pairs):
    freqs = rope_base ** (-2.0 * pairs.astype(f32) / HDIM)
    angles = positions.astype(f32)[:, None] * freqs[None, :]
    return jnp.cos(angles), jnp.sin(angles)


def shards(
    hidden_in,
    grad_out,
    doc_starts,
    norm_mixer,
    norm_ffn,
    mamba_z,
    mamba_x,
    mamba_bc,
    mamba_dt,
    conv_x,
    conv_bc,
    a_log,
    dt_bias,
    skip_gain,
    mamba_out,
    attn_query,
    attn_key,
    attn_value,
    attn_out,
    ffn_gate,
    ffn_up,
    ffn_down,
):
    own = hidden_in.shape[0]
    width = hidden_in.shape[1]
    nz, n_p = lax.axis_size("z"), lax.axis_size("p")
    zi, pi, ci = lax.axis_index("z"), lax.axis_index("p"), lax.axis_index("head")
    tok = own * n_p
    base = zi * tok
    positions = base + jnp.arange(tok, dtype=jnp.int32)
    edge = conv_x.shape[0] - 1
    ext_docs = doc_ids(base - edge + jnp.arange(tok + edge, dtype=jnp.int32), doc_starts)
    docs_here = ext_docs[edge:]
    prev_doc = ext_docs[edge - 1]
    rows = mamba_z.shape[0]
    n_heads = a_log.shape[0] // n_p
    xw = n_heads * MHDIM
    bcw = mamba_bc.shape[1] // (2 * n_p)
    kw = HDIM // n_p
    hk = kw // 2
    nchunk = tok // SPAN
    score_scale = HDIM ** (-0.5)

    def cols(w):
        w = w.astype(bf16)
        return w.reshape(w.shape[0], n_p, -1).transpose(1, 0, 2)

    def perm_cols(w):
        w = w.astype(bf16).reshape(rows, 2, n_p, hk)
        return w.transpose(2, 0, 1, 3).reshape(n_p, rows, kw)

    bc_mine = lax.dynamic_slice_in_dim(mamba_bc, ci * (bcw * n_p), bcw * n_p, 1)
    dt_cols = jnp.pad(cols(mamba_dt), ((0, 0), (0, 0), (0, 128 - n_heads)))
    q_cols = attn_query.astype(bf16).reshape(rows, n_p, 2, n_p, hk)
    q_cols = q_cols.transpose(1, 0, 3, 2, 4).reshape(n_p, rows, HDIM)
    pieces = [
        jnp.concatenate(
            [cols(mamba_x), cols(bc_mine), perm_cols(attn_key), cols(attn_value), dt_cols], axis=2
        ),
        jnp.concatenate([q_cols, cols(mamba_z)], axis=2),
        jnp.concatenate([cols(mamba_out.T), cols(attn_out.T)], axis=2),
        jnp.concatenate([cols(ffn_gate), cols(ffn_up)], axis=2),
        cols(ffn_down.T),
    ]

    def fetch(piece):
        piece = lax.all_to_all(piece, "p", 0, 0, tiled=True)
        piece = piece.reshape(n_p * rows, piece.shape[2])
        return lax.all_gather(piece, "z", axis=0, tiled=True)

    w_a, w_b, w_c, w_d, w_e = [fetch(piece) for piece in pieces]

    gains = lax.all_gather(
        jnp.stack([norm_mixer, norm_ffn]).astype(bf16), ("z", "p"), axis=1, tiled=True
    )
    gain_mix, gain_ffn = gains[0], gains[1]
    scale_one, normed_own = norm_rows(hidden_in, gain_mix)
    both = lax.all_gather(
        jnp.stack([normed_own, grad_out.astype(bf16)]), "p", axis=1, tiled=True
    )
    normed_one, g_ffn = both[0], both[1]

    in_a = product(normed_one, w_a)
    in_b = product(normed_one, w_b)
    pre = in_a[:, : xw + bcw].astype(bf16)
    dt_raw = in_a[:, xw + bcw + 2 * kw : xw + bcw + 2 * kw + n_heads]
    gate_z = in_b[:, HDIM:]
    taps = jnp.concatenate(
        [
            lax.dynamic_slice_in_dim(conv_x, pi * xw, xw, 1),
            lax.dynamic_slice_in_dim(conv_bc, (ci * n_p + pi) * bcw, bcw, 1),
        ],
        axis=1,
    )
    prev_rows = passed_along(pre[tok - edge :], "z", 1)
    ext = jnp.concatenate([prev_rows, pre], axis=0)
    conv_in = convolve(ext, taps, ext_docs, tok)
    ssm = jax.nn.silu(conv_in).astype(bf16)
    head_slice = lambda v: lax.dynamic_slice_in_dim(v, pi * n_heads, n_heads, 0)
    my_bias, my_a, my_skip = head_slice(dt_bias), head_slice(a_log), head_slice(skip_gain)
    dt_pre = dt_raw + my_bias[None, :]
    dt_val = jax.nn.softplus(dt_pre)
    log_decay = -jnp.exp(my_a)[None, :] * dt_val
    x_heads = ssm[:, :xw].astype(f32).reshape(tok, n_heads, MHDIM)
    bc_all = lax.all_gather(ssm[:, xw:], ("p", "head"), axis=0)
    bc_all = bc_all.reshape(n_p, 2, tok, bcw).transpose(1, 2, 0, 3).reshape(2, tok, n_p * bcw)
    b_mat, c_mat = bc_all[0].astype(f32), bc_all[1].astype(f32)
    pair_ids = pi * hk + jnp.arange(hk)
    cos_k, sin_k = rope_tables(positions, pair_ids)
    k_pre = in_a[:, xw + bcw : xw + bcw + kw]
    k0, k1 = k_pre[:, :hk], k_pre[:, hk:]
    key_own = jnp.concatenate([k0 * cos_k - k1 * sin_k, k1 * cos_k + k0 * sin_k], axis=1)
    val_own = in_a[:, xw + bcw + kw : xw + bcw + 2 * kw]
    kv_own = jnp.concatenate([key_own, val_own], axis=1).astype(bf16)
    kv = lax.all_gather(kv_own, ("z", "p"), axis=0)
    kv = kv.reshape(nz, n_p, tok, 2 * kw).transpose(0, 2, 1, 3).reshape(nz * tok, n_p, 2 * kw)
    keys = kv[:, :, :kw].reshape(nz * tok, HDIM)
    values = kv[:, :, kw:].reshape(nz * tok, HDIM)
    cos_q, sin_q = rope_tables(positions, jnp.arange(HDIM // 2))
    cos_q, sin_q = cos_q.reshape(tok, n_p, hk), sin_q.reshape(tok, n_p, hk)

    def rope_q(v, sign):
        v = v.reshape(tok, n_p, 2, hk)
        a, b = v[:, :, 0], v[:, :, 1]
        return jnp.stack(
            [a * cos_q - sign * b * sin_q, b * cos_q + sign * a * sin_q], axis=2
        ).reshape(tok, HDIM)

    queries = rope_q(in_b[:, :HDIM], 1.0).astype(bf16)

    span_prev = jnp.concatenate([prev_doc[None], docs_here[SPAN - 1 :: SPAN][:-1]])

    def spanned(v):
        return v.reshape((nchunk, SPAN) + v.shape[1:])

    def forward_step(state_in, inputs):
        xs_c, b_c, c_c, dt_c, la_c, docs_c, before = inputs
        y_c, state_out = span_ssd(state_in, xs_c, b_c, c_c, dt_c, la_c, docs_c, before)
        return (state_out, (y_c, state_in))

    local_state, (y_spans, span_starts) = lax.scan(
        forward_step,
        jnp.zeros((n_heads, MHDIM, NSTATE), f32),
        (
            spanned(x_heads),
            spanned(b_mat),
            spanned(c_mat),
            spanned(dt_val),
            spanned(log_decay),
            spanned(docs_here),
            span_prev,
        ),
    )
    cum_dev = jnp.cumsum(log_decay, axis=0)
    dev_decay = jnp.where((docs_here == prev_doc)[:, None], jnp.exp(cum_dev), 0.0)
    total_decay = dev_decay[-1]
    in_decay, in_state = carried_in(
        (total_decay, local_state),
        "z",
        link_states,
        (jnp.ones_like(total_decay), jnp.zeros_like(local_state)),
        False,
    )
    y_carry = jnp.einsum("tn,hpn->thp", c_mat, in_state, precision=top_prec) * dev_decay[:, :, None]
    y_heads = (
        y_spans.reshape(tok, n_heads, MHDIM) + y_carry + my_skip[None, :, None] * x_heads
    )
    y_flat = y_heads.reshape(tok, xw)
    silu_z = jax.nn.silu(gate_z)
    gated = (y_flat * silu_z).astype(bf16)

    key_pos = jnp.arange(nz * tok, dtype=jnp.int32)
    key_docs = doc_ids(key_pos, doc_starts)
    visible = (positions[:, None] >= key_pos[None, :]) & (docs_here[:, None] == key_docs[None, :])
    scores = product_nt(queries, keys) * score_scale
    scores = jnp.where(visible, scores, neg_large)
    row_max = jnp.max(scores, axis=1, keepdims=True)
    weights = jnp.where(visible, jnp.exp(scores - row_max), 0.0)
    row_sum = jnp.sum(weights, axis=1, keepdims=True)
    probs = weights / row_sum
    probs_low = probs.astype(bf16)
    attn_f32 = product(probs_low, values)
    attn_low = attn_f32.astype(bf16)

    def plane_sum(part):
        part = lax.psum_scatter(part, "p", scatter_dimension=0, tiled=True)
        return lax.psum(part, "head")

    mixed = jnp.concatenate([gated, attn_low], axis=1)
    mid = hidden_in + plane_sum(product_nt(mixed, w_c))
    scale_two, normed_two_own = norm_rows(mid, gain_ffn)
    normed_two = lax.all_gather(normed_two_own, "p", axis=0, tiled=True)
    gu = product(normed_two, w_d)
    ffw = gu.shape[1] // 2
    gate_val, up_val = gu[:, :ffw], gu[:, ffw:]
    silu_gate = jax.nn.silu(gate_val)
    activated = (silu_gate * up_val).astype(bf16)
    block_out = mid + plane_sum(product_nt(activated, w_e))

    grad_e = product_t(g_ffn, activated)
    d_act = product(g_ffn, w_e)
    d_gu = jnp.concatenate(
        [d_act * up_val * silu_slope(gate_val), d_act * silu_gate], axis=1
    ).astype(bf16)
    grad_d = product_t(normed_two, d_gu)
    d_two = plane_sum(product_nt(d_gu, w_d))
    d_mid_norm, grad_gain_ffn = norm_back(mid, scale_two, gain_ffn, d_two)
    d_mid = grad_out + d_mid_norm
    g_mid = lax.all_gather(d_mid.astype(bf16), "p", axis=0, tiled=True)
    grad_c = product_t(g_mid, mixed)
    d_mixed = product(g_mid, w_c)
    d_gated = d_mixed[:, :xw]
    d_attn = d_mixed[:, xw:].astype(bf16)
    d_y_flat = d_gated * silu_z
    d_z = (d_gated * y_flat * silu_slope(gate_z)).astype(bf16)
    d_y_heads = d_y_flat.reshape(tok, n_heads, MHDIM)
    grad_skip = jnp.sum(d_y_heads * x_heads, axis=(0, 2))

    d_in_local = jnp.einsum("th,thp,tn->hpn", dev_decay, d_y_heads, c_mat, precision=top_prec)
    out_decay, state_grad = carried_in(
        (total_decay, d_in_local),
        "z",
        link_states,
        (jnp.ones_like(total_decay), jnp.zeros_like(d_in_local)),
        True,
    )
    before_cum = jnp.concatenate([jnp.zeros((1, n_heads), f32), cum_dev[:-1]], axis=0)[::SPAN]
    start_decay = jnp.where((span_prev == prev_doc)[:, None], jnp.exp(before_cum), 0.0)
    true_starts = span_starts + start_decay[:, :, None, None] * in_state[None]

    def back_step(grad_state, inputs):
        start_state, xs_c, b_c, c_c, dt_c, la_c, docs_c, before, dy_c = inputs

        def local_span(state_arg, xs_arg, b_arg, c_arg, dt_arg, la_arg):
            return span_ssd(state_arg, xs_arg, b_arg, c_arg, dt_arg, la_arg, docs_c, before)

        ignored, pullback = jax.vjp(local_span, start_state, xs_c, b_c, c_c, dt_c, la_c)
        span_grad = pullback((dy_c, grad_state))
        return (span_grad[0], span_grad[1:])

    ignored_state, (d_xs_c, d_b_c, d_c_c, d_dt_c, d_la_c) = lax.scan(
        back_step,
        state_grad,
        (
            true_starts,
            spanned(x_heads),
            spanned(b_mat),
            spanned(c_mat),
            spanned(dt_val),
            spanned(log_decay),
            spanned(docs_here),
            span_prev,
            spanned(d_y_heads),
        ),
        reverse=True,
    )
    d_xs = d_xs_c.reshape(tok, n_heads, MHDIM) + my_skip[None, :, None] * d_y_heads
    d_log = d_la_c.reshape(tok, n_heads)
    grad_a_log = jnp.sum(d_log * log_decay, axis=0)
    d_dt_in = (
        d_dt_c.reshape(tok, n_heads) - jnp.exp(my_a)[None, :] * d_log
    ) * jax.nn.sigmoid(dt_pre)
    grad_dt_bias = jnp.sum(d_dt_in, axis=0)
    d_dt_raw = d_dt_in.astype(bf16)
    d_bc = jnp.stack([d_b_c.reshape(tok, NSTATE), d_c_c.reshape(tok, NSTATE)])
    d_bc = d_bc.reshape(2, tok, n_p, bcw).transpose(2, 0, 1, 3).reshape(2 * n_p * tok, bcw)
    d_bc = lax.psum_scatter(d_bc, ("p", "head"), scatter_dimension=0, tiled=True)
    du = jnp.concatenate([d_xs.reshape(tok, xw), d_bc], axis=1) * silu_slope(conv_in)
    d_ext, grad_taps = convolve_back(du, ext, taps, ext_docs, tok)
    next_rows = passed_along(d_ext[:edge], "z", -1)
    d_pre = (d_ext[edge:] + jnp.pad(next_rows, ((tok - edge, 0), (0, 0)))).astype(bf16)

    d_probs = product_nt(d_attn, values)
    delta = jnp.sum(d_attn.astype(f32) * attn_f32, axis=1, keepdims=True)
    d_scores = (probs * (d_probs - delta)).astype(bf16)
    d_query = product(d_scores, keys) * score_scale
    d_key = product_t(d_scores, queries) * score_scale
    d_value = product_t(probs_low, d_attn)
    d_q_pre = rope_q(d_query, -1.0).astype(bf16)
    d_kv = jnp.concatenate(
        [d_key.reshape(nz * tok, n_p, kw), d_value.reshape(nz * tok, n_p, kw)], axis=2
    )
    d_kv = d_kv.reshape(nz, tok, n_p, 2 * kw).transpose(0, 2, 1, 3)
    d_kv = d_kv.reshape(nz * n_p * tok, 2 * kw)
    d_kv = lax.psum_scatter(d_kv, ("z", "p"), scatter_dimension=0, tiled=True)
    dk0, dk1 = d_kv[:, :hk], d_kv[:, hk:kw]
    d_kv_low = jnp.concatenate(
        [dk0 * cos_k + dk1 * sin_k, dk1 * cos_k - dk0 * sin_k, d_kv[:, kw:]], axis=1
    ).astype(bf16)
    d_a = jnp.concatenate(
        [d_pre, d_kv_low, jnp.pad(d_dt_raw, ((0, 0), (0, 128 - n_heads)))], axis=1
    )
    d_b = jnp.concatenate([d_q_pre, d_z], axis=1)
    grad_a = product_t(normed_one, d_a)
    grad_b = product_t(normed_one, d_b)
    d_one = plane_sum(product_nt(d_a, w_a) + product_nt(d_b, w_b))
    d_in_norm, grad_gain_mix = norm_back(hidden_in, scale_one, gain_mix, d_one)
    grad_in = d_mid + d_in_norm

    def give(grad):
        grad = lax.psum_scatter(grad.astype(bf16), "z", scatter_dimension=0, tiled=True)
        grad = grad.reshape(n_p, rows, grad.shape[1])
        return lax.all_to_all(grad, "p", 0, 0, tiled=True).astype(f32)

    ga, gb, gc, gd, ge = [give(g) for g in (grad_a, grad_b, grad_c, grad_d, grad_e)]

    def uncols(g):
        return g.transpose(1, 0, 2).reshape(rows, -1)

    g_x = uncols(ga[:, :, :xw])
    g_bc = lax.all_gather(uncols(ga[:, :, xw : xw + bcw]), "head", axis=1, tiled=True)
    g_k = ga[:, :, xw + bcw : xw + bcw + kw].reshape(n_p, rows, 2, hk)
    g_k = g_k.transpose(1, 2, 0, 3).reshape(rows, HDIM)
    g_v = uncols(ga[:, :, xw + bcw + kw : xw + bcw + 2 * kw])
    g_dt = uncols(ga[:, :, xw + bcw + 2 * kw : xw + bcw + 2 * kw + n_heads])
    g_q = gb[:, :, :HDIM].reshape(n_p, rows, n_p, 2, hk)
    g_q = g_q.transpose(1, 0, 3, 2, 4).reshape(rows, n_p * HDIM)
    g_z = uncols(gb[:, :, HDIM:])
    g_mout = uncols(gc[:, :, :xw]).T
    g_aout = uncols(gc[:, :, xw:]).T
    g_gate = uncols(gd[:, :, :ffw])
    g_up = uncols(gd[:, :, ffw:])
    g_down = uncols(ge).T

    spread_x = lax.dynamic_update_slice(jnp.zeros(conv_x.shape, f32), grad_taps[:, :xw], (0, pi * xw))
    spread_bc = lax.dynamic_update_slice(
        jnp.zeros(conv_bc.shape, f32), grad_taps[:, xw:], (0, (ci * n_p + pi) * bcw)
    )
    per_head = jnp.stack([grad_a_log, grad_dt_bias, grad_skip])
    spread_h = lax.dynamic_update_slice(
        jnp.zeros((3, a_log.shape[0]), f32), per_head, (0, pi * n_heads)
    )
    s_x, s_h, s_mix, s_ffn = lax.psum(
        (spread_x, spread_h, grad_gain_mix, grad_gain_ffn), ("z", "p")
    )
    s_bc = lax.psum(spread_bc, ("z", "p", "head"))
    si = zi * n_p + pi
    s_mix = lax.dynamic_slice_in_dim(s_mix, si * rows, rows, 0)
    s_ffn = lax.dynamic_slice_in_dim(s_ffn, si * rows, rows, 0)
    return (
        block_out,
        grad_in,
        s_mix,
        s_ffn,
        g_z,
        g_x,
        g_bc,
        g_dt,
        s_x,
        s_bc,
        s_h[0],
        s_h[1],
        s_h[2],
        g_mout,
        g_q,
        g_k,
        g_v,
        g_aout,
        g_gate,
        g_up,
        g_down,
    )


def solution(mesh):
    seq, head = mesh.shape["seq"], mesh.shape["head"]
    plane = math.gcd(seq, 4)
    grid = Mesh(mesh.devices.reshape(seq // plane, plane, head), ("z", "p", "head"))
    s = ("z", "p")
    h = "head"
    placed = (
        P(s, None), P(s, None), P(), P(s), P(s), P(s, h), P(s, h), P(s, None), P(s, h),
        P(None, h), P(), P(h), P(h), P(h), P(h, s), P(s, h), P(s, h), P(s, h), P(h, s),
        P(s, h), P(s, h), P(h, s),
    )
    given = (
        P(s, None), P(s, None), P(s), P(s), P(s, h), P(s, h), P(s, None), P(s, h),
        P(None, h), P(), P(h), P(h), P(h), P(h, s), P(s, h), P(s, h), P(s, h), P(h, s),
        P(s, h), P(s, h), P(h, s),
    )
    return jax.shard_map(shards, mesh=grid, in_specs=placed, out_specs=given, check_vma=False)
```

```python
import functools
import math

import jax
import jax.numpy as jnp
from jax import lax
from jax.experimental import pallas as pl
from jax.experimental.pallas import tpu as pltpu
from jax.sharding import Mesh
from jax.sharding import PartitionSpec as P

MHDIM = 64
NSTATE = 256
HDIM = 128
SPAN = 128

eps_norm = 1e-05
rope_base = 100000000000.0
neg_large = -1e30
top_prec = lax.Precision.HIGHEST
bf16 = jnp.bfloat16
f32 = jnp.float32
MESH = pl.DeviceIdType.MESH
VMEM_LIMIT = 56 * 1024 * 1024


def doc_ids(positions, doc_starts):
    return jnp.sum((doc_starts[None, :] <= positions[:, None]).astype(jnp.int32), axis=1) - 1


def product(left, right):
    return jnp.dot(left, right, preferred_element_type=f32)


def product_t(left, right):
    return lax.dot_general(left, right, (((0,), (0,)), ((), ())), preferred_element_type=f32)


def product_nt(left, right):
    return lax.dot_general(left, right, (((1,), (1,)), ((), ())), preferred_element_type=f32)


def silu_slope(values):
    sigma_val = jax.nn.sigmoid(values)
    return sigma_val * (1.0 + values * (1.0 - sigma_val))


def passed_along(block, axis, distance):
    devices = range(lax.axis_size(axis))
    route = [(i - distance, i) for i in devices if i - distance in devices]
    return lax.ppermute(block, axis, route)


def convolve(extended, weights, ext_docs, tok_count):
    edge_rows = weights.shape[0] - 1
    summed = jnp.zeros((tok_count, extended.shape[1]), f32)
    for tap_index in range(weights.shape[0]):
        begin_row = edge_rows - tap_index
        same_doc = (ext_docs[begin_row : begin_row + tok_count] == ext_docs[edge_rows:])[:, None]
        summed = (
            summed
            + jnp.where(same_doc, extended[begin_row : begin_row + tok_count].astype(f32), 0.0)
            * weights[tap_index][None, :]
        )
    return summed


def convolve_back(d_conv, extended, weights, ext_docs, tok_count):
    edge_rows = weights.shape[0] - 1
    d_extended = jnp.zeros((tok_count + edge_rows, d_conv.shape[1]), f32)
    tap_grads = []
    for tap_index in range(weights.shape[0]):
        begin_row = edge_rows - tap_index
        same_doc = (ext_docs[begin_row : begin_row + tok_count] == ext_docs[edge_rows:])[:, None]
        masked_grad = jnp.where(same_doc, d_conv, 0.0)
        tap_grads.append(
            jnp.sum(
                masked_grad * extended[begin_row : begin_row + tok_count].astype(f32), axis=0
            )
        )
        d_extended = d_extended + jnp.pad(
            masked_grad * weights[tap_index][None, :], ((begin_row, edge_rows - begin_row), (0, 0))
        )
    return (d_extended, jnp.stack(tap_grads))


def tri_dot(a, b, dims=((1,), (0,))):
    return lax.dot_general(a, b, (dims, ((), ())), precision=top_prec, preferred_element_type=f32)


def dot_nn(a, b):
    return lax.dot_general(a, b, (((1,), (0,)), ((), ())), preferred_element_type=f32)


def dot_nt(a, b):
    return lax.dot_general(a, b, (((1,), (1,)), ((), ())), preferred_element_type=f32)


def dot_tn(a, b):
    return lax.dot_general(a, b, (((0,), (0,)), ((), ())), preferred_element_type=f32)


def iota2(shape, dim):
    return lax.broadcasted_iota(jnp.int32, shape, dim)


def docs_of(pos, starts_ref):
    count = jnp.where(starts_ref[0] <= pos, 1, 0)
    for i in range(1, starts_ref.shape[0]):
        count = count + jnp.where(starts_ref[i] <= pos, 1, 0)
    return count - 1


def softplus(v):
    return jnp.maximum(v, 0.0) + jnp.log(1.0 + jnp.exp(-jnp.abs(v)))


def head_maps(xw):
    lane_head = (iota2((128, xw), 1) // MHDIM == iota2((128, xw), 0)).astype(f32)
    row_head = (iota2((xw, 128), 0) // MHDIM == iota2((xw, 128), 1)).astype(f32)
    return lane_head, row_head


def span_setup(k, base_ref, starts_ref, dtp, nega):
    first = base_ref[0] + k * SPAN
    t_idx, s_idx = iota2((SPAN, SPAN), 0), iota2((SPAN, SPAN), 1)
    docs_t = docs_of(first + t_idx, starts_ref)
    docs_s = docs_of(first + s_idx, starts_ref)
    linked = (docs_t == docs_s) & (t_idx >= s_idx)
    dt = softplus(dtp)
    la = nega * dt
    tri = (t_idx >= s_idx).astype(f32)
    cum = tri_dot(tri, la)
    before = docs_of(first - 1, starts_ref)
    last_doc = docs_of(first + SPAN - 1, starts_ref)
    carried = jnp.where(docs_t == before, jnp.exp(cum), 0.0)
    cum_last = cum[SPAN - 1 : SPAN, :]
    tail = jnp.where(docs_t == last_doc, jnp.exp(cum_last - cum), 0.0)
    return docs_t, linked, dt, la, tri, cum, carried, tail


def ssd_forward_kernel(
    n_heads, base_ref, starts_ref, x_ref, b_ref, c_ref, dtp_ref, nega_ref, skip_ref,
    y_ref, span_ref, final_ref, decay_ref, state, running,
):
    k = pl.program_id(0)
    xw = n_heads * MHDIM

    @pl.when(k == 0)
    def _():
        state[...] = jnp.zeros_like(state)
        running[...] = jnp.zeros_like(running)

    docs_t, linked, dt, la, tri, cum, carried, tail = span_setup(
        k, base_ref, starts_ref, dtp_ref[...], nega_ref[...]
    )
    lane_head, row_head = head_maps(xw)
    prev_doc = docs_of(base_ref[0] - 1, starts_ref)
    decay_ref[...] = jnp.where(docs_t == prev_doc, jnp.exp(running[0:1, :] + cum), 0.0)
    running[...] = running[...] + cum[SPAN - 1 : SPAN, :]
    start = state[...]
    span_ref[0] = start
    x, b, c = x_ref[...], b_ref[...], c_ref[...]
    inner = dot_nt(c, b)
    cum_t, dt_t = cum.T, dt.T
    lane = iota2((SPAN, 128), 1)
    pieces = []
    for pair in range(n_heads // 2):
        xp = x[:, pair * 128 : pair * 128 + 128]
        got = []
        for h in (2 * pair, 2 * pair + 1):
            gap = jnp.where(linked, cum[:, h : h + 1] - cum_t[h : h + 1, :], neg_large)
            w = jnp.exp(gap) * inner * dt_t[h : h + 1, :]
            got.append(dot_nn(w.astype(bf16), xp))
        pieces.append(jnp.where(lane < MHDIM, got[0], got[1]))
    y = jnp.concatenate(pieces, axis=1)
    y = y + dot_nt(c, start.astype(bf16)) * tri_dot(carried, lane_head)
    xf = x.astype(f32)
    y_ref[...] = y + skip_ref[...] * xf
    xt = (xf * tri_dot(tail * dt, lane_head)).astype(bf16)
    keep = jnp.sum(row_head * carried[SPAN - 1 : SPAN, :], axis=1, keepdims=True)
    new = dot_tn(xt, b) + keep * start
    state[...] = new
    final_ref[...] = new


def ssd_forward(base, doc_starts, x, b, c, dtp, nega, skip):
    tok, xw = x.shape
    n_heads, nspan = xw // MHDIM, tok // SPAN
    row = lambda n: pl.BlockSpec((SPAN, n), lambda i: (i, 0))
    whole = lambda *s: pl.BlockSpec(s, lambda i: (0,) * len(s))
    smem = pl.BlockSpec(memory_space=pltpu.SMEM)
    return pl.pallas_call(
        functools.partial(ssd_forward_kernel, n_heads),
        grid=(nspan,),
        in_specs=[
            smem, smem, row(xw), row(NSTATE), row(NSTATE), row(128), whole(1, 128), whole(1, xw)
        ],
        out_specs=[
            row(xw),
            pl.BlockSpec((1, xw, NSTATE), lambda i: (i, 0, 0)),
            whole(xw, NSTATE),
            row(128),
        ],
        out_shape=[
            jax.ShapeDtypeStruct((tok, xw), f32),
            jax.ShapeDtypeStruct((nspan, xw, NSTATE), f32),
            jax.ShapeDtypeStruct((xw, NSTATE), f32),
            jax.ShapeDtypeStruct((tok, 128), f32),
        ],
        scratch_shapes=[pltpu.VMEM((xw, NSTATE), f32), pltpu.VMEM((8, 128), f32)],
        compiler_params=pltpu.CompilerParams(vmem_limit_bytes=VMEM_LIMIT),
        cost_estimate=pl.CostEstimate(
            flops=2 * tok * xw * NSTATE * 3, bytes_accessed=8 * tok * xw, transcendentals=0
        ),
        name="ssd_forward",
    )(base, doc_starts, x, b, c, dtp, nega, skip)


def ssd_backward_kernel(
    n_heads, base_ref, starts_ref, x_ref, b_ref, c_ref, dtp_ref, dy_ref, span_ref, decay_ref,
    nega_ref, skip_ref, in_ref, grad_ref,
    dx_ref, dbc_ref, ddt_ref, sums_ref, gskip_ref, gstate,
):
    step = pl.program_id(0)
    k = pl.num_programs(0) - 1 - step
    xw = n_heads * MHDIM

    @pl.when(step == 0)
    def _():
        gstate[...] = grad_ref[...]
        sums_ref[...] = jnp.zeros_like(sums_ref)
        gskip_ref[...] = jnp.zeros_like(gskip_ref)

    nega = nega_ref[...]
    docs_t, linked, dt, la, tri, cum, carried, tail = span_setup(
        k, base_ref, starts_ref, dtp_ref[...], nega
    )
    lane_head, row_head = head_maps(xw)
    begin = jnp.sum(row_head * decay_ref[0], axis=1, keepdims=True)
    start = span_ref[0] + begin * in_ref[...]
    start_low = start.astype(bf16)
    g = gstate[...]
    g_low = g.astype(bf16)
    x, b, c, dy = x_ref[...], b_ref[...], c_ref[...], dy_ref[...]
    dy_low = dy.astype(bf16)
    xf = x.astype(f32)
    inner = dot_nt(c, b)
    cum_t, dt_t = cum.T, dt.T
    lane = iota2((SPAN, 128), 1)
    row8 = iota2((SPAN, 128), 0)
    d_inner = jnp.zeros((SPAN, SPAN), f32)
    r_cols = jnp.zeros((SPAN, 128), f32)
    k_rows = jnp.zeros((SPAN, 128), f32)
    u_pieces = []
    for pair in range(n_heads // 2):
        xp = x[:, pair * 128 : pair * 128 + 128]
        dyp = dy_low[:, pair * 128 : pair * 128 + 128]
        got = []
        for j, h in enumerate((2 * pair, 2 * pair + 1)):
            mine = (lane < MHDIM) if j == 0 else (lane >= MHDIM)
            gap = jnp.where(linked, cum[:, h : h + 1] - cum_t[h : h + 1, :], neg_large)
            e = jnp.exp(gap)
            m = e * inner
            dyx = dot_nt(dyp, jnp.where(mine, xp, jnp.zeros_like(xp)))
            ed = dyx * dt_t[h : h + 1, :]
            d_inner = d_inner + e * ed
            pairs = m * ed
            r_cols = jnp.where(lane == h, jnp.sum(pairs, axis=1, keepdims=True), r_cols)
            k_rows = jnp.where(row8 == h, jnp.sum(pairs, axis=0, keepdims=True), k_rows)
            got.append(dot_tn(m.astype(bf16), dyp))
        u_pieces.append(jnp.where(lane < MHDIM, got[0], got[1]))
    u = jnp.concatenate(u_pieces, axis=1)
    dye = dy * tri_dot(carried, lane_head)
    dye_low = dye.astype(bf16)
    di_low = d_inner.astype(bf16)
    r_state = tri_dot(dye * dot_nt(c, start_low), row_head)
    u_state = dot_nt(b, g_low) * tri_dot(tail, lane_head)
    u = u + u_state
    dt_full = tri_dot(dt, lane_head)
    k_state = dt * tri_dot(xf * u_state, row_head)
    d_dt = tri_dot(xf * u, row_head)
    tail_x = (xf * tri_dot(tail * dt, lane_head)).astype(bf16)
    dx_ref[...] = dt_full * u + skip_ref[...] * dy
    dbc_ref[:, :NSTATE] = dot_nn(tail_x, g_low) + dot_tn(di_low, c)
    dbc_ref[:, NSTATE:] = dot_nn(dye_low, start_low) + dot_nn(di_low, b)
    gs = jnp.sum(g * start, axis=1, keepdims=True)
    gs_row = jnp.sum(row_head * gs, axis=0, keepdims=True)
    last = jnp.sum(k_state, axis=0, keepdims=True) + carried[SPAN - 1 : SPAN, :] * gs_row
    d_cum = r_cols - k_rows.T + r_state - k_state + jnp.where(row8 == SPAN - 1, last, 0.0)
    d_la = tri_dot(tri, d_cum, ((0,), (0,)))
    live = lane < n_heads
    dtp = dtp_ref[...]
    d_in = jnp.where(live, (d_dt + nega * d_la) * jax.nn.sigmoid(dtp), 0.0)
    ddt_ref[...] = d_in
    sum_a = jnp.sum(jnp.where(live, d_la * la, 0.0), axis=0, keepdims=True)
    sum_b = jnp.sum(d_in, axis=0, keepdims=True)
    pick = iota2((8, 128), 0)
    sums_ref[...] += jnp.where(pick == 0, sum_a, jnp.where(pick == 1, sum_b, 0.0))
    gskip_ref[...] += jnp.sum(dy * xf, axis=0, keepdims=True)
    keep = jnp.sum(row_head * carried[SPAN - 1 : SPAN, :], axis=1, keepdims=True)
    gstate[...] = keep * g + dot_tn(dye_low, c)


def ssd_backward(
    base, doc_starts, x, b, c, dtp, dy, span_starts, start_decay, nega, skip, in_state, grad_state
):
    tok, xw = x.shape
    n_heads, nspan = xw // MHDIM, tok // SPAN
    row = lambda n: pl.BlockSpec((SPAN, n), lambda i: (nspan - 1 - i, 0))
    whole = lambda *s: pl.BlockSpec(s, lambda i: (0,) * len(s))
    smem = pl.BlockSpec(memory_space=pltpu.SMEM)
    return pl.pallas_call(
        functools.partial(ssd_backward_kernel, n_heads),
        grid=(nspan,),
        in_specs=[
            smem, smem, row(xw), row(NSTATE), row(NSTATE), row(128), row(xw),
            pl.BlockSpec((1, xw, NSTATE), lambda i: (nspan - 1 - i, 0, 0)),
            pl.BlockSpec((1, 1, 128), lambda i: (nspan - 1 - i, 0, 0)),
            whole(1, 128), whole(1, xw), whole(xw, NSTATE), whole(xw, NSTATE),
        ],
        out_specs=[row(xw), row(2 * NSTATE), row(128), whole(8, 128), whole(1, xw)],
        out_shape=[
            jax.ShapeDtypeStruct((tok, xw), f32),
            jax.ShapeDtypeStruct((tok, 2 * NSTATE), f32),
            jax.ShapeDtypeStruct((tok, 128), f32),
            jax.ShapeDtypeStruct((8, 128), f32),
            jax.ShapeDtypeStruct((1, xw), f32),
        ],
        scratch_shapes=[pltpu.VMEM((xw, NSTATE), f32)],
        compiler_params=pltpu.CompilerParams(vmem_limit_bytes=VMEM_LIMIT),
        cost_estimate=pl.CostEstimate(
            flops=2 * tok * xw * NSTATE * 8, bytes_accessed=16 * tok * xw, transcendentals=0
        ),
        name="ssd_backward",
    )(base, doc_starts, x, b, c, dtp, dy, span_starts, start_decay, nega, skip, in_state, grad_state)


QB = 256
KB = 512


def seen(base_ref, starts_ref, q_first, k_first):
    q_pos = base_ref[0] + q_first + iota2((QB, KB), 0)
    k_pos = k_first + iota2((QB, KB), 1)
    return (q_pos >= k_pos) & (docs_of(q_pos, starts_ref) == docs_of(k_pos, starts_ref))


def attend_kernel(scale, base_ref, starts_ref, q_ref, k_ref, v_ref, o_ref, lse_ref):
    i = pl.program_id(0)
    q = q_ref[...]
    blocks = (base_ref[0] + (i + 1) * QB + KB - 1) // KB

    def turn(j, carry):
        m, l, acc = carry
        at = pl.ds(pl.multiple_of(j * KB, KB), KB)
        s = dot_nt(q, k_ref[at, :]) * scale
        visible = seen(base_ref, starts_ref, i * QB, j * KB)
        s = jnp.where(visible, s, neg_large)
        m_new = jnp.maximum(m, jnp.max(s, axis=1, keepdims=True))
        w = jnp.where(visible, jnp.exp(s - m_new), 0.0)
        r = jnp.exp(m - m_new)
        l = l * r + jnp.sum(w, axis=1, keepdims=True)
        return m_new, l, acc * r + dot_nn(w.astype(bf16), v_ref[at, :])

    m, l, acc = lax.fori_loop(
        0,
        blocks,
        turn,
        (jnp.full((QB, 1), neg_large, f32), jnp.zeros((QB, 1), f32), jnp.zeros((QB, HDIM), f32)),
    )
    o_ref[...] = acc / l
    lse_ref[...] = jnp.broadcast_to(m + jnp.log(l), (QB, 128))


def attend(base, doc_starts, q, k, v):
    tok = q.shape[0]
    row = pl.BlockSpec((QB, HDIM), lambda i: (i, 0))
    whole = pl.BlockSpec(k.shape, lambda i: (0, 0))
    smem = pl.BlockSpec(memory_space=pltpu.SMEM)
    return pl.pallas_call(
        functools.partial(attend_kernel, HDIM ** (-0.5)),
        grid=(tok // QB,),
        in_specs=[smem, smem, row, whole, whole],
        out_specs=[row, row],
        out_shape=[jax.ShapeDtypeStruct((tok, HDIM), f32)] * 2,
        compiler_params=pltpu.CompilerParams(vmem_limit_bytes=VMEM_LIMIT),
        cost_estimate=pl.CostEstimate(
            flops=4 * tok * k.shape[0] * HDIM, bytes_accessed=8 * k.size, transcendentals=0
        ),
        name="attend",
    )(base, doc_starts, q, k, v)


def attend_back_kernel(
    scale, base_ref, starts_ref, q_ref, do_ref, o_ref, lse_ref, k_ref, v_ref,
    dq_ref, dk_ref, dv_ref,
):
    i = pl.program_id(0)

    @pl.when(i == 0)
    def _():
        dk_ref[...] = jnp.zeros_like(dk_ref)
        dv_ref[...] = jnp.zeros_like(dv_ref)

    q, do = q_ref[...], do_ref[...]
    delta = jnp.sum(do.astype(f32) * o_ref[...], axis=1, keepdims=True)
    lse = lse_ref[:, 0:1]
    blocks = (base_ref[0] + (i + 1) * QB + KB - 1) // KB

    def turn(j, dq):
        at = pl.ds(pl.multiple_of(j * KB, KB), KB)
        k, v = k_ref[at, :], v_ref[at, :]
        visible = seen(base_ref, starts_ref, i * QB, j * KB)
        s = dot_nt(q, k) * scale
        p = jnp.exp(jnp.where(visible, s - lse, neg_large))
        ds = (p * (dot_nt(do, v) - delta)).astype(bf16)
        dv_ref[at, :] += dot_tn(p.astype(bf16), do)
        dk_ref[at, :] += dot_tn(ds, q) * scale
        return dq + dot_nn(ds, k)

    dq_ref[...] = lax.fori_loop(0, blocks, turn, jnp.zeros((QB, HDIM), f32)) * scale


def attend_back(base, doc_starts, q, do, o, lse, k, v):
    tok = q.shape[0]
    row = pl.BlockSpec((QB, HDIM), lambda i: (i, 0))
    whole = pl.BlockSpec(k.shape, lambda i: (0, 0))
    smem = pl.BlockSpec(memory_space=pltpu.SMEM)
    return pl.pallas_call(
        functools.partial(attend_back_kernel, HDIM ** (-0.5)),
        grid=(tok // QB,),
        in_specs=[smem, smem, row, row, row, row, whole, whole],
        out_specs=[row, whole, whole],
        out_shape=[
            jax.ShapeDtypeStruct((tok, HDIM), f32),
            jax.ShapeDtypeStruct(k.shape, f32),
            jax.ShapeDtypeStruct(k.shape, f32),
        ],
        compiler_params=pltpu.CompilerParams(vmem_limit_bytes=VMEM_LIMIT),
        cost_estimate=pl.CostEstimate(
            flops=10 * tok * k.shape[0] * HDIM, bytes_accessed=20 * k.size, transcendentals=0
        ),
        name="attend_back",
    )(base, doc_starts, q, do, o, lse, k, v)


def at_rows(first, count):
    return pl.ds(pl.multiple_of(first, count), count)


def place():
    return lax.axis_index("z"), lax.axis_index("p"), lax.axis_index("head")


def hop(p, d):
    x, y = lax.rem(p, 2), p // 2
    return lax.rem(y + d // 2, 2) * 2 + lax.rem(x + d % 2, 2)


def chip(z, p, c):
    return (z, p, c)


def meet(others):
    barrier = pltpu.get_barrier_semaphore()
    for other in others:
        pl.semaphore_signal(barrier, inc=1, device_id=other, device_id_type=MESH)
    pl.semaphore_wait(barrier, len(others))


def send(src, dst, send_sem, recv_sem, to):
    copy = pltpu.make_async_remote_copy(
        src_ref=src, dst_ref=dst, send_sem=send_sem, recv_sem=recv_sem,
        device_id=to, device_id_type=MESH,
    )
    copy.start()
    return copy


HOPS = (3, 1, 2)


def share_rows(full_ref, half, own_sems, far_sems, near_sems):
    z, p, c = place()
    other = chip(z, p, 1 - c)
    mine = full_ref.at[at_rows((p * 2 + c) * half, half), :]
    copies = []
    for i, d in enumerate(HOPS):
        copies.append(send(mine, mine, far_sems.at[0, i], far_sems.at[1, i], chip(z, hop(p, d), c)))
    copies.append(send(mine, mine, own_sems.at[0], own_sems.at[1], other))
    onward = []
    for i, d in ((1, 1), (2, 2), (0, 3)):
        copies[i].wait_recv()
        came = full_ref.at[at_rows((hop(p, d) * 2 + c) * half, half), :]
        onward.append(send(came, came, near_sems.at[0, i], near_sems.at[1, i], other))
    return copies, onward


def finish_share(copies, onward):
    for copy in copies[:3]:
        copy.wait_send()
    copies[3].wait()
    for copy in onward:
        copy.wait()


def reduce_blocks(pairs, part, keep, sib_out, sib_in, out, came, near_sems, far_sems):
    z, p, c = place()
    other = chip(z, p, 1 - c)
    half = keep.shape[1]
    width = keep.shape[2]
    tile = part.shape[1]
    near, far = [], []

    def pass_on(i, d):
        near[i].wait_recv()

        @pl.loop(0, half // 16)
        def _(r):
            at = at_rows(r * 16, 16)
            out[i, at, :] = (keep[i, at, :] + sib_in[i, at, :].astype(f32)).astype(bf16)

        far.append(
            send(out.at[i], came.at[i], far_sems.at[0, i], far_sems.at[1, i], chip(z, hop(p, d), c))
        )

    order = HOPS + (0,)
    for i, d in enumerate(order):
        rows = at_rows(hop(p, d) * (2 * half), 2 * half)

        @pl.loop(0, width // tile)
        def _(n):
            cols = at_rows(n * tile, tile)
            total = dot_nt(pairs[0][0][rows, :], pairs[0][1][cols, :])
            for left, right in pairs[1:]:
                total = total + dot_nt(left[rows, :], right[cols, :])
            part[...] = total
            keep[i, :, cols] = part[at_rows(c * half, half), :]
            sib_out[i, :, cols] = part[at_rows((1 - c) * half, half), :].astype(bf16)

        near.append(
            send(sib_out.at[i], sib_in.at[i], near_sems.at[0, i], near_sems.at[1, i], other)
        )
        if i:
            pass_on(i - 1, order[i - 1])
    near[3].wait_recv()
    for copy in far:
        copy.wait_recv()

    def total_rows(at):
        total = keep[3, at, :] + sib_in[3, at, :].astype(f32)
        return total + came[0, at, :].astype(f32) + came[1, at, :].astype(f32) + came[2, at, :].astype(f32)

    def done():
        for copy in near + far:
            copy.wait_send()

    return total_rows, done


def greet():
    z, p, c = place()
    meet([chip(z, p, 1 - c)] + [chip(z, hop(p, d), c) for d in HOPS])


def rms(rows):
    return lax.rsqrt(jnp.mean(rows * rows, axis=1, keepdims=True) + eps_norm)


def mid_kernel(
    left, right, resid, gain, mid_ref, full_ref,
    part, keep, sib_out, sib_in, out, came, n_sems, f_sems, own_sems, far_sems, near_sems,
):
    greet()
    z, p, c = place()
    half = keep.shape[1]
    total_rows, done = reduce_blocks(
        [(left, right)], part, keep, sib_out, sib_in, out, came, n_sems, f_sems
    )
    g = gain[...]

    @pl.loop(0, half // 16)
    def _(r):
        at = at_rows(r * 16, 16)
        mid = resid[at, :] + total_rows(at)
        mid_ref[at, :] = mid
        full_ref[at_rows((p * 2 + c) * half + r * 16, 16), :] = (mid * rms(mid) * g).astype(bf16)

    copies, onward = share_rows(full_ref, half, own_sems, far_sems, near_sems)
    done()
    finish_share(copies, onward)


def two_kernel(
    left, right, mid_own, grad_own, gain, dmid_ref, ggain_ref, full_ref,
    part, keep, sib_out, sib_in, out, came, n_sems, f_sems, own_sems, far_sems, near_sems,
):
    greet()
    z, p, c = place()
    half = keep.shape[1]
    total_rows, done = reduce_blocks(
        [(left, right)], part, keep, sib_out, sib_in, out, came, n_sems, f_sems
    )
    g = gain[...]
    ggain_ref[...] = jnp.zeros_like(ggain_ref)

    @pl.loop(0, half // 16)
    def _(r):
        at = at_rows(r * 16, 16)
        d_two, mid = total_rows(at), mid_own[at, :]
        scale = rms(mid)
        w = d_two * g
        d_mid = grad_own[at, :] + scale * w - mid * (scale * scale * scale) * jnp.mean(
            w * mid, axis=1, keepdims=True
        )
        ggain_ref[...] += jnp.sum(d_two * mid * scale, axis=0, keepdims=True)
        dmid_ref[at, :] = d_mid
        full_ref[at_rows((p * 2 + c) * half + r * 16, 16), :] = d_mid.astype(bf16)

    copies, onward = share_rows(full_ref, half, own_sems, far_sems, near_sems)
    done()
    finish_share(copies, onward)


def one_kernel(
    left_a, right_a, left_b, right_b, hidden_own, dmid_own, gain, grad_ref, ggain_ref,
    part, keep, sib_out, sib_in, out, came, n_sems, f_sems, own_sems,
):
    greet()
    z, p, c = place()
    half = keep.shape[1]
    total_rows, done = reduce_blocks(
        [(left_a, right_a), (left_b, right_b)],
        part, keep, sib_out, sib_in, out, came, n_sems, f_sems,
    )
    g = gain[...]
    ggain_ref[...] = jnp.zeros_like(ggain_ref)

    @pl.loop(0, half // 16)
    def _(r):
        at = at_rows(r * 16, 16)
        d_one, hid = total_rows(at), hidden_own[at, :]
        scale = rms(hid)
        w = d_one * g
        d_in = dmid_own[at, :] + scale * w - hid * (scale * scale * scale) * jnp.mean(
            w * hid, axis=1, keepdims=True
        )
        ggain_ref[...] += jnp.sum(d_one * hid * scale, axis=0, keepdims=True)
        grad_ref[at_rows(c * half + r * 16, 16), :] = d_in

    mine = grad_ref.at[at_rows(c * half, half), :]
    copy = send(mine, mine, own_sems.at[0], own_sems.at[1], chip(z, p, 1 - c))
    done()
    copy.wait()


VM = pl.BlockSpec(memory_space=pltpu.VMEM)


def reduce_scratch(half, width):
    return [
        pltpu.VMEM((2 * half, 512), f32),
        pltpu.VMEM((4, half, width), f32),
        pltpu.VMEM((4, half, width), bf16),
        pltpu.VMEM((4, half, width), bf16),
        pltpu.VMEM((3, half, width), bf16),
        pltpu.VMEM((3, half, width), bf16),
        pltpu.SemaphoreType.DMA((2, 4)),
        pltpu.SemaphoreType.DMA((2, 3)),
    ]


SHARE_SEMS = [
    pltpu.SemaphoreType.DMA((2,)),
    pltpu.SemaphoreType.DMA((2, 3)),
    pltpu.SemaphoreType.DMA((2, 3)),
]


def plane_call(kernel, name, number, args, shapes, scratch, flops=0):
    return pl.pallas_call(
        kernel,
        in_specs=[VM] * len(args),
        out_specs=[VM] * len(shapes),
        out_shape=[jax.ShapeDtypeStruct(s, t) for s, t in shapes],
        scratch_shapes=scratch,
        compiler_params=pltpu.CompilerParams(
            collective_id=number, has_side_effects=True, vmem_limit_bytes=VMEM_LIMIT
        ),
        cost_estimate=pl.CostEstimate(flops=flops, bytes_accessed=150_000_000, transcendentals=0),
        name=name,
    )(*args)


def mid_step(mixed, w, resid_own, gain):
    tok, width = mixed.shape[0], w.shape[0]
    half = resid_own.shape[0]
    return plane_call(
        mid_kernel, "mid_step", 1, (mixed, w, resid_own, gain),
        [((half, width), f32), ((tok, width), bf16)],
        reduce_scratch(half, width) + SHARE_SEMS,
    )


def two_step(d_gu, w, mid_own, grad_own, gain):
    tok, width = d_gu.shape[0], w.shape[0]
    half = mid_own.shape[0]
    return plane_call(
        two_kernel, "two_step", 2, (d_gu, w, mid_own, grad_own, gain),
        [((half, width), f32), ((1, width), f32), ((tok, width), bf16)],
        reduce_scratch(half, width) + SHARE_SEMS,
    )


def one_step(d_a, w_a, d_b, w_b, hidden_own, dmid_own, gain):
    width = w_a.shape[0]
    half = hidden_own.shape[0]
    return plane_call(
        one_kernel, "one_step", 3, (d_a, w_a, d_b, w_b, hidden_own, dmid_own, gain),
        [((2 * half, width), f32), ((1, width), f32)],
        reduce_scratch(half, width) + [pltpu.SemaphoreType.DMA((2,))],
    )


def open_kernel(gains_ref, a_ref, gain_out, a_out, z_sems, p_sems, a_sems, loc_sems):
    z, p, c = place()
    nz = gain_out.shape[1]
    ups = [chip(lax.rem(z + d, nz), p, c) for d in range(1, nz)]
    meet(ups + [chip(z, hop(p, d), c) for d in HOPS])
    gain_out[p, z] = gains_ref[...]
    copies = []
    for d in range(1, nz):
        copies.append(
            send(gain_out.at[p, z], gain_out.at[p, z], z_sems.at[0, d - 1], z_sems.at[1, d - 1], ups[d - 1])
        )
    for i, d in enumerate(HOPS):
        q = hop(p, d)
        copies.append(
            send(a_ref.at[q], a_out.at[p], a_sems.at[0, i], a_sems.at[1, i], chip(z, q, c))
        )
    local = pltpu.make_async_copy(a_ref.at[p], a_out.at[p], loc_sems.at[0])
    local.start()
    for copy in copies[: nz - 1]:
        copy.wait_recv()
    late = []
    for i, d in enumerate(HOPS):
        late.append(
            send(gain_out.at[p], gain_out.at[p], p_sems.at[0, i], p_sems.at[1, i], chip(z, hop(p, d), c))
        )
    for copy in copies[: nz - 1]:
        copy.wait_send()
    for copy in copies[nz - 1 :] + late:
        copy.wait()
    local.wait()


def open_step(gains, piece, nz):
    n_p = piece.shape[0]
    return plane_call(
        open_kernel, "open_step", 4, (gains, piece),
        [((n_p, nz) + gains.shape, f32), (piece.shape, bf16)],
        [
            pltpu.SemaphoreType.DMA((2, nz - 1)),
            pltpu.SemaphoreType.DMA((2, 3)),
            pltpu.SemaphoreType.DMA((2, 3)),
            pltpu.SemaphoreType.DMA((1,)),
        ],
    )


def share_kernel(n, *refs):
    hid, grad, gain = refs[:3]
    w_refs, (full_ref, gfull_ref), w_outs = refs[3 : 3 + n], refs[3 + n : 5 + n], refs[5 + n : 5 + 2 * n]
    own_sems, far_sems, near_sems, own_g, far_g, near_g, w_sems, loc_sems = refs[5 + 2 * n :]
    greet()
    z, p, c = place()
    half = hid.shape[0]
    g = gain[...]

    @pl.loop(0, half // 16)
    def _(r):
        at = at_rows(r * 16, 16)
        to = at_rows((p * 2 + c) * half + r * 16, 16)
        rows = hid[at, :]
        full_ref[to, :] = (rows * rms(rows) * g).astype(bf16)
        gfull_ref[to, :] = grad[at, :].astype(bf16)

    local = []
    for j in range(n):
        local.append(pltpu.make_async_copy(w_refs[j].at[p], w_outs[j].at[p], loc_sems.at[j]))
        local[j].start()
    copies, onward = share_rows(full_ref, half, own_sems, far_sems, near_sems)
    moved = []
    for j in range(n):
        for i, d in enumerate(HOPS):
            q = hop(p, d)
            moved.append(
                send(
                    w_refs[j].at[q], w_outs[j].at[p], w_sems.at[0, j, i], w_sems.at[1, j, i],
                    chip(z, q, c),
                )
            )
    copies_g, onward_g = share_rows(gfull_ref, half, own_g, far_g, near_g)
    finish_share(copies, onward)
    finish_share(copies_g, onward_g)
    for copy in moved:
        copy.wait()
    for copy in local:
        copy.wait()


def share_step(hid, grad, gain, rest, tok):
    width, n = hid.shape[1], len(rest)
    anywhere = pl.BlockSpec(memory_space=pl.ANY)
    return pl.pallas_call(
        functools.partial(share_kernel, n),
        in_specs=[VM, VM, VM] + [anywhere] * n,
        out_specs=[VM, VM] + [anywhere] * n,
        out_shape=[jax.ShapeDtypeStruct((tok, width), bf16)] * 2
        + [jax.ShapeDtypeStruct(r.shape, bf16) for r in rest],
        scratch_shapes=SHARE_SEMS
        + SHARE_SEMS
        + [pltpu.SemaphoreType.DMA((2, n, 3)), pltpu.SemaphoreType.DMA((n,))],
        compiler_params=pltpu.CompilerParams(
            collective_id=5, has_side_effects=True, vmem_limit_bytes=VMEM_LIMIT
        ),
        cost_estimate=pl.CostEstimate(flops=0, bytes_accessed=200_000_000, transcendentals=0),
        name="share_step",
    )(hid, grad, gain, *rest)


def sums_kernel(v_ref, out_ref, came, z_sems, p_sems, c_sems):
    z, p, c = place()
    nz = came.shape[0]
    ups = [chip(lax.rem(z + d, nz), p, c) for d in range(1, nz)]
    other = chip(z, p, 1 - c)
    meet(ups + [chip(z, hop(p, d), c) for d in HOPS] + [other])
    copies = []
    for d in range(1, nz):
        copies.append(
            send(v_ref, came.at[d], z_sems.at[0, d - 1], z_sems.at[1, d - 1], ups[d - 1])
        )
    total = v_ref[...]
    for d in range(1, nz):
        copies[d - 1].wait_recv()
        total = total + came[d]
    out_ref[c, p] = total
    far = []
    for i, d in enumerate(HOPS):
        far.append(
            send(out_ref.at[c, p], out_ref.at[c, p], p_sems.at[0, i], p_sems.at[1, i], chip(z, hop(p, d), c))
        )
    for copy in far:
        copy.wait_recv()
    near = send(out_ref.at[c], out_ref.at[c], c_sems.at[0], c_sems.at[1], other)
    for copy in copies + far:
        copy.wait_send()
    near.wait()


def sums_step(v, nz, n_p):
    return plane_call(
        sums_kernel, "sums_step", 6, (v,),
        [((2, n_p) + v.shape, f32)],
        [
            pltpu.VMEM((nz,) + v.shape, f32),
            pltpu.SemaphoreType.DMA((2, nz - 1)),
            pltpu.SemaphoreType.DMA((2, 3)),
            pltpu.SemaphoreType.DMA((2,)),
        ],
    )[0]


def rope_tables(positions, pairs):
    freqs = rope_base ** (-2.0 * pairs.astype(f32) / HDIM)
    angles = positions.astype(f32)[:, None] * freqs[None, :]
    return jnp.cos(angles), jnp.sin(angles)


def plane_swap(x):
    n_p = lax.axis_size("p")
    p = lax.axis_index("p")
    out = x
    for d in range(1, n_p):
        other = jnp.bitwise_xor(p, d)
        block = lax.dynamic_index_in_dim(x, other, 0, keepdims=True)
        came = lax.ppermute(block, "p", [(i, i ^ d) for i in range(n_p)])
        out = lax.dynamic_update_slice_in_dim(out, came, other, 0)
    return out


def plane_gather(x):
    n_p = lax.axis_size("p")
    p = lax.axis_index("p")
    out = jnp.zeros((n_p,) + x.shape, x.dtype)
    out = lax.dynamic_update_slice_in_dim(out, x[None], p, 0)
    for d in range(1, n_p):
        came = lax.ppermute(x, "p", [(i, i ^ d) for i in range(n_p)])
        out = lax.dynamic_update_slice_in_dim(out, came[None], jnp.bitwise_xor(p, d), 0)
    return out


def plane_sum(x):
    n_p = lax.axis_size("p")
    p = lax.axis_index("p")
    total = lax.dynamic_index_in_dim(x, p, 0, keepdims=False).astype(f32)
    for d in range(1, n_p):
        block = lax.dynamic_index_in_dim(x, jnp.bitwise_xor(p, d), 0, keepdims=False)
        came = lax.ppermute(block.astype(bf16), "p", [(i, i ^ d) for i in range(n_p)])
        total = total + came.astype(f32)
    return total


def swap_core(x):
    return lax.ppermute(x, "head", [(0, 1), (1, 0)])


def block_sum(part):
    ci = lax.axis_index("head")
    mine = lax.dynamic_index_in_dim(part, ci, 1, keepdims=False)
    other = lax.dynamic_index_in_dim(part, 1 - ci, 1, keepdims=False)
    return plane_sum(mine + swap_core(other.astype(bf16)).astype(f32))


def join_cores(mine):
    ci = lax.axis_index("head")
    other = swap_core(mine)
    out = jnp.concatenate([mine, mine])
    return lax.dynamic_update_slice_in_dim(out, other, (1 - ci) * mine.shape[0], 0)


def carry_states(state, decays, sign):
    nz = lax.axis_size("z")
    low = state.astype(bf16)
    total, factor = None, None
    for d in range(1, nz):
        route = [(i, i + sign * d) for i in range(nz) if 0 <= i + sign * d < nz]
        came = lax.ppermute(low, "z", route).astype(f32)
        rate = lax.ppermute(decays, "z", route)
        total = came if total is None else total + factor * came
        factor = rate if factor is None else factor * rate
    return total


def shards(
    hidden_in,
    grad_out,
    doc_starts,
    norm_mixer,
    norm_ffn,
    mamba_z,
    mamba_x,
    mamba_bc,
    mamba_dt,
    conv_x,
    conv_bc,
    a_log,
    dt_bias,
    skip_gain,
    mamba_out,
    attn_query,
    attn_key,
    attn_value,
    attn_out,
    ffn_gate,
    ffn_up,
    ffn_down,
):
    own = hidden_in.shape[0]
    width = hidden_in.shape[1]
    half = own // 2
    nz, n_p = lax.axis_size("z"), lax.axis_size("p")
    zi, pi, ci = lax.axis_index("z"), lax.axis_index("p"), lax.axis_index("head")
    tok = own * n_p
    base = zi * tok
    positions = base + jnp.arange(tok, dtype=jnp.int32)
    edge = conv_x.shape[0] - 1
    ext_docs = doc_ids(base - edge + jnp.arange(tok + edge, dtype=jnp.int32), doc_starts)
    rows = mamba_z.shape[0]
    n_heads = a_log.shape[0] // n_p
    xw = n_heads * MHDIM
    bw = mamba_bc.shape[1] // (2 * n_p)
    cw = xw + 2 * bw
    kw = HDIM // n_p
    hk = kw // 2
    tail_w = 128 - 2 * kw - n_heads

    def cols(w):
        w = w.astype(bf16)
        return w.reshape(w.shape[0], n_p, -1).transpose(1, 0, 2)

    k_cols = attn_key.astype(bf16).reshape(rows, 2, n_p, hk)
    k_cols = k_cols.transpose(2, 0, 1, 3).reshape(n_p, rows, kw)
    bc_cols = mamba_bc.astype(bf16).reshape(rows, 2, n_p, bw)
    bc_cols = bc_cols.transpose(2, 0, 1, 3).reshape(n_p, rows, 2 * bw)
    q_cols = attn_query.astype(bf16).reshape(rows, n_p, 2, n_p, hk)
    q_cols = q_cols.transpose(1, 0, 3, 2, 4).reshape(n_p, rows, HDIM)
    piece_a = jnp.concatenate(
        [
            cols(mamba_x), bc_cols, k_cols, cols(attn_value), cols(mamba_dt),
            jnp.zeros((n_p, rows, tail_w), bf16),
        ],
        axis=2,
    )
    rest = [
        jnp.concatenate([q_cols, cols(mamba_z)], axis=2),
        jnp.concatenate([cols(mamba_out.T), cols(attn_out.T)], axis=2),
        jnp.concatenate([cols(ffn_gate), cols(ffn_up)], axis=2),
        cols(ffn_down.T),
    ]

    def along_z(piece):
        piece = piece.reshape(n_p * rows, piece.shape[2])
        return lax.all_gather(piece, "z", axis=0, tiled=True)

    gains_own = jnp.pad(
        jnp.stack([norm_mixer, norm_ffn]).astype(bf16).astype(f32), ((0, 6), (0, 128 - rows))
    )
    gains, piece_a = open_step(gains_own, piece_a, nz)
    w_a = along_z(piece_a)
    gains = gains.transpose(2, 1, 0, 3)[:, :, :, :rows].reshape(8, 1, width)
    gain_mix, gain_ffn = gains[0], gains[1]
    my_half = lambda v: lax.dynamic_slice_in_dim(v, ci * half, half, 0)
    hidden_own, grad_own = my_half(hidden_in), my_half(grad_out)
    normed_one, g_ffn, *rest = share_step(hidden_own, grad_own, gain_mix, rest, tok)
    w_b, w_c, w_d, w_e = [along_z(piece) for piece in rest]

    in_a = product(normed_one, w_a)
    in_b = product(normed_one, w_b)
    pre = in_a[:, :cw].astype(bf16)
    gate_z = in_b[:, HDIM:]
    slice_1 = lambda v, at, n: lax.dynamic_slice_in_dim(v, at, n, 1)
    taps = jnp.concatenate(
        [
            slice_1(conv_x, pi * xw, xw),
            slice_1(conv_bc, pi * bw, bw),
            slice_1(conv_bc, (n_p + pi) * bw, bw),
        ],
        axis=1,
    )
    prev_rows = passed_along(pre[tok - edge :], "z", 1)
    ext = jnp.concatenate([prev_rows, pre], axis=0)
    conv_in = convolve(ext, taps, ext_docs, tok)
    ssm = jax.nn.silu(conv_in).astype(bf16)
    head_slice = lambda v: lax.dynamic_slice_in_dim(v, pi * n_heads, n_heads, 0)
    my_bias, my_a, my_skip = head_slice(dt_bias), head_slice(a_log), head_slice(skip_gain)
    lanes = lambda v: jnp.pad(v, (0, 128 - n_heads))[None, :]
    dt_at = cw + 2 * kw
    dt_pre = jnp.pad(in_a[:, dt_at : dt_at + n_heads], ((0, 0), (0, 128 - n_heads))) + lanes(my_bias)
    neg_rate = lanes(-jnp.exp(my_a))
    skip_full = jnp.repeat(my_skip, MHDIM)[None, :]
    x_low = ssm[:, :xw]
    bc_all = plane_gather(ssm[:, xw:]).reshape(n_p, tok, 2, bw)
    bc_all = bc_all.transpose(2, 1, 0, 3).reshape(2, tok, n_p * bw)
    b_mat, c_mat = bc_all[0], bc_all[1]
    pair_ids = pi * hk + jnp.arange(hk)
    cos_k, sin_k = rope_tables(positions, pair_ids)
    k0, k1 = in_a[:, cw : cw + hk], in_a[:, cw + hk : cw + kw]
    key_own = jnp.concatenate([k0 * cos_k - k1 * sin_k, k1 * cos_k + k0 * sin_k], axis=1)
    val_own = in_a[:, cw + kw : cw + 2 * kw]
    kv_own = jnp.concatenate([key_own, val_own], axis=1).astype(bf16)
    kv = jnp.zeros((nz, tok, 2 * kw), bf16)
    kv = lax.dynamic_update_slice_in_dim(kv, kv_own[None], zi, 0)
    for d in range(1, nz):
        came = passed_along(kv_own, "z", d)
        kv = lax.dynamic_update_slice_in_dim(kv, came[None], (zi - d) % nz, 0)
    kv = plane_gather(kv).transpose(1, 2, 0, 3).reshape(nz * tok, n_p, 2 * kw)
    keys = kv[:, :, :kw].reshape(nz * tok, HDIM)
    values = kv[:, :, kw:].reshape(nz * tok, HDIM)
    cos_q, sin_q = rope_tables(positions, jnp.arange(HDIM // 2))
    cos_q, sin_q = cos_q.reshape(tok, n_p, hk), sin_q.reshape(tok, n_p, hk)

    def rope_q(v, sign):
        v = v.reshape(tok, n_p, 2, hk)
        a, b = v[:, :, 0], v[:, :, 1]
        return jnp.stack(
            [a * cos_q - sign * b * sin_q, b * cos_q + sign * a * sin_q], axis=2
        ).reshape(tok, HDIM)

    queries = rope_q(in_b[:, :HDIM], 1.0).astype(bf16)

    base_arr = jnp.reshape(base, (1,)).astype(jnp.int32)
    y_local, span_starts, local_state, dev_decay = ssd_forward(
        base_arr, doc_starts, x_low, b_mat, c_mat, dt_pre, neg_rate, skip_full
    )
    decay_full = jnp.repeat(dev_decay[:, :n_heads], MHDIM, axis=1)
    total_decay = decay_full[-1][:, None]
    in_state = carry_states(local_state, total_decay, 1)

    attn_f32, lse = attend(base_arr, doc_starts, queries, keys, values)
    attn_low = attn_f32.astype(bf16)
    y_flat = y_local + product_nt(c_mat, in_state.astype(bf16)) * decay_full
    silu_z = jax.nn.silu(gate_z)
    gated = (y_flat * silu_z).astype(bf16)
    mixed = jnp.concatenate([gated, attn_low], axis=1)

    mid_own, normed_two = mid_step(mixed, w_c, hidden_own, gain_ffn)
    gu = product(normed_two, w_d)
    ffw = gu.shape[1] // 2
    gate_val, up_val = gu[:, :ffw], gu[:, ffw:]
    silu_gate = jax.nn.silu(gate_val)
    activated = (silu_gate * up_val).astype(bf16)
    d_act = product(g_ffn, w_e)
    d_gu = jnp.concatenate(
        [d_act * up_val * silu_slope(gate_val), d_act * silu_gate], axis=1
    ).astype(bf16)
    grad_e = product_t(g_ffn, activated).astype(bf16)
    grad_d = product_t(normed_two, d_gu).astype(bf16)
    d_gu, grad_e, grad_d = lax.optimization_barrier((d_gu, grad_e, grad_d))

    def scattered(grad):
        grad = lax.psum_scatter(grad, "z", scatter_dimension=0, tiled=True)
        return plane_swap(grad.reshape(n_p, rows, grad.shape[1])).astype(f32)

    ge = scattered(grad_e)
    gd = scattered(grad_d)
    d_mid_own, grad_gain_ffn, g_mid = two_step(d_gu, w_d, mid_own, grad_own, gain_ffn)
    out_part = product_nt(activated, w_e).reshape(n_p, 2, half, width)
    block_out = join_cores(mid_own + block_sum(out_part))

    d_mixed = product(g_mid, w_c)
    grad_c = product_t(g_mid, mixed).astype(bf16)
    gc = scattered(grad_c)
    d_gated = d_mixed[:, :xw]
    d_attn = d_mixed[:, xw:].astype(bf16)
    d_y_flat = d_gated * silu_z
    d_z = (d_gated * y_flat * silu_slope(gate_z)).astype(bf16)
    d_in_local = product_t((d_y_flat * decay_full).astype(bf16), c_mat)
    state_grad = carry_states(d_in_local, total_decay, -1)
    d_query, d_key, d_value = attend_back(
        base_arr, doc_starts, queries, d_attn, attn_f32, lse, keys, values
    )
    d_q_pre = rope_q(d_query, -1.0).astype(bf16)
    d_b = jnp.concatenate([d_q_pre, d_z], axis=1)
    grad_b = product_t(normed_one, d_b).astype(bf16)
    gb = scattered(grad_b)
    d_kv = jnp.concatenate(
        [d_key.reshape(nz, tok, n_p, kw), d_value.reshape(nz, tok, n_p, kw)], axis=3
    )
    d_kv = plane_sum(d_kv.transpose(2, 0, 1, 3))
    d_kv_own = lax.dynamic_index_in_dim(d_kv, zi, 0, keepdims=False)
    for d in range(1, nz):
        block = lax.dynamic_index_in_dim(d_kv, (zi - d) % nz, 0, keepdims=False)
        d_kv_own = d_kv_own + passed_along(block.astype(bf16), "z", -d).astype(f32)
    dk0, dk1 = d_kv_own[:, :hk], d_kv_own[:, hk:kw]
    d_kv_low = jnp.concatenate(
        [dk0 * cos_k + dk1 * sin_k, dk1 * cos_k - dk0 * sin_k, d_kv_own[:, kw:]], axis=1
    ).astype(bf16)

    start_decay = jnp.concatenate([jnp.ones((1, 128), f32), dev_decay[SPAN - 1 :: SPAN][:-1]])
    d_xs, d_bc, d_dt, sums, skip_sums = ssd_backward(
        base_arr, doc_starts, x_low, b_mat, c_mat, dt_pre, d_y_flat, span_starts,
        start_decay[:, None, :], neg_rate, skip_full, in_state, state_grad,
    )
    d_bc = d_bc.reshape(2, tok // 2, 2, n_p, bw).transpose(3, 0, 1, 2, 4)
    d_bc = join_cores(block_sum(d_bc.reshape(n_p, 2, tok // 2, 2 * bw)))
    du = jnp.concatenate([d_xs, d_bc], axis=1) * silu_slope(conv_in)
    d_ext, grad_taps = convolve_back(du, ext, taps, ext_docs, tok)
    next_rows = passed_along(d_ext[:edge], "z", -1)
    d_pre = (d_ext[edge:] + jnp.pad(next_rows, ((tok - edge, 0), (0, 0)))).astype(bf16)
    d_last = jnp.concatenate(
        [d_kv_low, d_dt[:, :n_heads].astype(bf16), jnp.zeros((tok, tail_w), bf16)], axis=1
    )
    d_a = jnp.concatenate([d_pre, d_last], axis=1)
    grad_a = product_t(normed_one, d_a).astype(bf16)
    ga = scattered(grad_a)
    once = jnp.where(ci == 0, d_pre[:, xw:], jnp.zeros((), bf16))
    d_a_once = jnp.concatenate([d_pre[:, :xw], once, d_last], axis=1)
    d_a_once, grad_a = lax.optimization_barrier((d_a_once, grad_a))
    grad_in, grad_gain_mix = one_step(
        d_a_once, w_a, d_b, w_b, hidden_own, d_mid_own, gain_mix
    )

    flat = jnp.concatenate(
        [
            grad_gain_mix.reshape(-1, 128),
            grad_gain_ffn.reshape(-1, 128),
            grad_taps.reshape(-1, 128),
            sums[:2],
            jnp.pad(jnp.sum(skip_sums.reshape(n_heads, MHDIM), axis=1), (0, 128 - n_heads))[None],
        ]
    )
    flat = jnp.pad(flat, ((0, -flat.shape[0] % 8), (0, 0)))
    summed = sums_step(flat, nz, n_p)
    g_rows = width // 128
    t_rows = grad_taps.size // 128
    si = zi * n_p + pi
    gains_sum = jnp.sum(summed[:, :, : 2 * g_rows], axis=(0, 1)).reshape(2, width)
    gains_sum = lax.dynamic_slice_in_dim(gains_sum, si * rows, rows, 1)
    mine = lax.dynamic_index_in_dim(summed, ci, 0, keepdims=False)
    s_taps = mine[:, 2 * g_rows : 2 * g_rows + t_rows].reshape(n_p, edge + 1, cw).transpose(1, 0, 2)
    s_heads = mine[:, 2 * g_rows + t_rows : 2 * g_rows + t_rows + 3, :n_heads]
    s_heads = s_heads.transpose(1, 0, 2).reshape(3, n_p * n_heads)
    s_x = s_taps[:, :, :xw].reshape(edge + 1, n_p * xw)
    s_bc = summed[0][:, 2 * g_rows : 2 * g_rows + t_rows].reshape(n_p, edge + 1, cw)
    s_bc = s_bc[:, :, xw:].reshape(n_p, edge + 1, 2, bw).transpose(1, 2, 0, 3)
    s_bc = s_bc.reshape(edge + 1, 2 * n_p * bw)

    def uncols(g):
        return g.transpose(1, 0, 2).reshape(rows, -1)

    g_x = uncols(ga[:, :, :xw])
    g_bc = ga[:, :, xw:cw].reshape(n_p, rows, 2, bw).transpose(1, 2, 0, 3).reshape(rows, -1)
    g_k = ga[:, :, cw : cw + kw].reshape(n_p, rows, 2, hk)
    g_k = g_k.transpose(1, 2, 0, 3).reshape(rows, HDIM)
    g_v = uncols(ga[:, :, cw + kw : cw + 2 * kw])
    g_dt = uncols(ga[:, :, dt_at : dt_at + n_heads])
    g_q = gb[:, :, :HDIM].reshape(n_p, rows, n_p, 2, hk)
    g_q = g_q.transpose(1, 0, 3, 2, 4).reshape(rows, n_p * HDIM)
    g_z = uncols(gb[:, :, HDIM:])
    g_mout = uncols(gc[:, :, :xw]).T
    g_aout = uncols(gc[:, :, xw:]).T
    g_gate = uncols(gd[:, :, :ffw])
    g_up = uncols(gd[:, :, ffw:])
    g_down = uncols(ge).T
    return (
        block_out,
        grad_in,
        gains_sum[0],
        gains_sum[1],
        g_z,
        g_x,
        g_bc,
        g_dt,
        s_x,
        s_bc,
        s_heads[0],
        s_heads[1],
        s_heads[2],
        g_mout,
        g_q,
        g_k,
        g_v,
        g_aout,
        g_gate,
        g_up,
        g_down,
    )


def solution(mesh):
    seq, head = mesh.shape["seq"], mesh.shape["head"]
    plane = math.gcd(seq, 4)
    grid = Mesh(mesh.devices.reshape(seq // plane, plane, head), ("z", "p", "head"))
    s = ("z", "p")
    h = "head"
    placed = (
        P(s, None), P(s, None), P(), P(s), P(s), P(s, h), P(s, h), P(s, None), P(s, h),
        P(None, h), P(), P(h), P(h), P(h), P(h, s), P(s, h), P(s, h), P(s, h), P(h, s),
        P(s, h), P(s, h), P(h, s),
    )
    given = (
        P(s, None), P(s, None), P(s), P(s), P(s, h), P(s, h), P(s, None), P(s, h),
        P(None, h), P(), P(h), P(h), P(h), P(h, s), P(s, h), P(s, h), P(s, h), P(h, s),
        P(s, h), P(s, h), P(h, s),
    )
    return jax.shard_map(shards, mesh=grid, in_specs=placed, out_specs=given, check_vma=False)
```

```python
import functools
import math

import jax
import jax.numpy as jnp
from jax import lax
from jax.experimental import pallas as pl
from jax.experimental.pallas import tpu as pltpu
from jax.sharding import Mesh
from jax.sharding import PartitionSpec as P

MHDIM = 64
NSTATE = 256
HDIM = 128
SPAN = 128

eps_norm = 1e-05
rope_base = 100000000000.0
neg_large = -1e30
top_prec = lax.Precision.HIGHEST
bf16 = jnp.bfloat16
f32 = jnp.float32
MESH = pl.DeviceIdType.MESH
VMEM_LIMIT = 56 * 1024 * 1024


def doc_ids(positions, doc_starts):
    return jnp.sum((doc_starts[None, :] <= positions[:, None]).astype(jnp.int32), axis=1) - 1


def product(left, right):
    return jnp.dot(left, right, preferred_element_type=f32)


def product_t(left, right):
    return lax.dot_general(left, right, (((0,), (0,)), ((), ())), preferred_element_type=f32)


def product_nt(left, right):
    return lax.dot_general(left, right, (((1,), (1,)), ((), ())), preferred_element_type=f32)


def silu_slope(values):
    sigma_val = jax.nn.sigmoid(values)
    return sigma_val * (1.0 + values * (1.0 - sigma_val))


def passed_along(block, axis, distance):
    devices = range(lax.axis_size(axis))
    route = [(i - distance, i) for i in devices if i - distance in devices]
    return lax.ppermute(block, axis, route)


def convolve(extended, weights, ext_docs, tok_count):
    edge_rows = weights.shape[0] - 1
    summed = jnp.zeros((tok_count, extended.shape[1]), f32)
    for tap_index in range(weights.shape[0]):
        begin_row = edge_rows - tap_index
        same_doc = (ext_docs[begin_row : begin_row + tok_count] == ext_docs[edge_rows:])[:, None]
        summed = (
            summed
            + jnp.where(same_doc, extended[begin_row : begin_row + tok_count].astype(f32), 0.0)
            * weights[tap_index][None, :]
        )
    return summed


def convolve_back(d_conv, extended, weights, ext_docs, tok_count):
    edge_rows = weights.shape[0] - 1
    d_extended = jnp.zeros((tok_count + edge_rows, d_conv.shape[1]), f32)
    tap_grads = []
    for tap_index in range(weights.shape[0]):
        begin_row = edge_rows - tap_index
        same_doc = (ext_docs[begin_row : begin_row + tok_count] == ext_docs[edge_rows:])[:, None]
        masked_grad = jnp.where(same_doc, d_conv, 0.0)
        tap_grads.append(
            jnp.sum(
                masked_grad * extended[begin_row : begin_row + tok_count].astype(f32), axis=0
            )
        )
        d_extended = d_extended + jnp.pad(
            masked_grad * weights[tap_index][None, :], ((begin_row, edge_rows - begin_row), (0, 0))
        )
    return (d_extended, jnp.stack(tap_grads))


def tri_dot(a, b, dims=((1,), (0,))):
    return lax.dot_general(a, b, (dims, ((), ())), precision=top_prec, preferred_element_type=f32)


def dot_nn(a, b):
    return lax.dot_general(a, b, (((1,), (0,)), ((), ())), preferred_element_type=f32)


def dot_nt(a, b):
    return lax.dot_general(a, b, (((1,), (1,)), ((), ())), preferred_element_type=f32)


def dot_tn(a, b):
    return lax.dot_general(a, b, (((0,), (0,)), ((), ())), preferred_element_type=f32)


def iota2(shape, dim):
    return lax.broadcasted_iota(jnp.int32, shape, dim)


def docs_of(pos, starts_ref):
    count = jnp.where(starts_ref[0] <= pos, 1, 0)
    for i in range(1, starts_ref.shape[0]):
        count = count + jnp.where(starts_ref[i] <= pos, 1, 0)
    return count - 1


def softplus(v):
    return jnp.maximum(v, 0.0) + jnp.log(1.0 + jnp.exp(-jnp.abs(v)))


def head_maps(xw):
    lane_head = (iota2((128, xw), 1) // MHDIM == iota2((128, xw), 0)).astype(f32)
    row_head = (iota2((xw, 128), 0) // MHDIM == iota2((xw, 128), 1)).astype(f32)
    return lane_head, row_head


def span_setup(k, base_ref, starts_ref, dtp, nega):
    first = base_ref[0] + k * SPAN
    t_idx, s_idx = iota2((SPAN, SPAN), 0), iota2((SPAN, SPAN), 1)
    docs_t = docs_of(first + t_idx, starts_ref)
    docs_s = docs_of(first + s_idx, starts_ref)
    linked = (docs_t == docs_s) & (t_idx >= s_idx)
    dt = softplus(dtp)
    la = nega * dt
    tri = (t_idx >= s_idx).astype(f32)
    cum = tri_dot(tri, la)
    before = docs_of(first - 1, starts_ref)
    last_doc = docs_of(first + SPAN - 1, starts_ref)
    carried = jnp.where(docs_t == before, jnp.exp(cum), 0.0)
    cum_last = cum[SPAN - 1 : SPAN, :]
    tail = jnp.where(docs_t == last_doc, jnp.exp(cum_last - cum), 0.0)
    return docs_t, linked, dt, la, tri, cum, carried, tail


def split_bc(bc_ref):
    parts = [bc_ref[q] for q in range(bc_ref.shape[0])]
    half = parts[0].shape[1] // 2
    return (
        jnp.concatenate([part[:, :half] for part in parts], axis=1),
        jnp.concatenate([part[:, half:] for part in parts], axis=1),
    )


def ssd_forward_kernel(
    n_heads, base_ref, starts_ref, x_ref, bc_ref, dtp_ref, nega_ref, skip_ref,
    y_ref, span_ref, final_ref, decay_ref, wide_ref, c_out, state, running,
):
    k = pl.program_id(0)
    xw = n_heads * MHDIM

    @pl.when(k == 0)
    def _():
        state[...] = jnp.zeros_like(state)
        running[...] = jnp.zeros_like(running)

    docs_t, linked, dt, la, tri, cum, carried, tail = span_setup(
        k, base_ref, starts_ref, dtp_ref[...], nega_ref[...]
    )
    lane_head, row_head = head_maps(xw)
    prev_doc = docs_of(base_ref[0] - 1, starts_ref)
    since = jnp.where(docs_t == prev_doc, jnp.exp(running[0:1, :] + cum), 0.0)
    decay_ref[...] = since
    wide_ref[...] = tri_dot(since, lane_head)
    running[...] = running[...] + cum[SPAN - 1 : SPAN, :]
    start = state[...]
    span_ref[0] = start
    x, (b, c) = x_ref[...], split_bc(bc_ref)
    c_out[...] = c
    inner = dot_nt(c, b)
    cum_t, dt_t = cum.T, dt.T
    lane = iota2((SPAN, 128), 1)
    pieces = []
    for pair in range(n_heads // 2):
        xp = x[:, pair * 128 : pair * 128 + 128]
        got = []
        for h in (2 * pair, 2 * pair + 1):
            gap = jnp.where(linked, cum[:, h : h + 1] - cum_t[h : h + 1, :], neg_large)
            w = jnp.exp(gap) * inner * dt_t[h : h + 1, :]
            got.append(dot_nn(w.astype(bf16), xp))
        pieces.append(jnp.where(lane < MHDIM, got[0], got[1]))
    y = jnp.concatenate(pieces, axis=1)
    y = y + dot_nt(c, start.astype(bf16)) * tri_dot(carried, lane_head)
    xf = x.astype(f32)
    y_ref[...] = y + skip_ref[...] * xf
    xt = (xf * tri_dot(tail * dt, lane_head)).astype(bf16)
    keep = jnp.sum(row_head * carried[SPAN - 1 : SPAN, :], axis=1, keepdims=True)
    new = dot_tn(xt, b) + keep * start
    state[...] = new
    final_ref[...] = new


def ssd_forward(base, doc_starts, x, bc, dtp, nega, skip):
    tok, xw, n_p = x.shape[0], skip.shape[1], bc.shape[0]
    n_heads, nspan = xw // MHDIM, tok // SPAN
    row = lambda n: pl.BlockSpec((SPAN, n), lambda i: (i, 0))
    whole = lambda *s: pl.BlockSpec(s, lambda i: (0,) * len(s))
    smem = pl.BlockSpec(memory_space=pltpu.SMEM)
    return pl.pallas_call(
        functools.partial(ssd_forward_kernel, n_heads),
        grid=(nspan,),
        in_specs=[
            smem, smem, row(xw), pl.BlockSpec((n_p, SPAN, 128), lambda i: (0, i, 0)), row(128),
            whole(1, 128), whole(1, xw),
        ],
        out_specs=[
            row(xw),
            pl.BlockSpec((1, xw, NSTATE), lambda i: (i, 0, 0)),
            whole(xw, NSTATE),
            row(128),
            row(xw),
            row(NSTATE),
        ],
        out_shape=[
            jax.ShapeDtypeStruct((tok, xw), f32),
            jax.ShapeDtypeStruct((nspan, xw, NSTATE), f32),
            jax.ShapeDtypeStruct((xw, NSTATE), f32),
            jax.ShapeDtypeStruct((tok, 128), f32),
            jax.ShapeDtypeStruct((tok, xw), f32),
            jax.ShapeDtypeStruct((tok, NSTATE), bf16),
        ],
        scratch_shapes=[pltpu.VMEM((xw, NSTATE), f32), pltpu.VMEM((8, 128), f32)],
        compiler_params=pltpu.CompilerParams(vmem_limit_bytes=VMEM_LIMIT),
        cost_estimate=pl.CostEstimate(
            flops=2 * tok * xw * NSTATE * 3, bytes_accessed=40_000_000, transcendentals=0
        ),
        name="ssd_forward",
    )(base, doc_starts, x, bc, dtp, nega, skip)


def ssd_backward_kernel(
    n_heads, base_ref, starts_ref, x_ref, bc_ref, dtp_ref, dy_ref, span_ref, decay_ref,
    nega_ref, skip_ref, in_ref, grad_ref,
    dx_ref, dbc_ref, ddt_ref, sums_ref, gskip_ref, gstate,
):
    step = pl.program_id(0)
    k = pl.num_programs(0) - 1 - step
    xw = n_heads * MHDIM

    @pl.when(step == 0)
    def _():
        gstate[...] = grad_ref[...]
        sums_ref[...] = jnp.zeros_like(sums_ref)
        gskip_ref[...] = jnp.zeros_like(gskip_ref)

    nega = nega_ref[...]
    docs_t, linked, dt, la, tri, cum, carried, tail = span_setup(
        k, base_ref, starts_ref, dtp_ref[...], nega
    )
    lane_head, row_head = head_maps(xw)
    begin = jnp.sum(row_head * decay_ref[0], axis=1, keepdims=True)
    start = span_ref[0] + begin * in_ref[...]
    start_low = start.astype(bf16)
    g = gstate[...]
    g_low = g.astype(bf16)
    x, (b, c), dy = x_ref[...], split_bc(bc_ref), dy_ref[...]
    dy_low = dy.astype(bf16)
    xf = x.astype(f32)
    inner = dot_nt(c, b)
    cum_t, dt_t = cum.T, dt.T
    lane = iota2((SPAN, 128), 1)
    row8 = iota2((SPAN, 128), 0)
    d_inner = jnp.zeros((SPAN, SPAN), f32)
    r_cols = jnp.zeros((SPAN, 128), f32)
    k_rows = jnp.zeros((SPAN, 128), f32)
    u_pieces = []
    for pair in range(n_heads // 2):
        xp = x[:, pair * 128 : pair * 128 + 128]
        dyp = dy_low[:, pair * 128 : pair * 128 + 128]
        got = []
        for j, h in enumerate((2 * pair, 2 * pair + 1)):
            mine = (lane < MHDIM) if j == 0 else (lane >= MHDIM)
            gap = jnp.where(linked, cum[:, h : h + 1] - cum_t[h : h + 1, :], neg_large)
            e = jnp.exp(gap)
            m = e * inner
            dyx = dot_nt(dyp, jnp.where(mine, xp, jnp.zeros_like(xp)))
            ed = dyx * dt_t[h : h + 1, :]
            d_inner = d_inner + e * ed
            pairs = m * ed
            r_cols = jnp.where(lane == h, jnp.sum(pairs, axis=1, keepdims=True), r_cols)
            k_rows = jnp.where(row8 == h, jnp.sum(pairs, axis=0, keepdims=True), k_rows)
            got.append(dot_tn(m.astype(bf16), dyp))
        u_pieces.append(jnp.where(lane < MHDIM, got[0], got[1]))
    u = jnp.concatenate(u_pieces, axis=1)
    dye = dy * tri_dot(carried, lane_head)
    dye_low = dye.astype(bf16)
    di_low = d_inner.astype(bf16)
    r_state = tri_dot(dye * dot_nt(c, start_low), row_head)
    u_state = dot_nt(b, g_low) * tri_dot(tail, lane_head)
    u = u + u_state
    dt_full = tri_dot(dt, lane_head)
    k_state = dt * tri_dot(xf * u_state, row_head)
    d_dt = tri_dot(xf * u, row_head)
    tail_x = (xf * tri_dot(tail * dt, lane_head)).astype(bf16)
    dx_ref[...] = dt_full * u + skip_ref[...] * dy
    d_b = dot_nn(tail_x, g_low) + dot_tn(di_low, c)
    d_c = dot_nn(dye_low, start_low) + dot_nn(di_low, b)
    bw = 64
    for q in range(dbc_ref.shape[0]):
        cut = slice(q * bw, q * bw + bw)
        dbc_ref[q] = jnp.concatenate([d_b[:, cut], d_c[:, cut]], axis=1)
    gs = jnp.sum(g * start, axis=1, keepdims=True)
    gs_row = jnp.sum(row_head * gs, axis=0, keepdims=True)
    last = jnp.sum(k_state, axis=0, keepdims=True) + carried[SPAN - 1 : SPAN, :] * gs_row
    d_cum = r_cols - k_rows.T + r_state - k_state + jnp.where(row8 == SPAN - 1, last, 0.0)
    d_la = tri_dot(tri, d_cum, ((0,), (0,)))
    live = lane < n_heads
    dtp = dtp_ref[...]
    d_in = jnp.where(live, (d_dt + nega * d_la) * jax.nn.sigmoid(dtp), 0.0)
    ddt_ref[...] = d_in
    sum_a = jnp.sum(jnp.where(live, d_la * la, 0.0), axis=0, keepdims=True)
    sum_b = jnp.sum(d_in, axis=0, keepdims=True)
    pick = iota2((8, 128), 0)
    sums_ref[...] += jnp.where(pick == 0, sum_a, jnp.where(pick == 1, sum_b, 0.0))
    gskip_ref[...] += jnp.sum(dy * xf, axis=0, keepdims=True)
    keep = jnp.sum(row_head * carried[SPAN - 1 : SPAN, :], axis=1, keepdims=True)
    gstate[...] = keep * g + dot_tn(dye_low, c)


def ssd_backward(
    base, doc_starts, x, bc, dtp, dy, span_starts, start_decay, nega, skip, in_state, grad_state
):
    tok, xw, n_p = x.shape[0], skip.shape[1], bc.shape[0]
    wide = pl.BlockSpec((n_p, SPAN, 128), lambda i: (0, nspan - 1 - i, 0))
    n_heads, nspan = xw // MHDIM, tok // SPAN
    row = lambda n: pl.BlockSpec((SPAN, n), lambda i: (nspan - 1 - i, 0))
    whole = lambda *s: pl.BlockSpec(s, lambda i: (0,) * len(s))
    smem = pl.BlockSpec(memory_space=pltpu.SMEM)
    return pl.pallas_call(
        functools.partial(ssd_backward_kernel, n_heads),
        grid=(nspan,),
        in_specs=[
            smem, smem, row(xw), wide, row(128), row(xw),
            pl.BlockSpec((1, xw, NSTATE), lambda i: (nspan - 1 - i, 0, 0)),
            pl.BlockSpec((1, 1, 128), lambda i: (nspan - 1 - i, 0, 0)),
            whole(1, 128), whole(1, xw), whole(xw, NSTATE), whole(xw, NSTATE),
        ],
        out_specs=[row(xw), wide, row(128), whole(8, 128), whole(1, xw)],
        out_shape=[
            jax.ShapeDtypeStruct((tok, xw), f32),
            jax.ShapeDtypeStruct((n_p, tok, 128), f32),
            jax.ShapeDtypeStruct((tok, 128), f32),
            jax.ShapeDtypeStruct((8, 128), f32),
            jax.ShapeDtypeStruct((1, xw), f32),
        ],
        scratch_shapes=[pltpu.VMEM((xw, NSTATE), f32)],
        compiler_params=pltpu.CompilerParams(vmem_limit_bytes=VMEM_LIMIT),
        cost_estimate=pl.CostEstimate(
            flops=2 * tok * xw * NSTATE * 8, bytes_accessed=80_000_000, transcendentals=0
        ),
        name="ssd_backward",
    )(base, doc_starts, x, bc, dtp, dy, span_starts, start_decay, nega, skip, in_state, grad_state)


QB = 256
KB = 512


def seen(base_ref, starts_ref, q_first, k_first):
    q_pos = base_ref[0] + q_first + iota2((QB, KB), 0)
    k_pos = k_first + iota2((QB, KB), 1)
    return (q_pos >= k_pos) & (docs_of(q_pos, starts_ref) == docs_of(k_pos, starts_ref))


def attend_kernel(scale, base_ref, starts_ref, q_ref, kv_ref, o_ref, lse_ref, k_ref, v_ref):
    i = pl.program_id(0)

    @pl.when(i == 0)
    def _():
        n_p, nz, rows, _ = kv_ref.shape
        kw = HDIM // n_p

        @pl.loop(0, nz)
        def _(z):
            parts = [kv_ref[q, z] for q in range(n_p)]
            for t in range(2):
                at = pl.ds(pl.multiple_of((2 * z + t) * rows, rows), rows)
                lo = 2 * kw * t
                k_ref[at, :] = jnp.concatenate([v[:, lo : lo + kw] for v in parts], axis=1)
                v_ref[at, :] = jnp.concatenate([v[:, lo + kw : lo + 2 * kw] for v in parts], axis=1)

    q = q_ref[...]
    blocks = (base_ref[0] + (i + 1) * QB + KB - 1) // KB

    def turn(j, carry):
        m, l, acc = carry
        at = pl.ds(pl.multiple_of(j * KB, KB), KB)
        s = dot_nt(q, k_ref[at, :]) * scale
        visible = seen(base_ref, starts_ref, i * QB, j * KB)
        s = jnp.where(visible, s, neg_large)
        m_new = jnp.maximum(m, jnp.max(s, axis=1, keepdims=True))
        w = jnp.where(visible, jnp.exp(s - m_new), 0.0)
        r = jnp.exp(m - m_new)
        l = l * r + jnp.sum(w, axis=1, keepdims=True)
        return m_new, l, acc * r + dot_nn(w.astype(bf16), v_ref[at, :])

    m, l, acc = lax.fori_loop(
        0,
        blocks,
        turn,
        (jnp.full((QB, 1), neg_large, f32), jnp.zeros((QB, 1), f32), jnp.zeros((QB, HDIM), f32)),
    )
    o_ref[...] = acc / l
    lse_ref[...] = jnp.broadcast_to(m + jnp.log(l), (QB, 128))


def attend(base, doc_starts, q, kv):
    tok = q.shape[0]
    keys = kv.shape[1] * kv.shape[2] * 2
    row = pl.BlockSpec((QB, HDIM), lambda i: (i, 0))
    whole = lambda s: pl.BlockSpec(s, lambda i: (0,) * len(s))
    smem = pl.BlockSpec(memory_space=pltpu.SMEM)
    return pl.pallas_call(
        functools.partial(attend_kernel, HDIM ** (-0.5)),
        grid=(tok // QB,),
        in_specs=[smem, smem, row, whole(kv.shape)],
        out_specs=[row, row, whole((keys, HDIM)), whole((keys, HDIM))],
        out_shape=[jax.ShapeDtypeStruct((tok, HDIM), f32)] * 2
        + [jax.ShapeDtypeStruct((keys, HDIM), bf16)] * 2,
        compiler_params=pltpu.CompilerParams(vmem_limit_bytes=VMEM_LIMIT),
        cost_estimate=pl.CostEstimate(
            flops=4 * tok * keys * HDIM, bytes_accessed=30_000_000, transcendentals=0
        ),
        name="attend",
    )(base, doc_starts, q, kv)


def attend_back_kernel(
    scale, base_ref, starts_ref, q_ref, do_ref, o_ref, lse_ref, k_ref, v_ref,
    dq_ref, dkv_ref, dk_ref, dv_ref,
):
    i = pl.program_id(0)

    @pl.when(i == 0)
    def _():
        dk_ref[...] = jnp.zeros_like(dk_ref)
        dv_ref[...] = jnp.zeros_like(dv_ref)

    q, do = q_ref[...], do_ref[...]
    delta = jnp.sum(do.astype(f32) * o_ref[...], axis=1, keepdims=True)
    lse = lse_ref[:, 0:1]
    blocks = (base_ref[0] + (i + 1) * QB + KB - 1) // KB

    def turn(j, dq):
        at = pl.ds(pl.multiple_of(j * KB, KB), KB)
        k, v = k_ref[at, :], v_ref[at, :]
        visible = seen(base_ref, starts_ref, i * QB, j * KB)
        s = dot_nt(q, k) * scale
        p = jnp.exp(jnp.where(visible, s - lse, neg_large))
        ds = (p * (dot_nt(do, v) - delta)).astype(bf16)
        dv_ref[at, :] += dot_tn(p.astype(bf16), do)
        dk_ref[at, :] += dot_tn(ds, q) * scale
        return dq + dot_nn(ds, k)

    dq_ref[...] = lax.fori_loop(0, blocks, turn, jnp.zeros((QB, HDIM), f32)) * scale

    @pl.when(i == pl.num_programs(0) - 1)
    def _():
        n_p, nz, rows, _ = dkv_ref.shape
        kw = HDIM // n_p

        @pl.loop(0, nz)
        def _(z):
            got = []
            for t in range(2):
                at = pl.ds(pl.multiple_of((2 * z + t) * rows, rows), rows)
                got += [dk_ref[at, :].astype(bf16), dv_ref[at, :].astype(bf16)]
            for q in range(n_p):
                cut = slice(q * kw, q * kw + kw)
                dkv_ref[q, z] = jnp.concatenate([v[:, cut] for v in got], axis=1)


def attend_back(base, doc_starts, q, do, o, lse, k, v, packed):
    tok = q.shape[0]
    row = pl.BlockSpec((QB, HDIM), lambda i: (i, 0))
    whole = lambda s: pl.BlockSpec(s, lambda i: (0,) * len(s))
    smem = pl.BlockSpec(memory_space=pltpu.SMEM)
    return pl.pallas_call(
        functools.partial(attend_back_kernel, HDIM ** (-0.5)),
        grid=(tok // QB,),
        in_specs=[smem, smem, row, row, row, row, whole(k.shape), whole(k.shape)],
        out_specs=[row, whole(packed)],
        out_shape=[
            jax.ShapeDtypeStruct((tok, HDIM), f32),
            jax.ShapeDtypeStruct(packed, bf16),
        ],
        scratch_shapes=[pltpu.VMEM(k.shape, f32), pltpu.VMEM(k.shape, f32)],
        compiler_params=pltpu.CompilerParams(vmem_limit_bytes=VMEM_LIMIT),
        cost_estimate=pl.CostEstimate(
            flops=10 * tok * k.shape[0] * HDIM, bytes_accessed=40_000_000, transcendentals=0
        ),
        name="attend_back",
    )(base, doc_starts, q, do, o, lse, k, v)


def at_rows(first, count):
    return pl.ds(pl.multiple_of(first, count), count)


def place():
    return lax.axis_index("z"), lax.axis_index("p"), lax.axis_index("head")


def hop(p, d):
    x, y = lax.rem(p, 2), p // 2
    return lax.rem(y + d // 2, 2) * 2 + lax.rem(x + d % 2, 2)


def chip(z, p, c):
    return (z, p, c)


def meet(others):
    barrier = pltpu.get_barrier_semaphore()
    for other in others:
        pl.semaphore_signal(barrier, inc=1, device_id=other, device_id_type=MESH)
    pl.semaphore_wait(barrier, len(others))


def send(src, dst, send_sem, recv_sem, to):
    copy = pltpu.make_async_remote_copy(
        src_ref=src, dst_ref=dst, send_sem=send_sem, recv_sem=recv_sem,
        device_id=to, device_id_type=MESH,
    )
    copy.start()
    return copy


HOPS = (3, 1, 2)


def share_rows(full_ref, half, own_sems, far_sems, near_sems):
    z, p, c = place()
    other = chip(z, p, 1 - c)
    mine = full_ref.at[at_rows((p * 2 + c) * half, half), :]
    copies = []
    for i, d in enumerate(HOPS):
        copies.append(send(mine, mine, far_sems.at[0, i], far_sems.at[1, i], chip(z, hop(p, d), c)))
    copies.append(send(mine, mine, own_sems.at[0], own_sems.at[1], other))
    onward = []
    for i, d in ((1, 1), (2, 2), (0, 3)):
        copies[i].wait_recv()
        came = full_ref.at[at_rows((hop(p, d) * 2 + c) * half, half), :]
        onward.append(send(came, came, near_sems.at[0, i], near_sems.at[1, i], other))
    return copies, onward


def finish_share(copies, onward):
    for copy in copies[:3]:
        copy.wait_send()
    copies[3].wait()
    for copy in onward:
        copy.wait()


def reduce_blocks(pairs, part, keep, sib_out, sib_in, out, came, near_sems, far_sems):
    z, p, c = place()
    other = chip(z, p, 1 - c)
    half = keep.shape[1]
    width = keep.shape[2]
    tile = part.shape[1]
    near, far = [], []

    def pass_on(i, d):
        near[i].wait_recv()

        @pl.loop(0, half // 16)
        def _(r):
            at = at_rows(r * 16, 16)
            out[i, at, :] = (keep[i, at, :] + sib_in[i, at, :].astype(f32)).astype(bf16)

        far.append(
            send(out.at[i], came.at[i], far_sems.at[0, i], far_sems.at[1, i], chip(z, hop(p, d), c))
        )

    order = HOPS + (0,)
    for i, d in enumerate(order):
        rows = at_rows(hop(p, d) * (2 * half), 2 * half)

        @pl.loop(0, width // tile)
        def _(n):
            cols = at_rows(n * tile, tile)
            total = dot_nt(pairs[0][0][rows, :], pairs[0][1][cols, :])
            for left, right in pairs[1:]:
                total = total + dot_nt(left[rows, :], right[cols, :])
            part[...] = total
            keep[i, :, cols] = part[at_rows(c * half, half), :]
            sib_out[i, :, cols] = part[at_rows((1 - c) * half, half), :].astype(bf16)

        near.append(
            send(sib_out.at[i], sib_in.at[i], near_sems.at[0, i], near_sems.at[1, i], other)
        )
        if i:
            pass_on(i - 1, order[i - 1])
    near[3].wait_recv()
    for copy in far:
        copy.wait_recv()

    def total_rows(at):
        total = keep[3, at, :] + sib_in[3, at, :].astype(f32)
        return total + came[0, at, :].astype(f32) + came[1, at, :].astype(f32) + came[2, at, :].astype(f32)

    def done():
        for copy in near + far:
            copy.wait_send()

    return total_rows, done


def greet():
    z, p, c = place()
    meet([chip(z, p, 1 - c)] + [chip(z, hop(p, d), c) for d in HOPS])


def rms(rows):
    return lax.rsqrt(jnp.mean(rows * rows, axis=1, keepdims=True) + eps_norm)


def mid_kernel(
    left, right, resid, gain, mid_ref, full_ref,
    part, keep, sib_out, sib_in, out, came, n_sems, f_sems, own_sems, far_sems, near_sems,
):
    greet()
    z, p, c = place()
    half = keep.shape[1]
    total_rows, done = reduce_blocks(
        [(left, right)], part, keep, sib_out, sib_in, out, came, n_sems, f_sems
    )
    g = gain[...]

    @pl.loop(0, half // 16)
    def _(r):
        at = at_rows(r * 16, 16)
        mid = resid[at, :] + total_rows(at)
        mid_ref[at, :] = mid
        full_ref[at_rows((p * 2 + c) * half + r * 16, 16), :] = (mid * rms(mid) * g).astype(bf16)

    copies, onward = share_rows(full_ref, half, own_sems, far_sems, near_sems)
    done()
    finish_share(copies, onward)


def two_kernel(
    left, right, mid_own, grad_own, gain, dmid_ref, ggain_ref, full_ref,
    part, keep, sib_out, sib_in, out, came, n_sems, f_sems, own_sems, far_sems, near_sems,
):
    greet()
    z, p, c = place()
    half = keep.shape[1]
    total_rows, done = reduce_blocks(
        [(left, right)], part, keep, sib_out, sib_in, out, came, n_sems, f_sems
    )
    g = gain[...]
    ggain_ref[...] = jnp.zeros_like(ggain_ref)

    @pl.loop(0, half // 16)
    def _(r):
        at = at_rows(r * 16, 16)
        d_two, mid = total_rows(at), mid_own[at, :]
        scale = rms(mid)
        w = d_two * g
        d_mid = grad_own[at, :] + scale * w - mid * (scale * scale * scale) * jnp.mean(
            w * mid, axis=1, keepdims=True
        )
        ggain_ref[...] += jnp.sum(d_two * mid * scale, axis=0, keepdims=True)
        dmid_ref[at, :] = d_mid
        full_ref[at_rows((p * 2 + c) * half + r * 16, 16), :] = d_mid.astype(bf16)

    copies, onward = share_rows(full_ref, half, own_sems, far_sems, near_sems)
    done()
    finish_share(copies, onward)


def one_kernel(
    left_a, right_a, left_b, right_b, hidden_own, dmid_own, gain, grad_ref, ggain_ref,
    part, keep, sib_out, sib_in, out, came, n_sems, f_sems, own_sems,
):
    greet()
    z, p, c = place()
    half = keep.shape[1]
    total_rows, done = reduce_blocks(
        [(left_a, right_a), (left_b, right_b)],
        part, keep, sib_out, sib_in, out, came, n_sems, f_sems,
    )
    g = gain[...]
    ggain_ref[...] = jnp.zeros_like(ggain_ref)

    @pl.loop(0, half // 16)
    def _(r):
        at = at_rows(r * 16, 16)
        d_one, hid = total_rows(at), hidden_own[at, :]
        scale = rms(hid)
        w = d_one * g
        d_in = dmid_own[at, :] + scale * w - hid * (scale * scale * scale) * jnp.mean(
            w * hid, axis=1, keepdims=True
        )
        ggain_ref[...] += jnp.sum(d_one * hid * scale, axis=0, keepdims=True)
        grad_ref[at_rows(c * half + r * 16, 16), :] = d_in

    mine = grad_ref.at[at_rows(c * half, half), :]
    copy = send(mine, mine, own_sems.at[0], own_sems.at[1], chip(z, p, 1 - c))
    done()
    copy.wait()


VM = pl.BlockSpec(memory_space=pltpu.VMEM)


def reduce_scratch(half, width):
    return [
        pltpu.VMEM((2 * half, 512), f32),
        pltpu.VMEM((4, half, width), f32),
        pltpu.VMEM((4, half, width), bf16),
        pltpu.VMEM((4, half, width), bf16),
        pltpu.VMEM((3, half, width), bf16),
        pltpu.VMEM((3, half, width), bf16),
        pltpu.SemaphoreType.DMA((2, 4)),
        pltpu.SemaphoreType.DMA((2, 3)),
    ]


SHARE_SEMS = [
    pltpu.SemaphoreType.DMA((2,)),
    pltpu.SemaphoreType.DMA((2, 3)),
    pltpu.SemaphoreType.DMA((2, 3)),
]


def plane_call(kernel, name, number, args, shapes, scratch, nbytes=150_000_000):
    return pl.pallas_call(
        kernel,
        in_specs=[VM] * len(args),
        out_specs=[VM] * len(shapes),
        out_shape=[jax.ShapeDtypeStruct(s, t) for s, t in shapes],
        scratch_shapes=scratch,
        compiler_params=pltpu.CompilerParams(
            collective_id=number, has_side_effects=True, vmem_limit_bytes=VMEM_LIMIT
        ),
        cost_estimate=pl.CostEstimate(flops=0, bytes_accessed=nbytes, transcendentals=0),
        name=name,
    )(*args)


def mid_step(mixed, w, resid_own, gain):
    tok, width = mixed.shape[0], w.shape[0]
    half = resid_own.shape[0]
    return plane_call(
        mid_kernel, "mid_step", 1, (mixed, w, resid_own, gain),
        [((half, width), f32), ((tok, width), bf16)],
        reduce_scratch(half, width) + SHARE_SEMS,
    )


def two_step(d_gu, w, mid_own, grad_own, gain):
    tok, width = d_gu.shape[0], w.shape[0]
    half = mid_own.shape[0]
    return plane_call(
        two_kernel, "two_step", 2, (d_gu, w, mid_own, grad_own, gain),
        [((half, width), f32), ((1, width), f32), ((tok, width), bf16)],
        reduce_scratch(half, width) + SHARE_SEMS,
    )


def one_step(d_a, w_a, d_b, w_b, hidden_own, dmid_own, gain):
    width = w_a.shape[0]
    half = hidden_own.shape[0]
    return plane_call(
        one_kernel, "one_step", 3, (d_a, w_a, d_b, w_b, hidden_own, dmid_own, gain),
        [((2 * half, width), f32), ((1, width), f32)],
        reduce_scratch(half, width) + [pltpu.SemaphoreType.DMA((2,))],
    )


HALO = 16


def open_kernel(n, *refs):
    hid, grad, gains_ref, a_ref = refs[:4]
    w_refs = refs[4 : 4 + n]
    gain_out, full_ref, gfull_ref, a_out = refs[4 + n : 8 + n]
    w_outs = refs[8 + n : 8 + 2 * n]
    (
        g_vec, gz_sems, gp_sems, a_sems, up_sems, down_sems, own_sems, far_sems, near_sems,
        own_g, far_g, near_g, w_sems, loc_sems, halo_sems,
    ) = refs[8 + 2 * n :]
    z, p, c = place()
    nz, half, rows = a_out.shape[0], hid.shape[0], a_ref.shape[1]
    tok = gfull_ref.shape[0]
    ups = [chip(lax.rem(z + d, nz), p, c) for d in range(1, nz)]
    flat = [chip(z, hop(p, d), c) for d in HOPS]
    meet(ups + flat + [chip(z, p, 1 - c)])
    gain_out[p, z] = gains_ref[...]
    gz = [
        send(gain_out.at[p, z], gain_out.at[p, z], gz_sems.at[0, d], gz_sems.at[1, d], ups[d])
        for d in range(nz - 1)
    ]
    to_plane = []
    for i, d in enumerate(HOPS):
        to_plane.append(
            send(a_ref.at[hop(p, d)], a_out.at[z, p], a_sems.at[0, i], a_sems.at[1, i], flat[i])
        )
    local = [pltpu.make_async_copy(a_ref.at[p], a_out.at[z, p], loc_sems.at[n])]
    for j in range(n):
        local.append(pltpu.make_async_copy(w_refs[j].at[p], w_outs[j].at[p], loc_sems.at[j]))
    for copy in local:
        copy.start()

    @pl.loop(0, half // 16)
    def _(r):
        at = at_rows(r * 16, 16)
        gfull_ref[at_rows((p * 2 + c) * half + r * 16, 16), :] = grad[at, :].astype(bf16)

    for copy in gz:
        copy.wait_recv()
    gp = [
        send(gain_out.at[p], gain_out.at[p], gp_sems.at[0, i], gp_sems.at[1, i], flat[i])
        for i in range(3)
    ]
    for copy in gp:
        copy.wait_recv()
    for i in range(nz):
        for j in range(gain_out.shape[0]):
            first = (i * gain_out.shape[0] + j) * rows
            g_vec[:, first : first + rows] = gain_out[j, i][:, :rows]
    g = g_vec[0:1, :]

    @pl.loop(0, half // 16)
    def _(r):
        rows_in = hid[at_rows(r * 16, 16), :]
        full_ref[at_rows((p * 2 + c) * half + r * 16, 16), :] = (
            rows_in * rms(rows_in) * g
        ).astype(bf16)

    other = chip(z, p, 1 - c)
    mine = full_ref.at[at_rows((p * 2 + c) * half, half), :]
    rows_out = [
        send(mine, mine, far_sems.at[0, i], far_sems.at[1, i], flat[i]) for i in range(3)
    ] + [send(mine, mine, own_sems.at[0], own_sems.at[1], other)]

    def block_up(k):
        at = a_out.at[z - k]
        return pltpu.make_async_remote_copy(
            src_ref=at, dst_ref=at, send_sem=up_sems.at[0, k], recv_sem=up_sems.at[1, k],
            device_id=chip(z + 1, p, c), device_id_type=MESH,
        )

    def block_down(k):
        at = a_out.at[z + k]
        return pltpu.make_async_remote_copy(
            src_ref=at, dst_ref=at, send_sem=down_sems.at[0, k], recv_sem=down_sems.at[1, k],
            device_id=chip(z - 1, p, c), device_id_type=MESH,
        )

    def got_up(k):
        at = a_out.at[z - k]
        pltpu.make_async_remote_copy(
            src_ref=at, dst_ref=at, send_sem=up_sems.at[0, k - 1], recv_sem=up_sems.at[1, k - 1],
            device_id=chip(z - 1, p, c), device_id_type=MESH,
        ).wait_recv()

    def got_down(k):
        at = a_out.at[z + k]
        pltpu.make_async_remote_copy(
            src_ref=at, dst_ref=at, send_sem=down_sems.at[0, k - 1],
            recv_sem=down_sems.at[1, k - 1],
            device_id=chip(z + 1, p, c), device_id_type=MESH,
        ).wait_recv()

    def stage(k):
        if k:

            @pl.when(z - k >= 0)
            def _():
                got_up(k)

        @pl.when((z - k >= 0) & (z + 1 < nz))
        def _():
            block_up(k).start()

        if k:

            @pl.when(z + k < nz)
            def _():
                got_down(k)

        @pl.when((z + k < nz) & (z > 0))
        def _():
            block_down(k).start()

    for copy in to_plane:
        copy.wait_recv()
    for copy in local:
        copy.wait()
    stage(0)
    if nz > 2:
        stage(1)
    onward = []
    for i, d in ((1, 1), (2, 2), (0, 3)):
        rows_out[i].wait_recv()
        came = full_ref.at[at_rows((hop(p, d) * 2 + c) * half, half), :]
        onward.append(send(came, came, near_sems.at[0, i], near_sems.at[1, i], other))
    moved = []
    for j in range(n):
        for i, d in enumerate(HOPS):
            moved.append(
                send(
                    w_refs[j].at[hop(p, d)], w_outs[j].at[p], w_sems.at[0, j, i],
                    w_sems.at[1, j, i], flat[i],
                )
            )
    finish_share(rows_out, onward)
    halo_from = full_ref.at[at_rows(tok - HALO, HALO), :]
    halo_to = full_ref.at[at_rows(tok, HALO), :]

    def halo(to):
        return pltpu.make_async_remote_copy(
            src_ref=halo_from, dst_ref=halo_to, send_sem=halo_sems.at[0],
            recv_sem=halo_sems.at[1], device_id=to, device_id_type=MESH,
        )

    @pl.when(z + 1 < nz)
    def _():
        halo(chip(z + 1, p, c)).start()

    @pl.when(z == 0)
    def _():
        full_ref[at_rows(tok, HALO), :] = jnp.zeros((HALO, full_ref.shape[1]), bf16)

    for k in range(2, nz):
        stage(k)
    copies_g, onward_g = share_rows(gfull_ref, half, own_g, far_g, near_g)

    @pl.when(z > 0)
    def _():
        halo(chip(z - 1, p, c)).wait_recv()

    @pl.when(z + 1 < nz)
    def _():
        halo(chip(z + 1, p, c)).wait_send()

    for k in range(nz):

        @pl.when((z - k >= 0) & (z + 1 < nz))
        def _():
            block_up(k).wait_send()

        @pl.when((z + k < nz) & (z > 0))
        def _():
            block_down(k).wait_send()

    finish_share(copies_g, onward_g)
    for copy in moved:
        copy.wait()
    for copy in gz + gp + to_plane:
        copy.wait_send()


def open_step(hid, grad, gains, piece, rest, tok, nz):
    width, n, n_p = hid.shape[1], len(rest), piece.shape[0]
    anywhere = pl.BlockSpec(memory_space=pl.ANY)
    dma = pltpu.SemaphoreType.DMA
    return pl.pallas_call(
        functools.partial(open_kernel, n),
        in_specs=[VM, VM, VM] + [anywhere] * (n + 1),
        out_specs=[VM, VM, VM] + [anywhere] * (n + 1),
        out_shape=[
            jax.ShapeDtypeStruct((n_p, nz) + gains.shape, f32),
            jax.ShapeDtypeStruct((tok + HALO, width), bf16),
            jax.ShapeDtypeStruct((tok, width), bf16),
            jax.ShapeDtypeStruct((nz,) + piece.shape, bf16),
        ]
        + [jax.ShapeDtypeStruct(r.shape, bf16) for r in rest],
        scratch_shapes=[
            pltpu.VMEM((8, width), f32), dma((2, nz - 1)), dma((2, 3)), dma((2, 3)), dma((2, nz)),
            dma((2, nz)),
        ]
        + SHARE_SEMS
        + SHARE_SEMS
        + [dma((2, n, 3)), dma((n + 1,)), dma((2,))],
        compiler_params=pltpu.CompilerParams(
            collective_id=4, has_side_effects=True, vmem_limit_bytes=VMEM_LIMIT
        ),
        cost_estimate=pl.CostEstimate(flops=0, bytes_accessed=250_000_000, transcendentals=0),
        name="open_step",
    )(hid, grad, gains, piece, *rest)


def gather_bc_kernel(x_ref, full_ref, far_sems, near_sems):
    greet()
    z, p, c = place()
    half = x_ref.shape[0] // 2
    full_ref[p] = x_ref[...]
    rows = at_rows(c * half, half)
    mine = full_ref.at[p, rows, :]
    copies = [
        send(mine, mine, far_sems.at[0, i], far_sems.at[1, i], chip(z, hop(p, d), c))
        for i, d in enumerate(HOPS)
    ]
    onward = []
    for i, d in ((1, 1), (2, 2), (0, 3)):
        copies[i].wait_recv()
        came = full_ref.at[hop(p, d), rows, :]
        onward.append(
            send(came, came, near_sems.at[0, i], near_sems.at[1, i], chip(z, p, 1 - c))
        )
    for copy in copies:
        copy.wait_send()
    for copy in onward:
        copy.wait()


def gather_bc(x, at, n_p):
    tok = x.shape[0]
    return pl.pallas_call(
        gather_bc_kernel,
        grid=(1,),
        in_specs=[pl.BlockSpec((tok, 128), lambda i: (0, at))],
        out_specs=pl.BlockSpec((n_p, tok, 128), lambda i: (0, 0, 0)),
        out_shape=jax.ShapeDtypeStruct((n_p, tok, 128), bf16),
        scratch_shapes=[pltpu.SemaphoreType.DMA((2, 3)), pltpu.SemaphoreType.DMA((2, 3))],
        compiler_params=pltpu.CompilerParams(
            collective_id=5, has_side_effects=True, vmem_limit_bytes=VMEM_LIMIT
        ),
        cost_estimate=pl.CostEstimate(flops=0, bytes_accessed=30_000_000, transcendentals=0),
        name="gather_bc",
    )(x)


def reduce_bc_kernel(x_ref, out_ref, sib_out, sib_in, out, came, n_sems, f_sems, own_sems):
    greet()
    z, p, c = place()
    half = x_ref.shape[1] // 2
    other = chip(z, p, 1 - c)
    near, far = [], []
    order = HOPS + (0,)
    for i, d in enumerate(order):
        q = hop(p, d)
        sib_out[i] = x_ref[q, at_rows((1 - c) * half, half), :].astype(bf16)
        near.append(
            send(sib_out.at[i], sib_in.at[i], n_sems.at[0, i], n_sems.at[1, i], other)
        )
    for i, d in enumerate(HOPS):
        q = hop(p, d)
        near[i].wait_recv()
        out[i] = (x_ref[q, at_rows(c * half, half), :] + sib_in[i].astype(f32)).astype(bf16)
        far.append(
            send(out.at[i], came.at[i], f_sems.at[0, i], f_sems.at[1, i], chip(z, q, c))
        )
    near[3].wait_recv()
    total = x_ref[p, at_rows(c * half, half), :] + sib_in[3].astype(f32)
    for i in (1, 2, 0):
        far[i].wait_recv()
        total = total + came[i].astype(f32)
    mine = out_ref.at[at_rows(c * half, half), :]
    out_ref[at_rows(c * half, half), :] = total
    copy = send(mine, mine, own_sems.at[0], own_sems.at[1], other)
    for done in near + far:
        done.wait_send()
    copy.wait()


def reduce_bc(x):
    n_p, tok, _ = x.shape
    half = tok // 2
    return plane_call(
        reduce_bc_kernel, "reduce_bc", 7, (x,), [((tok, 128), f32)],
        [
            pltpu.VMEM((4, half, 128), bf16),
            pltpu.VMEM((4, half, 128), bf16),
            pltpu.VMEM((3, half, 128), bf16),
            pltpu.VMEM((3, half, 128), bf16),
            pltpu.SemaphoreType.DMA((2, 4)),
            pltpu.SemaphoreType.DMA((2, 3)),
            pltpu.SemaphoreType.DMA((2,)),
        ],
        nbytes=40_000_000,
    )[0]


def sums_kernel(v_ref, out_ref, came, z_sems, p_sems, c_sems):
    z, p, c = place()
    nz = came.shape[0]
    ups = [chip(lax.rem(z + d, nz), p, c) for d in range(1, nz)]
    other = chip(z, p, 1 - c)
    meet(ups + [chip(z, hop(p, d), c) for d in HOPS] + [other])
    copies = []
    for d in range(1, nz):
        copies.append(
            send(v_ref, came.at[d], z_sems.at[0, d - 1], z_sems.at[1, d - 1], ups[d - 1])
        )
    total = v_ref[...]
    for d in range(1, nz):
        copies[d - 1].wait_recv()
        total = total + came[d]
    out_ref[c, p] = total
    far = []
    for i, d in enumerate(HOPS):
        far.append(
            send(out_ref.at[c, p], out_ref.at[c, p], p_sems.at[0, i], p_sems.at[1, i], chip(z, hop(p, d), c))
        )
    for copy in far:
        copy.wait_recv()
    near = send(out_ref.at[c], out_ref.at[c], c_sems.at[0], c_sems.at[1], other)
    for copy in copies + far:
        copy.wait_send()
    near.wait()


def sums_step(v, nz, n_p):
    return plane_call(
        sums_kernel, "sums_step", 6, (v,),
        [((2, n_p) + v.shape, f32)],
        [
            pltpu.VMEM((nz,) + v.shape, f32),
            pltpu.SemaphoreType.DMA((2, nz - 1)),
            pltpu.SemaphoreType.DMA((2, 3)),
            pltpu.SemaphoreType.DMA((2,)),
        ],
    )[0]


def rope_tables(positions, pairs):
    freqs = rope_base ** (-2.0 * pairs.astype(f32) / HDIM)
    angles = positions.astype(f32)[:, None] * freqs[None, :]
    return jnp.cos(angles), jnp.sin(angles)


def plane_swap(x):
    n_p = lax.axis_size("p")
    p = lax.axis_index("p")
    out = x
    for d in range(1, n_p):
        other = jnp.bitwise_xor(p, d)
        block = lax.dynamic_index_in_dim(x, other, 0, keepdims=True)
        came = lax.ppermute(block, "p", [(i, i ^ d) for i in range(n_p)])
        out = lax.dynamic_update_slice_in_dim(out, came, other, 0)
    return out


def plane_gather(x):
    n_p = lax.axis_size("p")
    p = lax.axis_index("p")
    out = jnp.zeros((n_p,) + x.shape, x.dtype)
    out = lax.dynamic_update_slice_in_dim(out, x[None], p, 0)
    for d in range(1, n_p):
        came = lax.ppermute(x, "p", [(i, i ^ d) for i in range(n_p)])
        out = lax.dynamic_update_slice_in_dim(out, came[None], jnp.bitwise_xor(p, d), 0)
    return out


def plane_sum(x):
    n_p = lax.axis_size("p")
    p = lax.axis_index("p")
    total = lax.dynamic_index_in_dim(x, p, 0, keepdims=False).astype(f32)
    for d in range(1, n_p):
        block = lax.dynamic_index_in_dim(x, jnp.bitwise_xor(p, d), 0, keepdims=False)
        came = lax.ppermute(block.astype(bf16), "p", [(i, i ^ d) for i in range(n_p)])
        total = total + came.astype(f32)
    return total


def swap_core(x):
    return lax.ppermute(x, "head", [(0, 1), (1, 0)])


def block_sum(part):
    ci = lax.axis_index("head")
    mine = lax.dynamic_index_in_dim(part, ci, 1, keepdims=False)
    other = lax.dynamic_index_in_dim(part, 1 - ci, 1, keepdims=False)
    return plane_sum(mine + swap_core(other.astype(bf16)).astype(f32))


def join_cores(mine):
    ci = lax.axis_index("head")
    other = swap_core(mine)
    out = jnp.concatenate([mine, mine])
    return lax.dynamic_update_slice_in_dim(out, other, (1 - ci) * mine.shape[0], 0)


def carry_states(state, decays, sign):
    nz = lax.axis_size("z")
    low = state.astype(bf16)
    total, factor = None, None
    for d in range(1, nz):
        route = [(i, i + sign * d) for i in range(nz) if 0 <= i + sign * d < nz]
        came = lax.ppermute(low, "z", route).astype(f32)
        rate = lax.ppermute(decays, "z", route)
        total = came if total is None else total + factor * came
        factor = rate if factor is None else factor * rate
    return total


def shards(
    hidden_in,
    grad_out,
    doc_starts,
    norm_mixer,
    norm_ffn,
    mamba_z,
    mamba_x,
    mamba_bc,
    mamba_dt,
    conv_x,
    conv_bc,
    a_log,
    dt_bias,
    skip_gain,
    mamba_out,
    attn_query,
    attn_key,
    attn_value,
    attn_out,
    ffn_gate,
    ffn_up,
    ffn_down,
):
    own = hidden_in.shape[0]
    width = hidden_in.shape[1]
    half = own // 2
    nz, n_p = lax.axis_size("z"), lax.axis_size("p")
    zi, pi, ci = lax.axis_index("z"), lax.axis_index("p"), lax.axis_index("head")
    tok = own * n_p
    base = zi * tok
    positions = base + jnp.arange(tok, dtype=jnp.int32)
    edge = conv_x.shape[0] - 1
    ext_docs = doc_ids(base - edge + jnp.arange(tok + edge, dtype=jnp.int32), doc_starts)
    rows = mamba_z.shape[0]
    n_heads = a_log.shape[0] // n_p
    xw = n_heads * MHDIM
    bw = mamba_bc.shape[1] // (2 * n_p)
    cw = xw + 2 * bw
    kw = HDIM // n_p
    hk = kw // 2
    tail_w = 128 - 2 * kw - n_heads

    def cols(w):
        w = w.astype(bf16)
        return w.reshape(w.shape[0], n_p, -1).transpose(1, 0, 2)

    k_cols = attn_key.astype(bf16).reshape(rows, 2, n_p, hk)
    k_cols = k_cols.transpose(2, 0, 1, 3).reshape(n_p, rows, kw)
    bc_cols = mamba_bc.astype(bf16).reshape(rows, 2, n_p, bw)
    bc_cols = bc_cols.transpose(2, 0, 1, 3).reshape(n_p, rows, 2 * bw)
    q_cols = attn_query.astype(bf16).reshape(rows, n_p, 2, n_p, hk)
    q_cols = q_cols.transpose(1, 0, 3, 2, 4).reshape(n_p, rows, HDIM)
    piece_a = jnp.concatenate(
        [
            cols(mamba_x), bc_cols, k_cols, cols(attn_value), cols(mamba_dt),
            jnp.zeros((n_p, rows, tail_w), bf16),
        ],
        axis=2,
    )
    rest = [
        jnp.concatenate([q_cols, cols(mamba_z)], axis=2),
        jnp.concatenate([cols(mamba_out.T), cols(attn_out.T)], axis=2),
        jnp.concatenate([cols(ffn_gate), cols(ffn_up)], axis=2),
        cols(ffn_down.T),
    ]

    def along_z(piece):
        piece = piece.reshape(n_p * rows, piece.shape[2])
        return lax.all_gather(piece, "z", axis=0, tiled=True)

    gains_own = jnp.pad(
        jnp.stack([norm_mixer, norm_ffn]).astype(bf16).astype(f32), ((0, 6), (0, 128 - rows))
    )
    my_half = lambda v: lax.dynamic_slice_in_dim(v, ci * half, half, 0)
    hidden_own, grad_own = my_half(hidden_in), my_half(grad_out)
    gains, normed_one, g_ffn, w_a, *rest = open_step(
        hidden_own, grad_own, gains_own, piece_a, rest, tok, nz
    )
    w_a = w_a.reshape(nz * n_p * rows, w_a.shape[3])
    gains = gains.transpose(2, 1, 0, 3)[:, :, :, :rows].reshape(8, 1, width)
    gain_mix, gain_ffn = gains[0], gains[1]
    w_b, w_c, w_d, w_e = [along_z(piece) for piece in rest]

    in_ext = product(normed_one, w_a)
    in_b = product(normed_one, w_b)[:tok]
    in_a = in_ext[:tok]
    pre_ext = in_ext[:, :cw].astype(bf16)
    gate_z = in_b[:, HDIM:]
    slice_1 = lambda v, at, n: lax.dynamic_slice_in_dim(v, at, n, 1)
    taps = jnp.concatenate(
        [
            slice_1(conv_x, pi * xw, xw),
            slice_1(conv_bc, pi * bw, bw),
            slice_1(conv_bc, (n_p + pi) * bw, bw),
        ],
        axis=1,
    )
    ext = jnp.concatenate([pre_ext[tok + HALO - edge :], pre_ext[:tok]], axis=0)
    conv_in = convolve(ext, taps, ext_docs, tok)
    ssm = jax.nn.silu(conv_in).astype(bf16)
    head_slice = lambda v: lax.dynamic_slice_in_dim(v, pi * n_heads, n_heads, 0)
    my_bias, my_a, my_skip = head_slice(dt_bias), head_slice(a_log), head_slice(skip_gain)
    lanes = lambda v: jnp.pad(v, (0, 128 - n_heads))[None, :]
    dt_at = cw + 2 * kw
    dt_pre = jnp.pad(in_a[:, dt_at : dt_at + n_heads], ((0, 0), (0, 128 - n_heads))) + lanes(my_bias)
    neg_rate = lanes(-jnp.exp(my_a))
    skip_full = jnp.repeat(my_skip, MHDIM)[None, :]
    bc_all = gather_bc(ssm, xw // 128, n_p)
    pair_ids = pi * hk + jnp.arange(hk)
    cos_k, sin_k = rope_tables(positions, pair_ids)
    k0, k1 = in_a[:, cw : cw + hk], in_a[:, cw + hk : cw + kw]
    key_own = jnp.concatenate([k0 * cos_k - k1 * sin_k, k1 * cos_k + k0 * sin_k], axis=1)
    val_own = in_a[:, cw + kw : cw + 2 * kw]
    kv_own = jnp.concatenate([key_own, val_own], axis=1).astype(bf16)
    kv_own = jnp.concatenate([kv_own[: tok // 2], kv_own[tok // 2 :]], axis=1)
    kv = jnp.zeros((nz, tok // 2, 4 * kw), bf16)
    kv = lax.dynamic_update_slice_in_dim(kv, kv_own[None], zi, 0)
    for d in range(1, nz):
        came = passed_along(kv_own, "z", d)
        kv = lax.dynamic_update_slice_in_dim(kv, came[None], (zi - d) % nz, 0)
    kv = plane_gather(kv)
    cos_q, sin_q = rope_tables(positions, jnp.arange(HDIM // 2))
    cos_q, sin_q = cos_q.reshape(tok, n_p, hk), sin_q.reshape(tok, n_p, hk)

    def rope_q(v, sign):
        v = v.reshape(tok, n_p, 2, hk)
        a, b = v[:, :, 0], v[:, :, 1]
        return jnp.stack(
            [a * cos_q - sign * b * sin_q, b * cos_q + sign * a * sin_q], axis=2
        ).reshape(tok, HDIM)

    queries = rope_q(in_b[:, :HDIM], 1.0).astype(bf16)

    base_arr = jnp.reshape(base, (1,)).astype(jnp.int32)
    y_local, span_starts, local_state, dev_decay, decay_full, c_mat = ssd_forward(
        base_arr, doc_starts, ssm, bc_all, dt_pre, neg_rate, skip_full
    )
    total_decay = decay_full[-1][:, None]
    in_state = carry_states(local_state, total_decay, 1)

    attn_f32, lse, keys, values = attend(base_arr, doc_starts, queries, kv)
    attn_low = attn_f32.astype(bf16)
    y_flat = y_local + product_nt(c_mat, in_state.astype(bf16)) * decay_full
    silu_z = jax.nn.silu(gate_z)
    gated = (y_flat * silu_z).astype(bf16)
    mixed = jnp.concatenate([gated, attn_low], axis=1)

    mid_own, normed_two = mid_step(mixed, w_c, hidden_own, gain_ffn)
    gu = product(normed_two, w_d)
    ffw = gu.shape[1] // 2
    gate_val, up_val = gu[:, :ffw], gu[:, ffw:]
    silu_gate = jax.nn.silu(gate_val)
    activated = (silu_gate * up_val).astype(bf16)
    d_act = product(g_ffn, w_e)
    d_gu = jnp.concatenate(
        [d_act * up_val * silu_slope(gate_val), d_act * silu_gate], axis=1
    ).astype(bf16)
    grad_e = product_t(g_ffn, activated).astype(bf16)
    grad_d = product_t(normed_two, d_gu).astype(bf16)
    d_gu, grad_e, grad_d = lax.optimization_barrier((d_gu, grad_e, grad_d))

    def scattered(grad):
        return lax.psum_scatter(grad, "z", scatter_dimension=0, tiled=True)

    def swapped(grad):
        return plane_swap(grad.reshape(n_p, rows, grad.shape[1])).astype(f32)

    ge = scattered(grad_e)
    gd = scattered(grad_d)
    d_mid_own, grad_gain_ffn, g_mid = two_step(d_gu, w_d, mid_own, grad_own, gain_ffn)
    g_mid, ge = lax.optimization_barrier((g_mid, ge))
    ge = swapped(ge)
    out_part = product_nt(activated, w_e).reshape(n_p, 2, half, width)
    block_out = join_cores(mid_own + block_sum(out_part))

    d_mixed = product(g_mid, w_c)
    grad_c = product_t(g_mid, mixed).astype(bf16)
    gc = scattered(grad_c)
    d_gated = d_mixed[:, :xw]
    d_attn = d_mixed[:, xw:].astype(bf16)
    d_y_flat = d_gated * silu_z
    d_z = (d_gated * y_flat * silu_slope(gate_z)).astype(bf16)
    d_in_local = product_t((d_y_flat * decay_full).astype(bf16), c_mat)
    state_grad = carry_states(d_in_local, total_decay, -1)
    d_query, d_kv = attend_back(
        base_arr, doc_starts, queries, d_attn, attn_f32, lse, keys, values, kv.shape
    )
    d_q_pre = rope_q(d_query, -1.0).astype(bf16)
    d_b = jnp.concatenate([d_q_pre, d_z], axis=1)
    more = lambda v: jnp.pad(v, ((0, HALO), (0, 0)))
    grad_b = product_t(normed_one, more(d_b)).astype(bf16)
    gb = scattered(grad_b)
    d_kv = plane_sum(d_kv)
    d_kv_own = lax.dynamic_index_in_dim(d_kv, zi, 0, keepdims=False)
    for d in range(1, nz):
        block = lax.dynamic_index_in_dim(d_kv, (zi - d) % nz, 0, keepdims=False)
        d_kv_own = d_kv_own + passed_along(block.astype(bf16), "z", -d).astype(f32)
    d_kv_own = jnp.concatenate([d_kv_own[:, : 2 * kw], d_kv_own[:, 2 * kw :]], axis=0)
    dk0, dk1 = d_kv_own[:, :hk], d_kv_own[:, hk:kw]
    d_kv_low = jnp.concatenate(
        [dk0 * cos_k + dk1 * sin_k, dk1 * cos_k - dk0 * sin_k, d_kv_own[:, kw:]], axis=1
    ).astype(bf16)

    start_decay = jnp.concatenate([jnp.ones((1, 128), f32), dev_decay[SPAN - 1 :: SPAN][:-1]])
    d_y_flat, gd = lax.optimization_barrier((d_y_flat, gd))
    gd = swapped(gd)
    d_xs, d_bc, d_dt, sums, skip_sums = ssd_backward(
        base_arr, doc_starts, ssm, bc_all, dt_pre, d_y_flat, span_starts,
        start_decay[:, None, :], neg_rate, skip_full, in_state, state_grad,
    )
    d_bc, gc = lax.optimization_barrier((d_bc, gc))
    gc = swapped(gc)
    d_bc = reduce_bc(d_bc)
    du = jnp.concatenate([d_xs, d_bc], axis=1) * silu_slope(conv_in)
    d_ext, grad_taps = convolve_back(du, ext, taps, ext_docs, tok)
    next_rows = passed_along(d_ext[:edge], "z", -1)
    d_pre = (d_ext[edge:] + jnp.pad(next_rows, ((tok - edge, 0), (0, 0)))).astype(bf16)
    d_last = jnp.concatenate(
        [d_kv_low, d_dt[:, :n_heads].astype(bf16), jnp.zeros((tok, tail_w), bf16)], axis=1
    )
    d_a = jnp.concatenate([d_pre, d_last], axis=1)
    grad_a = product_t(normed_one, more(d_a)).astype(bf16)
    ga = swapped(scattered(grad_a))
    once = jnp.where(ci == 0, d_pre[:, xw:], jnp.zeros((), bf16))
    d_a_once = jnp.concatenate([d_pre[:, :xw], once, d_last], axis=1)
    d_a_once, grad_a, gb = lax.optimization_barrier((d_a_once, grad_a, gb))
    gb = swapped(gb)
    grad_in, grad_gain_mix = one_step(
        d_a_once, w_a, d_b, w_b, hidden_own, d_mid_own, gain_mix
    )

    flat = jnp.concatenate(
        [
            grad_gain_mix.reshape(-1, 128),
            grad_gain_ffn.reshape(-1, 128),
            grad_taps.reshape(-1, 128),
            sums[:2],
            jnp.pad(jnp.sum(skip_sums.reshape(n_heads, MHDIM), axis=1), (0, 128 - n_heads))[None],
        ]
    )
    flat = jnp.pad(flat, ((0, -flat.shape[0] % 8), (0, 0)))
    summed = sums_step(flat, nz, n_p)
    g_rows = width // 128
    t_rows = grad_taps.size // 128
    si = zi * n_p + pi
    gains_sum = jnp.sum(summed[:, :, : 2 * g_rows], axis=(0, 1)).reshape(2, width)
    gains_sum = lax.dynamic_slice_in_dim(gains_sum, si * rows, rows, 1)
    mine = lax.dynamic_index_in_dim(summed, ci, 0, keepdims=False)
    s_taps = mine[:, 2 * g_rows : 2 * g_rows + t_rows].reshape(n_p, edge + 1, cw).transpose(1, 0, 2)
    s_heads = mine[:, 2 * g_rows + t_rows : 2 * g_rows + t_rows + 3, :n_heads]
    s_heads = s_heads.transpose(1, 0, 2).reshape(3, n_p * n_heads)
    s_x = s_taps[:, :, :xw].reshape(edge + 1, n_p * xw)
    s_bc = summed[0][:, 2 * g_rows : 2 * g_rows + t_rows].reshape(n_p, edge + 1, cw)
    s_bc = s_bc[:, :, xw:].reshape(n_p, edge + 1, 2, bw).transpose(1, 2, 0, 3)
    s_bc = s_bc.reshape(edge + 1, 2 * n_p * bw)

    def uncols(g):
        return g.transpose(1, 0, 2).reshape(rows, -1)

    g_x = uncols(ga[:, :, :xw])
    g_bc = ga[:, :, xw:cw].reshape(n_p, rows, 2, bw).transpose(1, 2, 0, 3).reshape(rows, -1)
    g_k = ga[:, :, cw : cw + kw].reshape(n_p, rows, 2, hk)
    g_k = g_k.transpose(1, 2, 0, 3).reshape(rows, HDIM)
    g_v = uncols(ga[:, :, cw + kw : cw + 2 * kw])
    g_dt = uncols(ga[:, :, dt_at : dt_at + n_heads])
    g_q = gb[:, :, :HDIM].reshape(n_p, rows, n_p, 2, hk)
    g_q = g_q.transpose(1, 0, 3, 2, 4).reshape(rows, n_p * HDIM)
    g_z = uncols(gb[:, :, HDIM:])
    g_mout = uncols(gc[:, :, :xw]).T
    g_aout = uncols(gc[:, :, xw:]).T
    g_gate = uncols(gd[:, :, :ffw])
    g_up = uncols(gd[:, :, ffw:])
    g_down = uncols(ge).T
    return (
        block_out,
        grad_in,
        gains_sum[0],
        gains_sum[1],
        g_z,
        g_x,
        g_bc,
        g_dt,
        s_x,
        s_bc,
        s_heads[0],
        s_heads[1],
        s_heads[2],
        g_mout,
        g_q,
        g_k,
        g_v,
        g_aout,
        g_gate,
        g_up,
        g_down,
    )


def solution(mesh):
    seq, head = mesh.shape["seq"], mesh.shape["head"]
    plane = math.gcd(seq, 4)
    grid = Mesh(mesh.devices.reshape(seq // plane, plane, head), ("z", "p", "head"))
    s = ("z", "p")
    h = "head"
    placed = (
        P(s, None), P(s, None), P(), P(s), P(s), P(s, h), P(s, h), P(s, None), P(s, h),
        P(None, h), P(), P(h), P(h), P(h), P(h, s), P(s, h), P(s, h), P(s, h), P(h, s),
        P(s, h), P(s, h), P(h, s),
    )
    given = (
        P(s, None), P(s, None), P(s), P(s), P(s, h), P(s, h), P(s, None), P(s, h),
        P(None, h), P(), P(h), P(h), P(h), P(h, s), P(s, h), P(s, h), P(s, h), P(h, s),
        P(s, h), P(s, h), P(h, s),
    )
    return jax.shard_map(shards, mesh=grid, in_specs=placed, out_specs=given, check_vma=False)
```

```python
import functools
import math

import jax
import jax.numpy as jnp
from jax import lax
from jax.experimental import pallas as pl
from jax.experimental.pallas import tpu as pltpu
from jax.sharding import Mesh
from jax.sharding import PartitionSpec as P

MHDIM = 64
NSTATE = 256
HDIM = 128
SPAN = 128

eps_norm = 1e-05
rope_base = 100000000000.0
neg_large = -1e30
top_prec = lax.Precision.HIGHEST
bf16 = jnp.bfloat16
f32 = jnp.float32
MESH = pl.DeviceIdType.MESH
VMEM_LIMIT = 56 * 1024 * 1024


def doc_ids(positions, doc_starts):
    return jnp.sum((doc_starts[None, :] <= positions[:, None]).astype(jnp.int32), axis=1) - 1


def product(left, right):
    return jnp.dot(left, right, preferred_element_type=f32)


def product_t(left, right):
    return lax.dot_general(left, right, (((0,), (0,)), ((), ())), preferred_element_type=f32)


def product_nt(left, right):
    return lax.dot_general(left, right, (((1,), (1,)), ((), ())), preferred_element_type=f32)


def silu_slope(values):
    sigma_val = jax.nn.sigmoid(values)
    return sigma_val * (1.0 + values * (1.0 - sigma_val))


def convolve(extended, weights, ext_docs, tok_count):
    edge_rows = weights.shape[0] - 1
    here = ext_docs[edge_rows : edge_rows + tok_count]
    summed = jnp.zeros((tok_count, extended.shape[1]), f32)
    for tap_index in range(weights.shape[0]):
        begin_row = edge_rows - tap_index
        same_doc = (ext_docs[begin_row : begin_row + tok_count] == here)[:, None]
        rows = extended[begin_row : begin_row + tok_count].astype(f32)
        summed = summed + jnp.where(same_doc, rows, 0.0) * weights[tap_index][None, :]
    return summed


def convolve_back(d_conv, extended, weights, ext_docs, tok_count):
    edge_rows = weights.shape[0] - 1
    here = ext_docs[edge_rows : edge_rows + tok_count]
    d_rows = jnp.zeros((tok_count, d_conv.shape[1]), f32)
    tap_grads = []
    for tap_index in range(weights.shape[0]):
        begin_row = edge_rows - tap_index
        before = (ext_docs[begin_row : begin_row + tok_count] == here)[:, None]
        rows = extended[begin_row : begin_row + tok_count].astype(f32)
        tap_grads.append(jnp.sum(jnp.where(before, d_conv[:tok_count] * rows, 0.0), axis=0))
        last = edge_rows + tap_index
        after = (ext_docs[last : last + tok_count] == here)[:, None]
        ahead = d_conv[tap_index : tap_index + tok_count]
        d_rows = d_rows + jnp.where(after, ahead, 0.0) * weights[tap_index][None, :]
    return (d_rows, jnp.stack(tap_grads))


def tri_dot(a, b, dims=((1,), (0,))):
    return lax.dot_general(a, b, (dims, ((), ())), precision=top_prec, preferred_element_type=f32)


def dot_nn(a, b):
    return lax.dot_general(a, b, (((1,), (0,)), ((), ())), preferred_element_type=f32)


def dot_nt(a, b):
    return lax.dot_general(a, b, (((1,), (1,)), ((), ())), preferred_element_type=f32)


def dot_tn(a, b):
    return lax.dot_general(a, b, (((0,), (0,)), ((), ())), preferred_element_type=f32)


def iota2(shape, dim):
    return lax.broadcasted_iota(jnp.int32, shape, dim)


def docs_of(pos, starts_ref):
    count = jnp.where(starts_ref[0] <= pos, 1, 0)
    for i in range(1, starts_ref.shape[0]):
        count = count + jnp.where(starts_ref[i] <= pos, 1, 0)
    return count - 1


def softplus(v):
    return jnp.maximum(v, 0.0) + jnp.log(1.0 + jnp.exp(-jnp.abs(v)))


def head_maps(xw):
    lane_head = (iota2((128, xw), 1) // MHDIM == iota2((128, xw), 0)).astype(f32)
    row_head = (iota2((xw, 128), 0) // MHDIM == iota2((xw, 128), 1)).astype(f32)
    return lane_head, row_head


def span_setup(k, base_ref, starts_ref, dtp, nega):
    first = base_ref[0] + k * SPAN
    t_idx, s_idx = iota2((SPAN, SPAN), 0), iota2((SPAN, SPAN), 1)
    docs_t = docs_of(first + t_idx, starts_ref)
    docs_s = docs_of(first + s_idx, starts_ref)
    linked = (docs_t == docs_s) & (t_idx >= s_idx)
    dt = softplus(dtp)
    la = nega * dt
    tri = (t_idx >= s_idx).astype(f32)
    cum = tri_dot(tri, la)
    before = docs_of(first - 1, starts_ref)
    last_doc = docs_of(first + SPAN - 1, starts_ref)
    carried = jnp.where(docs_t == before, jnp.exp(cum), 0.0)
    cum_last = cum[SPAN - 1 : SPAN, :]
    tail = jnp.where(docs_t == last_doc, jnp.exp(cum_last - cum), 0.0)
    return docs_t, linked, dt, la, tri, cum, carried, tail


def split_bc(bc_ref):
    parts = [bc_ref[q] for q in range(bc_ref.shape[0])]
    half = parts[0].shape[1] // 2
    return (
        jnp.concatenate([part[:, :half] for part in parts], axis=1),
        jnp.concatenate([part[:, half:] for part in parts], axis=1),
    )


def ssd_forward_kernel(
    n_heads, base_ref, starts_ref, x_ref, bc_ref, dtp_ref, nega_ref, skip_ref,
    y_ref, span_ref, final_ref, decay_ref, wide_ref, c_out, state, running,
):
    k = pl.program_id(0)
    xw = n_heads * MHDIM

    @pl.when(k == 0)
    def _():
        state[...] = jnp.zeros_like(state)
        running[...] = jnp.zeros_like(running)

    docs_t, linked, dt, la, tri, cum, carried, tail = span_setup(
        k, base_ref, starts_ref, dtp_ref[...], nega_ref[...]
    )
    lane_head, row_head = head_maps(xw)
    prev_doc = docs_of(base_ref[0] - 1, starts_ref)
    since = jnp.where(docs_t == prev_doc, jnp.exp(running[0:1, :] + cum), 0.0)
    decay_ref[...] = since
    wide_ref[...] = tri_dot(since, lane_head)
    running[...] = running[...] + cum[SPAN - 1 : SPAN, :]
    start = state[...]
    span_ref[0] = start
    x, (b, c) = x_ref[...], split_bc(bc_ref)
    c_out[...] = c
    inner = dot_nt(c, b)
    cum_t, dt_t = cum.T, dt.T
    lane = iota2((SPAN, 128), 1)
    pieces = []
    for pair in range(n_heads // 2):
        xp = x[:, pair * 128 : pair * 128 + 128]
        got = []
        for h in (2 * pair, 2 * pair + 1):
            gap = jnp.where(linked, cum[:, h : h + 1] - cum_t[h : h + 1, :], neg_large)
            w = jnp.exp(gap) * inner * dt_t[h : h + 1, :]
            got.append(dot_nn(w.astype(bf16), xp))
        pieces.append(jnp.where(lane < MHDIM, got[0], got[1]))
    y = jnp.concatenate(pieces, axis=1)
    y = y + dot_nt(c, start.astype(bf16)) * tri_dot(carried, lane_head)
    xf = x.astype(f32)
    y_ref[...] = y + skip_ref[...] * xf
    xt = (xf * tri_dot(tail * dt, lane_head)).astype(bf16)
    keep = jnp.sum(row_head * carried[SPAN - 1 : SPAN, :], axis=1, keepdims=True)
    new = dot_tn(xt, b) + keep * start
    state[...] = new
    final_ref[...] = new


def ssd_forward(base, doc_starts, x, bc, dtp, nega, skip):
    tok, xw, n_p = x.shape[0], skip.shape[1], bc.shape[0]
    n_heads, nspan = xw // MHDIM, tok // SPAN
    row = lambda n: pl.BlockSpec((SPAN, n), lambda i: (i, 0))
    whole = lambda *s: pl.BlockSpec(s, lambda i: (0,) * len(s))
    smem = pl.BlockSpec(memory_space=pltpu.SMEM)
    return pl.pallas_call(
        functools.partial(ssd_forward_kernel, n_heads),
        grid=(nspan,),
        in_specs=[
            smem, smem, row(xw), pl.BlockSpec((n_p, SPAN, 128), lambda i: (0, i, 0)), row(128),
            whole(1, 128), whole(1, xw),
        ],
        out_specs=[
            row(xw),
            pl.BlockSpec((1, xw, NSTATE), lambda i: (i, 0, 0)),
            whole(xw, NSTATE),
            row(128),
            row(xw),
            row(NSTATE),
        ],
        out_shape=[
            jax.ShapeDtypeStruct((tok, xw), f32),
            jax.ShapeDtypeStruct((nspan, xw, NSTATE), f32),
            jax.ShapeDtypeStruct((xw, NSTATE), f32),
            jax.ShapeDtypeStruct((tok, 128), f32),
            jax.ShapeDtypeStruct((tok, xw), f32),
            jax.ShapeDtypeStruct((tok, NSTATE), bf16),
        ],
        scratch_shapes=[pltpu.VMEM((xw, NSTATE), f32), pltpu.VMEM((8, 128), f32)],
        compiler_params=pltpu.CompilerParams(vmem_limit_bytes=VMEM_LIMIT),
        cost_estimate=pl.CostEstimate(
            flops=2 * tok * xw * NSTATE * 3, bytes_accessed=40_000_000, transcendentals=0
        ),
        name="ssd_forward",
    )(base, doc_starts, x, bc, dtp, nega, skip)


def ssd_backward_kernel(
    n_heads, base_ref, starts_ref, x_ref, bc_ref, dtp_ref, dy_ref, span_ref, decay_ref,
    nega_ref, skip_ref, in_ref, grad_ref,
    dx_ref, dbc_ref, ddt_ref, sums_ref, gskip_ref, gstate,
):
    step = pl.program_id(0)
    k = pl.num_programs(0) - 1 - step
    xw = n_heads * MHDIM

    @pl.when(step == 0)
    def _():
        gstate[...] = grad_ref[...]
        sums_ref[...] = jnp.zeros_like(sums_ref)
        gskip_ref[...] = jnp.zeros_like(gskip_ref)

    nega = nega_ref[...]
    docs_t, linked, dt, la, tri, cum, carried, tail = span_setup(
        k, base_ref, starts_ref, dtp_ref[...], nega
    )
    lane_head, row_head = head_maps(xw)
    begin = jnp.sum(row_head * decay_ref[0], axis=1, keepdims=True)
    start = span_ref[0] + begin * in_ref[...]
    start_low = start.astype(bf16)
    g = gstate[...]
    g_low = g.astype(bf16)
    x, (b, c), dy = x_ref[...], split_bc(bc_ref), dy_ref[...]
    dy_low = dy.astype(bf16)
    xf = x.astype(f32)
    inner = dot_nt(c, b)
    cum_t, dt_t = cum.T, dt.T
    lane = iota2((SPAN, 128), 1)
    row8 = iota2((SPAN, 128), 0)
    d_inner = jnp.zeros((SPAN, SPAN), f32)
    r_cols = jnp.zeros((SPAN, 128), f32)
    k_rows = jnp.zeros((SPAN, 128), f32)
    u_pieces = []
    for pair in range(n_heads // 2):
        xp = x[:, pair * 128 : pair * 128 + 128]
        dyp = dy_low[:, pair * 128 : pair * 128 + 128]
        got = []
        for j, h in enumerate((2 * pair, 2 * pair + 1)):
            mine = (lane < MHDIM) if j == 0 else (lane >= MHDIM)
            gap = jnp.where(linked, cum[:, h : h + 1] - cum_t[h : h + 1, :], neg_large)
            e = jnp.exp(gap)
            m = e * inner
            dyx = dot_nt(dyp, jnp.where(mine, xp, jnp.zeros_like(xp)))
            ed = dyx * dt_t[h : h + 1, :]
            d_inner = d_inner + e * ed
            pairs = m * ed
            r_cols = jnp.where(lane == h, jnp.sum(pairs, axis=1, keepdims=True), r_cols)
            k_rows = jnp.where(row8 == h, jnp.sum(pairs, axis=0, keepdims=True), k_rows)
            got.append(dot_tn(m.astype(bf16), dyp))
        u_pieces.append(jnp.where(lane < MHDIM, got[0], got[1]))
    u = jnp.concatenate(u_pieces, axis=1)
    dye = dy * tri_dot(carried, lane_head)
    dye_low = dye.astype(bf16)
    di_low = d_inner.astype(bf16)
    r_state = tri_dot(dye * dot_nt(c, start_low), row_head)
    u_state = dot_nt(b, g_low) * tri_dot(tail, lane_head)
    u = u + u_state
    dt_full = tri_dot(dt, lane_head)
    k_state = dt * tri_dot(xf * u_state, row_head)
    d_dt = tri_dot(xf * u, row_head)
    tail_x = (xf * tri_dot(tail * dt, lane_head)).astype(bf16)
    dx_ref[...] = dt_full * u + skip_ref[...] * dy
    d_b = dot_nn(tail_x, g_low) + dot_tn(di_low, c)
    d_c = dot_nn(dye_low, start_low) + dot_nn(di_low, b)
    bw = 64
    for q in range(dbc_ref.shape[0]):
        cut = slice(q * bw, q * bw + bw)
        dbc_ref[q] = jnp.concatenate([d_b[:, cut], d_c[:, cut]], axis=1)
    gs = jnp.sum(g * start, axis=1, keepdims=True)
    gs_row = jnp.sum(row_head * gs, axis=0, keepdims=True)
    last = jnp.sum(k_state, axis=0, keepdims=True) + carried[SPAN - 1 : SPAN, :] * gs_row
    d_cum = r_cols - k_rows.T + r_state - k_state + jnp.where(row8 == SPAN - 1, last, 0.0)
    d_la = tri_dot(tri, d_cum, ((0,), (0,)))
    live = lane < n_heads
    dtp = dtp_ref[...]
    d_in = jnp.where(live, (d_dt + nega * d_la) * jax.nn.sigmoid(dtp), 0.0)
    ddt_ref[...] = d_in
    sum_a = jnp.sum(jnp.where(live, d_la * la, 0.0), axis=0, keepdims=True)
    sum_b = jnp.sum(d_in, axis=0, keepdims=True)
    pick = iota2((8, 128), 0)
    sums_ref[...] += jnp.where(pick == 0, sum_a, jnp.where(pick == 1, sum_b, 0.0))
    gskip_ref[...] += jnp.sum(dy * xf, axis=0, keepdims=True)
    keep = jnp.sum(row_head * carried[SPAN - 1 : SPAN, :], axis=1, keepdims=True)
    gstate[...] = keep * g + dot_tn(dye_low, c)


def ssd_backward(
    base, doc_starts, x, bc, dtp, dy, span_starts, start_decay, nega, skip, in_state, grad_state
):
    tok, xw, n_p = x.shape[0], skip.shape[1], bc.shape[0]
    wide = pl.BlockSpec((n_p, SPAN, 128), lambda i: (0, nspan - 1 - i, 0))
    n_heads, nspan = xw // MHDIM, tok // SPAN
    row = lambda n: pl.BlockSpec((SPAN, n), lambda i: (nspan - 1 - i, 0))
    whole = lambda *s: pl.BlockSpec(s, lambda i: (0,) * len(s))
    smem = pl.BlockSpec(memory_space=pltpu.SMEM)
    return pl.pallas_call(
        functools.partial(ssd_backward_kernel, n_heads),
        grid=(nspan,),
        in_specs=[
            smem, smem, row(xw), wide, row(128), row(xw),
            pl.BlockSpec((1, xw, NSTATE), lambda i: (nspan - 1 - i, 0, 0)),
            pl.BlockSpec((1, 1, 128), lambda i: (nspan - 1 - i, 0, 0)),
            whole(1, 128), whole(1, xw), whole(xw, NSTATE), whole(xw, NSTATE),
        ],
        out_specs=[row(xw), wide, row(128), whole(8, 128), whole(1, xw)],
        out_shape=[
            jax.ShapeDtypeStruct((tok, xw), f32),
            jax.ShapeDtypeStruct((n_p, tok, 128), f32),
            jax.ShapeDtypeStruct((tok, 128), f32),
            jax.ShapeDtypeStruct((8, 128), f32),
            jax.ShapeDtypeStruct((1, xw), f32),
        ],
        scratch_shapes=[pltpu.VMEM((xw, NSTATE), f32)],
        compiler_params=pltpu.CompilerParams(vmem_limit_bytes=VMEM_LIMIT),
        cost_estimate=pl.CostEstimate(
            flops=2 * tok * xw * NSTATE * 8, bytes_accessed=80_000_000, transcendentals=0
        ),
        name="ssd_backward",
    )(base, doc_starts, x, bc, dtp, dy, span_starts, start_decay, nega, skip, in_state, grad_state)


QB = 512
KB = 512


def sight(base_ref, starts_ref, q_first):
    q_pos = base_ref[0] + q_first + iota2((QB, 1), 0)
    low = jnp.zeros((QB, 1), jnp.int32)
    for i in range(starts_ref.shape[0]):
        low = jnp.where(starts_ref[i] <= q_pos, starts_ref[i], low)
    return jnp.broadcast_to(low, (QB, KB)), jnp.broadcast_to(q_pos, (QB, KB))


def seen(low, high, k_first):
    k_pos = k_first + iota2((QB, KB), 1)
    return (k_pos >= low) & (k_pos <= high)


def attend_kernel(scale, base_ref, starts_ref, q_ref, kv_ref, o_ref, lse_ref, k_ref, v_ref):
    i = pl.program_id(0)

    @pl.when(i == 0)
    def _():
        n_p, nz, rows, _ = kv_ref.shape
        kw = HDIM // n_p

        @pl.loop(0, nz)
        def _(z):
            parts = [kv_ref[q, z] for q in range(n_p)]
            for t in range(2):
                at = pl.ds(pl.multiple_of((2 * z + t) * rows, rows), rows)
                lo = 2 * kw * t
                k_ref[at, :] = jnp.concatenate([v[:, lo : lo + kw] for v in parts], axis=1)
                v_ref[at, :] = jnp.concatenate([v[:, lo + kw : lo + 2 * kw] for v in parts], axis=1)

    q = q_ref[...]
    low, high = sight(base_ref, starts_ref, i * QB)
    blocks = (base_ref[0] + (i + 1) * QB + KB - 1) // KB

    def turn(j, carry):
        m, l, acc = carry
        at = pl.ds(pl.multiple_of(j * KB, KB), KB)
        s = dot_nt(q, k_ref[at, :]) * scale
        s = jnp.where(seen(low, high, j * KB), s, neg_large)
        m_new = jnp.maximum(m, jnp.max(s, axis=1, keepdims=True))
        w = jnp.exp(s - m_new)
        r = jnp.exp(m - m_new)
        l = l * r + jnp.sum(w, axis=1, keepdims=True)
        return m_new, l, acc * r + dot_nn(w.astype(bf16), v_ref[at, :])

    m, l, acc = lax.fori_loop(
        0,
        blocks,
        turn,
        (jnp.full((QB, 1), 0.1 * neg_large, f32), jnp.zeros((QB, 1), f32), jnp.zeros((QB, HDIM), f32)),
    )
    o_ref[...] = acc / l
    lse_ref[...] = jnp.broadcast_to(m + jnp.log(l), (QB, 128))


def attend(base, doc_starts, q, kv):
    tok = q.shape[0]
    keys = kv.shape[1] * kv.shape[2] * 2
    row = pl.BlockSpec((QB, HDIM), lambda i: (i, 0))
    whole = lambda s: pl.BlockSpec(s, lambda i: (0,) * len(s))
    smem = pl.BlockSpec(memory_space=pltpu.SMEM)
    return pl.pallas_call(
        functools.partial(attend_kernel, HDIM ** (-0.5)),
        grid=(tok // QB,),
        in_specs=[smem, smem, row, whole(kv.shape)],
        out_specs=[row, row, whole((keys, HDIM)), whole((keys, HDIM))],
        out_shape=[jax.ShapeDtypeStruct((tok, HDIM), f32)] * 2
        + [jax.ShapeDtypeStruct((keys, HDIM), bf16)] * 2,
        compiler_params=pltpu.CompilerParams(vmem_limit_bytes=VMEM_LIMIT),
        cost_estimate=pl.CostEstimate(
            flops=4 * tok * keys * HDIM, bytes_accessed=30_000_000, transcendentals=0
        ),
        name="attend",
    )(base, doc_starts, q, kv)


def attend_back_kernel(
    scale, base_ref, starts_ref, q_ref, do_ref, o_ref, lse_ref, k_ref, v_ref,
    dq_ref, dkv_ref, dk_ref, dv_ref,
):
    i = pl.program_id(0)

    @pl.when(i == 0)
    def _():
        dk_ref[...] = jnp.zeros_like(dk_ref)
        dv_ref[...] = jnp.zeros_like(dv_ref)

    q, do = q_ref[...], do_ref[...]
    delta = jnp.sum(do.astype(f32) * o_ref[...], axis=1, keepdims=True)
    lse = lse_ref[:, 0:1]
    low, high = sight(base_ref, starts_ref, i * QB)
    blocks = (base_ref[0] + (i + 1) * QB + KB - 1) // KB

    def turn(j, dq):
        at = pl.ds(pl.multiple_of(j * KB, KB), KB)
        k, v = k_ref[at, :], v_ref[at, :]
        visible = seen(low, high, j * KB)
        s = dot_nt(q, k) * scale
        p = jnp.exp(jnp.where(visible, s - lse, neg_large))
        ds = (p * (dot_nt(do, v) - delta)).astype(bf16)
        dv_ref[at, :] += dot_tn(p.astype(bf16), do)
        dk_ref[at, :] += dot_tn(ds, q) * scale
        return dq + dot_nn(ds, k)

    dq_ref[...] = lax.fori_loop(0, blocks, turn, jnp.zeros((QB, HDIM), f32)) * scale

    @pl.when(i == pl.num_programs(0) - 1)
    def _():
        n_p, nz, rows, _ = dkv_ref.shape
        kw = HDIM // n_p

        @pl.loop(0, nz)
        def _(z):
            got = []
            for t in range(2):
                at = pl.ds(pl.multiple_of((2 * z + t) * rows, rows), rows)
                got += [dk_ref[at, :].astype(bf16), dv_ref[at, :].astype(bf16)]
            for q in range(n_p):
                cut = slice(q * kw, q * kw + kw)
                dkv_ref[q, z] = jnp.concatenate([v[:, cut] for v in got], axis=1)


def attend_back(base, doc_starts, q, do, o, lse, k, v, packed):
    tok = q.shape[0]
    row = pl.BlockSpec((QB, HDIM), lambda i: (i, 0))
    whole = lambda s: pl.BlockSpec(s, lambda i: (0,) * len(s))
    smem = pl.BlockSpec(memory_space=pltpu.SMEM)
    return pl.pallas_call(
        functools.partial(attend_back_kernel, HDIM ** (-0.5)),
        grid=(tok // QB,),
        in_specs=[smem, smem, row, row, row, row, whole(k.shape), whole(k.shape)],
        out_specs=[row, whole(packed)],
        out_shape=[
            jax.ShapeDtypeStruct((tok, HDIM), f32),
            jax.ShapeDtypeStruct(packed, bf16),
        ],
        scratch_shapes=[pltpu.VMEM(k.shape, f32), pltpu.VMEM(k.shape, f32)],
        compiler_params=pltpu.CompilerParams(vmem_limit_bytes=VMEM_LIMIT),
        cost_estimate=pl.CostEstimate(
            flops=10 * tok * k.shape[0] * HDIM, bytes_accessed=40_000_000, transcendentals=0
        ),
        name="attend_back",
    )(base, doc_starts, q, do, o, lse, k, v)


def one_at(shape, source, where=True):
    lane = iota2(shape, 1)
    return ((iota2(shape, 0) == source(lane)) & where).astype(bf16)


def eye(n):
    return one_at((n, n), lambda lane: lane)


def q_order(kw):
    hk = kw // 2
    return one_at(
        (HDIM, HDIM), lambda l: ((l % kw) // hk) * (HDIM // 2) + (l // kw) * hk + l % hk
    )


def bc_order(p, bw, n_p):
    return one_at((2 * n_p * bw, 2 * bw), lambda l: (l // bw) * (n_p * bw) + p * bw + l % bw)


def last_order(p, kw, n_heads, dt_rows):
    hk = kw // 2
    lane = iota2((HDIM, 128), 1)
    lane_dt = iota2((dt_rows, 128), 1)
    key = one_at((HDIM, 128), lambda l: (l // hk) * (HDIM // 2) + p * hk + l % hk, lane < kw)
    value = one_at((HDIM, 128), lambda l: p * kw + l - kw, (lane >= kw) & (lane < 2 * kw))
    step = one_at(
        (dt_rows, 128),
        lambda l: p * n_heads + l - 2 * kw,
        (lane_dt >= 2 * kw) & (lane_dt < 2 * kw + n_heads),
    )
    return key, value, step


def pack_kernel(
    x_ref, bc_ref, k_ref, v_ref, dt_ref, q_ref, z_ref, mout_ref, aout_ref, gate_ref, up_ref,
    down_ref, a_ref, b_ref, c_ref, d_ref, e_ref,
):
    n_p = a_ref.shape[0]
    xw, bw, kw = x_ref.shape[1] // n_p, bc_ref.shape[1] // (2 * n_p), HDIM // n_p
    n_heads, ff, aw = dt_ref.shape[1] // n_p, gate_ref.shape[1] // n_p, q_ref.shape[1] // n_p
    bc, key, value = bc_ref[...].astype(bf16), k_ref[...].astype(bf16), v_ref[...].astype(bf16)
    step = dt_ref[...].astype(bf16)
    order = q_order(kw)
    for p in range(n_p):
        cut = lambda ref, n: ref[:, p * n : p * n + n].astype(bf16)
        flip = lambda ref, n: dot_tn(ref[p * n : p * n + n, :].astype(bf16), eye(n)).astype(bf16)
        a_ref[p, :, :xw] = cut(x_ref, xw)
        a_ref[p, :, xw : xw + 2 * bw] = dot_nn(bc, bc_order(p, bw, n_p)).astype(bf16)
        s_key, s_value, s_step = last_order(p, kw, n_heads, dt_ref.shape[1])
        a_ref[p, :, xw + 2 * bw :] = (
            dot_nn(key, s_key) + dot_nn(value, s_value) + dot_nn(step, s_step)
        ).astype(bf16)
        b_ref[p, :, :HDIM] = dot_nn(cut(q_ref, aw), order).astype(bf16)
        b_ref[p, :, HDIM:] = cut(z_ref, xw)
        c_ref[p, :, :xw] = flip(mout_ref, xw)
        c_ref[p, :, xw:] = flip(aout_ref, aw)
        d_ref[p, :, :ff] = cut(gate_ref, ff)
        d_ref[p, :, ff:] = cut(up_ref, ff)
        e_ref[p] = flip(down_ref, ff)


def pack(n_p, *weights):
    x, bc, k, v, dt, q, z, mout, aout, gate, up, down = weights
    rows = x.shape[0]
    ff, xw = gate.shape[1] // n_p, x.shape[1] // n_p
    widths = (xw + bc.shape[1] // n_p + 128, HDIM + xw, xw + HDIM, 2 * ff, ff)
    vm = pl.BlockSpec(memory_space=pltpu.VMEM)
    return pl.pallas_call(
        pack_kernel,
        in_specs=[vm] * 12,
        out_specs=[vm] * 5,
        out_shape=[jax.ShapeDtypeStruct((n_p, rows, w), bf16) for w in widths],
        compiler_params=pltpu.CompilerParams(vmem_limit_bytes=VMEM_LIMIT),
        cost_estimate=pl.CostEstimate(flops=0, bytes_accessed=10_000_000, transcendentals=0),
        name="pack",
    )(*weights)


def unpack_kernel(
    a_ref, b_ref, c_ref, d_ref, e_ref,
    x_ref, bc_ref, k_ref, v_ref, dt_ref, q_ref, z_ref, mout_ref, aout_ref, gate_ref, up_ref,
    down_ref,
):
    n_p, rows = a_ref.shape[0], a_ref.shape[1]
    xw, bw, kw = x_ref.shape[1] // n_p, bc_ref.shape[1] // (2 * n_p), HDIM // n_p
    n_heads, ff, aw = dt_ref.shape[1] // n_p, gate_ref.shape[1] // n_p, q_ref.shape[1] // n_p
    order, turn = q_order(kw), eye(rows)
    bc, key = jnp.zeros(bc_ref.shape, f32), jnp.zeros(k_ref.shape, f32)
    value, step = jnp.zeros(v_ref.shape, f32), jnp.zeros(dt_ref.shape, f32)
    for p in range(n_p):
        cut = lambda n: slice(p * n, p * n + n)
        x_ref[:, cut(xw)] = a_ref[p, :, :xw].astype(f32)
        bc = bc + dot_nt(a_ref[p, :, xw : xw + 2 * bw], bc_order(p, bw, n_p))
        last = a_ref[p, :, xw + 2 * bw :]
        s_key, s_value, s_step = last_order(p, kw, n_heads, dt_ref.shape[1])
        key, value = key + dot_nt(last, s_key), value + dot_nt(last, s_value)
        step = step + dot_nt(last, s_step)
        q_ref[:, cut(aw)] = dot_nt(b_ref[p, :, :HDIM], order)
        z_ref[:, cut(xw)] = b_ref[p, :, HDIM:].astype(f32)
        mout_ref[cut(xw), :] = dot_tn(c_ref[p, :, :xw], turn)
        aout_ref[cut(aw), :] = dot_tn(c_ref[p, :, xw:], turn)
        gate_ref[:, cut(ff)] = d_ref[p, :, :ff].astype(f32)
        up_ref[:, cut(ff)] = d_ref[p, :, ff:].astype(f32)
        down_ref[cut(ff), :] = dot_tn(e_ref[p], turn)
    bc_ref[...] = bc
    k_ref[...], v_ref[...], dt_ref[...] = key, value, step


def unpack(pieces, like):
    vm = pl.BlockSpec(memory_space=pltpu.VMEM)
    return pl.pallas_call(
        unpack_kernel,
        in_specs=[vm] * 5,
        out_specs=[vm] * 12,
        out_shape=[jax.ShapeDtypeStruct(w.shape, f32) for w in like],
        compiler_params=pltpu.CompilerParams(vmem_limit_bytes=VMEM_LIMIT),
        cost_estimate=pl.CostEstimate(flops=0, bytes_accessed=10_000_000, transcendentals=0),
        name="unpack",
    )(*pieces)


def at_rows(first, count):
    return pl.ds(pl.multiple_of(first, count), count)


def place():
    return lax.axis_index("z"), lax.axis_index("p"), lax.axis_index("head")


def hop(p, d):
    x, y = lax.rem(p, 2), p // 2
    return lax.rem(y + d // 2, 2) * 2 + lax.rem(x + d % 2, 2)


def chip(z, p, c):
    return (z, p, c)


def meet(others):
    barrier = pltpu.get_barrier_semaphore()
    for other in others:
        pl.semaphore_signal(barrier, inc=1, device_id=other, device_id_type=MESH)
    pl.semaphore_wait(barrier, len(others))


def send(src, dst, send_sem, recv_sem, to):
    copy = pltpu.make_async_remote_copy(
        src_ref=src, dst_ref=dst, send_sem=send_sem, recv_sem=recv_sem,
        device_id=to, device_id_type=MESH,
    )
    copy.start()
    return copy


HOPS = (3, 1, 2)


def z_chain(ref, up_sems, down_sems):
    z, p, c = place()
    nz = ref.shape[0]

    def block_up(k):
        at = ref.at[z - k]
        return pltpu.make_async_remote_copy(
            src_ref=at, dst_ref=at, send_sem=up_sems.at[0, k], recv_sem=up_sems.at[1, k],
            device_id=chip(z + 1, p, c), device_id_type=MESH,
        )

    def block_down(k):
        at = ref.at[z + k]
        return pltpu.make_async_remote_copy(
            src_ref=at, dst_ref=at, send_sem=down_sems.at[0, k], recv_sem=down_sems.at[1, k],
            device_id=chip(z - 1, p, c), device_id_type=MESH,
        )

    def got_up(k):
        at = ref.at[z - k]
        pltpu.make_async_remote_copy(
            src_ref=at, dst_ref=at, send_sem=up_sems.at[0, k - 1], recv_sem=up_sems.at[1, k - 1],
            device_id=chip(z - 1, p, c), device_id_type=MESH,
        ).wait_recv()

    def got_down(k):
        at = ref.at[z + k]
        pltpu.make_async_remote_copy(
            src_ref=at, dst_ref=at, send_sem=down_sems.at[0, k - 1],
            recv_sem=down_sems.at[1, k - 1],
            device_id=chip(z + 1, p, c), device_id_type=MESH,
        ).wait_recv()

    def stage(k):
        if k:

            @pl.when(z - k >= 0)
            def _():
                got_up(k)

        @pl.when((z - k >= 0) & (z + 1 < nz))
        def _():
            block_up(k).start()

        if k:

            @pl.when(z + k < nz)
            def _():
                got_down(k)

        @pl.when((z + k < nz) & (z > 0))
        def _():
            block_down(k).start()

    def done():
        for k in range(nz):

            @pl.when((z - k >= 0) & (z + 1 < nz))
            def _():
                block_up(k).wait_send()

            @pl.when((z + k < nz) & (z > 0))
            def _():
                block_down(k).wait_send()

    return stage, done


def share_rows(full_ref, half, own_sems, far_sems, near_sems, between=None):
    z, p, c = place()
    other = chip(z, p, 1 - c)
    mine = full_ref.at[at_rows((p * 2 + c) * half, half), :]
    copies = []
    for i, d in enumerate(HOPS):
        copies.append(send(mine, mine, far_sems.at[0, i], far_sems.at[1, i], chip(z, hop(p, d), c)))
    copies.append(send(mine, mine, own_sems.at[0], own_sems.at[1], other))
    if between is not None:
        between()
    onward = []
    for i, d in ((1, 1), (2, 2), (0, 3)):
        copies[i].wait_recv()
        came = full_ref.at[at_rows((hop(p, d) * 2 + c) * half, half), :]
        onward.append(send(came, came, near_sems.at[0, i], near_sems.at[1, i], other))
    return copies, onward


def finish_share(copies, onward):
    for copy in copies[:3]:
        copy.wait_send()
    copies[3].wait()
    for copy in onward:
        copy.wait()


def reduce_blocks(pairs, part, keep, sib_out, sib_in, out, came, near_sems, far_sems):
    z, p, c = place()
    other = chip(z, p, 1 - c)
    half = keep.shape[1]
    width = keep.shape[2]
    tile = part.shape[1]
    near, far = [], []

    def pass_on(i, d):
        near[i].wait_recv()

        @pl.loop(0, half // 16)
        def _(r):
            at = at_rows(r * 16, 16)
            out[i, at, :] = (keep[i, at, :] + sib_in[i, at, :].astype(f32)).astype(bf16)

        far.append(
            send(out.at[i], came.at[i], far_sems.at[0, i], far_sems.at[1, i], chip(z, hop(p, d), c))
        )

    order = HOPS + (0,)
    for i, d in enumerate(order):
        rows = at_rows(hop(p, d) * (2 * half), 2 * half)

        @pl.loop(0, width // tile)
        def _(n):
            cols = at_rows(n * tile, tile)
            total = dot_nt(pairs[0][0][rows, :], pairs[0][1][cols, :])
            for left, right in pairs[1:]:
                total = total + dot_nt(left[rows, :], right[cols, :])
            part[...] = total
            keep[i, :, cols] = part[at_rows(c * half, half), :]
            sib_out[i, :, cols] = part[at_rows((1 - c) * half, half), :].astype(bf16)

        near.append(
            send(sib_out.at[i], sib_in.at[i], near_sems.at[0, i], near_sems.at[1, i], other)
        )
        if i:
            pass_on(i - 1, order[i - 1])
    def finish():
        near[3].wait_recv()
        for copy in far:
            copy.wait_recv()

    def total_rows(at):
        total = keep[3, at, :] + sib_in[3, at, :].astype(f32)
        return total + came[0, at, :].astype(f32) + came[1, at, :].astype(f32) + came[2, at, :].astype(f32)

    def done():
        for copy in near + far:
            copy.wait_send()

    return total_rows, finish, done


def greet():
    z, p, c = place()
    meet([chip(z, p, 1 - c)] + [chip(z, hop(p, d), c) for d in HOPS])


def rms(rows):
    return lax.rsqrt(jnp.mean(rows * rows, axis=1, keepdims=True) + eps_norm)


def mid_kernel(
    left, right, resid, gain, w_ref, mid_ref, full_ref, w_out,
    part, keep, sib_out, sib_in, out, came, n_sems, f_sems, own_sems, far_sems, near_sems,
    up_sems, down_sems, loc_sems,
):
    z, p, c = place()
    nz = w_out.shape[0]
    meet(
        [chip(z, p, 1 - c)]
        + [chip(z, hop(p, d), c) for d in HOPS]
        + [chip(lax.rem(z + d, nz), p, c) for d in (1, nz - 1)]
    )
    local = pltpu.make_async_copy(w_ref, w_out.at[z], loc_sems.at[0])
    local.start()
    local.wait()
    stage, chain_done = z_chain(w_out, up_sems, down_sems)
    stage(0)
    half = keep.shape[1]
    total_rows, finish, done = reduce_blocks(
        [(left, right)], part, keep, sib_out, sib_in, out, came, n_sems, f_sems
    )
    stage(1)
    finish()
    g = gain[...]

    @pl.loop(0, half // 16)
    def _(r):
        at = at_rows(r * 16, 16)
        mid = resid[at, :] + total_rows(at)
        mid_ref[at, :] = mid
        full_ref[at_rows((p * 2 + c) * half + r * 16, 16), :] = (mid * rms(mid) * g).astype(bf16)

    between = lambda: stage(2) if nz > 2 else None
    copies, onward = share_rows(full_ref, half, own_sems, far_sems, near_sems, between)
    for k in range(3, nz):
        stage(k)
    done()
    finish_share(copies, onward)
    chain_done()


def two_kernel(
    left, right, mid_own, grad_own, gain, dmid_ref, ggain_ref, full_ref,
    part, keep, sib_out, sib_in, out, came, n_sems, f_sems, own_sems, far_sems, near_sems,
):
    greet()
    z, p, c = place()
    half = keep.shape[1]
    total_rows, finish, done = reduce_blocks(
        [(left, right)], part, keep, sib_out, sib_in, out, came, n_sems, f_sems
    )
    finish()
    g = gain[...]
    ggain_ref[...] = jnp.zeros_like(ggain_ref)

    @pl.loop(0, half // 16)
    def _(r):
        at = at_rows(r * 16, 16)
        d_two, mid = total_rows(at), mid_own[at, :]
        scale = rms(mid)
        w = d_two * g
        d_mid = grad_own[at, :] + scale * w - mid * (scale * scale * scale) * jnp.mean(
            w * mid, axis=1, keepdims=True
        )
        ggain_ref[...] += jnp.sum(d_two * mid * scale, axis=0, keepdims=True)
        dmid_ref[at, :] = d_mid
        full_ref[at_rows((p * 2 + c) * half + r * 16, 16), :] = d_mid.astype(bf16)

    copies, onward = share_rows(full_ref, half, own_sems, far_sems, near_sems)
    done()
    finish_share(copies, onward)


def one_kernel(
    n, left_a, right_a, left_b, right_b, hidden_own, dmid_own, gain, act, w_act, mid_own, *refs
):
    ins, (grad_ref, block_ref, ggain_ref), outs = refs[:n], refs[n : n + 3], refs[n + 3 : 2 * n + 3]
    first, second = refs[2 * n + 3 : 2 * n + 11], refs[2 * n + 11 : 2 * n + 19]
    own_sems, w_sems, loc_sems = refs[2 * n + 19 :]
    greet()
    z, p, c = place()
    half = hidden_own.shape[0]
    total_rows, finish, done = reduce_blocks([(left_a, right_a), (left_b, right_b)], *first)
    total_out, finish_out, done_out = reduce_blocks([(act, w_act)], *second)
    moved = swap_begin(ins, outs, w_sems, loc_sems)
    g = gain[...]
    ggain_ref[...] = jnp.zeros_like(ggain_ref)
    finish()

    @pl.loop(0, half // 16)
    def _(r):
        at = at_rows(r * 16, 16)
        d_one, hid = total_rows(at), hidden_own[at, :]
        scale = rms(hid)
        w = d_one * g
        d_in = dmid_own[at, :] + scale * w - hid * (scale * scale * scale) * jnp.mean(
            w * hid, axis=1, keepdims=True
        )
        ggain_ref[...] += jnp.sum(d_one * hid * scale, axis=0, keepdims=True)
        grad_ref[at_rows(c * half + r * 16, 16), :] = d_in

    mine = at_rows(c * half, half)
    other = chip(z, p, 1 - c)
    copies = [
        send(grad_ref.at[mine, :], grad_ref.at[mine, :], own_sems.at[0, 0], own_sems.at[1, 0], other)
    ]
    finish_out()

    @pl.loop(0, half // 16)
    def _(r):
        at = at_rows(r * 16, 16)
        block_ref[at_rows(c * half + r * 16, 16), :] = mid_own[at, :] + total_out(at)

    copies.append(
        send(block_ref.at[mine, :], block_ref.at[mine, :], own_sems.at[0, 1], own_sems.at[1, 1], other)
    )
    done()
    done_out()
    for copy in copies + moved:
        copy.wait()


VM = pl.BlockSpec(memory_space=pltpu.VMEM)
ANYWHERE = pl.BlockSpec(memory_space=pl.ANY)


def swap_begin(ins, outs, sems, loc_sems):
    z, p, c = place()
    copies = []
    for j, (src, dst) in enumerate(zip(ins, outs)):
        for i, d in enumerate(HOPS):
            q = hop(p, d)
            copies.append(
                send(src.at[q], dst.at[p], sems.at[0, j, i], sems.at[1, j, i], chip(z, q, c))
            )
        local = pltpu.make_async_copy(src.at[p], dst.at[p], loc_sems.at[j])
        local.start()
        copies.append(local)
    return copies


def swap_sems(n):
    return [pltpu.SemaphoreType.DMA((2, n, 3)), pltpu.SemaphoreType.DMA((n,))]


def reduce_scratch(half, width):
    return [
        pltpu.VMEM((2 * half, 512), f32),
        pltpu.VMEM((4, half, width), f32),
        pltpu.VMEM((4, half, width), bf16),
        pltpu.VMEM((4, half, width), bf16),
        pltpu.VMEM((3, half, width), bf16),
        pltpu.VMEM((3, half, width), bf16),
        pltpu.SemaphoreType.DMA((2, 4)),
        pltpu.SemaphoreType.DMA((2, 3)),
    ]


SHARE_SEMS = [
    pltpu.SemaphoreType.DMA((2,)),
    pltpu.SemaphoreType.DMA((2, 3)),
    pltpu.SemaphoreType.DMA((2, 3)),
]


def plane_call(kernel, name, number, args, shapes, scratch, nbytes=150_000_000, moved=()):
    n = len(moved)
    if n:
        kernel = functools.partial(kernel, n)
        scratch = scratch + swap_sems(n)
    return pl.pallas_call(
        kernel,
        in_specs=[VM] * len(args) + [ANYWHERE] * n,
        out_specs=[VM] * len(shapes) + [ANYWHERE] * n,
        out_shape=[jax.ShapeDtypeStruct(s, t) for s, t in shapes]
        + [jax.ShapeDtypeStruct(m.shape, m.dtype) for m in moved],
        scratch_shapes=scratch,
        compiler_params=pltpu.CompilerParams(
            collective_id=number, has_side_effects=True, vmem_limit_bytes=VMEM_LIMIT
        ),
        cost_estimate=pl.CostEstimate(flops=0, bytes_accessed=nbytes, transcendentals=0),
        name=name,
    )(*args, *moved)


def mid_step(mixed, w, resid_own, gain, piece, nz):
    tok, width = mixed.shape[0], w.shape[0]
    half = resid_own.shape[0]
    dma = pltpu.SemaphoreType.DMA
    return pl.pallas_call(
        mid_kernel,
        in_specs=[VM] * 4 + [ANYWHERE],
        out_specs=[VM] * 2 + [ANYWHERE],
        out_shape=[
            jax.ShapeDtypeStruct((half, width), f32),
            jax.ShapeDtypeStruct((tok, width), bf16),
            jax.ShapeDtypeStruct((nz,) + piece.shape, bf16),
        ],
        scratch_shapes=reduce_scratch(half, width)
        + SHARE_SEMS
        + [dma((2, nz)), dma((2, nz)), dma((1,))],
        compiler_params=pltpu.CompilerParams(
            collective_id=1, has_side_effects=True, vmem_limit_bytes=VMEM_LIMIT
        ),
        cost_estimate=pl.CostEstimate(flops=0, bytes_accessed=150_000_000, transcendentals=0),
        name="mid_step",
    )(mixed, w, resid_own, gain, piece)


def two_step(d_gu, w, mid_own, grad_own, gain):
    tok, width = d_gu.shape[0], w.shape[0]
    half = mid_own.shape[0]
    return plane_call(
        two_kernel, "two_step", 2, (d_gu, w, mid_own, grad_own, gain),
        [((half, width), f32), ((1, width), f32), ((tok, width), bf16)],
        reduce_scratch(half, width) + SHARE_SEMS,
    )


def one_step(d_a, w_a, d_b, w_b, hidden_own, dmid_own, gain, act, w_act, mid_own, moved):
    width = w_a.shape[0]
    half = hidden_own.shape[0]
    return plane_call(
        one_kernel, "one_step", 3,
        (d_a, w_a, d_b, w_b, hidden_own, dmid_own, gain, act, w_act, mid_own),
        [((2 * half, width), f32), ((2 * half, width), f32), ((1, width), f32)],
        reduce_scratch(half, width)
        + reduce_scratch(half, width)
        + [pltpu.SemaphoreType.DMA((2, 2))],
        moved=moved,
    )


HALO = 16


def open_kernel(n, *refs):
    hid, gains_ref, a_ref = refs[:3]
    w_refs = refs[3 : 3 + n]
    gain_out, full_ref, a_out = refs[3 + n : 6 + n]
    w_outs = refs[6 + n : 6 + 2 * n]
    (
        g_vec, gz_sems, gp_sems, a_sems, up_sems, down_sems, own_sems, far_sems, near_sems,
        w_sems, loc_sems, halo_sems,
    ) = refs[6 + 2 * n :]
    z, p, c = place()
    nz, half, rows = a_out.shape[0], hid.shape[0], a_ref.shape[1]
    tok = full_ref.shape[0] - HALO
    ups = [chip(lax.rem(z + d, nz), p, c) for d in range(1, nz)]
    flat = [chip(z, hop(p, d), c) for d in HOPS]
    meet(ups + flat + [chip(z, p, 1 - c)])
    gain_out[p, z] = gains_ref[...]
    gz = [
        send(gain_out.at[p, z], gain_out.at[p, z], gz_sems.at[0, d], gz_sems.at[1, d], ups[d])
        for d in range(nz - 1)
    ]
    to_plane = []
    for i, d in enumerate(HOPS):
        to_plane.append(
            send(a_ref.at[hop(p, d)], a_out.at[z, p], a_sems.at[0, i], a_sems.at[1, i], flat[i])
        )
    local = [pltpu.make_async_copy(a_ref.at[p], a_out.at[z, p], loc_sems.at[n])]
    for j in range(n):
        local.append(pltpu.make_async_copy(w_refs[j].at[p], w_outs[j].at[p], loc_sems.at[j]))
    for copy in local:
        copy.start()

    for copy in gz:
        copy.wait_recv()
    gp = [
        send(gain_out.at[p], gain_out.at[p], gp_sems.at[0, i], gp_sems.at[1, i], flat[i])
        for i in range(3)
    ]
    for copy in gp:
        copy.wait_recv()
    for i in range(nz):
        for j in range(gain_out.shape[0]):
            first = (i * gain_out.shape[0] + j) * rows
            g_vec[:, first : first + rows] = gain_out[j, i][:, :rows]
    g = g_vec[0:1, :]

    @pl.loop(0, half // 16)
    def _(r):
        rows_in = hid[at_rows(r * 16, 16), :]
        full_ref[at_rows((p * 2 + c) * half + r * 16, 16), :] = (
            rows_in * rms(rows_in) * g
        ).astype(bf16)

    other = chip(z, p, 1 - c)
    mine = full_ref.at[at_rows((p * 2 + c) * half, half), :]
    rows_out = [
        send(mine, mine, far_sems.at[0, i], far_sems.at[1, i], flat[i]) for i in range(3)
    ] + [send(mine, mine, own_sems.at[0], own_sems.at[1], other)]

    stage, chain_done = z_chain(a_out, up_sems, down_sems)
    for copy in to_plane:
        copy.wait_recv()
    for copy in local:
        copy.wait()
    stage(0)
    if nz > 2:
        stage(1)
    onward = []
    for i, d in ((1, 1), (2, 2), (0, 3)):
        rows_out[i].wait_recv()
        came = full_ref.at[at_rows((hop(p, d) * 2 + c) * half, half), :]
        onward.append(send(came, came, near_sems.at[0, i], near_sems.at[1, i], other))
    moved = []
    for j in range(n):
        for i, d in enumerate(HOPS):
            moved.append(
                send(
                    w_refs[j].at[hop(p, d)], w_outs[j].at[p], w_sems.at[0, j, i],
                    w_sems.at[1, j, i], flat[i],
                )
            )
    finish_share(rows_out, onward)
    halo_from = full_ref.at[at_rows(tok - HALO, HALO), :]
    halo_to = full_ref.at[at_rows(tok, HALO), :]

    def halo(to):
        return pltpu.make_async_remote_copy(
            src_ref=halo_from, dst_ref=halo_to, send_sem=halo_sems.at[0],
            recv_sem=halo_sems.at[1], device_id=to, device_id_type=MESH,
        )

    @pl.when(z + 1 < nz)
    def _():
        halo(chip(z + 1, p, c)).start()

    @pl.when(z == 0)
    def _():
        full_ref[at_rows(tok, HALO), :] = jnp.zeros((HALO, full_ref.shape[1]), bf16)

    for k in range(2, nz):
        stage(k)

    @pl.when(z > 0)
    def _():
        halo(chip(z - 1, p, c)).wait_recv()

    @pl.when(z + 1 < nz)
    def _():
        halo(chip(z + 1, p, c)).wait_send()

    chain_done()
    for copy in moved:
        copy.wait()
    for copy in gz + gp + to_plane:
        copy.wait_send()


def open_step(hid, gains, piece, rest, tok, nz):
    width, n, n_p = hid.shape[1], len(rest), piece.shape[0]
    anywhere = pl.BlockSpec(memory_space=pl.ANY)
    dma = pltpu.SemaphoreType.DMA
    return pl.pallas_call(
        functools.partial(open_kernel, n),
        in_specs=[VM, VM] + [anywhere] * (n + 1),
        out_specs=[VM, VM] + [anywhere] * (n + 1),
        out_shape=[
            jax.ShapeDtypeStruct((n_p, nz) + gains.shape, f32),
            jax.ShapeDtypeStruct((tok + HALO, width), bf16),
            jax.ShapeDtypeStruct((nz,) + piece.shape, bf16),
        ]
        + [jax.ShapeDtypeStruct(r.shape, bf16) for r in rest],
        scratch_shapes=[
            pltpu.VMEM((8, width), f32), dma((2, nz - 1)), dma((2, 3)), dma((2, 3)), dma((2, nz)),
            dma((2, nz)),
        ]
        + SHARE_SEMS
        + [dma((2, n, 3)), dma((n + 1,)), dma((2,))],
        compiler_params=pltpu.CompilerParams(
            collective_id=4, has_side_effects=True, vmem_limit_bytes=VMEM_LIMIT
        ),
        cost_estimate=pl.CostEstimate(flops=0, bytes_accessed=250_000_000, transcendentals=0),
        name="open_step",
    )(hid, gains, piece, *rest)


def gather_bc_kernel(
    x_ref, kv_ref, grad_ref, full_ref, kvz_ref, g_ref,
    far_sems, near_sems, z_sems, own_g, far_g, near_g,
):
    z, p, c = place()
    nz = kvz_ref.shape[0]
    other = chip(z, p, 1 - c)
    meet(
        [other]
        + [chip(z, hop(p, d), c) for d in HOPS]
        + [chip(lax.rem(z + d, nz), p, c) for d in range(1, nz)]
    )
    kvz_ref[z] = kv_ref[...]

    def up(d):
        return pltpu.make_async_remote_copy(
            src_ref=kv_ref, dst_ref=kvz_ref.at[z], send_sem=z_sems.at[0, d - 1],
            recv_sem=z_sems.at[1, d - 1], device_id=chip(z + d, p, c), device_id_type=MESH,
        )

    for d in range(1, nz):

        @pl.when(z + d < nz)
        def _():
            up(d).start()

    half = x_ref.shape[0] // 2
    full_ref[p] = x_ref[...]
    rows = at_rows(c * half, half)
    mine = full_ref.at[p, rows, :]
    copies = [
        send(mine, mine, far_sems.at[0, i], far_sems.at[1, i], chip(z, hop(p, d), c))
        for i, d in enumerate(HOPS)
    ]
    onward = []
    for i, d in ((1, 1), (2, 2), (0, 3)):
        copies[i].wait_recv()
        came = full_ref.at[hop(p, d), rows, :]
        onward.append(send(came, came, near_sems.at[0, i], near_sems.at[1, i], other))
    g_half = grad_ref.shape[0]
    g_ref[at_rows((p * 2 + c) * g_half, g_half), :] = grad_ref[...].astype(bf16)
    g_copies, g_onward = share_rows(g_ref, g_half, own_g, far_g, near_g)
    for d in range(1, nz):

        @pl.when(z - d >= 0)
        def _():
            pltpu.make_async_remote_copy(
                src_ref=kv_ref, dst_ref=kvz_ref.at[z - d], send_sem=z_sems.at[0, d - 1],
                recv_sem=z_sems.at[1, d - 1], device_id=chip(z - d, p, c), device_id_type=MESH,
            ).wait_recv()

        @pl.when(z + d < nz)
        def _():
            kvz_ref[z + d] = jnp.zeros(kv_ref.shape, kv_ref.dtype)
            up(d).wait_send()

    for copy in copies:
        copy.wait_send()
    for copy in onward:
        copy.wait()
    finish_share(g_copies, g_onward)


def gather_bc(x, at, n_p, kv, nz, grad):
    tok = x.shape[0]
    dma = pltpu.SemaphoreType.DMA
    whole = lambda s: pl.BlockSpec(s, lambda i: (0,) * len(s))
    return pl.pallas_call(
        gather_bc_kernel,
        grid=(1,),
        in_specs=[
            pl.BlockSpec((tok, 128), lambda i: (0, at)), whole(kv.shape), whole(grad.shape)
        ],
        out_specs=[
            whole((n_p, tok, 128)), whole((nz,) + kv.shape), whole((tok, grad.shape[1]))
        ],
        out_shape=[
            jax.ShapeDtypeStruct((n_p, tok, 128), bf16),
            jax.ShapeDtypeStruct((nz,) + kv.shape, bf16),
            jax.ShapeDtypeStruct((tok, grad.shape[1]), bf16),
        ],
        scratch_shapes=[dma((2, 3)), dma((2, 3)), dma((2, nz - 1))] + SHARE_SEMS,
        compiler_params=pltpu.CompilerParams(
            collective_id=5, has_side_effects=True, vmem_limit_bytes=VMEM_LIMIT
        ),
        cost_estimate=pl.CostEstimate(flops=0, bytes_accessed=40_000_000, transcendentals=0),
        name="gather_bc",
    )(x, kv, grad)


def carry_kernel(state_ref, rate_ref, kvz_ref, in_ref, kv_ref, low, came, rates, factor, s_sems, r_sems, p_sems):
    z, p, c = place()
    nz = kvz_ref.shape[0]
    meet(
        [chip(z, hop(p, d), c) for d in HOPS]
        + [chip(lax.rem(z + d, nz), p, c) for d in range(1, nz)]
    )
    low[...] = state_ref[...].astype(bf16)

    def up(d):
        to = chip(z + d, p, c)
        return (
            pltpu.make_async_remote_copy(
                src_ref=low, dst_ref=came.at[d - 1], send_sem=s_sems.at[0, d - 1],
                recv_sem=s_sems.at[1, d - 1], device_id=to, device_id_type=MESH,
            ),
            pltpu.make_async_remote_copy(
                src_ref=rate_ref, dst_ref=rates.at[d - 1], send_sem=r_sems.at[0, d - 1],
                recv_sem=r_sems.at[1, d - 1], device_id=to, device_id_type=MESH,
            ),
        )

    for d in range(1, nz):

        @pl.when(z + d < nz)
        def _():
            for copy in up(d):
                copy.start()

    kv_ref[p] = kvz_ref[...]
    mine = kv_ref.at[p]
    copies = [
        send(mine, mine, p_sems.at[0, i], p_sems.at[1, i], chip(z, hop(p, d), c))
        for i, d in enumerate(HOPS)
    ]
    in_ref[...] = jnp.zeros_like(in_ref)
    factor[...] = jnp.ones_like(factor)
    lane_head, row_head = head_maps(state_ref.shape[0])
    for d in range(1, nz):

        @pl.when(z - d >= 0)
        def _():
            fro = chip(z - d, p, c)
            pltpu.make_async_remote_copy(
                src_ref=low, dst_ref=came.at[d - 1], send_sem=s_sems.at[0, d - 1],
                recv_sem=s_sems.at[1, d - 1], device_id=fro, device_id_type=MESH,
            ).wait_recv()
            pltpu.make_async_remote_copy(
                src_ref=rate_ref, dst_ref=rates.at[d - 1], send_sem=r_sems.at[0, d - 1],
                recv_sem=r_sems.at[1, d - 1], device_id=fro, device_id_type=MESH,
            ).wait_recv()
            scale = jnp.sum(row_head * factor[0:1, :], axis=1, keepdims=True)
            in_ref[...] += scale * came[d - 1].astype(f32)
            factor[...] = factor[...] * rates[d - 1]

        @pl.when(z + d < nz)
        def _():
            for copy in up(d):
                copy.wait_send()

    for copy in copies:
        copy.wait()


def carry_step(state, rate, kvz, n_p):
    nz = kvz.shape[0]
    dma = pltpu.SemaphoreType.DMA
    return plane_call(
        carry_kernel, "carry_step", 8, (state, rate, kvz),
        [(state.shape, f32), ((n_p,) + kvz.shape, bf16)],
        [
            pltpu.VMEM(state.shape, bf16),
            pltpu.VMEM((nz - 1,) + state.shape, bf16),
            pltpu.VMEM((nz - 1,) + rate.shape, f32),
            pltpu.VMEM(rate.shape, f32),
            dma((2, nz - 1)), dma((2, nz - 1)), dma((2, 3)),
        ],
        nbytes=80_000_000,
    )


def reduce_bc_kernel(n, x_ref, dkv_ref, dx_ref, slope_ref, *refs):
    ins, (out_ref, own_ref, next_ref), outs = refs[:n], refs[n : n + 3], refs[n + 3 : 2 * n + 3]
    (
        sib_out, sib_in, out, came, z_came, first, n_sems, f_sems, own_sems, z_sems, h_sems,
        w_sems, loc_sems,
    ) = refs[2 * n + 3 :]
    z, p, c = place()
    nz = dkv_ref.shape[0]
    half = x_ref.shape[1] // 2
    xw = dx_ref.shape[1]
    other = chip(z, p, 1 - c)
    meet(
        [other]
        + [chip(z, hop(p, d), c) for d in HOPS]
        + [chip(lax.rem(z + d, nz), p, c) for d in range(1, nz)]
    )

    def down(d):
        return pltpu.make_async_remote_copy(
            src_ref=dkv_ref.at[z - d], dst_ref=z_came.at[d - 1], send_sem=z_sems.at[0, d - 1],
            recv_sem=z_sems.at[1, d - 1], device_id=chip(z - d, p, c), device_id_type=MESH,
        )

    for d in range(1, nz):

        @pl.when(z - d >= 0)
        def _():
            down(d).start()

    near, far = [], []
    order = HOPS + (0,)
    for i, d in enumerate(order):
        q = hop(p, d)
        sib_out[i] = x_ref[q, at_rows((1 - c) * half, half), :].astype(bf16)
        near.append(
            send(sib_out.at[i], sib_in.at[i], n_sems.at[0, i], n_sems.at[1, i], other)
        )
    for i, d in enumerate(HOPS):
        q = hop(p, d)
        near[i].wait_recv()
        out[i] = (x_ref[q, at_rows(c * half, half), :] + sib_in[i].astype(f32)).astype(bf16)
        far.append(
            send(out.at[i], came.at[i], f_sems.at[0, i], f_sems.at[1, i], chip(z, q, c))
        )
    moved = swap_begin(ins, outs, w_sems, loc_sems)
    near[3].wait_recv()
    total = x_ref[p, at_rows(c * half, half), :] + sib_in[3].astype(f32)
    for i in (1, 2, 0):
        far[i].wait_recv()
        total = total + came[i].astype(f32)
    mine = out_ref.at[at_rows(c * half, half), :]
    out_ref[at_rows(c * half, half), :] = total
    copy = send(mine, mine, own_sems.at[0], own_sems.at[1], other)
    copy.wait()
    first[:, :xw] = dx_ref[...] * slope_ref[:, :xw]
    first[:, xw:] = out_ref[0:8, :] * slope_ref[:, xw:]

    def edge(to):
        return pltpu.make_async_remote_copy(
            src_ref=first, dst_ref=next_ref, send_sem=h_sems.at[0], recv_sem=h_sems.at[1],
            device_id=to, device_id_type=MESH,
        )

    @pl.when(z > 0)
    def _():
        edge(chip(z - 1, p, c)).start()

    own_ref[...] = dkv_ref[z].astype(f32)
    for d in range(1, nz):

        @pl.when(z + d < nz)
        def _():
            pltpu.make_async_remote_copy(
                src_ref=dkv_ref.at[z], dst_ref=z_came.at[d - 1], send_sem=z_sems.at[0, d - 1],
                recv_sem=z_sems.at[1, d - 1], device_id=chip(z + d, p, c), device_id_type=MESH,
            ).wait_recv()
            own_ref[...] += z_came[d - 1].astype(f32)

        @pl.when(z - d >= 0)
        def _():
            down(d).wait_send()

    @pl.when(z + 1 == nz)
    def _():
        next_ref[...] = jnp.zeros_like(next_ref)

    @pl.when(z + 1 < nz)
    def _():
        edge(chip(z + 1, p, c)).wait_recv()

    @pl.when(z > 0)
    def _():
        edge(chip(z - 1, p, c)).wait_send()

    for done in near + far:
        done.wait_send()
    for copy in moved:
        copy.wait()


def reduce_bc(x, dkv, dx, slope, moved):
    n_p, tok, _ = x.shape
    half, nz = tok // 2, dkv.shape[0]
    dma = pltpu.SemaphoreType.DMA
    return plane_call(
        reduce_bc_kernel, "reduce_bc", 7, (x, dkv, dx, slope),
        [((tok, 128), f32), (dkv.shape[1:], f32), (slope.shape, f32)],
        [
            pltpu.VMEM((4, half, 128), bf16),
            pltpu.VMEM((4, half, 128), bf16),
            pltpu.VMEM((3, half, 128), bf16),
            pltpu.VMEM((3, half, 128), bf16),
            pltpu.VMEM((nz - 1,) + dkv.shape[1:], bf16),
            pltpu.VMEM(slope.shape, f32),
            dma((2, 4)), dma((2, 3)), dma((2,)), dma((2, nz - 1)), dma((2,)),
        ],
        nbytes=100_000_000,
        moved=moved,
    )


def sums_kernel(n, v_ref, *refs):
    ins, out_ref, outs = refs[:n], refs[n], refs[n + 1 : 2 * n + 1]
    came, z_sems, p_sems, c_sems, w_sems, loc_sems = refs[2 * n + 1 :]
    z, p, c = place()
    nz = came.shape[0]
    ups = [chip(lax.rem(z + d, nz), p, c) for d in range(1, nz)]
    other = chip(z, p, 1 - c)
    meet(ups + [chip(z, hop(p, d), c) for d in HOPS] + [other])
    moved = swap_begin(ins, outs, w_sems, loc_sems)
    copies = []
    for d in range(1, nz):
        copies.append(
            send(v_ref, came.at[d], z_sems.at[0, d - 1], z_sems.at[1, d - 1], ups[d - 1])
        )
    total = v_ref[...]
    for d in range(1, nz):
        copies[d - 1].wait_recv()
        total = total + came[d]
    out_ref[c, p] = total
    far = []
    for i, d in enumerate(HOPS):
        far.append(
            send(out_ref.at[c, p], out_ref.at[c, p], p_sems.at[0, i], p_sems.at[1, i], chip(z, hop(p, d), c))
        )
    for copy in far:
        copy.wait_recv()
    near = send(out_ref.at[c], out_ref.at[c], c_sems.at[0], c_sems.at[1], other)
    for copy in copies + far:
        copy.wait_send()
    near.wait()
    for copy in moved:
        copy.wait()


def sums_step(v, nz, n_p, moved):
    return plane_call(
        sums_kernel, "sums_step", 6, (v,),
        [((2, n_p) + v.shape, f32)],
        [
            pltpu.VMEM((nz,) + v.shape, f32),
            pltpu.SemaphoreType.DMA((2, nz - 1)),
            pltpu.SemaphoreType.DMA((2, 3)),
            pltpu.SemaphoreType.DMA((2,)),
        ],
        moved=moved,
    )


def rope_tables(positions, pairs):
    freqs = rope_base ** (-2.0 * pairs.astype(f32) / HDIM)
    angles = positions.astype(f32)[:, None] * freqs[None, :]
    return jnp.cos(angles), jnp.sin(angles)


def carry_states(state, decays, sign):
    nz = lax.axis_size("z")
    low = state.astype(bf16)
    total, factor = None, None
    for d in range(1, nz):
        route = [(i, i + sign * d) for i in range(nz) if 0 <= i + sign * d < nz]
        came = lax.ppermute(low, "z", route).astype(f32)
        rate = lax.ppermute(decays, "z", route)
        total = came if total is None else total + factor * came
        factor = rate if factor is None else factor * rate
    return total


def shards(
    hidden_in,
    grad_out,
    doc_starts,
    norm_mixer,
    norm_ffn,
    mamba_z,
    mamba_x,
    mamba_bc,
    mamba_dt,
    conv_x,
    conv_bc,
    a_log,
    dt_bias,
    skip_gain,
    mamba_out,
    attn_query,
    attn_key,
    attn_value,
    attn_out,
    ffn_gate,
    ffn_up,
    ffn_down,
):
    own = hidden_in.shape[0]
    width = hidden_in.shape[1]
    half = own // 2
    nz, n_p = lax.axis_size("z"), lax.axis_size("p")
    zi, pi, ci = lax.axis_index("z"), lax.axis_index("p"), lax.axis_index("head")
    tok = own * n_p
    base = zi * tok
    positions = base + jnp.arange(tok, dtype=jnp.int32)
    edge = conv_x.shape[0] - 1
    ext_docs = doc_ids(base - edge + jnp.arange(tok + 2 * edge, dtype=jnp.int32), doc_starts)
    rows = mamba_z.shape[0]
    n_heads = a_log.shape[0] // n_p
    xw = n_heads * MHDIM
    bw = mamba_bc.shape[1] // (2 * n_p)
    cw = xw + 2 * bw
    kw = HDIM // n_p
    hk = kw // 2
    tail_w = 128 - 2 * kw - n_heads

    weights = (
        mamba_x, mamba_bc, attn_key, attn_value, mamba_dt, attn_query, mamba_z, mamba_out, attn_out,
        ffn_gate, ffn_up, ffn_down,
    )
    piece_a, *rest = pack(n_p, *weights)

    def along_z(piece):
        piece = piece.reshape(n_p * rows, piece.shape[2])
        return lax.all_gather(piece, "z", axis=0, tiled=True)

    gains_own = jnp.pad(
        jnp.stack([norm_mixer, norm_ffn]).astype(bf16).astype(f32), ((0, 6), (0, 128 - rows))
    )
    my_half = lambda v: lax.dynamic_slice_in_dim(v, ci * half, half, 0)
    hidden_own, grad_own = my_half(hidden_in), my_half(grad_out)
    gains, normed_one, w_a, *rest = open_step(hidden_own, gains_own, piece_a, rest, tok, nz)
    w_a = w_a.reshape(nz * n_p * rows, w_a.shape[3])
    gains = gains.transpose(2, 1, 0, 3)[:, :, :, :rows].reshape(8, 1, width)
    gain_mix, gain_ffn = gains[0], gains[1]
    w_b, w_c, w_d = [along_z(piece) for piece in rest[:3]]

    in_ext = product(normed_one, w_a)
    in_b = product(normed_one, w_b)[:tok]
    in_a = in_ext[:tok]
    pre_ext = in_ext[:, :cw].astype(bf16)
    gate_z = in_b[:, HDIM:]
    slice_1 = lambda v, at, n: lax.dynamic_slice_in_dim(v, at, n, 1)
    taps = jnp.concatenate(
        [
            slice_1(conv_x, pi * xw, xw),
            slice_1(conv_bc, pi * bw, bw),
            slice_1(conv_bc, (n_p + pi) * bw, bw),
        ],
        axis=1,
    )
    ext = jnp.concatenate([pre_ext[tok + HALO - edge :], pre_ext[:tok]], axis=0)
    conv_in = convolve(ext, taps, ext_docs, tok)
    ssm = jax.nn.silu(conv_in).astype(bf16)
    head_slice = lambda v: lax.dynamic_slice_in_dim(v, pi * n_heads, n_heads, 0)
    my_bias, my_a, my_skip = head_slice(dt_bias), head_slice(a_log), head_slice(skip_gain)
    lanes = lambda v: jnp.pad(v, (0, 128 - n_heads))[None, :]
    dt_at = cw + 2 * kw
    dt_pre = jnp.pad(in_a[:, dt_at : dt_at + n_heads], ((0, 0), (0, 128 - n_heads))) + lanes(my_bias)
    neg_rate = lanes(-jnp.exp(my_a))
    skip_full = jnp.repeat(my_skip, MHDIM)[None, :]
    pair_ids = pi * hk + jnp.arange(hk)
    cos_k, sin_k = rope_tables(positions, pair_ids)
    k0, k1 = in_a[:, cw : cw + hk], in_a[:, cw + hk : cw + kw]
    key_own = jnp.concatenate([k0 * cos_k - k1 * sin_k, k1 * cos_k + k0 * sin_k], axis=1)
    val_own = in_a[:, cw + kw : cw + 2 * kw]
    kv_own = jnp.concatenate([key_own, val_own], axis=1).astype(bf16)
    kv_own = jnp.concatenate([kv_own[: tok // 2], kv_own[tok // 2 :]], axis=1)
    bc_all, kvz, g_ffn = gather_bc(ssm, xw // 128, n_p, kv_own, nz, grad_own)
    cos_q, sin_q = rope_tables(positions, jnp.arange(HDIM // 2))
    cos_q, sin_q = cos_q.reshape(tok, n_p, hk), sin_q.reshape(tok, n_p, hk)

    def rope_q(v, sign):
        v = v.reshape(tok, n_p, 2, hk)
        a, b = v[:, :, 0], v[:, :, 1]
        return jnp.stack(
            [a * cos_q - sign * b * sin_q, b * cos_q + sign * a * sin_q], axis=2
        ).reshape(tok, HDIM)

    queries = rope_q(in_b[:, :HDIM], 1.0).astype(bf16)

    base_arr = jnp.reshape(base, (1,)).astype(jnp.int32)
    y_local, span_starts, local_state, dev_decay, decay_full, c_mat = ssd_forward(
        base_arr, doc_starts, ssm, bc_all, dt_pre, neg_rate, skip_full
    )
    total_decay = decay_full[-1][:, None]
    rate = jnp.broadcast_to(dev_decay[tok - 1 :], (8, 128))
    in_state, kv = carry_step(local_state, rate, kvz, n_p)

    attn_f32, lse, keys, values = attend(base_arr, doc_starts, queries, kv)
    attn_low = attn_f32.astype(bf16)
    y_flat = y_local + product_nt(c_mat, in_state.astype(bf16)) * decay_full
    silu_z = jax.nn.silu(gate_z)
    gated = (y_flat * silu_z).astype(bf16)
    mixed = jnp.concatenate([gated, attn_low], axis=1)

    mid_own, normed_two, w_e = mid_step(mixed, w_c, hidden_own, gain_ffn, rest[3], nz)
    w_e = w_e.reshape(width, -1)
    gu = product(normed_two, w_d)
    ffw = gu.shape[1] // 2
    gate_val, up_val = gu[:, :ffw], gu[:, ffw:]
    silu_gate = jax.nn.silu(gate_val)
    activated = (silu_gate * up_val).astype(bf16)
    d_act = product(g_ffn, w_e)
    d_gu = jnp.concatenate(
        [d_act * up_val * silu_slope(gate_val), d_act * silu_gate], axis=1
    ).astype(bf16)
    grad_e = product_t(g_ffn, activated).astype(bf16)
    grad_d = product_t(normed_two, d_gu).astype(bf16)
    d_gu, grad_e, grad_d = lax.optimization_barrier((d_gu, grad_e, grad_d))

    def scattered(grad):
        return lax.psum_scatter(grad, "z", scatter_dimension=0, tiled=True)

    def by_owner(grad):
        return grad.reshape(n_p, rows, grad.shape[1])

    ge = scattered(grad_e)
    gd = scattered(grad_d)
    d_mid_own, grad_gain_ffn, g_mid = two_step(d_gu, w_d, mid_own, grad_own, gain_ffn)
    g_mid, ge = lax.optimization_barrier((g_mid, ge))

    d_mixed = product(g_mid, w_c)
    grad_c = product_t(g_mid, mixed).astype(bf16)
    gc = scattered(grad_c)
    d_gated = d_mixed[:, :xw]
    d_attn = d_mixed[:, xw:].astype(bf16)
    d_y_flat = d_gated * silu_z
    d_z = (d_gated * y_flat * silu_slope(gate_z)).astype(bf16)
    d_in_local = product_t((d_y_flat * decay_full).astype(bf16), c_mat)
    d_in_local, d_attn = lax.optimization_barrier((d_in_local, d_attn))
    state_grad = carry_states(d_in_local, total_decay, -1)
    d_query, d_kv = attend_back(
        base_arr, doc_starts, queries, d_attn, attn_f32, lse, keys, values, kv.shape
    )
    d_q_pre = rope_q(d_query, -1.0).astype(bf16)
    d_b = jnp.concatenate([d_q_pre, d_z], axis=1)
    d_b, state_grad = lax.optimization_barrier((d_b, state_grad))
    more = lambda v: jnp.pad(v, ((0, HALO), (0, 0)))
    grad_b = product_t(normed_one, more(d_b)).astype(bf16)
    gb = scattered(grad_b)
    d_kv_parts = [lax.dynamic_index_in_dim(d_kv, pi, 0, keepdims=False)]
    for d in range(1, n_p):
        part = lax.dynamic_index_in_dim(d_kv, jnp.bitwise_xor(pi, d), 0, keepdims=False)
        d_kv_parts.append(lax.ppermute(part, "p", [(i, i ^ d) for i in range(n_p)]))

    start_decay = jnp.concatenate([jnp.ones((1, 128), f32), dev_decay[SPAN - 1 :: SPAN][:-1]])
    d_y_flat, gd = lax.optimization_barrier((d_y_flat, gd))
    d_xs, d_bc, d_dt, sums, skip_sums = ssd_backward(
        base_arr, doc_starts, ssm, bc_all, dt_pre, d_y_flat, span_starts,
        start_decay[:, None, :], neg_rate, skip_full, in_state, state_grad,
    )
    d_bc, d_kv_parts = lax.optimization_barrier((d_bc, d_kv_parts))
    d_kv = sum(part.astype(f32) for part in d_kv_parts).astype(bf16)
    slope = silu_slope(conv_in)
    d_bc, d_kv_own, du_next, ge, gd = reduce_bc(
        d_bc, d_kv, d_xs[:8], slope[:8], (by_owner(ge), by_owner(gd))
    )
    d_kv_own = jnp.concatenate([d_kv_own[:, : 2 * kw], d_kv_own[:, 2 * kw :]], axis=0)
    dk0, dk1 = d_kv_own[:, :hk], d_kv_own[:, hk:kw]
    d_kv_low = jnp.concatenate(
        [dk0 * cos_k + dk1 * sin_k, dk1 * cos_k - dk0 * sin_k, d_kv_own[:, kw:]], axis=1
    ).astype(bf16)
    du = jnp.concatenate([d_xs, d_bc], axis=1) * slope
    du = jnp.concatenate([du, du_next[:edge]], axis=0)
    d_pre, grad_taps = convolve_back(du, ext, taps, ext_docs, tok)
    d_pre = d_pre.astype(bf16)
    d_last = jnp.concatenate(
        [d_kv_low, d_dt[:, :n_heads].astype(bf16), jnp.zeros((tok, tail_w), bf16)], axis=1
    )
    d_a = jnp.concatenate([d_pre, d_last], axis=1)
    grad_a = product_t(normed_one, more(d_a)).astype(bf16)
    ga = scattered(grad_a)
    once = jnp.where(ci == 0, d_pre[:, xw:], jnp.zeros((), bf16))
    d_a_once = jnp.concatenate([d_pre[:, :xw], once, d_last], axis=1)
    d_a_once, grad_a, gc = lax.optimization_barrier((d_a_once, grad_a, gc))
    grad_in, block_out, grad_gain_mix, gc = one_step(
        d_a_once, w_a, d_b, w_b, hidden_own, d_mid_own, gain_mix, activated, w_e, mid_own,
        (by_owner(gc),),
    )

    flat = jnp.concatenate(
        [
            grad_gain_mix.reshape(-1, 128),
            grad_gain_ffn.reshape(-1, 128),
            grad_taps.reshape(-1, 128),
            sums[:2],
            jnp.pad(jnp.sum(skip_sums.reshape(n_heads, MHDIM), axis=1), (0, 128 - n_heads))[None],
        ]
    )
    flat = jnp.pad(flat, ((0, -flat.shape[0] % 8), (0, 0)))
    summed, ga, gb = sums_step(flat, nz, n_p, (by_owner(ga), by_owner(gb)))
    g_rows = width // 128
    t_rows = grad_taps.size // 128
    si = zi * n_p + pi
    gains_sum = jnp.sum(summed[:, :, : 2 * g_rows], axis=(0, 1)).reshape(2, width)
    gains_sum = lax.dynamic_slice_in_dim(gains_sum, si * rows, rows, 1)
    mine = lax.dynamic_index_in_dim(summed, ci, 0, keepdims=False)
    s_taps = mine[:, 2 * g_rows : 2 * g_rows + t_rows].reshape(n_p, edge + 1, cw).transpose(1, 0, 2)
    s_heads = mine[:, 2 * g_rows + t_rows : 2 * g_rows + t_rows + 3, :n_heads]
    s_heads = s_heads.transpose(1, 0, 2).reshape(3, n_p * n_heads)
    s_x = s_taps[:, :, :xw].reshape(edge + 1, n_p * xw)
    s_bc = summed[0][:, 2 * g_rows : 2 * g_rows + t_rows].reshape(n_p, edge + 1, cw)
    s_bc = s_bc[:, :, xw:].reshape(n_p, edge + 1, 2, bw).transpose(1, 2, 0, 3)
    s_bc = s_bc.reshape(edge + 1, 2 * n_p * bw)

    g_x, g_bc, g_k, g_v, g_dt, g_q, g_z, g_mout, g_aout, g_gate, g_up, g_down = unpack(
        (ga, gb, gc, gd, ge), weights
    )
    return (
        block_out,
        grad_in,
        gains_sum[0],
        gains_sum[1],
        g_z,
        g_x,
        g_bc,
        g_dt,
        s_x,
        s_bc,
        s_heads[0],
        s_heads[1],
        s_heads[2],
        g_mout,
        g_q,
        g_k,
        g_v,
        g_aout,
        g_gate,
        g_up,
        g_down,
    )


def solution(mesh):
    seq, head = mesh.shape["seq"], mesh.shape["head"]
    plane = math.gcd(seq, 4)
    grid = Mesh(mesh.devices.reshape(seq // plane, plane, head), ("z", "p", "head"))
    s = ("z", "p")
    h = "head"
    placed = (
        P(s, None), P(s, None), P(), P(s), P(s), P(s, h), P(s, h), P(s, None), P(s, h),
        P(None, h), P(), P(h), P(h), P(h), P(h, s), P(s, h), P(s, h), P(s, h), P(h, s),
        P(s, h), P(s, h), P(h, s),
    )
    given = (
        P(s, None), P(s, None), P(s), P(s), P(s, h), P(s, h), P(s, None), P(s, h),
        P(None, h), P(), P(h), P(h), P(h), P(h, s), P(s, h), P(s, h), P(s, h), P(h, s),
        P(s, h), P(s, h), P(h, s),
    )
    return jax.shard_map(shards, mesh=grid, in_specs=placed, out_specs=given, check_vma=False)
```

```python
import functools
import math

import jax
import jax.numpy as jnp
from jax import lax
from jax.experimental import pallas as pl
from jax.experimental.pallas import tpu as pltpu
from jax.sharding import Mesh
from jax.sharding import PartitionSpec as P

MHDIM = 64
NSTATE = 256
HDIM = 128
SPAN = 128

eps_norm = 1e-05
rope_base = 100000000000.0
neg_large = -1e30
top_prec = lax.Precision.HIGHEST
bf16 = jnp.bfloat16
f32 = jnp.float32
MESH = pl.DeviceIdType.MESH
VMEM_LIMIT = 56 * 1024 * 1024


def doc_ids(positions, doc_starts):
    return jnp.sum((doc_starts[None, :] <= positions[:, None]).astype(jnp.int32), axis=1) - 1


def product(left, right):
    return jnp.dot(left, right, preferred_element_type=f32)


def product_t(left, right):
    return lax.dot_general(left, right, (((0,), (0,)), ((), ())), preferred_element_type=f32)


def product_nt(left, right):
    return lax.dot_general(left, right, (((1,), (1,)), ((), ())), preferred_element_type=f32)


def silu_slope(values):
    sigma_val = jax.nn.sigmoid(values)
    return sigma_val * (1.0 + values * (1.0 - sigma_val))


def convolve(extended, weights, ext_docs, tok_count):
    edge_rows = weights.shape[0] - 1
    here = ext_docs[edge_rows : edge_rows + tok_count]
    summed = jnp.zeros((tok_count, extended.shape[1]), f32)
    for tap_index in range(weights.shape[0]):
        begin_row = edge_rows - tap_index
        same_doc = (ext_docs[begin_row : begin_row + tok_count] == here)[:, None]
        rows = extended[begin_row : begin_row + tok_count].astype(f32)
        summed = summed + jnp.where(same_doc, rows, 0.0) * weights[tap_index][None, :]
    return summed


def convolve_back(d_conv, extended, weights, ext_docs, tok_count):
    edge_rows = weights.shape[0] - 1
    here = ext_docs[edge_rows : edge_rows + tok_count]
    d_rows = jnp.zeros((tok_count, d_conv.shape[1]), f32)
    tap_grads = []
    for tap_index in range(weights.shape[0]):
        begin_row = edge_rows - tap_index
        before = (ext_docs[begin_row : begin_row + tok_count] == here)[:, None]
        rows = extended[begin_row : begin_row + tok_count].astype(f32)
        tap_grads.append(jnp.sum(jnp.where(before, d_conv[:tok_count] * rows, 0.0), axis=0))
        last = edge_rows + tap_index
        after = (ext_docs[last : last + tok_count] == here)[:, None]
        ahead = d_conv[tap_index : tap_index + tok_count]
        d_rows = d_rows + jnp.where(after, ahead, 0.0) * weights[tap_index][None, :]
    return (d_rows, jnp.stack(tap_grads))


def tri_dot(a, b, dims=((1,), (0,))):
    return lax.dot_general(a, b, (dims, ((), ())), precision=top_prec, preferred_element_type=f32)


def dot_nn(a, b):
    return lax.dot_general(a, b, (((1,), (0,)), ((), ())), preferred_element_type=f32)


def dot_nt(a, b):
    return lax.dot_general(a, b, (((1,), (1,)), ((), ())), preferred_element_type=f32)


def dot_tn(a, b):
    return lax.dot_general(a, b, (((0,), (0,)), ((), ())), preferred_element_type=f32)


def iota2(shape, dim):
    return lax.broadcasted_iota(jnp.int32, shape, dim)


def docs_of(pos, starts_ref):
    count = jnp.where(starts_ref[0] <= pos, 1, 0)
    for i in range(1, starts_ref.shape[0]):
        count = count + jnp.where(starts_ref[i] <= pos, 1, 0)
    return count - 1


def softplus(v):
    return jnp.maximum(v, 0.0) + jnp.log(1.0 + jnp.exp(-jnp.abs(v)))


def head_maps(xw):
    lane_head = (iota2((128, xw), 1) // MHDIM == iota2((128, xw), 0)).astype(f32)
    row_head = (iota2((xw, 128), 0) // MHDIM == iota2((xw, 128), 1)).astype(f32)
    return lane_head, row_head


def span_setup(k, base_ref, starts_ref, dtp, nega):
    first = base_ref[0] + k * SPAN
    t_idx, s_idx = iota2((SPAN, SPAN), 0), iota2((SPAN, SPAN), 1)
    docs_t = docs_of(first + t_idx, starts_ref)
    docs_s = docs_of(first + s_idx, starts_ref)
    linked = (docs_t == docs_s) & (t_idx >= s_idx)
    dt = softplus(dtp)
    la = nega * dt
    tri = (t_idx >= s_idx).astype(f32)
    cum = tri_dot(tri, la)
    before = docs_of(first - 1, starts_ref)
    last_doc = docs_of(first + SPAN - 1, starts_ref)
    carried = jnp.where(docs_t == before, jnp.exp(cum), 0.0)
    cum_last = cum[SPAN - 1 : SPAN, :]
    tail = jnp.where(docs_t == last_doc, jnp.exp(cum_last - cum), 0.0)
    return docs_t, linked, dt, la, tri, cum, carried, tail


def split_bc(bc_ref):
    parts = [bc_ref[q] for q in range(bc_ref.shape[0])]
    half = parts[0].shape[1] // 2
    return (
        jnp.concatenate([part[:, :half] for part in parts], axis=1),
        jnp.concatenate([part[:, half:] for part in parts], axis=1),
    )


def ssd_forward_kernel(
    n_heads, base_ref, starts_ref, x_ref, bc_ref, dtp_ref, nega_ref, skip_ref,
    y_ref, span_ref, final_ref, decay_ref, wide_ref, c_out, state, running,
):
    k = pl.program_id(0)
    xw = n_heads * MHDIM

    @pl.when(k == 0)
    def _():
        state[...] = jnp.zeros_like(state)
        running[...] = jnp.zeros_like(running)

    docs_t, linked, dt, la, tri, cum, carried, tail = span_setup(
        k, base_ref, starts_ref, dtp_ref[...], nega_ref[...]
    )
    lane_head, row_head = head_maps(xw)
    prev_doc = docs_of(base_ref[0] - 1, starts_ref)
    since = jnp.where(docs_t == prev_doc, jnp.exp(running[0:1, :] + cum), 0.0)
    decay_ref[...] = since
    wide_ref[...] = tri_dot(since, lane_head)
    running[...] = running[...] + cum[SPAN - 1 : SPAN, :]
    start = state[...]
    span_ref[0] = start
    x, (b, c) = x_ref[...], split_bc(bc_ref)
    c_out[...] = c
    inner = dot_nt(c, b)
    cum_t, dt_t = cum.T, dt.T
    lane = iota2((SPAN, 128), 1)
    pieces = []
    for pair in range(n_heads // 2):
        xp = x[:, pair * 128 : pair * 128 + 128]
        got = []
        for h in (2 * pair, 2 * pair + 1):
            gap = jnp.where(linked, cum[:, h : h + 1] - cum_t[h : h + 1, :], neg_large)
            w = jnp.exp(gap) * inner * dt_t[h : h + 1, :]
            got.append(dot_nn(w.astype(bf16), xp))
        pieces.append(jnp.where(lane < MHDIM, got[0], got[1]))
    y = jnp.concatenate(pieces, axis=1)
    y = y + dot_nt(c, start.astype(bf16)) * tri_dot(carried, lane_head)
    xf = x.astype(f32)
    y_ref[...] = y + skip_ref[...] * xf
    xt = (xf * tri_dot(tail * dt, lane_head)).astype(bf16)
    keep = jnp.sum(row_head * carried[SPAN - 1 : SPAN, :], axis=1, keepdims=True)
    new = dot_tn(xt, b) + keep * start
    state[...] = new
    final_ref[...] = new


def ssd_forward(base, doc_starts, x, bc, dtp, nega, skip):
    tok, xw, n_p = x.shape[0], skip.shape[1], bc.shape[0]
    n_heads, nspan = xw // MHDIM, tok // SPAN
    row = lambda n: pl.BlockSpec((SPAN, n), lambda i: (i, 0))
    whole = lambda *s: pl.BlockSpec(s, lambda i: (0,) * len(s))
    smem = pl.BlockSpec(memory_space=pltpu.SMEM)
    return pl.pallas_call(
        functools.partial(ssd_forward_kernel, n_heads),
        grid=(nspan,),
        in_specs=[
            smem, smem, row(xw), pl.BlockSpec((n_p, SPAN, 128), lambda i: (0, i, 0)), row(128),
            whole(1, 128), whole(1, xw),
        ],
        out_specs=[
            row(xw),
            pl.BlockSpec((1, xw, NSTATE), lambda i: (i, 0, 0)),
            whole(xw, NSTATE),
            row(128),
            row(xw),
            row(NSTATE),
        ],
        out_shape=[
            jax.ShapeDtypeStruct((tok, xw), f32),
            jax.ShapeDtypeStruct((nspan, xw, NSTATE), f32),
            jax.ShapeDtypeStruct((xw, NSTATE), f32),
            jax.ShapeDtypeStruct((tok, 128), f32),
            jax.ShapeDtypeStruct((tok, xw), f32),
            jax.ShapeDtypeStruct((tok, NSTATE), bf16),
        ],
        scratch_shapes=[pltpu.VMEM((xw, NSTATE), f32), pltpu.VMEM((8, 128), f32)],
        compiler_params=pltpu.CompilerParams(vmem_limit_bytes=VMEM_LIMIT),
        cost_estimate=pl.CostEstimate(
            flops=2 * tok * xw * NSTATE * 3, bytes_accessed=40_000_000, transcendentals=0
        ),
        name="ssd_forward",
    )(base, doc_starts, x, bc, dtp, nega, skip)


def ssd_backward_kernel(
    n_heads, base_ref, starts_ref, x_ref, bc_ref, dtp_ref, dy_ref, span_ref, decay_ref,
    nega_ref, skip_ref, in_ref, grad_ref,
    dx_ref, dbc_ref, ddt_ref, sums_ref, gskip_ref, gstate,
):
    step = pl.program_id(0)
    k = pl.num_programs(0) - 1 - step
    xw = n_heads * MHDIM

    @pl.when(step == 0)
    def _():
        gstate[...] = grad_ref[...]
        sums_ref[...] = jnp.zeros_like(sums_ref)
        gskip_ref[...] = jnp.zeros_like(gskip_ref)

    nega = nega_ref[...]
    docs_t, linked, dt, la, tri, cum, carried, tail = span_setup(
        k, base_ref, starts_ref, dtp_ref[...], nega
    )
    lane_head, row_head = head_maps(xw)
    begin = jnp.sum(row_head * decay_ref[0], axis=1, keepdims=True)
    start = span_ref[0] + begin * in_ref[...]
    start_low = start.astype(bf16)
    g = gstate[...]
    g_low = g.astype(bf16)
    x, (b, c), dy = x_ref[...], split_bc(bc_ref), dy_ref[...]
    dy_low = dy.astype(bf16)
    xf = x.astype(f32)
    inner = dot_nt(c, b)
    cum_t, dt_t = cum.T, dt.T
    lane = iota2((SPAN, 128), 1)
    row8 = iota2((SPAN, 128), 0)
    d_inner = jnp.zeros((SPAN, SPAN), f32)
    r_cols = jnp.zeros((SPAN, 128), f32)
    k_rows = jnp.zeros((SPAN, 128), f32)
    u_pieces = []
    for pair in range(n_heads // 2):
        xp = x[:, pair * 128 : pair * 128 + 128]
        dyp = dy_low[:, pair * 128 : pair * 128 + 128]
        got = []
        for j, h in enumerate((2 * pair, 2 * pair + 1)):
            mine = (lane < MHDIM) if j == 0 else (lane >= MHDIM)
            gap = jnp.where(linked, cum[:, h : h + 1] - cum_t[h : h + 1, :], neg_large)
            e = jnp.exp(gap)
            m = e * inner
            dyx = dot_nt(dyp, jnp.where(mine, xp, jnp.zeros_like(xp)))
            ed = dyx * dt_t[h : h + 1, :]
            d_inner = d_inner + e * ed
            pairs = m * ed
            r_cols = jnp.where(lane == h, jnp.sum(pairs, axis=1, keepdims=True), r_cols)
            k_rows = jnp.where(row8 == h, jnp.sum(pairs, axis=0, keepdims=True), k_rows)
            got.append(dot_tn(m.astype(bf16), dyp))
        u_pieces.append(jnp.where(lane < MHDIM, got[0], got[1]))
    u = jnp.concatenate(u_pieces, axis=1)
    dye = dy * tri_dot(carried, lane_head)
    dye_low = dye.astype(bf16)
    di_low = d_inner.astype(bf16)
    r_state = tri_dot(dye * dot_nt(c, start_low), row_head)
    u_state = dot_nt(b, g_low) * tri_dot(tail, lane_head)
    u = u + u_state
    dt_full = tri_dot(dt, lane_head)
    k_state = dt * tri_dot(xf * u_state, row_head)
    d_dt = tri_dot(xf * u, row_head)
    tail_x = (xf * tri_dot(tail * dt, lane_head)).astype(bf16)
    dx_ref[...] = dt_full * u + skip_ref[...] * dy
    d_b = dot_nn(tail_x, g_low) + dot_tn(di_low, c)
    d_c = dot_nn(dye_low, start_low) + dot_nn(di_low, b)
    bw = 64
    for q in range(dbc_ref.shape[0]):
        cut = slice(q * bw, q * bw + bw)
        dbc_ref[q] = jnp.concatenate([d_b[:, cut], d_c[:, cut]], axis=1)
    gs = jnp.sum(g * start, axis=1, keepdims=True)
    gs_row = jnp.sum(row_head * gs, axis=0, keepdims=True)
    last = jnp.sum(k_state, axis=0, keepdims=True) + carried[SPAN - 1 : SPAN, :] * gs_row
    d_cum = r_cols - k_rows.T + r_state - k_state + jnp.where(row8 == SPAN - 1, last, 0.0)
    d_la = tri_dot(tri, d_cum, ((0,), (0,)))
    live = lane < n_heads
    dtp = dtp_ref[...]
    d_in = jnp.where(live, (d_dt + nega * d_la) * jax.nn.sigmoid(dtp), 0.0)
    ddt_ref[...] = d_in
    sum_a = jnp.sum(jnp.where(live, d_la * la, 0.0), axis=0, keepdims=True)
    sum_b = jnp.sum(d_in, axis=0, keepdims=True)
    pick = iota2((8, 128), 0)
    sums_ref[...] += jnp.where(pick == 0, sum_a, jnp.where(pick == 1, sum_b, 0.0))
    gskip_ref[...] += jnp.sum(dy * xf, axis=0, keepdims=True)
    keep = jnp.sum(row_head * carried[SPAN - 1 : SPAN, :], axis=1, keepdims=True)
    gstate[...] = keep * g + dot_tn(dye_low, c)


def ssd_backward(
    base, doc_starts, x, bc, dtp, dy, span_starts, start_decay, nega, skip, in_state, grad_state
):
    tok, xw, n_p = x.shape[0], skip.shape[1], bc.shape[0]
    wide = pl.BlockSpec((n_p, SPAN, 128), lambda i: (0, nspan - 1 - i, 0))
    n_heads, nspan = xw // MHDIM, tok // SPAN
    row = lambda n: pl.BlockSpec((SPAN, n), lambda i: (nspan - 1 - i, 0))
    whole = lambda *s: pl.BlockSpec(s, lambda i: (0,) * len(s))
    smem = pl.BlockSpec(memory_space=pltpu.SMEM)
    return pl.pallas_call(
        functools.partial(ssd_backward_kernel, n_heads),
        grid=(nspan,),
        in_specs=[
            smem, smem, row(xw), wide, row(128), row(xw),
            pl.BlockSpec((1, xw, NSTATE), lambda i: (nspan - 1 - i, 0, 0)),
            pl.BlockSpec((1, 1, 128), lambda i: (nspan - 1 - i, 0, 0)),
            whole(1, 128), whole(1, xw), whole(xw, NSTATE), whole(xw, NSTATE),
        ],
        out_specs=[row(xw), wide, row(128), whole(8, 128), whole(1, xw)],
        out_shape=[
            jax.ShapeDtypeStruct((tok, xw), f32),
            jax.ShapeDtypeStruct((n_p, tok, 128), f32),
            jax.ShapeDtypeStruct((tok, 128), f32),
            jax.ShapeDtypeStruct((8, 128), f32),
            jax.ShapeDtypeStruct((1, xw), f32),
        ],
        scratch_shapes=[pltpu.VMEM((xw, NSTATE), f32)],
        compiler_params=pltpu.CompilerParams(vmem_limit_bytes=VMEM_LIMIT),
        cost_estimate=pl.CostEstimate(
            flops=2 * tok * xw * NSTATE * 8, bytes_accessed=80_000_000, transcendentals=0
        ),
        name="ssd_backward",
    )(base, doc_starts, x, bc, dtp, dy, span_starts, start_decay, nega, skip, in_state, grad_state)


QB = 512
KB = 512


def sight(base_ref, starts_ref, q_first):
    q_pos = base_ref[0] + q_first + iota2((QB, 1), 0)
    low = jnp.zeros((QB, 1), jnp.int32)
    for i in range(starts_ref.shape[0]):
        low = jnp.where(starts_ref[i] <= q_pos, starts_ref[i], low)
    return jnp.broadcast_to(low, (QB, KB)), jnp.broadcast_to(q_pos, (QB, KB))


def seen(low, high, k_first):
    k_pos = k_first + iota2((QB, KB), 1)
    return (k_pos >= low) & (k_pos <= high)


def attend_kernel(scale, base_ref, starts_ref, q_ref, kv_ref, o_ref, lse_ref, k_ref, v_ref):
    i = pl.program_id(0)

    @pl.when(i == 0)
    def _():
        n_p, nz, rows, _ = kv_ref.shape
        kw = HDIM // n_p

        @pl.loop(0, nz)
        def _(z):
            parts = [kv_ref[q, z] for q in range(n_p)]
            for t in range(2):
                at = pl.ds(pl.multiple_of((2 * z + t) * rows, rows), rows)
                lo = 2 * kw * t
                k_ref[at, :] = jnp.concatenate([v[:, lo : lo + kw] for v in parts], axis=1)
                v_ref[at, :] = jnp.concatenate([v[:, lo + kw : lo + 2 * kw] for v in parts], axis=1)

    q = q_ref[...]
    low, high = sight(base_ref, starts_ref, i * QB)
    blocks = (base_ref[0] + (i + 1) * QB + KB - 1) // KB

    def turn(j, carry):
        m, l, acc = carry
        at = pl.ds(pl.multiple_of(j * KB, KB), KB)
        s = dot_nt(q, k_ref[at, :]) * scale
        s = jnp.where(seen(low, high, j * KB), s, neg_large)
        m_new = jnp.maximum(m, jnp.max(s, axis=1, keepdims=True))
        w = jnp.exp(s - m_new)
        r = jnp.exp(m - m_new)
        l = l * r + jnp.sum(w, axis=1, keepdims=True)
        return m_new, l, acc * r + dot_nn(w.astype(bf16), v_ref[at, :])

    m, l, acc = lax.fori_loop(
        0,
        blocks,
        turn,
        (jnp.full((QB, 1), 0.1 * neg_large, f32), jnp.zeros((QB, 1), f32), jnp.zeros((QB, HDIM), f32)),
    )
    o_ref[...] = acc / l
    lse_ref[...] = jnp.broadcast_to(m + jnp.log(l), (QB, 128))


def attend(base, doc_starts, q, kv):
    tok = q.shape[0]
    keys = kv.shape[1] * kv.shape[2] * 2
    row = pl.BlockSpec((QB, HDIM), lambda i: (i, 0))
    whole = lambda s: pl.BlockSpec(s, lambda i: (0,) * len(s))
    smem = pl.BlockSpec(memory_space=pltpu.SMEM)
    return pl.pallas_call(
        functools.partial(attend_kernel, HDIM ** (-0.5)),
        grid=(tok // QB,),
        in_specs=[smem, smem, row, whole(kv.shape)],
        out_specs=[row, row, whole((keys, HDIM)), whole((keys, HDIM))],
        out_shape=[jax.ShapeDtypeStruct((tok, HDIM), f32)] * 2
        + [jax.ShapeDtypeStruct((keys, HDIM), bf16)] * 2,
        compiler_params=pltpu.CompilerParams(vmem_limit_bytes=VMEM_LIMIT),
        cost_estimate=pl.CostEstimate(
            flops=4 * tok * keys * HDIM, bytes_accessed=30_000_000, transcendentals=0
        ),
        name="attend",
    )(base, doc_starts, q, kv)


def attend_back_kernel(
    scale, base_ref, starts_ref, q_ref, do_ref, o_ref, lse_ref, k_ref, v_ref,
    dq_ref, dkv_ref, dk_ref, dv_ref,
):
    i = pl.program_id(0)

    @pl.when(i == 0)
    def _():
        dk_ref[...] = jnp.zeros_like(dk_ref)
        dv_ref[...] = jnp.zeros_like(dv_ref)

    q, do = q_ref[...], do_ref[...]
    delta = jnp.sum(do.astype(f32) * o_ref[...], axis=1, keepdims=True)
    lse = lse_ref[:, 0:1]
    low, high = sight(base_ref, starts_ref, i * QB)
    blocks = (base_ref[0] + (i + 1) * QB + KB - 1) // KB

    def turn(j, dq):
        at = pl.ds(pl.multiple_of(j * KB, KB), KB)
        k, v = k_ref[at, :], v_ref[at, :]
        visible = seen(low, high, j * KB)
        s = dot_nt(q, k) * scale
        p = jnp.exp(jnp.where(visible, s - lse, neg_large))
        ds = (p * (dot_nt(do, v) - delta)).astype(bf16)
        dv_ref[at, :] += dot_tn(p.astype(bf16), do)
        dk_ref[at, :] += dot_tn(ds, q) * scale
        return dq + dot_nn(ds, k)

    dq_ref[...] = lax.fori_loop(0, blocks, turn, jnp.zeros((QB, HDIM), f32)) * scale

    @pl.when(i == pl.num_programs(0) - 1)
    def _():
        n_p, nz, rows, _ = dkv_ref.shape
        kw = HDIM // n_p

        @pl.loop(0, nz)
        def _(z):
            got = []
            for t in range(2):
                at = pl.ds(pl.multiple_of((2 * z + t) * rows, rows), rows)
                got += [dk_ref[at, :].astype(bf16), dv_ref[at, :].astype(bf16)]
            for q in range(n_p):
                cut = slice(q * kw, q * kw + kw)
                dkv_ref[q, z] = jnp.concatenate([v[:, cut] for v in got], axis=1)


def attend_back(base, doc_starts, q, do, o, lse, k, v, packed):
    tok = q.shape[0]
    row = pl.BlockSpec((QB, HDIM), lambda i: (i, 0))
    whole = lambda s: pl.BlockSpec(s, lambda i: (0,) * len(s))
    smem = pl.BlockSpec(memory_space=pltpu.SMEM)
    return pl.pallas_call(
        functools.partial(attend_back_kernel, HDIM ** (-0.5)),
        grid=(tok // QB,),
        in_specs=[smem, smem, row, row, row, row, whole(k.shape), whole(k.shape)],
        out_specs=[row, whole(packed)],
        out_shape=[
            jax.ShapeDtypeStruct((tok, HDIM), f32),
            jax.ShapeDtypeStruct(packed, bf16),
        ],
        scratch_shapes=[pltpu.VMEM(k.shape, f32), pltpu.VMEM(k.shape, f32)],
        compiler_params=pltpu.CompilerParams(vmem_limit_bytes=VMEM_LIMIT),
        cost_estimate=pl.CostEstimate(
            flops=10 * tok * k.shape[0] * HDIM, bytes_accessed=40_000_000, transcendentals=0
        ),
        name="attend_back",
    )(base, doc_starts, q, do, o, lse, k, v)


def one_at(shape, source, where=True):
    lane = iota2(shape, 1)
    return ((iota2(shape, 0) == source(lane)) & where).astype(bf16)


def eye(n):
    return one_at((n, n), lambda lane: lane)


def q_order(kw):
    hk = kw // 2
    return one_at(
        (HDIM, HDIM), lambda l: ((l % kw) // hk) * (HDIM // 2) + (l // kw) * hk + l % hk
    )


def bc_order(p, bw, n_p):
    return one_at((2 * n_p * bw, 2 * bw), lambda l: (l // bw) * (n_p * bw) + p * bw + l % bw)


def last_order(p, kw, n_heads, dt_rows):
    hk = kw // 2
    lane = iota2((HDIM, 128), 1)
    lane_dt = iota2((dt_rows, 128), 1)
    key = one_at((HDIM, 128), lambda l: (l // hk) * (HDIM // 2) + p * hk + l % hk, lane < kw)
    value = one_at((HDIM, 128), lambda l: p * kw + l - kw, (lane >= kw) & (lane < 2 * kw))
    step = one_at(
        (dt_rows, 128),
        lambda l: p * n_heads + l - 2 * kw,
        (lane_dt >= 2 * kw) & (lane_dt < 2 * kw + n_heads),
    )
    return key, value, step


def pack_kernel(
    x_ref, bc_ref, k_ref, v_ref, dt_ref, q_ref, z_ref, mout_ref, aout_ref, gate_ref, up_ref,
    down_ref, a_ref, b_ref, c_ref, d_ref, e_ref,
):
    n_p = a_ref.shape[0]
    xw, bw, kw = x_ref.shape[1] // n_p, bc_ref.shape[1] // (2 * n_p), HDIM // n_p
    n_heads, ff, aw = dt_ref.shape[1] // n_p, gate_ref.shape[1] // n_p, q_ref.shape[1] // n_p
    bc, key, value = bc_ref[...].astype(bf16), k_ref[...].astype(bf16), v_ref[...].astype(bf16)
    step = dt_ref[...].astype(bf16)
    order = q_order(kw)
    for p in range(n_p):
        cut = lambda ref, n: ref[:, p * n : p * n + n].astype(bf16)
        flip = lambda ref, n: dot_tn(ref[p * n : p * n + n, :].astype(bf16), eye(n)).astype(bf16)
        a_ref[p, :, :xw] = cut(x_ref, xw)
        a_ref[p, :, xw : xw + 2 * bw] = dot_nn(bc, bc_order(p, bw, n_p)).astype(bf16)
        s_key, s_value, s_step = last_order(p, kw, n_heads, dt_ref.shape[1])
        a_ref[p, :, xw + 2 * bw :] = (
            dot_nn(key, s_key) + dot_nn(value, s_value) + dot_nn(step, s_step)
        ).astype(bf16)
        b_ref[p, :, :HDIM] = dot_nn(cut(q_ref, aw), order).astype(bf16)
        b_ref[p, :, HDIM:] = cut(z_ref, xw)
        c_ref[p, :, :xw] = flip(mout_ref, xw)
        c_ref[p, :, xw:] = flip(aout_ref, aw)
        d_ref[p, :, :ff] = cut(gate_ref, ff)
        d_ref[p, :, ff:] = cut(up_ref, ff)
        e_ref[p] = flip(down_ref, ff)


def pack(n_p, *weights):
    x, bc, k, v, dt, q, z, mout, aout, gate, up, down = weights
    rows = x.shape[0]
    ff, xw = gate.shape[1] // n_p, x.shape[1] // n_p
    widths = (xw + bc.shape[1] // n_p + 128, HDIM + xw, xw + HDIM, 2 * ff, ff)
    vm = pl.BlockSpec(memory_space=pltpu.VMEM)
    return pl.pallas_call(
        pack_kernel,
        in_specs=[vm] * 12,
        out_specs=[vm] * 5,
        out_shape=[jax.ShapeDtypeStruct((n_p, rows, w), bf16) for w in widths],
        compiler_params=pltpu.CompilerParams(vmem_limit_bytes=VMEM_LIMIT),
        cost_estimate=pl.CostEstimate(flops=0, bytes_accessed=10_000_000, transcendentals=0),
        name="pack",
    )(*weights)


def unpack_kernel(
    a_ref, b_ref, c_ref, d_ref, e_ref,
    x_ref, bc_ref, k_ref, v_ref, dt_ref, q_ref, z_ref, mout_ref, aout_ref, gate_ref, up_ref,
    down_ref,
):
    n_p, rows = a_ref.shape[0], a_ref.shape[1]
    xw, bw, kw = x_ref.shape[1] // n_p, bc_ref.shape[1] // (2 * n_p), HDIM // n_p
    n_heads, ff, aw = dt_ref.shape[1] // n_p, gate_ref.shape[1] // n_p, q_ref.shape[1] // n_p
    order, turn = q_order(kw), eye(rows)
    bc, key = jnp.zeros(bc_ref.shape, f32), jnp.zeros(k_ref.shape, f32)
    value, step = jnp.zeros(v_ref.shape, f32), jnp.zeros(dt_ref.shape, f32)
    for p in range(n_p):
        cut = lambda n: slice(p * n, p * n + n)
        x_ref[:, cut(xw)] = a_ref[p, :, :xw].astype(f32)
        bc = bc + dot_nt(a_ref[p, :, xw : xw + 2 * bw], bc_order(p, bw, n_p))
        last = a_ref[p, :, xw + 2 * bw :]
        s_key, s_value, s_step = last_order(p, kw, n_heads, dt_ref.shape[1])
        key, value = key + dot_nt(last, s_key), value + dot_nt(last, s_value)
        step = step + dot_nt(last, s_step)
        q_ref[:, cut(aw)] = dot_nt(b_ref[p, :, :HDIM], order)
        z_ref[:, cut(xw)] = b_ref[p, :, HDIM:].astype(f32)
        mout_ref[cut(xw), :] = dot_tn(c_ref[p, :, :xw], turn)
        aout_ref[cut(aw), :] = dot_tn(c_ref[p, :, xw:], turn)
        gate_ref[:, cut(ff)] = d_ref[p, :, :ff].astype(f32)
        up_ref[:, cut(ff)] = d_ref[p, :, ff:].astype(f32)
        down_ref[cut(ff), :] = dot_tn(e_ref[p], turn)
    bc_ref[...] = bc
    k_ref[...], v_ref[...], dt_ref[...] = key, value, step


def unpack(pieces, like):
    vm = pl.BlockSpec(memory_space=pltpu.VMEM)
    return pl.pallas_call(
        unpack_kernel,
        in_specs=[vm] * 5,
        out_specs=[vm] * 12,
        out_shape=[jax.ShapeDtypeStruct(w.shape, f32) for w in like],
        compiler_params=pltpu.CompilerParams(vmem_limit_bytes=VMEM_LIMIT),
        cost_estimate=pl.CostEstimate(flops=0, bytes_accessed=10_000_000, transcendentals=0),
        name="unpack",
    )(*pieces)


def at_rows(first, count):
    return pl.ds(pl.multiple_of(first, count), count)


def place():
    return lax.axis_index("z"), lax.axis_index("p"), lax.axis_index("head")


def hop(p, d):
    x, y = lax.rem(p, 2), p // 2
    return lax.rem(y + d // 2, 2) * 2 + lax.rem(x + d % 2, 2)


def chip(z, p, c):
    return (z, p, c)


def meet(others):
    barrier = pltpu.get_barrier_semaphore()
    for other in others:
        pl.semaphore_signal(barrier, inc=1, device_id=other, device_id_type=MESH)
    pl.semaphore_wait(barrier, len(others))


def send(src, dst, send_sem, recv_sem, to):
    copy = pltpu.make_async_remote_copy(
        src_ref=src, dst_ref=dst, send_sem=send_sem, recv_sem=recv_sem,
        device_id=to, device_id_type=MESH,
    )
    copy.start()
    return copy


HOPS = (3, 1, 2)


def z_chain(ref, up_sems, down_sems):
    z, p, c = place()
    nz = ref.shape[0]

    def block_up(k):
        at = ref.at[z - k]
        return pltpu.make_async_remote_copy(
            src_ref=at, dst_ref=at, send_sem=up_sems.at[0, k], recv_sem=up_sems.at[1, k],
            device_id=chip(z + 1, p, c), device_id_type=MESH,
        )

    def block_down(k):
        at = ref.at[z + k]
        return pltpu.make_async_remote_copy(
            src_ref=at, dst_ref=at, send_sem=down_sems.at[0, k], recv_sem=down_sems.at[1, k],
            device_id=chip(z - 1, p, c), device_id_type=MESH,
        )

    def got_up(k):
        at = ref.at[z - k]
        pltpu.make_async_remote_copy(
            src_ref=at, dst_ref=at, send_sem=up_sems.at[0, k - 1], recv_sem=up_sems.at[1, k - 1],
            device_id=chip(z - 1, p, c), device_id_type=MESH,
        ).wait_recv()

    def got_down(k):
        at = ref.at[z + k]
        pltpu.make_async_remote_copy(
            src_ref=at, dst_ref=at, send_sem=down_sems.at[0, k - 1],
            recv_sem=down_sems.at[1, k - 1],
            device_id=chip(z + 1, p, c), device_id_type=MESH,
        ).wait_recv()

    def stage(k):
        if k:

            @pl.when(z - k >= 0)
            def _():
                got_up(k)

        @pl.when((z - k >= 0) & (z + 1 < nz))
        def _():
            block_up(k).start()

        if k:

            @pl.when(z + k < nz)
            def _():
                got_down(k)

        @pl.when((z + k < nz) & (z > 0))
        def _():
            block_down(k).start()

    def done():
        for k in range(nz):

            @pl.when((z - k >= 0) & (z + 1 < nz))
            def _():
                block_up(k).wait_send()

            @pl.when((z + k < nz) & (z > 0))
            def _():
                block_down(k).wait_send()

    return stage, done


def share(block, part, far_sems, near_sems, own_sems=None):
    z, p, c = place()
    other = chip(z, p, 1 - c)
    x, y, far = hop(p, 1), hop(p, 2), hop(p, 3)

    def far_send(ref, i, q):
        return send(ref, ref, far_sems.at[0, i], far_sems.at[1, i], chip(z, q, c))

    def near_send(q, i):
        return send(block(q), block(q), near_sems.at[0, i], near_sems.at[1, i], other)

    out = [far_send(block(p), 0, x), far_send(block(p), 1, y)]
    near = []
    if own_sems is not None:
        near.append(send(block(p), block(p), own_sems.at[0], own_sems.at[1], other))

    def middle():
        out[0].wait_recv()
        out.append(far_send(part(x, 0), 2, y))
        out[1].wait_recv()
        out.append(far_send(part(y, 1), 3, x))
        if near_sems is not None:
            near.append(near_send(x, 0))
            near.append(near_send(y, 1))

    def end():
        out[2].wait_recv()
        out[3].wait_recv()
        if near_sems is not None:
            near.append(near_send(far, 2))
        for copy in out:
            copy.wait_send()
        for copy in near:
            copy.wait()

    return middle, end


def share_rows(full_ref, half, own_sems, far_sems, near_sems):
    z, p, c = place()
    rows = lambda q: (q * 2 + c) * half
    return share(
        lambda q: full_ref.at[at_rows(rows(q), half), :],
        lambda q, i: full_ref.at[at_rows(rows(q) + i * (half // 2), half // 2), :],
        far_sems, near_sems, own_sems,
    )


def reduce_blocks(pairs, part, keep, sib_out, sib_in, out, relay, came, near_sems, far_sems):
    z, p, c = place()
    other = chip(z, p, 1 - c)
    half, width = keep.shape[1], keep.shape[2]
    tile, quarter = part.shape[1], half // 2
    x, y = chip(z, hop(p, 1), c), chip(z, hop(p, 2), c)
    first, second = at_rows(0, quarter), at_rows(quarter, quarter)
    near, far = [], []

    def far_send(src, dst, i, to):
        far.append(send(src, dst, far_sems.at[0, i], far_sems.at[1, i], to))

    def total_of(i, rows, extra=None):
        @pl.loop(0, quarter // 16)
        def _(r):
            at = at_rows(rows + r * 16, 16)
            total = keep[i, at, :] + sib_in[i, at, :].astype(f32)
            if extra is not None:
                total = total + relay[extra, at_rows(r * 16, 16), :].astype(f32)
            out[i, at, :] = total.astype(bf16)

    def pass_on(i):
        near[i].wait_recv()
        if i == 0:
            total_of(0, 0)
            far_send(out.at[0, first, :], relay.at[0], 0, x)
            total_of(0, quarter)
            far_send(out.at[0, second, :], relay.at[1], 1, y)
        if i == 1:
            total_of(1, 0)
            far_send(out.at[1, first, :], came.at[0, first, :], 2, x)
        if i == 2:
            total_of(2, quarter)
            far_send(out.at[2, second, :], came.at[1, second, :], 3, y)

    for i, d in enumerate((3, 1, 2, 0)):
        rows = at_rows(hop(p, d) * (2 * half), 2 * half)

        @pl.loop(0, width // tile)
        def _(n):
            cols = at_rows(n * tile, tile)
            total = dot_nt(pairs[0][0][rows, :], pairs[0][1][cols, :])
            for left, right in pairs[1:]:
                total = total + dot_nt(left[rows, :], right[cols, :])
            part[...] = total
            keep[i, :, cols] = part[at_rows(c * half, half), :]
            sib_out[i, :, cols] = part[at_rows((1 - c) * half, half), :].astype(bf16)

        near.append(
            send(sib_out.at[i], sib_in.at[i], near_sems.at[0, i], near_sems.at[1, i], other)
        )
        if i:
            pass_on(i - 1)

    def middle():
        far[1].wait_recv()
        total_of(1, quarter, 1)
        far_send(out.at[1, second, :], came.at[0, second, :], 4, x)
        far[0].wait_recv()
        total_of(2, 0, 0)
        far_send(out.at[2, first, :], came.at[1, first, :], 5, y)

    def finish():
        near[3].wait_recv()
        for copy in far[2:]:
            copy.wait_recv()

    def total_rows(at):
        total = keep[3, at, :] + sib_in[3, at, :].astype(f32)
        return total + came[0, at, :].astype(f32) + came[1, at, :].astype(f32)

    def done():
        for copy in near + far:
            copy.wait_send()

    return total_rows, middle, finish, done


def greet():
    z, p, c = place()
    meet([chip(z, p, 1 - c)] + [chip(z, hop(p, d), c) for d in HOPS])


def rms(rows):
    return lax.rsqrt(jnp.mean(rows * rows, axis=1, keepdims=True) + eps_norm)


def mid_kernel(
    left, right, resid, gain, mid_ref, full_ref,
    part, keep, sib_out, sib_in, out, relay, came, n_sems, f_sems, own_sems, far_sems, near_sems,
):
    greet()
    z, p, c = place()
    half = keep.shape[1]
    total_rows, middle, finish, done = reduce_blocks(
        [(left, right)], part, keep, sib_out, sib_in, out, relay, came, n_sems, f_sems
    )
    middle()
    finish()
    g = gain[...]

    @pl.loop(0, half // 16)
    def _(r):
        at = at_rows(r * 16, 16)
        mid = resid[at, :] + total_rows(at)
        mid_ref[at, :] = mid
        full_ref[at_rows((p * 2 + c) * half + r * 16, 16), :] = (mid * rms(mid) * g).astype(bf16)

    share_middle, share_end = share_rows(full_ref, half, own_sems, far_sems, near_sems)
    share_middle()
    done()
    share_end()


def two_kernel(
    left, right, mid_own, grad_own, gain, dmid_ref, ggain_ref, full_ref,
    part, keep, sib_out, sib_in, out, relay, came, n_sems, f_sems, own_sems, far_sems, near_sems,
):
    greet()
    z, p, c = place()
    half = keep.shape[1]
    total_rows, middle, finish, done = reduce_blocks(
        [(left, right)], part, keep, sib_out, sib_in, out, relay, came, n_sems, f_sems
    )
    middle()
    finish()
    g = gain[...]
    ggain_ref[...] = jnp.zeros_like(ggain_ref)

    @pl.loop(0, half // 16)
    def _(r):
        at = at_rows(r * 16, 16)
        d_two, mid = total_rows(at), mid_own[at, :]
        scale = rms(mid)
        w = d_two * g
        d_mid = grad_own[at, :] + scale * w - mid * (scale * scale * scale) * jnp.mean(
            w * mid, axis=1, keepdims=True
        )
        ggain_ref[...] += jnp.sum(d_two * mid * scale, axis=0, keepdims=True)
        dmid_ref[at, :] = d_mid
        full_ref[at_rows((p * 2 + c) * half + r * 16, 16), :] = d_mid.astype(bf16)

    share_middle, share_end = share_rows(full_ref, half, own_sems, far_sems, near_sems)
    share_middle()
    done()
    share_end()


def one_kernel(
    n, left_a, right_a, left_b, right_b, hidden_own, dmid_own, gain, act, w_act, mid_own, *refs
):
    ins, (grad_ref, block_ref, ggain_ref), outs = refs[:n], refs[n : n + 3], refs[n + 3 : 2 * n + 3]
    first, second = refs[2 * n + 3 : 2 * n + 12], refs[2 * n + 12 : 2 * n + 21]
    own_sems, w_sems, loc_sems = refs[2 * n + 21 :]
    greet()
    z, p, c = place()
    half = hidden_own.shape[0]
    total_rows, middle, finish, done = reduce_blocks(
        [(left_a, right_a), (left_b, right_b)], *first
    )
    middle()
    total_out, middle_out, finish_out, done_out = reduce_blocks([(act, w_act)], *second)
    moved = swap_begin(ins, outs, w_sems, loc_sems)
    g = gain[...]
    ggain_ref[...] = jnp.zeros_like(ggain_ref)
    middle_out()
    finish()

    @pl.loop(0, half // 16)
    def _(r):
        at = at_rows(r * 16, 16)
        d_one, hid = total_rows(at), hidden_own[at, :]
        scale = rms(hid)
        w = d_one * g
        d_in = dmid_own[at, :] + scale * w - hid * (scale * scale * scale) * jnp.mean(
            w * hid, axis=1, keepdims=True
        )
        ggain_ref[...] += jnp.sum(d_one * hid * scale, axis=0, keepdims=True)
        grad_ref[at_rows(c * half + r * 16, 16), :] = d_in

    mine = at_rows(c * half, half)
    other = chip(z, p, 1 - c)
    copies = [
        send(grad_ref.at[mine, :], grad_ref.at[mine, :], own_sems.at[0, 0], own_sems.at[1, 0], other)
    ]
    finish_out()

    @pl.loop(0, half // 16)
    def _(r):
        at = at_rows(r * 16, 16)
        block_ref[at_rows(c * half + r * 16, 16), :] = mid_own[at, :] + total_out(at)

    copies.append(
        send(block_ref.at[mine, :], block_ref.at[mine, :], own_sems.at[0, 1], own_sems.at[1, 1], other)
    )
    done()
    done_out()
    for copy in copies + moved:
        copy.wait()


VM = pl.BlockSpec(memory_space=pltpu.VMEM)
ANYWHERE = pl.BlockSpec(memory_space=pl.ANY)


def swap_begin(ins, outs, sems, loc_sems):
    z, p, c = place()
    copies = []
    for j, (src, dst) in enumerate(zip(ins, outs)):
        for i, d in enumerate(HOPS):
            q = hop(p, d)
            copies.append(
                send(src.at[q], dst.at[p], sems.at[0, j, i], sems.at[1, j, i], chip(z, q, c))
            )
        local = pltpu.make_async_copy(src.at[p], dst.at[p], loc_sems.at[j])
        local.start()
        copies.append(local)
    return copies


def swap_sems(n):
    return [pltpu.SemaphoreType.DMA((2, n, 3)), pltpu.SemaphoreType.DMA((n,))]


def reduce_scratch(half, width):
    return [
        pltpu.VMEM((2 * half, 512), f32),
        pltpu.VMEM((4, half, width), f32),
        pltpu.VMEM((4, half, width), bf16),
        pltpu.VMEM((4, half, width), bf16),
        pltpu.VMEM((3, half, width), bf16),
        pltpu.VMEM((2, half // 2, width), bf16),
        pltpu.VMEM((2, half, width), bf16),
        pltpu.SemaphoreType.DMA((2, 4)),
        pltpu.SemaphoreType.DMA((2, 6)),
    ]


SHARE_SEMS = [
    pltpu.SemaphoreType.DMA((2,)),
    pltpu.SemaphoreType.DMA((2, 4)),
    pltpu.SemaphoreType.DMA((2, 3)),
]


def plane_call(kernel, name, number, args, shapes, scratch, nbytes=150_000_000, moved=()):
    n = len(moved)
    if n:
        kernel = functools.partial(kernel, n)
        scratch = scratch + swap_sems(n)
    return pl.pallas_call(
        kernel,
        in_specs=[VM] * (len(args) + n),
        out_specs=[VM] * len(shapes) + [ANYWHERE] * n,
        out_shape=[jax.ShapeDtypeStruct(s, t) for s, t in shapes]
        + [jax.ShapeDtypeStruct(m.shape, m.dtype) for m in moved],
        scratch_shapes=scratch,
        compiler_params=pltpu.CompilerParams(
            collective_id=number, has_side_effects=True, vmem_limit_bytes=VMEM_LIMIT
        ),
        cost_estimate=pl.CostEstimate(flops=0, bytes_accessed=nbytes, transcendentals=0),
        name=name,
    )(*args, *moved)


def mid_step(mixed, w, resid_own, gain):
    tok, width = mixed.shape[0], w.shape[0]
    half = resid_own.shape[0]
    return plane_call(
        mid_kernel, "mid_step", 1, (mixed, w, resid_own, gain),
        [((half, width), f32), ((tok, width), bf16)],
        reduce_scratch(half, width) + SHARE_SEMS,
    )


def two_step(d_gu, w, mid_own, grad_own, gain):
    tok, width = d_gu.shape[0], w.shape[0]
    half = mid_own.shape[0]
    return plane_call(
        two_kernel, "two_step", 2, (d_gu, w, mid_own, grad_own, gain),
        [((half, width), f32), ((1, width), f32), ((tok, width), bf16)],
        reduce_scratch(half, width) + SHARE_SEMS,
    )


def one_step(d_a, w_a, d_b, w_b, hidden_own, dmid_own, gain, act, w_act, mid_own, moved):
    width = w_a.shape[0]
    half = hidden_own.shape[0]
    return plane_call(
        one_kernel, "one_step", 3,
        (d_a, w_a, d_b, w_b, hidden_own, dmid_own, gain, act, w_act, mid_own),
        [((2 * half, width), f32), ((2 * half, width), f32), ((1, width), f32)],
        reduce_scratch(half, width)
        + reduce_scratch(half, width)
        + [pltpu.SemaphoreType.DMA((2, 2))],
        moved=moved,
    )


HALO = 16


def open_kernel(n, *refs):
    hid, gains_ref, a_ref = refs[:3]
    w_refs = refs[3 : 3 + n]
    gain_out, full_ref, a_out = refs[3 + n : 6 + n]
    w_outs = refs[6 + n : 6 + 2 * n]
    (
        g_vec, gz_sems, gp_sems, a_sems, up_sems, down_sems, own_sems, far_sems, near_sems,
        w_sems, loc_sems, halo_sems,
    ) = refs[6 + 2 * n :]
    z, p, c = place()
    nz, half, rows = a_out.shape[0], hid.shape[0], a_ref.shape[1]
    tok = full_ref.shape[0] - HALO
    ups = [chip(lax.rem(z + d, nz), p, c) for d in range(1, nz)]
    flat = [chip(z, hop(p, d), c) for d in HOPS]
    meet(ups + flat + [chip(z, p, 1 - c)])
    gain_out[p, z] = gains_ref[...]
    gz = [
        send(gain_out.at[p, z], gain_out.at[p, z], gz_sems.at[0, d], gz_sems.at[1, d], ups[d])
        for d in range(nz - 1)
    ]
    to_plane = []
    for i, d in enumerate(HOPS):
        to_plane.append(
            send(a_ref.at[hop(p, d)], a_out.at[z, p], a_sems.at[0, i], a_sems.at[1, i], flat[i])
        )
    local = [pltpu.make_async_copy(a_ref.at[p], a_out.at[z, p], loc_sems.at[n])]
    for j in range(n):
        local.append(pltpu.make_async_copy(w_refs[j].at[p], w_outs[j].at[p], loc_sems.at[j]))
    for copy in local:
        copy.start()

    for copy in gz:
        copy.wait_recv()
    gp = [
        send(gain_out.at[p], gain_out.at[p], gp_sems.at[0, i], gp_sems.at[1, i], flat[i])
        for i in range(3)
    ]
    for copy in gp:
        copy.wait_recv()
    for i in range(nz):
        for j in range(gain_out.shape[0]):
            first = (i * gain_out.shape[0] + j) * rows
            g_vec[:, first : first + rows] = gain_out[j, i][:, :rows]
    g = g_vec[0:1, :]

    @pl.loop(0, half // 16)
    def _(r):
        rows_in = hid[at_rows(r * 16, 16), :]
        full_ref[at_rows((p * 2 + c) * half + r * 16, 16), :] = (
            rows_in * rms(rows_in) * g
        ).astype(bf16)

    share_middle, share_end = share_rows(full_ref, half, own_sems, far_sems, near_sems)

    stage, chain_done = z_chain(a_out, up_sems, down_sems)
    for copy in to_plane:
        copy.wait_recv()
    local[0].wait()
    stage(0)
    share_middle()
    if nz > 2:
        stage(1)
    moved = []
    for j in range(n):
        for i, d in enumerate(HOPS):
            moved.append(
                send(
                    w_refs[j].at[hop(p, d)], w_outs[j].at[p], w_sems.at[0, j, i],
                    w_sems.at[1, j, i], flat[i],
                )
            )
    share_end()
    halo_from = full_ref.at[at_rows(tok - HALO, HALO), :]
    halo_to = full_ref.at[at_rows(tok, HALO), :]

    def halo(to):
        return pltpu.make_async_remote_copy(
            src_ref=halo_from, dst_ref=halo_to, send_sem=halo_sems.at[0],
            recv_sem=halo_sems.at[1], device_id=to, device_id_type=MESH,
        )

    @pl.when(z + 1 < nz)
    def _():
        halo(chip(z + 1, p, c)).start()

    @pl.when(z == 0)
    def _():
        full_ref[at_rows(tok, HALO), :] = jnp.zeros((HALO, full_ref.shape[1]), bf16)

    for k in range(2, nz):
        stage(k)

    @pl.when(z > 0)
    def _():
        halo(chip(z - 1, p, c)).wait_recv()

    @pl.when(z + 1 < nz)
    def _():
        halo(chip(z + 1, p, c)).wait_send()

    chain_done()
    for copy in moved + local[1:]:
        copy.wait()
    for copy in gz + gp + to_plane:
        copy.wait_send()


def open_step(hid, gains, piece, rest, tok, nz):
    width, n, n_p = hid.shape[1], len(rest), piece.shape[0]
    anywhere = pl.BlockSpec(memory_space=pl.ANY)
    dma = pltpu.SemaphoreType.DMA
    return pl.pallas_call(
        functools.partial(open_kernel, n),
        in_specs=[VM] * (n + 3),
        out_specs=[VM, VM] + [anywhere] * (n + 1),
        out_shape=[
            jax.ShapeDtypeStruct((n_p, nz) + gains.shape, f32),
            jax.ShapeDtypeStruct((tok + HALO, width), bf16),
            jax.ShapeDtypeStruct((nz,) + piece.shape, bf16),
        ]
        + [jax.ShapeDtypeStruct(r.shape, bf16) for r in rest],
        scratch_shapes=[
            pltpu.VMEM((8, width), f32), dma((2, nz - 1)), dma((2, 3)), dma((2, 3)), dma((2, nz)),
            dma((2, nz)),
        ]
        + SHARE_SEMS
        + [dma((2, n, 3)), dma((n + 1,)), dma((2,))],
        compiler_params=pltpu.CompilerParams(
            collective_id=4, has_side_effects=True, vmem_limit_bytes=VMEM_LIMIT
        ),
        cost_estimate=pl.CostEstimate(flops=0, bytes_accessed=250_000_000, transcendentals=0),
        name="open_step",
    )(hid, gains, piece, *rest)


def gather_bc_kernel(
    x_ref, kv_ref, grad_ref, full_ref, kvz_ref, g_ref,
    far_sems, near_sems, z_sems, own_g, far_g, near_g,
):
    z, p, c = place()
    nz = kvz_ref.shape[0]
    other = chip(z, p, 1 - c)
    meet(
        [other]
        + [chip(z, hop(p, d), c) for d in HOPS]
        + [chip(lax.rem(z + d, nz), p, c) for d in range(1, nz)]
    )
    kvz_ref[z] = kv_ref[...]

    def up(d):
        return pltpu.make_async_remote_copy(
            src_ref=kv_ref, dst_ref=kvz_ref.at[z], send_sem=z_sems.at[0, d - 1],
            recv_sem=z_sems.at[1, d - 1], device_id=chip(z + d, p, c), device_id_type=MESH,
        )

    for d in range(1, nz):

        @pl.when(z + d < nz)
        def _():
            up(d).start()

    half = x_ref.shape[0] // 2
    full_ref[p] = x_ref[...]
    bc_middle, bc_end = share(
        lambda q: full_ref.at[q, at_rows(c * half, half), :],
        lambda q, i: full_ref.at[q, at_rows(c * half + i * (half // 2), half // 2), :],
        far_sems, near_sems,
    )
    bc_middle()
    g_half = grad_ref.shape[0]
    g_ref[at_rows((p * 2 + c) * g_half, g_half), :] = grad_ref[...].astype(bf16)
    g_middle, g_end = share_rows(g_ref, g_half, own_g, far_g, near_g)
    bc_end()
    g_middle()
    for d in range(1, nz):

        @pl.when(z - d >= 0)
        def _():
            pltpu.make_async_remote_copy(
                src_ref=kv_ref, dst_ref=kvz_ref.at[z - d], send_sem=z_sems.at[0, d - 1],
                recv_sem=z_sems.at[1, d - 1], device_id=chip(z - d, p, c), device_id_type=MESH,
            ).wait_recv()

        @pl.when(z + d < nz)
        def _():
            kvz_ref[z + d] = jnp.zeros(kv_ref.shape, kv_ref.dtype)
            up(d).wait_send()

    g_end()


def gather_bc(x, at, n_p, kv, nz, grad):
    tok = x.shape[0]
    dma = pltpu.SemaphoreType.DMA
    whole = lambda s: pl.BlockSpec(s, lambda i: (0,) * len(s))
    return pl.pallas_call(
        gather_bc_kernel,
        grid=(1,),
        in_specs=[
            pl.BlockSpec((tok, 128), lambda i: (0, at)), whole(kv.shape), whole(grad.shape)
        ],
        out_specs=[
            whole((n_p, tok, 128)), whole((nz,) + kv.shape), whole((tok, grad.shape[1]))
        ],
        out_shape=[
            jax.ShapeDtypeStruct((n_p, tok, 128), bf16),
            jax.ShapeDtypeStruct((nz,) + kv.shape, bf16),
            jax.ShapeDtypeStruct((tok, grad.shape[1]), bf16),
        ],
        scratch_shapes=[dma((2, 4)), dma((2, 3)), dma((2, nz - 1))] + SHARE_SEMS,
        compiler_params=pltpu.CompilerParams(
            collective_id=5, has_side_effects=True, vmem_limit_bytes=VMEM_LIMIT
        ),
        cost_estimate=pl.CostEstimate(flops=0, bytes_accessed=40_000_000, transcendentals=0),
        name="gather_bc",
    )(x, kv, grad)


def carry_kernel(
    state_ref, rate_ref, kvz_ref, in_ref, kv_ref, rates_ref,
    low, came, factor, s_sems, r_sems, p_sems,
):
    z, p, c = place()
    nz = kvz_ref.shape[0]
    ups = [chip(lax.rem(z + d, nz), p, c) for d in range(1, nz)]
    meet([chip(z, hop(p, d), c) for d in (1, 2)] + ups)
    low[...] = state_ref[...].astype(bf16)
    rates_ref[z] = rate_ref[...]
    rates = [
        send(rates_ref.at[z], rates_ref.at[z], r_sems.at[0, d], r_sems.at[1, d], ups[d])
        for d in range(nz - 1)
    ]

    def up(d):
        return pltpu.make_async_remote_copy(
            src_ref=low, dst_ref=came.at[d - 1], send_sem=s_sems.at[0, d - 1],
            recv_sem=s_sems.at[1, d - 1], device_id=chip(z + d, p, c), device_id_type=MESH,
        )

    for d in range(1, nz):

        @pl.when(z + d < nz)
        def _():
            up(d).start()

    kv_ref[p] = kvz_ref[...]
    kv_middle, kv_end = share(
        lambda q: kv_ref.at[q],
        lambda q, i: kv_ref.at[q, pl.ds(i * (nz // 2), nz // 2)],
        p_sems, None,
    )
    in_ref[...] = jnp.zeros_like(in_ref)
    factor[...] = jnp.ones_like(factor)
    lane_head, row_head = head_maps(state_ref.shape[0])
    kv_middle()
    for copy in rates:
        copy.wait_recv()
    for d in range(1, nz):

        @pl.when(z - d >= 0)
        def _():
            pltpu.make_async_remote_copy(
                src_ref=low, dst_ref=came.at[d - 1], send_sem=s_sems.at[0, d - 1],
                recv_sem=s_sems.at[1, d - 1], device_id=chip(z - d, p, c), device_id_type=MESH,
            ).wait_recv()
            scale = jnp.sum(row_head * factor[0:1, :], axis=1, keepdims=True)
            in_ref[...] += scale * came[d - 1].astype(f32)
            factor[...] = factor[...] * rates_ref[z - d]

        @pl.when(z + d < nz)
        def _():
            up(d).wait_send()

    kv_end()
    for copy in rates:
        copy.wait_send()


def carry_step(state, rate, kvz, n_p):
    nz = kvz.shape[0]
    dma = pltpu.SemaphoreType.DMA
    return plane_call(
        carry_kernel, "carry_step", 8, (state, rate, kvz),
        [(state.shape, f32), ((n_p,) + kvz.shape, bf16), ((nz,) + rate.shape, f32)],
        [
            pltpu.VMEM(state.shape, bf16),
            pltpu.VMEM((nz - 1,) + state.shape, bf16),
            pltpu.VMEM(rate.shape, f32),
            dma((2, nz - 1)), dma((2, nz - 1)), dma((2, 4)),
        ],
        nbytes=80_000_000,
    )


def reduce_bc_kernel(n, x_ref, dkv_ref, dx_ref, slope_ref, *refs):
    ins, (out_ref, own_ref, next_ref), outs = refs[:n], refs[n : n + 3], refs[n + 3 : 2 * n + 3]
    (
        sib_out, sib_in, out, came, z_came, first, n_sems, f_sems, own_sems, z_sems, h_sems,
        w_sems, loc_sems,
    ) = refs[2 * n + 3 :]
    z, p, c = place()
    nz = dkv_ref.shape[0]
    half = x_ref.shape[1] // 2
    xw = dx_ref.shape[1]
    other = chip(z, p, 1 - c)
    meet(
        [other]
        + [chip(z, hop(p, d), c) for d in HOPS]
        + [chip(lax.rem(z + d, nz), p, c) for d in range(1, nz)]
    )

    def down(d):
        return pltpu.make_async_remote_copy(
            src_ref=dkv_ref.at[z - d], dst_ref=z_came.at[d - 1], send_sem=z_sems.at[0, d - 1],
            recv_sem=z_sems.at[1, d - 1], device_id=chip(z - d, p, c), device_id_type=MESH,
        )

    for d in range(1, nz):

        @pl.when(z - d >= 0)
        def _():
            down(d).start()

    near, far = [], []
    order = HOPS + (0,)
    for i, d in enumerate(order):
        q = hop(p, d)
        sib_out[i] = x_ref[q, at_rows((1 - c) * half, half), :].astype(bf16)
        near.append(
            send(sib_out.at[i], sib_in.at[i], n_sems.at[0, i], n_sems.at[1, i], other)
        )
    for i, d in enumerate(HOPS):
        q = hop(p, d)
        near[i].wait_recv()
        out[i] = (x_ref[q, at_rows(c * half, half), :] + sib_in[i].astype(f32)).astype(bf16)
        far.append(
            send(out.at[i], came.at[i], f_sems.at[0, i], f_sems.at[1, i], chip(z, q, c))
        )
    moved = swap_begin(ins, outs, w_sems, loc_sems)
    near[3].wait_recv()
    total = x_ref[p, at_rows(c * half, half), :] + sib_in[3].astype(f32)
    for i in (1, 2, 0):
        far[i].wait_recv()
        total = total + came[i].astype(f32)
    mine = out_ref.at[at_rows(c * half, half), :]
    out_ref[at_rows(c * half, half), :] = total
    copy = send(mine, mine, own_sems.at[0], own_sems.at[1], other)
    copy.wait()
    first[:, :xw] = dx_ref[...] * slope_ref[:, :xw]
    first[:, xw:] = out_ref[0:8, :] * slope_ref[:, xw:]

    def edge(to):
        return pltpu.make_async_remote_copy(
            src_ref=first, dst_ref=next_ref, send_sem=h_sems.at[0], recv_sem=h_sems.at[1],
            device_id=to, device_id_type=MESH,
        )

    @pl.when(z > 0)
    def _():
        edge(chip(z - 1, p, c)).start()

    own_ref[...] = dkv_ref[z].astype(f32)
    for d in range(1, nz):

        @pl.when(z + d < nz)
        def _():
            pltpu.make_async_remote_copy(
                src_ref=dkv_ref.at[z], dst_ref=z_came.at[d - 1], send_sem=z_sems.at[0, d - 1],
                recv_sem=z_sems.at[1, d - 1], device_id=chip(z + d, p, c), device_id_type=MESH,
            ).wait_recv()
            own_ref[...] += z_came[d - 1].astype(f32)

        @pl.when(z - d >= 0)
        def _():
            down(d).wait_send()

    @pl.when(z + 1 == nz)
    def _():
        next_ref[...] = jnp.zeros_like(next_ref)

    @pl.when(z + 1 < nz)
    def _():
        edge(chip(z + 1, p, c)).wait_recv()

    @pl.when(z > 0)
    def _():
        edge(chip(z - 1, p, c)).wait_send()

    for done in near + far:
        done.wait_send()
    for copy in moved:
        copy.wait()


def reduce_bc(x, dkv, dx, slope, moved):
    n_p, tok, _ = x.shape
    half, nz = tok // 2, dkv.shape[0]
    dma = pltpu.SemaphoreType.DMA
    return plane_call(
        reduce_bc_kernel, "reduce_bc", 7, (x, dkv, dx, slope),
        [((tok, 128), f32), (dkv.shape[1:], f32), (slope.shape, f32)],
        [
            pltpu.VMEM((4, half, 128), bf16),
            pltpu.VMEM((4, half, 128), bf16),
            pltpu.VMEM((3, half, 128), bf16),
            pltpu.VMEM((3, half, 128), bf16),
            pltpu.VMEM((nz - 1,) + dkv.shape[1:], bf16),
            pltpu.VMEM(slope.shape, f32),
            dma((2, 4)), dma((2, 3)), dma((2,)), dma((2, nz - 1)), dma((2,)),
        ],
        nbytes=100_000_000,
        moved=moved,
    )


def sums_kernel(n, v_ref, *refs):
    ins, out_ref, outs = refs[:n], refs[n], refs[n + 1 : 2 * n + 1]
    came, z_sems, p_sems, c_sems, w_sems, loc_sems = refs[2 * n + 1 :]
    z, p, c = place()
    nz = came.shape[0]
    ups = [chip(lax.rem(z + d, nz), p, c) for d in range(1, nz)]
    other = chip(z, p, 1 - c)
    meet(ups + [chip(z, hop(p, d), c) for d in HOPS] + [other])
    moved = swap_begin(ins, outs, w_sems, loc_sems)
    copies = []
    for d in range(1, nz):
        copies.append(
            send(v_ref, came.at[d], z_sems.at[0, d - 1], z_sems.at[1, d - 1], ups[d - 1])
        )
    total = v_ref[...]
    for d in range(1, nz):
        copies[d - 1].wait_recv()
        total = total + came[d]
    out_ref[c, p] = total
    far = []
    for i, d in enumerate(HOPS):
        far.append(
            send(out_ref.at[c, p], out_ref.at[c, p], p_sems.at[0, i], p_sems.at[1, i], chip(z, hop(p, d), c))
        )
    for copy in far:
        copy.wait_recv()
    near = send(out_ref.at[c], out_ref.at[c], c_sems.at[0], c_sems.at[1], other)
    for copy in copies + far:
        copy.wait_send()
    near.wait()
    for copy in moved:
        copy.wait()


def sums_step(v, nz, n_p, moved):
    return plane_call(
        sums_kernel, "sums_step", 6, (v,),
        [((2, n_p) + v.shape, f32)],
        [
            pltpu.VMEM((nz,) + v.shape, f32),
            pltpu.SemaphoreType.DMA((2, nz - 1)),
            pltpu.SemaphoreType.DMA((2, 3)),
            pltpu.SemaphoreType.DMA((2,)),
        ],
        moved=moved,
    )


def rope_tables(positions, pairs):
    freqs = rope_base ** (-2.0 * pairs.astype(f32) / HDIM)
    angles = positions.astype(f32)[:, None] * freqs[None, :]
    return jnp.cos(angles), jnp.sin(angles)


def carry_back(state, rates):
    nz, zi = lax.axis_size("z"), lax.axis_index("z")
    low = state.astype(bf16)
    total, factor = None, None
    for d in range(1, nz):
        came = lax.ppermute(low, "z", [(i, i - d) for i in range(d, nz)]).astype(f32)
        total = came if total is None else total + factor * came
        rate = lax.dynamic_index_in_dim(rates, (zi + d) % nz, 0, keepdims=False)
        factor = rate if factor is None else factor * rate
    return total


def shards(
    hidden_in,
    grad_out,
    doc_starts,
    norm_mixer,
    norm_ffn,
    mamba_z,
    mamba_x,
    mamba_bc,
    mamba_dt,
    conv_x,
    conv_bc,
    a_log,
    dt_bias,
    skip_gain,
    mamba_out,
    attn_query,
    attn_key,
    attn_value,
    attn_out,
    ffn_gate,
    ffn_up,
    ffn_down,
):
    own = hidden_in.shape[0]
    width = hidden_in.shape[1]
    half = own // 2
    nz, n_p = lax.axis_size("z"), lax.axis_size("p")
    zi, pi, ci = lax.axis_index("z"), lax.axis_index("p"), lax.axis_index("head")
    tok = own * n_p
    base = zi * tok
    positions = base + jnp.arange(tok, dtype=jnp.int32)
    edge = conv_x.shape[0] - 1
    ext_docs = doc_ids(base - edge + jnp.arange(tok + 2 * edge, dtype=jnp.int32), doc_starts)
    rows = mamba_z.shape[0]
    n_heads = a_log.shape[0] // n_p
    xw = n_heads * MHDIM
    bw = mamba_bc.shape[1] // (2 * n_p)
    cw = xw + 2 * bw
    kw = HDIM // n_p
    hk = kw // 2
    tail_w = 128 - 2 * kw - n_heads

    weights = (
        mamba_x, mamba_bc, attn_key, attn_value, mamba_dt, attn_query, mamba_z, mamba_out, attn_out,
        ffn_gate, ffn_up, ffn_down,
    )
    piece_a, *rest = pack(n_p, *weights)

    def along_z(piece):
        piece = piece.reshape(n_p * rows, piece.shape[2])
        return lax.all_gather(piece, "z", axis=0, tiled=True)

    gains_own = jnp.pad(
        jnp.stack([norm_mixer, norm_ffn]).astype(bf16).astype(f32), ((0, 6), (0, 128 - rows))
    )
    my_half = lambda v: lax.dynamic_slice_in_dim(v, ci * half, half, 0)
    hidden_own, grad_own = my_half(hidden_in), my_half(grad_out)
    gains, normed_one, w_a, *rest = open_step(hidden_own, gains_own, piece_a, rest, tok, nz)
    w_a = w_a.reshape(nz * n_p * rows, w_a.shape[3])
    gains = gains.transpose(2, 1, 0, 3)[:, :, :, :rows].reshape(8, 1, width)
    gain_mix, gain_ffn = gains[0], gains[1]
    w_b, w_c, w_d, w_e = [along_z(piece) for piece in rest]

    in_ext = product(normed_one, w_a)
    in_b = product(normed_one, w_b)[:tok]
    in_a = in_ext[:tok]
    pre_ext = in_ext[:, :cw].astype(bf16)
    gate_z = in_b[:, HDIM:]
    slice_1 = lambda v, at, n: lax.dynamic_slice_in_dim(v, at, n, 1)
    taps = jnp.concatenate(
        [
            slice_1(conv_x, pi * xw, xw),
            slice_1(conv_bc, pi * bw, bw),
            slice_1(conv_bc, (n_p + pi) * bw, bw),
        ],
        axis=1,
    )
    ext = jnp.concatenate([pre_ext[tok + HALO - edge :], pre_ext[:tok]], axis=0)
    conv_in = convolve(ext, taps, ext_docs, tok)
    ssm = jax.nn.silu(conv_in).astype(bf16)
    head_slice = lambda v: lax.dynamic_slice_in_dim(v, pi * n_heads, n_heads, 0)
    my_bias, my_a, my_skip = head_slice(dt_bias), head_slice(a_log), head_slice(skip_gain)
    lanes = lambda v: jnp.pad(v, (0, 128 - n_heads))[None, :]
    dt_at = cw + 2 * kw
    dt_pre = jnp.pad(in_a[:, dt_at : dt_at + n_heads], ((0, 0), (0, 128 - n_heads))) + lanes(my_bias)
    neg_rate = lanes(-jnp.exp(my_a))
    skip_full = jnp.repeat(my_skip, MHDIM)[None, :]
    pair_ids = pi * hk + jnp.arange(hk)
    cos_k, sin_k = rope_tables(positions, pair_ids)
    k0, k1 = in_a[:, cw : cw + hk], in_a[:, cw + hk : cw + kw]
    key_own = jnp.concatenate([k0 * cos_k - k1 * sin_k, k1 * cos_k + k0 * sin_k], axis=1)
    val_own = in_a[:, cw + kw : cw + 2 * kw]
    kv_own = jnp.concatenate([key_own, val_own], axis=1).astype(bf16)
    kv_own = jnp.concatenate([kv_own[: tok // 2], kv_own[tok // 2 :]], axis=1)
    bc_all, kvz, g_ffn = gather_bc(ssm, xw // 128, n_p, kv_own, nz, grad_own)
    cos_q, sin_q = rope_tables(positions, jnp.arange(HDIM // 2))
    cos_q, sin_q = cos_q.reshape(tok, n_p, hk), sin_q.reshape(tok, n_p, hk)

    def rope_q(v, sign):
        v = v.reshape(tok, n_p, 2, hk)
        a, b = v[:, :, 0], v[:, :, 1]
        return jnp.stack(
            [a * cos_q - sign * b * sin_q, b * cos_q + sign * a * sin_q], axis=2
        ).reshape(tok, HDIM)

    queries = rope_q(in_b[:, :HDIM], 1.0).astype(bf16)

    base_arr = jnp.reshape(base, (1,)).astype(jnp.int32)
    y_local, span_starts, local_state, dev_decay, decay_full, c_mat = ssd_forward(
        base_arr, doc_starts, ssm, bc_all, dt_pre, neg_rate, skip_full
    )
    rate = jnp.broadcast_to(dev_decay[tok - 1 :], (8, 128))
    in_state, kv, rates = carry_step(local_state, rate, kvz, n_p)

    attn_f32, lse, keys, values = attend(base_arr, doc_starts, queries, kv)
    attn_low = attn_f32.astype(bf16)
    y_flat = y_local + product_nt(c_mat, in_state.astype(bf16)) * decay_full
    silu_z = jax.nn.silu(gate_z)
    gated = (y_flat * silu_z).astype(bf16)
    mixed = jnp.concatenate([gated, attn_low], axis=1)

    mid_own, normed_two = mid_step(mixed, w_c, hidden_own, gain_ffn)
    gu = product(normed_two, w_d)
    ffw = gu.shape[1] // 2
    gate_val, up_val = gu[:, :ffw], gu[:, ffw:]
    silu_gate = jax.nn.silu(gate_val)
    activated = (silu_gate * up_val).astype(bf16)
    grad_e = product_t(g_ffn, activated).astype(bf16)
    g_ffn, grad_e = lax.optimization_barrier((g_ffn, grad_e))
    d_act = product(g_ffn, w_e)
    d_gu = jnp.concatenate(
        [d_act * up_val * silu_slope(gate_val), d_act * silu_gate], axis=1
    ).astype(bf16)
    grad_d = product_t(normed_two, d_gu).astype(bf16)
    d_gu, grad_d = lax.optimization_barrier((d_gu, grad_d))

    def scattered(grad):
        return lax.psum_scatter(grad, "z", scatter_dimension=0, tiled=True)

    def by_owner(grad):
        return grad.reshape(n_p, rows, grad.shape[1])

    ge = scattered(grad_e)
    gd = scattered(grad_d)
    d_mid_own, grad_gain_ffn, g_mid = two_step(d_gu, w_d, mid_own, grad_own, gain_ffn)
    g_mid, ge = lax.optimization_barrier((g_mid, ge))

    d_mixed = product(g_mid, w_c)
    grad_c = product_t(g_mid, mixed).astype(bf16)
    gc = scattered(grad_c)
    d_gated = d_mixed[:, :xw]
    d_attn = d_mixed[:, xw:].astype(bf16)
    d_y_flat = d_gated * silu_z
    d_z = (d_gated * y_flat * silu_slope(gate_z)).astype(bf16)
    d_in_local = product_t((d_y_flat * decay_full).astype(bf16), c_mat)
    d_in_local, d_attn = lax.optimization_barrier((d_in_local, d_attn))
    rates = jnp.repeat(rates[:, 0, :n_heads], MHDIM, axis=1)[:, :, None]
    state_grad = carry_back(d_in_local, rates)
    d_query, d_kv = attend_back(
        base_arr, doc_starts, queries, d_attn, attn_f32, lse, keys, values, kv.shape
    )
    d_q_pre = rope_q(d_query, -1.0).astype(bf16)
    d_b = jnp.concatenate([d_q_pre, d_z], axis=1)
    d_b, state_grad = lax.optimization_barrier((d_b, state_grad))
    more = lambda v: jnp.pad(v, ((0, HALO), (0, 0)))
    grad_b = product_t(normed_one, more(d_b)).astype(bf16)
    gb = scattered(grad_b)
    d_kv_parts = [lax.dynamic_index_in_dim(d_kv, pi, 0, keepdims=False)]
    for d in range(1, n_p):
        part = lax.dynamic_index_in_dim(d_kv, jnp.bitwise_xor(pi, d), 0, keepdims=False)
        d_kv_parts.append(lax.ppermute(part, "p", [(i, i ^ d) for i in range(n_p)]))

    start_decay = jnp.concatenate([jnp.ones((1, 128), f32), dev_decay[SPAN - 1 :: SPAN][:-1]])
    d_y_flat, gd = lax.optimization_barrier((d_y_flat, gd))
    d_xs, d_bc, d_dt, sums, skip_sums = ssd_backward(
        base_arr, doc_starts, ssm, bc_all, dt_pre, d_y_flat, span_starts,
        start_decay[:, None, :], neg_rate, skip_full, in_state, state_grad,
    )
    d_bc, d_kv_parts = lax.optimization_barrier((d_bc, d_kv_parts))
    d_kv = sum(part.astype(f32) for part in d_kv_parts).astype(bf16)
    slope = silu_slope(conv_in)
    d_bc, d_kv_own, du_next, ge, gd = reduce_bc(
        d_bc, d_kv, d_xs[:8], slope[:8], (by_owner(ge), by_owner(gd))
    )
    d_kv_own = jnp.concatenate([d_kv_own[:, : 2 * kw], d_kv_own[:, 2 * kw :]], axis=0)
    dk0, dk1 = d_kv_own[:, :hk], d_kv_own[:, hk:kw]
    d_kv_low = jnp.concatenate(
        [dk0 * cos_k + dk1 * sin_k, dk1 * cos_k - dk0 * sin_k, d_kv_own[:, kw:]], axis=1
    ).astype(bf16)
    du = jnp.concatenate([d_xs, d_bc], axis=1) * slope
    du = jnp.concatenate([du, du_next[:edge]], axis=0)
    d_pre, grad_taps = convolve_back(du, ext, taps, ext_docs, tok)
    d_pre = d_pre.astype(bf16)
    d_last = jnp.concatenate(
        [d_kv_low, d_dt[:, :n_heads].astype(bf16), jnp.zeros((tok, tail_w), bf16)], axis=1
    )
    d_a = jnp.concatenate([d_pre, d_last], axis=1)
    grad_a = product_t(normed_one, more(d_a)).astype(bf16)
    ga = scattered(grad_a)
    once = jnp.where(ci == 0, d_pre[:, xw:], jnp.zeros((), bf16))
    d_a_once = jnp.concatenate([d_pre[:, :xw], once, d_last], axis=1)
    d_a_once, grad_a, gc, gb = lax.optimization_barrier((d_a_once, grad_a, gc, gb))
    grad_in, block_out, grad_gain_mix, gc, gb = one_step(
        d_a_once, w_a, d_b, w_b, hidden_own, d_mid_own, gain_mix, activated, w_e, mid_own,
        (by_owner(gc), by_owner(gb)),
    )

    flat = jnp.concatenate(
        [
            grad_gain_mix.reshape(-1, 128),
            grad_gain_ffn.reshape(-1, 128),
            grad_taps.reshape(-1, 128),
            sums[:2],
            jnp.pad(jnp.sum(skip_sums.reshape(n_heads, MHDIM), axis=1), (0, 128 - n_heads))[None],
        ]
    )
    flat = jnp.pad(flat, ((0, -flat.shape[0] % 8), (0, 0)))
    summed, ga = sums_step(flat, nz, n_p, (by_owner(ga),))
    g_rows = width // 128
    t_rows = grad_taps.size // 128
    si = zi * n_p + pi
    gains_sum = jnp.sum(summed[:, :, : 2 * g_rows], axis=(0, 1)).reshape(2, width)
    gains_sum = lax.dynamic_slice_in_dim(gains_sum, si * rows, rows, 1)
    mine = lax.dynamic_index_in_dim(summed, ci, 0, keepdims=False)
    s_taps = mine[:, 2 * g_rows : 2 * g_rows + t_rows].reshape(n_p, edge + 1, cw).transpose(1, 0, 2)
    s_heads = mine[:, 2 * g_rows + t_rows : 2 * g_rows + t_rows + 3, :n_heads]
    s_heads = s_heads.transpose(1, 0, 2).reshape(3, n_p * n_heads)
    s_x = s_taps[:, :, :xw].reshape(edge + 1, n_p * xw)
    s_bc = summed[0][:, 2 * g_rows : 2 * g_rows + t_rows].reshape(n_p, edge + 1, cw)
    s_bc = s_bc[:, :, xw:].reshape(n_p, edge + 1, 2, bw).transpose(1, 2, 0, 3)
    s_bc = s_bc.reshape(edge + 1, 2 * n_p * bw)

    g_x, g_bc, g_k, g_v, g_dt, g_q, g_z, g_mout, g_aout, g_gate, g_up, g_down = unpack(
        (ga, gb, gc, gd, ge), weights
    )
    return (
        block_out,
        grad_in,
        gains_sum[0],
        gains_sum[1],
        g_z,
        g_x,
        g_bc,
        g_dt,
        s_x,
        s_bc,
        s_heads[0],
        s_heads[1],
        s_heads[2],
        g_mout,
        g_q,
        g_k,
        g_v,
        g_aout,
        g_gate,
        g_up,
        g_down,
    )


def solution(mesh):
    seq, head = mesh.shape["seq"], mesh.shape["head"]
    plane = math.gcd(seq, 4)
    grid = Mesh(mesh.devices.reshape(seq // plane, plane, head), ("z", "p", "head"))
    s = ("z", "p")
    h = "head"
    placed = (
        P(s, None), P(s, None), P(), P(s), P(s), P(s, h), P(s, h), P(s, None), P(s, h),
        P(None, h), P(), P(h), P(h), P(h), P(h, s), P(s, h), P(s, h), P(s, h), P(h, s),
        P(s, h), P(s, h), P(h, s),
    )
    given = (
        P(s, None), P(s, None), P(s), P(s), P(s, h), P(s, h), P(s, None), P(s, h),
        P(None, h), P(), P(h), P(h), P(h), P(h, s), P(s, h), P(s, h), P(s, h), P(h, s),
        P(s, h), P(s, h), P(h, s),
    )
    return jax.shard_map(shards, mesh=grid, in_specs=placed, out_specs=given, check_vma=False)
```

```python
import functools
import math

import jax
import jax.numpy as jnp
from jax import lax
from jax.experimental import pallas as pl
from jax.experimental.pallas import tpu as pltpu
from jax.sharding import Mesh
from jax.sharding import PartitionSpec as P

MHDIM = 64
NSTATE = 256
HDIM = 128
SPAN = 128

eps_norm = 1e-05
rope_base = 100000000000.0
neg_large = -1e30
top_prec = lax.Precision.HIGHEST
bf16 = jnp.bfloat16
f32 = jnp.float32
MESH = pl.DeviceIdType.MESH
VMEM_LIMIT = 56 * 1024 * 1024


def doc_ids(positions, doc_starts):
    return jnp.sum((doc_starts[None, :] <= positions[:, None]).astype(jnp.int32), axis=1) - 1


def product(left, right):
    return jnp.dot(left, right, preferred_element_type=f32)


def product_t(left, right):
    return lax.dot_general(left, right, (((0,), (0,)), ((), ())), preferred_element_type=f32)


def product_nt(left, right):
    return lax.dot_general(left, right, (((1,), (1,)), ((), ())), preferred_element_type=f32)


def silu_slope(values):
    sigma_val = jax.nn.sigmoid(values)
    return sigma_val * (1.0 + values * (1.0 - sigma_val))


def convolve(extended, weights, ext_docs, tok_count):
    edge_rows = weights.shape[0] - 1
    here = ext_docs[edge_rows : edge_rows + tok_count]
    summed = jnp.zeros((tok_count, extended.shape[1]), f32)
    for tap_index in range(weights.shape[0]):
        begin_row = edge_rows - tap_index
        same_doc = (ext_docs[begin_row : begin_row + tok_count] == here)[:, None]
        rows = extended[begin_row : begin_row + tok_count].astype(f32)
        summed = summed + jnp.where(same_doc, rows, 0.0) * weights[tap_index][None, :]
    return summed


def convolve_back(d_conv, extended, weights, ext_docs, tok_count):
    edge_rows = weights.shape[0] - 1
    here = ext_docs[edge_rows : edge_rows + tok_count]
    d_rows = jnp.zeros((tok_count, d_conv.shape[1]), f32)
    tap_grads = []
    for tap_index in range(weights.shape[0]):
        begin_row = edge_rows - tap_index
        before = (ext_docs[begin_row : begin_row + tok_count] == here)[:, None]
        rows = extended[begin_row : begin_row + tok_count].astype(f32)
        tap_grads.append(jnp.sum(jnp.where(before, d_conv[:tok_count] * rows, 0.0), axis=0))
        last = edge_rows + tap_index
        after = (ext_docs[last : last + tok_count] == here)[:, None]
        ahead = d_conv[tap_index : tap_index + tok_count]
        d_rows = d_rows + jnp.where(after, ahead, 0.0) * weights[tap_index][None, :]
    return (d_rows, jnp.stack(tap_grads))


def tri_dot(a, b, dims=((1,), (0,))):
    return lax.dot_general(a, b, (dims, ((), ())), precision=top_prec, preferred_element_type=f32)


def dot_nn(a, b):
    return lax.dot_general(a, b, (((1,), (0,)), ((), ())), preferred_element_type=f32)


def dot_nt(a, b):
    return lax.dot_general(a, b, (((1,), (1,)), ((), ())), preferred_element_type=f32)


def dot_tn(a, b):
    return lax.dot_general(a, b, (((0,), (0,)), ((), ())), preferred_element_type=f32)


def iota2(shape, dim):
    return lax.broadcasted_iota(jnp.int32, shape, dim)


def docs_of(pos, starts_ref):
    count = jnp.where(starts_ref[0] <= pos, 1, 0)
    for i in range(1, starts_ref.shape[0]):
        count = count + jnp.where(starts_ref[i] <= pos, 1, 0)
    return count - 1


def softplus(v):
    return jnp.maximum(v, 0.0) + jnp.log(1.0 + jnp.exp(-jnp.abs(v)))


def head_maps(xw):
    lane_head = (iota2((128, xw), 1) // MHDIM == iota2((128, xw), 0)).astype(f32)
    row_head = (iota2((xw, 128), 0) // MHDIM == iota2((xw, 128), 1)).astype(f32)
    return lane_head, row_head


def span_setup(k, base_ref, starts_ref, dtp, nega):
    first = base_ref[0] + k * SPAN
    t_idx, s_idx = iota2((SPAN, SPAN), 0), iota2((SPAN, SPAN), 1)
    docs_t = docs_of(first + t_idx, starts_ref)
    docs_s = docs_of(first + s_idx, starts_ref)
    linked = (docs_t == docs_s) & (t_idx >= s_idx)
    dt = softplus(dtp)
    la = nega * dt
    tri = (t_idx >= s_idx).astype(f32)
    cum = tri_dot(tri, la)
    before = docs_of(first - 1, starts_ref)
    last_doc = docs_of(first + SPAN - 1, starts_ref)
    carried = jnp.where(docs_t == before, jnp.exp(cum), 0.0)
    cum_last = cum[SPAN - 1 : SPAN, :]
    tail = jnp.where(docs_t == last_doc, jnp.exp(cum_last - cum), 0.0)
    return docs_t, linked, dt, la, tri, cum, carried, tail


def split_bc(bc_ref):
    parts = [bc_ref[q] for q in range(bc_ref.shape[0])]
    half = parts[0].shape[1] // 2
    return (
        jnp.concatenate([part[:, :half] for part in parts], axis=1),
        jnp.concatenate([part[:, half:] for part in parts], axis=1),
    )


def ssd_forward_kernel(
    n_heads, base_ref, starts_ref, x_ref, bc_ref, dtp_ref, nega_ref, skip_ref,
    y_ref, span_ref, final_ref, decay_ref, wide_ref, c_out, state, running,
):
    k = pl.program_id(0)
    xw = n_heads * MHDIM

    @pl.when(k == 0)
    def _():
        state[...] = jnp.zeros_like(state)
        running[...] = jnp.zeros_like(running)

    docs_t, linked, dt, la, tri, cum, carried, tail = span_setup(
        k, base_ref, starts_ref, dtp_ref[...], nega_ref[...]
    )
    lane_head, row_head = head_maps(xw)
    prev_doc = docs_of(base_ref[0] - 1, starts_ref)
    since = jnp.where(docs_t == prev_doc, jnp.exp(running[0:1, :] + cum), 0.0)
    decay_ref[...] = since
    wide_ref[...] = tri_dot(since, lane_head)
    running[...] = running[...] + cum[SPAN - 1 : SPAN, :]
    start = state[...]
    span_ref[0] = start
    x, (b, c) = x_ref[...], split_bc(bc_ref)
    c_out[...] = c
    inner = dot_nt(c, b)
    cum_t, dt_t = cum.T, dt.T
    lane = iota2((SPAN, 128), 1)
    pieces = []
    for pair in range(n_heads // 2):
        xp = x[:, pair * 128 : pair * 128 + 128]
        got = []
        for h in (2 * pair, 2 * pair + 1):
            gap = jnp.where(linked, cum[:, h : h + 1] - cum_t[h : h + 1, :], neg_large)
            w = jnp.exp(gap) * inner * dt_t[h : h + 1, :]
            got.append(dot_nn(w.astype(bf16), xp))
        pieces.append(jnp.where(lane < MHDIM, got[0], got[1]))
    y = jnp.concatenate(pieces, axis=1)
    y = y + dot_nt(c, start.astype(bf16)) * tri_dot(carried, lane_head)
    xf = x.astype(f32)
    y_ref[...] = y + skip_ref[...] * xf
    xt = (xf * tri_dot(tail * dt, lane_head)).astype(bf16)
    keep = jnp.sum(row_head * carried[SPAN - 1 : SPAN, :], axis=1, keepdims=True)
    new = dot_tn(xt, b) + keep * start
    state[...] = new
    final_ref[...] = new


def ssd_forward(base, doc_starts, x, bc, dtp, nega, skip):
    tok, xw, n_p = x.shape[0], skip.shape[1], bc.shape[0]
    n_heads, nspan = xw // MHDIM, tok // SPAN
    row = lambda n: pl.BlockSpec((SPAN, n), lambda i: (i, 0))
    whole = lambda *s: pl.BlockSpec(s, lambda i: (0,) * len(s))
    smem = pl.BlockSpec(memory_space=pltpu.SMEM)
    return pl.pallas_call(
        functools.partial(ssd_forward_kernel, n_heads),
        grid=(nspan,),
        in_specs=[
            smem, smem, row(xw), pl.BlockSpec((n_p, SPAN, 128), lambda i: (0, i, 0)), row(128),
            whole(1, 128), whole(1, xw),
        ],
        out_specs=[
            row(xw),
            pl.BlockSpec((1, xw, NSTATE), lambda i: (i, 0, 0)),
            whole(xw, NSTATE),
            row(128),
            row(xw),
            row(NSTATE),
        ],
        out_shape=[
            jax.ShapeDtypeStruct((tok, xw), f32),
            jax.ShapeDtypeStruct((nspan, xw, NSTATE), f32),
            jax.ShapeDtypeStruct((xw, NSTATE), f32),
            jax.ShapeDtypeStruct((tok, 128), f32),
            jax.ShapeDtypeStruct((tok, xw), f32),
            jax.ShapeDtypeStruct((tok, NSTATE), bf16),
        ],
        scratch_shapes=[pltpu.VMEM((xw, NSTATE), f32), pltpu.VMEM((8, 128), f32)],
        compiler_params=pltpu.CompilerParams(vmem_limit_bytes=VMEM_LIMIT),
        cost_estimate=pl.CostEstimate(
            flops=2 * tok * xw * NSTATE * 3, bytes_accessed=40_000_000, transcendentals=0
        ),
        name="ssd_forward",
    )(base, doc_starts, x, bc, dtp, nega, skip)


def ssd_backward_kernel(
    n_heads, base_ref, starts_ref, x_ref, bc_ref, dtp_ref, dy_ref, span_ref, decay_ref,
    nega_ref, skip_ref, in_ref, grad_ref,
    dx_ref, dbc_ref, ddt_ref, sums_ref, gskip_ref, gstate,
):
    step = pl.program_id(0)
    k = pl.num_programs(0) - 1 - step
    xw = n_heads * MHDIM

    @pl.when(step == 0)
    def _():
        gstate[...] = grad_ref[...]
        sums_ref[...] = jnp.zeros_like(sums_ref)
        gskip_ref[...] = jnp.zeros_like(gskip_ref)

    nega = nega_ref[...]
    docs_t, linked, dt, la, tri, cum, carried, tail = span_setup(
        k, base_ref, starts_ref, dtp_ref[...], nega
    )
    lane_head, row_head = head_maps(xw)
    begin = jnp.sum(row_head * decay_ref[0], axis=1, keepdims=True)
    start = span_ref[0] + begin * in_ref[...]
    start_low = start.astype(bf16)
    g = gstate[...]
    g_low = g.astype(bf16)
    x, (b, c), dy = x_ref[...], split_bc(bc_ref), dy_ref[...]
    dy_low = dy.astype(bf16)
    xf = x.astype(f32)
    inner = dot_nt(c, b)
    cum_t, dt_t = cum.T, dt.T
    lane = iota2((SPAN, 128), 1)
    row8 = iota2((SPAN, 128), 0)
    d_inner = jnp.zeros((SPAN, SPAN), f32)
    r_cols = jnp.zeros((SPAN, 128), f32)
    k_rows = jnp.zeros((SPAN, 128), f32)
    u_pieces = []
    for pair in range(n_heads // 2):
        xp = x[:, pair * 128 : pair * 128 + 128]
        dyp = dy_low[:, pair * 128 : pair * 128 + 128]
        got = []
        for j, h in enumerate((2 * pair, 2 * pair + 1)):
            mine = (lane < MHDIM) if j == 0 else (lane >= MHDIM)
            gap = jnp.where(linked, cum[:, h : h + 1] - cum_t[h : h + 1, :], neg_large)
            e = jnp.exp(gap)
            m = e * inner
            dyx = dot_nt(dyp, jnp.where(mine, xp, jnp.zeros_like(xp)))
            ed = dyx * dt_t[h : h + 1, :]
            d_inner = d_inner + e * ed
            pairs = m * ed
            r_cols = jnp.where(lane == h, jnp.sum(pairs, axis=1, keepdims=True), r_cols)
            k_rows = jnp.where(row8 == h, jnp.sum(pairs, axis=0, keepdims=True), k_rows)
            got.append(dot_tn(m.astype(bf16), dyp))
        u_pieces.append(jnp.where(lane < MHDIM, got[0], got[1]))
    u = jnp.concatenate(u_pieces, axis=1)
    dye = dy * tri_dot(carried, lane_head)
    dye_low = dye.astype(bf16)
    di_low = d_inner.astype(bf16)
    r_state = tri_dot(dye * dot_nt(c, start_low), row_head)
    u_state = dot_nt(b, g_low) * tri_dot(tail, lane_head)
    u = u + u_state
    dt_full = tri_dot(dt, lane_head)
    k_state = dt * tri_dot(xf * u_state, row_head)
    d_dt = tri_dot(xf * u, row_head)
    tail_x = (xf * tri_dot(tail * dt, lane_head)).astype(bf16)
    dx_ref[...] = dt_full * u + skip_ref[...] * dy
    d_b = dot_nn(tail_x, g_low) + dot_tn(di_low, c)
    d_c = dot_nn(dye_low, start_low) + dot_nn(di_low, b)
    bw = 64
    for q in range(dbc_ref.shape[0]):
        cut = slice(q * bw, q * bw + bw)
        dbc_ref[q] = jnp.concatenate([d_b[:, cut], d_c[:, cut]], axis=1)
    gs = jnp.sum(g * start, axis=1, keepdims=True)
    gs_row = jnp.sum(row_head * gs, axis=0, keepdims=True)
    last = jnp.sum(k_state, axis=0, keepdims=True) + carried[SPAN - 1 : SPAN, :] * gs_row
    d_cum = r_cols - k_rows.T + r_state - k_state + jnp.where(row8 == SPAN - 1, last, 0.0)
    d_la = tri_dot(tri, d_cum, ((0,), (0,)))
    live = lane < n_heads
    dtp = dtp_ref[...]
    d_in = jnp.where(live, (d_dt + nega * d_la) * jax.nn.sigmoid(dtp), 0.0)
    ddt_ref[...] = d_in
    sum_a = jnp.sum(jnp.where(live, d_la * la, 0.0), axis=0, keepdims=True)
    sum_b = jnp.sum(d_in, axis=0, keepdims=True)
    pick = iota2((8, 128), 0)
    sums_ref[...] += jnp.where(pick == 0, sum_a, jnp.where(pick == 1, sum_b, 0.0))
    gskip_ref[...] += jnp.sum(dy * xf, axis=0, keepdims=True)
    keep = jnp.sum(row_head * carried[SPAN - 1 : SPAN, :], axis=1, keepdims=True)
    gstate[...] = keep * g + dot_tn(dye_low, c)


def ssd_backward(
    base, doc_starts, x, bc, dtp, dy, span_starts, start_decay, nega, skip, in_state, grad_state
):
    tok, xw, n_p = x.shape[0], skip.shape[1], bc.shape[0]
    wide = pl.BlockSpec((n_p, SPAN, 128), lambda i: (0, nspan - 1 - i, 0))
    n_heads, nspan = xw // MHDIM, tok // SPAN
    row = lambda n: pl.BlockSpec((SPAN, n), lambda i: (nspan - 1 - i, 0))
    whole = lambda *s: pl.BlockSpec(s, lambda i: (0,) * len(s))
    smem = pl.BlockSpec(memory_space=pltpu.SMEM)
    return pl.pallas_call(
        functools.partial(ssd_backward_kernel, n_heads),
        grid=(nspan,),
        in_specs=[
            smem, smem, row(xw), wide, row(128), row(xw),
            pl.BlockSpec((1, xw, NSTATE), lambda i: (nspan - 1 - i, 0, 0)),
            pl.BlockSpec((1, 1, 128), lambda i: (nspan - 1 - i, 0, 0)),
            whole(1, 128), whole(1, xw), whole(xw, NSTATE), whole(xw, NSTATE),
        ],
        out_specs=[row(xw), wide, row(128), whole(8, 128), whole(1, xw)],
        out_shape=[
            jax.ShapeDtypeStruct((tok, xw), f32),
            jax.ShapeDtypeStruct((n_p, tok, 128), f32),
            jax.ShapeDtypeStruct((tok, 128), f32),
            jax.ShapeDtypeStruct((8, 128), f32),
            jax.ShapeDtypeStruct((1, xw), f32),
        ],
        scratch_shapes=[pltpu.VMEM((xw, NSTATE), f32)],
        compiler_params=pltpu.CompilerParams(vmem_limit_bytes=VMEM_LIMIT),
        cost_estimate=pl.CostEstimate(
            flops=2 * tok * xw * NSTATE * 8, bytes_accessed=80_000_000, transcendentals=0
        ),
        name="ssd_backward",
    )(base, doc_starts, x, bc, dtp, dy, span_starts, start_decay, nega, skip, in_state, grad_state)


QB = 512
KB = 512


def sight(base_ref, starts_ref, q_first):
    q_pos = base_ref[0] + q_first + iota2((QB, 1), 0)
    low = jnp.zeros((QB, 1), jnp.int32)
    for i in range(starts_ref.shape[0]):
        low = jnp.where(starts_ref[i] <= q_pos, starts_ref[i], low)
    return jnp.broadcast_to(low, (QB, KB)), jnp.broadcast_to(q_pos, (QB, KB))


def seen(low, high, k_first):
    k_pos = k_first + iota2((QB, KB), 1)
    return (k_pos >= low) & (k_pos <= high)


def attend_kernel(scale, base_ref, starts_ref, q_ref, kv_ref, o_ref, lse_ref, k_ref, v_ref):
    i = pl.program_id(0)

    @pl.when(i == 0)
    def _():
        n_p, nz, rows, _ = kv_ref.shape
        kw = HDIM // n_p

        @pl.loop(0, nz)
        def _(z):
            parts = [kv_ref[q, z] for q in range(n_p)]
            for t in range(2):
                at = pl.ds(pl.multiple_of((2 * z + t) * rows, rows), rows)
                lo = 2 * kw * t
                k_ref[at, :] = jnp.concatenate([v[:, lo : lo + kw] for v in parts], axis=1)
                v_ref[at, :] = jnp.concatenate([v[:, lo + kw : lo + 2 * kw] for v in parts], axis=1)

    q = q_ref[...]
    low, high = sight(base_ref, starts_ref, i * QB)
    blocks = (base_ref[0] + (i + 1) * QB + KB - 1) // KB

    def turn(j, carry):
        m, l, acc = carry
        at = pl.ds(pl.multiple_of(j * KB, KB), KB)
        s = dot_nt(q, k_ref[at, :]) * scale
        s = jnp.where(seen(low, high, j * KB), s, neg_large)
        m_new = jnp.maximum(m, jnp.max(s, axis=1, keepdims=True))
        w = jnp.exp(s - m_new)
        r = jnp.exp(m - m_new)
        l = l * r + jnp.sum(w, axis=1, keepdims=True)
        return m_new, l, acc * r + dot_nn(w.astype(bf16), v_ref[at, :])

    m, l, acc = lax.fori_loop(
        0,
        blocks,
        turn,
        (jnp.full((QB, 1), 0.1 * neg_large, f32), jnp.zeros((QB, 1), f32), jnp.zeros((QB, HDIM), f32)),
    )
    o_ref[...] = acc / l
    lse_ref[...] = jnp.broadcast_to(m + jnp.log(l), (QB, 128))


def attend(base, doc_starts, q, kv):
    tok = q.shape[0]
    keys = kv.shape[1] * kv.shape[2] * 2
    row = pl.BlockSpec((QB, HDIM), lambda i: (i, 0))
    whole = lambda s: pl.BlockSpec(s, lambda i: (0,) * len(s))
    smem = pl.BlockSpec(memory_space=pltpu.SMEM)
    return pl.pallas_call(
        functools.partial(attend_kernel, HDIM ** (-0.5)),
        grid=(tok // QB,),
        in_specs=[smem, smem, row, whole(kv.shape)],
        out_specs=[row, row, whole((keys, HDIM)), whole((keys, HDIM))],
        out_shape=[jax.ShapeDtypeStruct((tok, HDIM), f32)] * 2
        + [jax.ShapeDtypeStruct((keys, HDIM), bf16)] * 2,
        compiler_params=pltpu.CompilerParams(vmem_limit_bytes=VMEM_LIMIT),
        cost_estimate=pl.CostEstimate(
            flops=4 * tok * keys * HDIM, bytes_accessed=30_000_000, transcendentals=0
        ),
        name="attend",
    )(base, doc_starts, q, kv)


def attend_back_kernel(
    scale, base_ref, starts_ref, q_ref, do_ref, o_ref, lse_ref, k_ref, v_ref,
    dq_ref, dkv_ref, dk_ref, dv_ref,
):
    i = pl.program_id(0)

    @pl.when(i == 0)
    def _():
        dk_ref[...] = jnp.zeros_like(dk_ref)
        dv_ref[...] = jnp.zeros_like(dv_ref)

    q, do = q_ref[...], do_ref[...]
    delta = jnp.sum(do.astype(f32) * o_ref[...], axis=1, keepdims=True)
    lse = lse_ref[:, 0:1]
    low, high = sight(base_ref, starts_ref, i * QB)
    blocks = (base_ref[0] + (i + 1) * QB + KB - 1) // KB

    def turn(j, dq):
        at = pl.ds(pl.multiple_of(j * KB, KB), KB)
        k, v = k_ref[at, :], v_ref[at, :]
        visible = seen(low, high, j * KB)
        s = dot_nt(q, k) * scale
        p = jnp.exp(jnp.where(visible, s - lse, neg_large))
        ds = (p * (dot_nt(do, v) - delta)).astype(bf16)
        dv_ref[at, :] += dot_tn(p.astype(bf16), do)
        dk_ref[at, :] += dot_tn(ds, q) * scale
        return dq + dot_nn(ds, k)

    dq_ref[...] = lax.fori_loop(0, blocks, turn, jnp.zeros((QB, HDIM), f32)) * scale

    @pl.when(i == pl.num_programs(0) - 1)
    def _():
        n_p, nz, rows, _ = dkv_ref.shape
        kw = HDIM // n_p

        @pl.loop(0, nz)
        def _(z):
            got = []
            for t in range(2):
                at = pl.ds(pl.multiple_of((2 * z + t) * rows, rows), rows)
                got += [dk_ref[at, :].astype(bf16), dv_ref[at, :].astype(bf16)]
            for q in range(n_p):
                cut = slice(q * kw, q * kw + kw)
                dkv_ref[q, z] = jnp.concatenate([v[:, cut] for v in got], axis=1)


def attend_back(base, doc_starts, q, do, o, lse, k, v, packed):
    tok = q.shape[0]
    row = pl.BlockSpec((QB, HDIM), lambda i: (i, 0))
    whole = lambda s: pl.BlockSpec(s, lambda i: (0,) * len(s))
    smem = pl.BlockSpec(memory_space=pltpu.SMEM)
    return pl.pallas_call(
        functools.partial(attend_back_kernel, HDIM ** (-0.5)),
        grid=(tok // QB,),
        in_specs=[smem, smem, row, row, row, row, whole(k.shape), whole(k.shape)],
        out_specs=[row, whole(packed)],
        out_shape=[
            jax.ShapeDtypeStruct((tok, HDIM), f32),
            jax.ShapeDtypeStruct(packed, bf16),
        ],
        scratch_shapes=[pltpu.VMEM(k.shape, f32), pltpu.VMEM(k.shape, f32)],
        compiler_params=pltpu.CompilerParams(vmem_limit_bytes=VMEM_LIMIT),
        cost_estimate=pl.CostEstimate(
            flops=10 * tok * k.shape[0] * HDIM, bytes_accessed=40_000_000, transcendentals=0
        ),
        name="attend_back",
    )(base, doc_starts, q, do, o, lse, k, v)


def one_at(shape, source, where=True):
    lane = iota2(shape, 1)
    return ((iota2(shape, 0) == source(lane)) & where).astype(bf16)


def eye(n):
    return one_at((n, n), lambda lane: lane)


def q_order(kw):
    hk = kw // 2
    return one_at(
        (HDIM, HDIM), lambda l: ((l % kw) // hk) * (HDIM // 2) + (l // kw) * hk + l % hk
    )


def bc_order(p, bw, n_p):
    return one_at((2 * n_p * bw, 2 * bw), lambda l: (l // bw) * (n_p * bw) + p * bw + l % bw)


def last_order(p, kw, n_heads, dt_rows):
    hk = kw // 2
    lane = iota2((HDIM, 128), 1)
    lane_dt = iota2((dt_rows, 128), 1)
    key = one_at((HDIM, 128), lambda l: (l // hk) * (HDIM // 2) + p * hk + l % hk, lane < kw)
    value = one_at((HDIM, 128), lambda l: p * kw + l - kw, (lane >= kw) & (lane < 2 * kw))
    step = one_at(
        (dt_rows, 128),
        lambda l: p * n_heads + l - 2 * kw,
        (lane_dt >= 2 * kw) & (lane_dt < 2 * kw + n_heads),
    )
    return key, value, step


def pack_kernel(
    x_ref, bc_ref, k_ref, v_ref, dt_ref, q_ref, z_ref, mout_ref, aout_ref, gate_ref, up_ref,
    down_ref, a_ref, b_ref, c_ref, d_ref, e_ref,
):
    n_p = a_ref.shape[0]
    xw, bw, kw = x_ref.shape[1] // n_p, bc_ref.shape[1] // (2 * n_p), HDIM // n_p
    n_heads, ff, aw = dt_ref.shape[1] // n_p, gate_ref.shape[1] // n_p, q_ref.shape[1] // n_p
    bc, key, value = bc_ref[...].astype(bf16), k_ref[...].astype(bf16), v_ref[...].astype(bf16)
    step = dt_ref[...].astype(bf16)
    order = q_order(kw)
    for p in range(n_p):
        cut = lambda ref, n: ref[:, p * n : p * n + n].astype(bf16)
        flip = lambda ref, n: dot_tn(ref[p * n : p * n + n, :].astype(bf16), eye(n)).astype(bf16)
        a_ref[p, :, :xw] = cut(x_ref, xw)
        a_ref[p, :, xw : xw + 2 * bw] = dot_nn(bc, bc_order(p, bw, n_p)).astype(bf16)
        s_key, s_value, s_step = last_order(p, kw, n_heads, dt_ref.shape[1])
        a_ref[p, :, xw + 2 * bw :] = (
            dot_nn(key, s_key) + dot_nn(value, s_value) + dot_nn(step, s_step)
        ).astype(bf16)
        b_ref[p, :, :HDIM] = dot_nn(cut(q_ref, aw), order).astype(bf16)
        b_ref[p, :, HDIM:] = cut(z_ref, xw)
        c_ref[p, :, :xw] = flip(mout_ref, xw)
        c_ref[p, :, xw:] = flip(aout_ref, aw)
        d_ref[p, :, :ff] = cut(gate_ref, ff)
        d_ref[p, :, ff:] = cut(up_ref, ff)
        e_ref[p] = flip(down_ref, ff)


def pack(n_p, *weights):
    x, bc, k, v, dt, q, z, mout, aout, gate, up, down = weights
    rows = x.shape[0]
    ff, xw = gate.shape[1] // n_p, x.shape[1] // n_p
    widths = (xw + bc.shape[1] // n_p + 128, HDIM + xw, xw + HDIM, 2 * ff, ff)
    vm = pl.BlockSpec(memory_space=pltpu.VMEM)
    return pl.pallas_call(
        pack_kernel,
        in_specs=[vm] * 12,
        out_specs=[vm] * 5,
        out_shape=[jax.ShapeDtypeStruct((n_p, rows, w), bf16) for w in widths],
        compiler_params=pltpu.CompilerParams(vmem_limit_bytes=VMEM_LIMIT),
        cost_estimate=pl.CostEstimate(flops=0, bytes_accessed=10_000_000, transcendentals=0),
        name="pack",
    )(*weights)


def unpack_kernel(
    a_ref, b_ref, c_ref, d_ref, e_ref, row_ref, grow_ref,
    x_ref, bc_ref, k_ref, v_ref, dt_ref, q_ref, z_ref, mout_ref, aout_ref, gate_ref, up_ref,
    down_ref, row_out, grow_out,
):
    row_out[...] = row_ref[...]
    grow_out[...] = grow_ref[...]
    n_p, rows = a_ref.shape[0], a_ref.shape[1]
    xw, bw, kw = x_ref.shape[1] // n_p, bc_ref.shape[1] // (2 * n_p), HDIM // n_p
    n_heads, ff, aw = dt_ref.shape[1] // n_p, gate_ref.shape[1] // n_p, q_ref.shape[1] // n_p
    order, turn = q_order(kw), eye(rows)
    bc, key = jnp.zeros(bc_ref.shape, f32), jnp.zeros(k_ref.shape, f32)
    value, step = jnp.zeros(v_ref.shape, f32), jnp.zeros(dt_ref.shape, f32)
    for p in range(n_p):
        cut = lambda n: slice(p * n, p * n + n)
        x_ref[:, cut(xw)] = a_ref[p, :, :xw].astype(f32)
        bc = bc + dot_nt(a_ref[p, :, xw : xw + 2 * bw], bc_order(p, bw, n_p))
        last = a_ref[p, :, xw + 2 * bw :]
        s_key, s_value, s_step = last_order(p, kw, n_heads, dt_ref.shape[1])
        key, value = key + dot_nt(last, s_key), value + dot_nt(last, s_value)
        step = step + dot_nt(last, s_step)
        q_ref[:, cut(aw)] = dot_nt(b_ref[p, :, :HDIM], order)
        z_ref[:, cut(xw)] = b_ref[p, :, HDIM:].astype(f32)
        mout_ref[cut(xw), :] = dot_tn(c_ref[p, :, :xw], turn)
        aout_ref[cut(aw), :] = dot_tn(c_ref[p, :, xw:], turn)
        gate_ref[:, cut(ff)] = d_ref[p, :, :ff].astype(f32)
        up_ref[:, cut(ff)] = d_ref[p, :, ff:].astype(f32)
        down_ref[cut(ff), :] = dot_tn(e_ref[p], turn)
    bc_ref[...] = bc
    k_ref[...], v_ref[...], dt_ref[...] = key, value, step


def unpack(pieces, like):
    vm = pl.BlockSpec(memory_space=pltpu.VMEM)
    return pl.pallas_call(
        unpack_kernel,
        in_specs=[vm] * 7,
        out_specs=[vm] * 14,
        out_shape=[jax.ShapeDtypeStruct(w.shape, f32) for w in like],
        compiler_params=pltpu.CompilerParams(vmem_limit_bytes=VMEM_LIMIT),
        cost_estimate=pl.CostEstimate(flops=0, bytes_accessed=10_000_000, transcendentals=0),
        name="unpack",
    )(*pieces)


def at_rows(first, count):
    return pl.ds(pl.multiple_of(first, count), count)


def place():
    return lax.axis_index("z"), lax.axis_index("p"), lax.axis_index("head")


def hop(p, d):
    x, y = lax.rem(p, 2), p // 2
    return lax.rem(y + d // 2, 2) * 2 + lax.rem(x + d % 2, 2)


def chip(z, p, c):
    return (z, p, c)


def meet(others):
    barrier = pltpu.get_barrier_semaphore()
    for other in others:
        pl.semaphore_signal(barrier, inc=1, device_id=other, device_id_type=MESH)
    pl.semaphore_wait(barrier, len(others))


def send(src, dst, send_sem, recv_sem, to):
    copy = pltpu.make_async_remote_copy(
        src_ref=src, dst_ref=dst, send_sem=send_sem, recv_sem=recv_sem,
        device_id=to, device_id_type=MESH,
    )
    copy.start()
    return copy


HOPS = (3, 1, 2)


def z_chain(ref, up_sems, down_sems, since=0):
    z, p, c = place()
    nz = ref.shape[0]

    def block_up(k):
        at = ref.at[z - k]
        return pltpu.make_async_remote_copy(
            src_ref=at, dst_ref=at, send_sem=up_sems.at[0, k], recv_sem=up_sems.at[1, k],
            device_id=chip(z + 1, p, c), device_id_type=MESH,
        )

    def block_down(k):
        at = ref.at[z + k]
        return pltpu.make_async_remote_copy(
            src_ref=at, dst_ref=at, send_sem=down_sems.at[0, k], recv_sem=down_sems.at[1, k],
            device_id=chip(z - 1, p, c), device_id_type=MESH,
        )

    def got_up(k):
        at = ref.at[z - k]
        pltpu.make_async_remote_copy(
            src_ref=at, dst_ref=at, send_sem=up_sems.at[0, k - 1], recv_sem=up_sems.at[1, k - 1],
            device_id=chip(z - 1, p, c), device_id_type=MESH,
        ).wait_recv()

    def got_down(k):
        at = ref.at[z + k]
        pltpu.make_async_remote_copy(
            src_ref=at, dst_ref=at, send_sem=down_sems.at[0, k - 1],
            recv_sem=down_sems.at[1, k - 1],
            device_id=chip(z + 1, p, c), device_id_type=MESH,
        ).wait_recv()

    def stage(k):
        if k > since:

            @pl.when(z - k >= 0)
            def _():
                got_up(k)

        @pl.when((z - k >= 0) & (z + 1 < nz))
        def _():
            block_up(k).start()

        if k > since:

            @pl.when(z + k < nz)
            def _():
                got_down(k)

        @pl.when((z + k < nz) & (z > 0))
        def _():
            block_down(k).start()

    def done():
        for k in range(since, nz):

            @pl.when((z - k >= 0) & (z + 1 < nz))
            def _():
                block_up(k).wait_send()

            @pl.when((z + k < nz) & (z > 0))
            def _():
                block_down(k).wait_send()

    return stage, done


def z_hop(ref, k, sems):
    z, p, c = place()
    nz = ref.shape[0]

    def move(slot, i, to):
        return pltpu.make_async_remote_copy(
            src_ref=ref.at[slot], dst_ref=ref.at[slot], send_sem=sems.at[0, i],
            recv_sem=sems.at[1, i], device_id=chip(to, p, c), device_id_type=MESH,
        )

    goes_up, goes_down = (z - k >= 0) & (z + 1 < nz), (z + k < nz) & (z > 0)

    @pl.when(goes_up)
    def _():
        move(z - k, 0, z + 1).start()

    @pl.when(goes_down)
    def _():
        move(z + k, 1, z - 1).start()

    def end():
        @pl.when(z - k - 1 >= 0)
        def _():
            move(z - k - 1, 0, z - 1).wait_recv()

        @pl.when(z + k + 1 < nz)
        def _():
            move(z + k + 1, 1, z + 1).wait_recv()

        @pl.when(goes_up)
        def _():
            move(z - k, 0, z + 1).wait_send()

        @pl.when(goes_down)
        def _():
            move(z + k, 1, z - 1).wait_send()

    return end


def share(block, part, far_sems, near_sems, own_sems=None):
    z, p, c = place()
    other = chip(z, p, 1 - c)
    x, y, far = hop(p, 1), hop(p, 2), hop(p, 3)

    def far_send(ref, i, q):
        return send(ref, ref, far_sems.at[0, i], far_sems.at[1, i], chip(z, q, c))

    def near_send(q, i):
        return send(block(q), block(q), near_sems.at[0, i], near_sems.at[1, i], other)

    out = [far_send(block(p), 0, x), far_send(block(p), 1, y)]
    near = []
    if own_sems is not None:
        near.append(send(block(p), block(p), own_sems.at[0], own_sems.at[1], other))

    def middle():
        out[0].wait_recv()
        out.append(far_send(part(x, 0), 2, y))
        out[1].wait_recv()
        out.append(far_send(part(y, 1), 3, x))
        if near_sems is not None:
            near.append(near_send(x, 0))
            near.append(near_send(y, 1))

    def end():
        out[2].wait_recv()
        out[3].wait_recv()
        if near_sems is not None:
            near.append(near_send(far, 2))
        for copy in out:
            copy.wait_send()
        for copy in near:
            copy.wait()

    return middle, end


def share_rows(full_ref, half, own_sems, far_sems, near_sems):
    z, p, c = place()
    rows = lambda q: (q * 2 + c) * half
    return share(
        lambda q: full_ref.at[at_rows(rows(q), half), :],
        lambda q, i: full_ref.at[at_rows(rows(q) + i * (half // 2), half // 2), :],
        far_sems, near_sems, own_sems,
    )


def reduce_blocks(pairs, part, keep, sib_out, sib_in, out, relay, came, near_sems, far_sems):
    z, p, c = place()
    other = chip(z, p, 1 - c)
    half, width = keep.shape[1], keep.shape[2]
    tile, quarter = part.shape[1], half // 2
    x, y = chip(z, hop(p, 1), c), chip(z, hop(p, 2), c)
    first, second = at_rows(0, quarter), at_rows(quarter, quarter)
    near, far = [], []

    def far_send(src, dst, i, to):
        far.append(send(src, dst, far_sems.at[0, i], far_sems.at[1, i], to))

    def total_of(i, rows, extra=None):
        @pl.loop(0, quarter // 16)
        def _(r):
            at = at_rows(rows + r * 16, 16)
            total = keep[i, at, :] + sib_in[i, at, :].astype(f32)
            if extra is not None:
                total = total + relay[extra, at_rows(r * 16, 16), :].astype(f32)
            out[i, at, :] = total.astype(bf16)

    def pass_on(i):
        near[i].wait_recv()
        if i == 0:
            total_of(0, 0)
            far_send(out.at[0, first, :], relay.at[0], 0, x)
            total_of(0, quarter)
            far_send(out.at[0, second, :], relay.at[1], 1, y)
        if i == 1:
            total_of(1, 0)
            far_send(out.at[1, first, :], came.at[0, first, :], 2, x)
        if i == 2:
            total_of(2, quarter)
            far_send(out.at[2, second, :], came.at[1, second, :], 3, y)

    for i, d in enumerate((3, 1, 2, 0)):
        rows = at_rows(hop(p, d) * (2 * half), 2 * half)

        @pl.loop(0, width // tile)
        def _(n):
            cols = at_rows(n * tile, tile)
            total = dot_nt(pairs[0][0][rows, :], pairs[0][1][cols, :])
            for left, right in pairs[1:]:
                total = total + dot_nt(left[rows, :], right[cols, :])
            part[...] = total
            keep[i, :, cols] = part[at_rows(c * half, half), :]
            sib_out[i, :, cols] = part[at_rows((1 - c) * half, half), :].astype(bf16)

        near.append(
            send(sib_out.at[i], sib_in.at[i], near_sems.at[0, i], near_sems.at[1, i], other)
        )
        if i:
            pass_on(i - 1)

    def middle():
        far[1].wait_recv()
        total_of(1, quarter, 1)
        far_send(out.at[1, second, :], came.at[0, second, :], 4, x)
        far[0].wait_recv()
        total_of(2, 0, 0)
        far_send(out.at[2, first, :], came.at[1, first, :], 5, y)

    def finish():
        near[3].wait_recv()
        for copy in far[2:]:
            copy.wait_recv()

    def total_rows(at):
        total = keep[3, at, :] + sib_in[3, at, :].astype(f32)
        return total + came[0, at, :].astype(f32) + came[1, at, :].astype(f32)

    def done():
        for copy in near + far:
            copy.wait_send()

    return total_rows, middle, finish, done


def greet():
    z, p, c = place()
    meet([chip(z, p, 1 - c)] + [chip(z, hop(p, d), c) for d in HOPS])


def rms(rows):
    return lax.rsqrt(jnp.mean(rows * rows, axis=1, keepdims=True) + eps_norm)


def mid_kernel(
    left, right, resid, gain, e_given, mid_ref, full_ref, e_ref,
    part, keep, sib_out, sib_in, out, relay, came, n_sems, f_sems, own_sems, far_sems, near_sems,
    up_sems, down_sems,
):
    z, p, c = place()
    nz = e_ref.shape[0]
    meet(
        [chip(z, p, 1 - c)]
        + [chip(z, hop(p, d), c) for d in HOPS]
        + [chip(lax.rem(z + d, nz), p, c) for d in (1, nz - 1)]
    )
    stage, chain_done = z_chain(e_ref, up_sems, down_sems, 2)
    stage(2)
    half = keep.shape[1]
    total_rows, middle, finish, done = reduce_blocks(
        [(left, right)], part, keep, sib_out, sib_in, out, relay, came, n_sems, f_sems
    )
    middle()
    finish()
    g = gain[...]

    @pl.loop(0, half // 16)
    def _(r):
        at = at_rows(r * 16, 16)
        mid = resid[at, :] + total_rows(at)
        mid_ref[at, :] = mid
        full_ref[at_rows((p * 2 + c) * half + r * 16, 16), :] = (mid * rms(mid) * g).astype(bf16)

    share_middle, share_end = share_rows(full_ref, half, own_sems, far_sems, near_sems)
    share_middle()
    for k in range(3, nz):
        stage(k)
    done()
    share_end()
    chain_done()


def two_kernel(
    left, right, mid_own, grad_own, gain, dmid_ref, ggain_ref, full_ref,
    part, keep, sib_out, sib_in, out, relay, came, n_sems, f_sems, own_sems, far_sems, near_sems,
):
    greet()
    z, p, c = place()
    half = keep.shape[1]
    total_rows, middle, finish, done = reduce_blocks(
        [(left, right)], part, keep, sib_out, sib_in, out, relay, came, n_sems, f_sems
    )
    middle()
    finish()
    g = gain[...]
    ggain_ref[...] = jnp.zeros_like(ggain_ref)

    @pl.loop(0, half // 16)
    def _(r):
        at = at_rows(r * 16, 16)
        d_two, mid = total_rows(at), mid_own[at, :]
        scale = rms(mid)
        w = d_two * g
        d_mid = grad_own[at, :] + scale * w - mid * (scale * scale * scale) * jnp.mean(
            w * mid, axis=1, keepdims=True
        )
        ggain_ref[...] += jnp.sum(d_two * mid * scale, axis=0, keepdims=True)
        dmid_ref[at, :] = d_mid
        full_ref[at_rows((p * 2 + c) * half + r * 16, 16), :] = d_mid.astype(bf16)

    share_middle, share_end = share_rows(full_ref, half, own_sems, far_sems, near_sems)
    share_middle()
    done()
    share_end()


def one_kernel(
    n, left_a, right_a, left_b, right_b, hidden_own, dmid_own, gain, act, w_act, mid_own, *refs
):
    ins, (grad_ref, block_ref, ggain_ref), outs = refs[:n], refs[n : n + 3], refs[n + 3 : 2 * n + 3]
    first, second = refs[2 * n + 3 : 2 * n + 12], refs[2 * n + 12 : 2 * n + 21]
    own_sems, w_sems, loc_sems = refs[2 * n + 21 :]
    greet()
    z, p, c = place()
    half = hidden_own.shape[0]
    total_rows, middle, finish, done = reduce_blocks(
        [(left_a, right_a), (left_b, right_b)], *first
    )
    middle()
    total_out, middle_out, finish_out, done_out = reduce_blocks([(act, w_act)], *second)
    moved = swap_begin(ins, outs, w_sems, loc_sems)
    g = gain[...]
    ggain_ref[...] = jnp.zeros_like(ggain_ref)
    middle_out()
    finish()

    @pl.loop(0, half // 16)
    def _(r):
        at = at_rows(r * 16, 16)
        d_one, hid = total_rows(at), hidden_own[at, :]
        scale = rms(hid)
        w = d_one * g
        d_in = dmid_own[at, :] + scale * w - hid * (scale * scale * scale) * jnp.mean(
            w * hid, axis=1, keepdims=True
        )
        ggain_ref[...] += jnp.sum(d_one * hid * scale, axis=0, keepdims=True)
        grad_ref[at_rows(c * half + r * 16, 16), :] = d_in

    mine = at_rows(c * half, half)
    other = chip(z, p, 1 - c)
    copies = [
        send(grad_ref.at[mine, :], grad_ref.at[mine, :], own_sems.at[0, 0], own_sems.at[1, 0], other)
    ]
    finish_out()

    @pl.loop(0, half // 16)
    def _(r):
        at = at_rows(r * 16, 16)
        block_ref[at_rows(c * half + r * 16, 16), :] = mid_own[at, :] + total_out(at)

    copies.append(
        send(block_ref.at[mine, :], block_ref.at[mine, :], own_sems.at[0, 1], own_sems.at[1, 1], other)
    )
    done()
    done_out()
    for copy in copies + moved:
        copy.wait()


VM = pl.BlockSpec(memory_space=pltpu.VMEM)
ANYWHERE = pl.BlockSpec(memory_space=pl.ANY)


def swap_begin(ins, outs, sems, loc_sems):
    z, p, c = place()
    copies = []
    for j, (src, dst) in enumerate(zip(ins, outs)):
        for i, d in enumerate(HOPS):
            q = hop(p, d)
            copies.append(
                send(src.at[q], dst.at[p], sems.at[0, j, i], sems.at[1, j, i], chip(z, q, c))
            )
        local = pltpu.make_async_copy(src.at[p], dst.at[p], loc_sems.at[j])
        local.start()
        copies.append(local)
    return copies


def swap_sems(n):
    return [pltpu.SemaphoreType.DMA((2, n, 3)), pltpu.SemaphoreType.DMA((n,))]


def reduce_scratch(half, width):
    return [
        pltpu.VMEM((2 * half, 512), f32),
        pltpu.VMEM((4, half, width), f32),
        pltpu.VMEM((4, half, width), bf16),
        pltpu.VMEM((4, half, width), bf16),
        pltpu.VMEM((3, half, width), bf16),
        pltpu.VMEM((2, half // 2, width), bf16),
        pltpu.VMEM((2, half, width), bf16),
        pltpu.SemaphoreType.DMA((2, 4)),
        pltpu.SemaphoreType.DMA((2, 6)),
    ]


SHARE_SEMS = [
    pltpu.SemaphoreType.DMA((2,)),
    pltpu.SemaphoreType.DMA((2, 4)),
    pltpu.SemaphoreType.DMA((2, 3)),
]


def plane_call(kernel, name, number, args, shapes, scratch, nbytes=150_000_000, moved=()):
    n = len(moved)
    if n:
        kernel = functools.partial(kernel, n)
        scratch = scratch + swap_sems(n)
    return pl.pallas_call(
        kernel,
        in_specs=[VM] * (len(args) + n),
        out_specs=[VM] * len(shapes) + [ANYWHERE] * n,
        out_shape=[jax.ShapeDtypeStruct(s, t) for s, t in shapes]
        + [jax.ShapeDtypeStruct(m.shape, m.dtype) for m in moved],
        scratch_shapes=scratch,
        compiler_params=pltpu.CompilerParams(
            collective_id=number, has_side_effects=True, vmem_limit_bytes=VMEM_LIMIT
        ),
        cost_estimate=pl.CostEstimate(flops=0, bytes_accessed=nbytes, transcendentals=0),
        name=name,
    )(*args, *moved)


def mid_step(mixed, w, resid_own, gain, piece):
    tok, width = mixed.shape[0], w.shape[0]
    half, nz = resid_own.shape[0], piece.shape[0]
    return pl.pallas_call(
        mid_kernel,
        in_specs=[VM] * 4 + [ANYWHERE],
        out_specs=[VM] * 2 + [ANYWHERE],
        out_shape=[
            jax.ShapeDtypeStruct((half, width), f32),
            jax.ShapeDtypeStruct((tok, width), bf16),
            jax.ShapeDtypeStruct(piece.shape, bf16),
        ],
        scratch_shapes=reduce_scratch(half, width)
        + SHARE_SEMS
        + [pltpu.SemaphoreType.DMA((2, nz))] * 2,
        input_output_aliases={4: 2},
        compiler_params=pltpu.CompilerParams(
            collective_id=1, has_side_effects=True, vmem_limit_bytes=VMEM_LIMIT
        ),
        cost_estimate=pl.CostEstimate(flops=0, bytes_accessed=150_000_000, transcendentals=0),
        name="mid_step",
    )(mixed, w, resid_own, gain, piece)


def two_step(d_gu, w, mid_own, grad_own, gain):
    tok, width = d_gu.shape[0], w.shape[0]
    half = mid_own.shape[0]
    return plane_call(
        two_kernel, "two_step", 2, (d_gu, w, mid_own, grad_own, gain),
        [((half, width), f32), ((1, width), f32), ((tok, width), bf16)],
        reduce_scratch(half, width) + SHARE_SEMS,
    )


def one_step(d_a, w_a, d_b, w_b, hidden_own, dmid_own, gain, act, w_act, mid_own, moved):
    width = w_a.shape[0]
    half = hidden_own.shape[0]
    return plane_call(
        one_kernel, "one_step", 3,
        (d_a, w_a, d_b, w_b, hidden_own, dmid_own, gain, act, w_act, mid_own),
        [((2 * half, width), f32), ((2 * half, width), f32), ((1, width), f32)],
        reduce_scratch(half, width)
        + reduce_scratch(half, width)
        + [pltpu.SemaphoreType.DMA((2, 2))],
        moved=moved,
    )


HALO = 16


def open_kernel(n, *refs):
    hid, gains_ref, a_ref = refs[:3]
    w_refs = refs[3 : 3 + n]
    gain_out, full_ref, a_out = refs[3 + n : 6 + n]
    w_outs = refs[6 + n : 6 + 2 * n]
    (
        g_vec, gz_sems, gp_sems, a_sems, up_sems, down_sems, own_sems, far_sems, near_sems,
        w_sems, loc_sems, halo_sems,
    ) = refs[6 + 2 * n :]
    z, p, c = place()
    nz, half, rows = a_out.shape[0], hid.shape[0], a_ref.shape[1]
    tok = full_ref.shape[0] - HALO
    ups = [chip(lax.rem(z + d, nz), p, c) for d in range(1, nz)]
    flat = [chip(z, hop(p, d), c) for d in HOPS]
    meet(ups + flat + [chip(z, p, 1 - c)])
    gain_out[p, z] = gains_ref[...]
    gz = [
        send(gain_out.at[p, z], gain_out.at[p, z], gz_sems.at[0, d], gz_sems.at[1, d], ups[d])
        for d in range(nz - 1)
    ]
    to_plane = []
    for i, d in enumerate(HOPS):
        to_plane.append(
            send(a_ref.at[hop(p, d)], a_out.at[z, p], a_sems.at[0, i], a_sems.at[1, i], flat[i])
        )
    local = [pltpu.make_async_copy(a_ref.at[p], a_out.at[z, p], loc_sems.at[n])]
    for j in range(n):
        local.append(pltpu.make_async_copy(w_refs[j].at[p], w_outs[j].at[p], loc_sems.at[j]))
    for copy in local:
        copy.start()

    for copy in gz:
        copy.wait_recv()
    gp = [
        send(gain_out.at[p], gain_out.at[p], gp_sems.at[0, i], gp_sems.at[1, i], flat[i])
        for i in range(3)
    ]
    for copy in gp:
        copy.wait_recv()
    for i in range(nz):
        for j in range(gain_out.shape[0]):
            first = (i * gain_out.shape[0] + j) * rows
            g_vec[:, first : first + rows] = gain_out[j, i][:, :rows]
    g = g_vec[0:1, :]

    @pl.loop(0, half // 16)
    def _(r):
        rows_in = hid[at_rows(r * 16, 16), :]
        full_ref[at_rows((p * 2 + c) * half + r * 16, 16), :] = (
            rows_in * rms(rows_in) * g
        ).astype(bf16)

    share_middle, share_end = share_rows(full_ref, half, own_sems, far_sems, near_sems)

    stage, chain_done = z_chain(a_out, up_sems, down_sems)
    for copy in to_plane:
        copy.wait_recv()
    local[0].wait()
    stage(0)
    share_middle()
    if nz > 2:
        stage(1)
    moved = []
    for j in range(n):
        for i, d in enumerate(HOPS):
            moved.append(
                send(
                    w_refs[j].at[hop(p, d)], w_outs[j].at[p], w_sems.at[0, j, i],
                    w_sems.at[1, j, i], flat[i],
                )
            )
    share_end()
    halo_from = full_ref.at[at_rows(tok - HALO, HALO), :]
    halo_to = full_ref.at[at_rows(tok, HALO), :]

    def halo(to):
        return pltpu.make_async_remote_copy(
            src_ref=halo_from, dst_ref=halo_to, send_sem=halo_sems.at[0],
            recv_sem=halo_sems.at[1], device_id=to, device_id_type=MESH,
        )

    @pl.when(z + 1 < nz)
    def _():
        halo(chip(z + 1, p, c)).start()

    @pl.when(z == 0)
    def _():
        full_ref[at_rows(tok, HALO), :] = jnp.zeros((HALO, full_ref.shape[1]), bf16)

    for k in range(2, nz):
        stage(k)

    @pl.when(z > 0)
    def _():
        halo(chip(z - 1, p, c)).wait_recv()

    @pl.when(z + 1 < nz)
    def _():
        halo(chip(z + 1, p, c)).wait_send()

    chain_done()
    for copy in moved + local[1:]:
        copy.wait()
    for copy in gz + gp + to_plane:
        copy.wait_send()


def open_step(hid, gains, piece, rest, tok, nz):
    width, n, n_p = hid.shape[1], len(rest), piece.shape[0]
    anywhere = pl.BlockSpec(memory_space=pl.ANY)
    dma = pltpu.SemaphoreType.DMA
    return pl.pallas_call(
        functools.partial(open_kernel, n),
        in_specs=[VM] * (n + 3),
        out_specs=[VM, VM] + [anywhere] * (n + 1),
        out_shape=[
            jax.ShapeDtypeStruct((n_p, nz) + gains.shape, f32),
            jax.ShapeDtypeStruct((tok + HALO, width), bf16),
            jax.ShapeDtypeStruct((nz,) + piece.shape, bf16),
        ]
        + [jax.ShapeDtypeStruct(r.shape, bf16) for r in rest],
        scratch_shapes=[
            pltpu.VMEM((8, width), f32), dma((2, nz - 1)), dma((2, 3)), dma((2, 3)), dma((2, nz)),
            dma((2, nz)),
        ]
        + SHARE_SEMS
        + [dma((2, n, 3)), dma((n + 1,)), dma((2,))],
        compiler_params=pltpu.CompilerParams(
            collective_id=4, has_side_effects=True, vmem_limit_bytes=VMEM_LIMIT
        ),
        cost_estimate=pl.CostEstimate(flops=0, bytes_accessed=250_000_000, transcendentals=0),
        name="open_step",
    )(hid, gains, piece, *rest)


def gather_bc_kernel(
    x_ref, kv_ref, grad_ref, e_ref, full_ref, kvz_ref, g_ref, e_out,
    far_sems, near_sems, z_sems, e_sems, loc_sems, own_g, far_g, near_g,
):
    z, p, c = place()
    nz = kvz_ref.shape[0]
    other = chip(z, p, 1 - c)
    meet(
        [other]
        + [chip(z, hop(p, d), c) for d in HOPS]
        + [chip(lax.rem(z + d, nz), p, c) for d in range(1, nz)]
    )
    local = pltpu.make_async_copy(e_ref, e_out.at[z], loc_sems.at[0])
    local.start()
    kvz_ref[z] = kv_ref[...]

    def up(d):
        return pltpu.make_async_remote_copy(
            src_ref=kv_ref, dst_ref=kvz_ref.at[z], send_sem=z_sems.at[0, d - 1],
            recv_sem=z_sems.at[1, d - 1], device_id=chip(z + d, p, c), device_id_type=MESH,
        )

    for d in range(1, nz):

        @pl.when(z + d < nz)
        def _():
            up(d).start()

    half = x_ref.shape[0] // 2
    full_ref[p] = x_ref[...]
    bc_middle, bc_end = share(
        lambda q: full_ref.at[q, at_rows(c * half, half), :],
        lambda q, i: full_ref.at[q, at_rows(c * half + i * (half // 2), half // 2), :],
        far_sems, near_sems,
    )
    local.wait()
    e_end = z_hop(e_out, 0, e_sems)
    bc_middle()
    g_half = grad_ref.shape[0]
    g_ref[at_rows((p * 2 + c) * g_half, g_half), :] = grad_ref[...].astype(bf16)
    g_middle, g_end = share_rows(g_ref, g_half, own_g, far_g, near_g)
    bc_end()
    g_middle()
    for d in range(1, nz):

        @pl.when(z - d >= 0)
        def _():
            pltpu.make_async_remote_copy(
                src_ref=kv_ref, dst_ref=kvz_ref.at[z - d], send_sem=z_sems.at[0, d - 1],
                recv_sem=z_sems.at[1, d - 1], device_id=chip(z - d, p, c), device_id_type=MESH,
            ).wait_recv()

        @pl.when(z + d < nz)
        def _():
            kvz_ref[z + d] = jnp.zeros(kv_ref.shape, kv_ref.dtype)
            up(d).wait_send()

    g_end()
    e_end()


def gather_bc(x, at, n_p, kv, nz, grad, piece):
    tok = x.shape[0]
    dma = pltpu.SemaphoreType.DMA
    whole = lambda s: pl.BlockSpec(s, lambda i: (0,) * len(s))
    return pl.pallas_call(
        gather_bc_kernel,
        grid=(1,),
        in_specs=[
            pl.BlockSpec((tok, 128), lambda i: (0, at)), whole(kv.shape), whole(grad.shape),
            whole(piece.shape),
        ],
        out_specs=[
            whole((n_p, tok, 128)), whole((nz,) + kv.shape), whole((tok, grad.shape[1])),
            ANYWHERE,
        ],
        out_shape=[
            jax.ShapeDtypeStruct((n_p, tok, 128), bf16),
            jax.ShapeDtypeStruct((nz,) + kv.shape, bf16),
            jax.ShapeDtypeStruct((tok, grad.shape[1]), bf16),
            jax.ShapeDtypeStruct((nz,) + piece.shape, bf16),
        ],
        scratch_shapes=[dma((2, 4)), dma((2, 3)), dma((2, nz - 1)), dma((2, 2)), dma((1,))]
        + SHARE_SEMS,
        compiler_params=pltpu.CompilerParams(
            collective_id=5, has_side_effects=True, vmem_limit_bytes=VMEM_LIMIT
        ),
        cost_estimate=pl.CostEstimate(flops=0, bytes_accessed=40_000_000, transcendentals=0),
        name="gather_bc",
    )(x, kv, grad, piece)


def carry_kernel(
    state_ref, rate_ref, kvz_ref, e_given, in_ref, kv_ref, rates_ref, e_ref,
    low, came, factor, s_sems, r_sems, p_sems, e_sems,
):
    z, p, c = place()
    nz = kvz_ref.shape[0]
    ups = [chip(lax.rem(z + d, nz), p, c) for d in range(1, nz)]
    meet([chip(z, hop(p, d), c) for d in (1, 2)] + ups)
    low[...] = state_ref[...].astype(bf16)
    rates_ref[z] = rate_ref[...]
    rates = [
        send(rates_ref.at[z], rates_ref.at[z], r_sems.at[0, d], r_sems.at[1, d], ups[d])
        for d in range(nz - 1)
    ]

    def up(d):
        return pltpu.make_async_remote_copy(
            src_ref=low, dst_ref=came.at[d - 1], send_sem=s_sems.at[0, d - 1],
            recv_sem=s_sems.at[1, d - 1], device_id=chip(z + d, p, c), device_id_type=MESH,
        )

    for d in range(1, nz):

        @pl.when(z + d < nz)
        def _():
            up(d).start()

    e_end = z_hop(e_ref, 1, e_sems)
    kv_ref[p] = kvz_ref[...]
    kv_middle, kv_end = share(
        lambda q: kv_ref.at[q],
        lambda q, i: kv_ref.at[q, pl.ds(i * (nz // 2), nz // 2)],
        p_sems, None,
    )
    in_ref[...] = jnp.zeros_like(in_ref)
    factor[...] = jnp.ones_like(factor)
    lane_head, row_head = head_maps(state_ref.shape[0])
    kv_middle()
    for copy in rates:
        copy.wait_recv()
    for d in range(1, nz):

        @pl.when(z - d >= 0)
        def _():
            pltpu.make_async_remote_copy(
                src_ref=low, dst_ref=came.at[d - 1], send_sem=s_sems.at[0, d - 1],
                recv_sem=s_sems.at[1, d - 1], device_id=chip(z - d, p, c), device_id_type=MESH,
            ).wait_recv()
            scale = jnp.sum(row_head * factor[0:1, :], axis=1, keepdims=True)
            in_ref[...] += scale * came[d - 1].astype(f32)
            factor[...] = factor[...] * rates_ref[z - d]

        @pl.when(z + d < nz)
        def _():
            up(d).wait_send()

    kv_end()
    e_end()
    for copy in rates:
        copy.wait_send()


def carry_step(state, rate, kvz, n_p, piece):
    nz = kvz.shape[0]
    dma = pltpu.SemaphoreType.DMA
    return pl.pallas_call(
        carry_kernel,
        in_specs=[VM] * 3 + [ANYWHERE],
        out_specs=[VM] * 3 + [ANYWHERE],
        out_shape=[
            jax.ShapeDtypeStruct(state.shape, f32),
            jax.ShapeDtypeStruct((n_p,) + kvz.shape, bf16),
            jax.ShapeDtypeStruct((nz,) + rate.shape, f32),
            jax.ShapeDtypeStruct(piece.shape, bf16),
        ],
        scratch_shapes=[
            pltpu.VMEM(state.shape, bf16),
            pltpu.VMEM((nz - 1,) + state.shape, bf16),
            pltpu.VMEM(rate.shape, f32),
            dma((2, nz - 1)), dma((2, nz - 1)), dma((2, 4)), dma((2, 2)),
        ],
        input_output_aliases={3: 3},
        compiler_params=pltpu.CompilerParams(
            collective_id=8, has_side_effects=True, vmem_limit_bytes=VMEM_LIMIT
        ),
        cost_estimate=pl.CostEstimate(flops=0, bytes_accessed=80_000_000, transcendentals=0),
        name="carry_step",
    )(state, rate, kvz, piece)


def reduce_bc_kernel(n, x_ref, dkv_ref, dx_ref, slope_ref, *refs):
    ins, (out_ref, own_ref, next_ref), outs = refs[:n], refs[n : n + 3], refs[n + 3 : 2 * n + 3]
    (
        sib_out, sib_in, out, came, z_came, first, n_sems, f_sems, own_sems, z_sems, h_sems,
        w_sems, loc_sems,
    ) = refs[2 * n + 3 :]
    z, p, c = place()
    nz = dkv_ref.shape[0]
    half = x_ref.shape[1] // 2
    xw = dx_ref.shape[1]
    other = chip(z, p, 1 - c)
    meet(
        [other]
        + [chip(z, hop(p, d), c) for d in HOPS]
        + [chip(lax.rem(z + d, nz), p, c) for d in range(1, nz)]
    )

    def down(d):
        return pltpu.make_async_remote_copy(
            src_ref=dkv_ref.at[z - d], dst_ref=z_came.at[d - 1], send_sem=z_sems.at[0, d - 1],
            recv_sem=z_sems.at[1, d - 1], device_id=chip(z - d, p, c), device_id_type=MESH,
        )

    for d in range(1, nz):

        @pl.when(z - d >= 0)
        def _():
            down(d).start()

    near, far = [], []
    order = HOPS + (0,)
    for i, d in enumerate(order):
        q = hop(p, d)
        sib_out[i] = x_ref[q, at_rows((1 - c) * half, half), :].astype(bf16)
        near.append(
            send(sib_out.at[i], sib_in.at[i], n_sems.at[0, i], n_sems.at[1, i], other)
        )
    for i, d in enumerate(HOPS):
        q = hop(p, d)
        near[i].wait_recv()
        out[i] = (x_ref[q, at_rows(c * half, half), :] + sib_in[i].astype(f32)).astype(bf16)
        far.append(
            send(out.at[i], came.at[i], f_sems.at[0, i], f_sems.at[1, i], chip(z, q, c))
        )
    moved = swap_begin(ins, outs, w_sems, loc_sems)
    near[3].wait_recv()
    total = x_ref[p, at_rows(c * half, half), :] + sib_in[3].astype(f32)
    for i in (1, 2, 0):
        far[i].wait_recv()
        total = total + came[i].astype(f32)
    mine = out_ref.at[at_rows(c * half, half), :]
    out_ref[at_rows(c * half, half), :] = total
    copy = send(mine, mine, own_sems.at[0], own_sems.at[1], other)
    copy.wait()
    first[:, :xw] = dx_ref[...] * slope_ref[:, :xw]
    first[:, xw:] = out_ref[0:8, :] * slope_ref[:, xw:]

    def edge(to):
        return pltpu.make_async_remote_copy(
            src_ref=first, dst_ref=next_ref, send_sem=h_sems.at[0], recv_sem=h_sems.at[1],
            device_id=to, device_id_type=MESH,
        )

    @pl.when(z > 0)
    def _():
        edge(chip(z - 1, p, c)).start()

    own_ref[...] = dkv_ref[z].astype(f32)
    for d in range(1, nz):

        @pl.when(z + d < nz)
        def _():
            pltpu.make_async_remote_copy(
                src_ref=dkv_ref.at[z], dst_ref=z_came.at[d - 1], send_sem=z_sems.at[0, d - 1],
                recv_sem=z_sems.at[1, d - 1], device_id=chip(z + d, p, c), device_id_type=MESH,
            ).wait_recv()
            own_ref[...] += z_came[d - 1].astype(f32)

        @pl.when(z - d >= 0)
        def _():
            down(d).wait_send()

    @pl.when(z + 1 == nz)
    def _():
        next_ref[...] = jnp.zeros_like(next_ref)

    @pl.when(z + 1 < nz)
    def _():
        edge(chip(z + 1, p, c)).wait_recv()

    @pl.when(z > 0)
    def _():
        edge(chip(z - 1, p, c)).wait_send()

    for done in near + far:
        done.wait_send()
    for copy in moved:
        copy.wait()


def reduce_bc(x, dkv, dx, slope, moved):
    n_p, tok, _ = x.shape
    half, nz = tok // 2, dkv.shape[0]
    dma = pltpu.SemaphoreType.DMA
    return plane_call(
        reduce_bc_kernel, "reduce_bc", 7, (x, dkv, dx, slope),
        [((tok, 128), f32), (dkv.shape[1:], f32), (slope.shape, f32)],
        [
            pltpu.VMEM((4, half, 128), bf16),
            pltpu.VMEM((4, half, 128), bf16),
            pltpu.VMEM((3, half, 128), bf16),
            pltpu.VMEM((3, half, 128), bf16),
            pltpu.VMEM((nz - 1,) + dkv.shape[1:], bf16),
            pltpu.VMEM(slope.shape, f32),
            dma((2, 4)), dma((2, 3)), dma((2,)), dma((2, nz - 1)), dma((2,)),
        ],
        nbytes=100_000_000,
        moved=moved,
    )


def sums_kernel(n, v_ref, *refs):
    ins, out_ref, outs = refs[:n], refs[n], refs[n + 1 : 2 * n + 1]
    came, z_sems, p_sems, c_sems, w_sems, loc_sems = refs[2 * n + 1 :]
    z, p, c = place()
    nz = came.shape[0]
    ups = [chip(lax.rem(z + d, nz), p, c) for d in range(1, nz)]
    other = chip(z, p, 1 - c)
    meet(ups + [chip(z, hop(p, d), c) for d in HOPS] + [other])
    moved = swap_begin(ins, outs, w_sems, loc_sems)
    copies = []
    for d in range(1, nz):
        copies.append(
            send(v_ref, came.at[d], z_sems.at[0, d - 1], z_sems.at[1, d - 1], ups[d - 1])
        )
    total = v_ref[...]
    for d in range(1, nz):
        copies[d - 1].wait_recv()
        total = total + came[d]
    out_ref[c, p] = total
    far = []
    for i, d in enumerate(HOPS):
        far.append(
            send(out_ref.at[c, p], out_ref.at[c, p], p_sems.at[0, i], p_sems.at[1, i], chip(z, hop(p, d), c))
        )
    for copy in far:
        copy.wait_recv()
    near = send(out_ref.at[c], out_ref.at[c], c_sems.at[0], c_sems.at[1], other)
    for copy in copies + far:
        copy.wait_send()
    near.wait()
    for copy in moved:
        copy.wait()


def sums_step(v, nz, n_p, moved):
    return plane_call(
        sums_kernel, "sums_step", 6, (v,),
        [((2, n_p) + v.shape, f32)],
        [
            pltpu.VMEM((nz,) + v.shape, f32),
            pltpu.SemaphoreType.DMA((2, nz - 1)),
            pltpu.SemaphoreType.DMA((2, 3)),
            pltpu.SemaphoreType.DMA((2,)),
        ],
        moved=moved,
    )


def rope_tables(positions, pairs):
    freqs = rope_base ** (-2.0 * pairs.astype(f32) / HDIM)
    angles = positions.astype(f32)[:, None] * freqs[None, :]
    return jnp.cos(angles), jnp.sin(angles)


def carry_back(state, rates):
    nz, zi = lax.axis_size("z"), lax.axis_index("z")
    low = state.astype(bf16)
    total, factor = None, None
    for d in range(1, nz):
        came = lax.ppermute(low, "z", [(i, i - d) for i in range(d, nz)]).astype(f32)
        total = came if total is None else total + factor * came
        rate = lax.dynamic_index_in_dim(rates, (zi + d) % nz, 0, keepdims=False)
        factor = rate if factor is None else factor * rate
    return total


def shards(
    hidden_in,
    grad_out,
    doc_starts,
    norm_mixer,
    norm_ffn,
    mamba_z,
    mamba_x,
    mamba_bc,
    mamba_dt,
    conv_x,
    conv_bc,
    a_log,
    dt_bias,
    skip_gain,
    mamba_out,
    attn_query,
    attn_key,
    attn_value,
    attn_out,
    ffn_gate,
    ffn_up,
    ffn_down,
):
    own = hidden_in.shape[0]
    width = hidden_in.shape[1]
    half = own // 2
    nz, n_p = lax.axis_size("z"), lax.axis_size("p")
    zi, pi, ci = lax.axis_index("z"), lax.axis_index("p"), lax.axis_index("head")
    tok = own * n_p
    base = zi * tok
    positions = base + jnp.arange(tok, dtype=jnp.int32)
    edge = conv_x.shape[0] - 1
    ext_docs = doc_ids(base - edge + jnp.arange(tok + 2 * edge, dtype=jnp.int32), doc_starts)
    rows = mamba_z.shape[0]
    n_heads = a_log.shape[0] // n_p
    xw = n_heads * MHDIM
    bw = mamba_bc.shape[1] // (2 * n_p)
    cw = xw + 2 * bw
    kw = HDIM // n_p
    hk = kw // 2
    tail_w = 128 - 2 * kw - n_heads

    weights = (
        mamba_x, mamba_bc, attn_key, attn_value, mamba_dt, attn_query, mamba_z, mamba_out, attn_out,
        ffn_gate, ffn_up, ffn_down,
    )
    piece_a, *rest = pack(n_p, *weights)

    def along_z(piece):
        piece = piece.reshape(n_p * rows, piece.shape[2])
        return lax.all_gather(piece, "z", axis=0, tiled=True)

    gains_own = jnp.pad(
        jnp.stack([norm_mixer, norm_ffn]).astype(bf16).astype(f32), ((0, 6), (0, 128 - rows))
    )
    my_half = lambda v: lax.dynamic_slice_in_dim(v, ci * half, half, 0)
    hidden_own, grad_own = my_half(hidden_in), my_half(grad_out)
    gains, normed_one, w_a, *rest = open_step(hidden_own, gains_own, piece_a, rest, tok, nz)
    w_a = w_a.reshape(nz * n_p * rows, w_a.shape[3])
    gains = gains.transpose(2, 1, 0, 3)[:, :, :, :rows].reshape(8, 1, width)
    gain_mix, gain_ffn = gains[0], gains[1]
    w_b, w_c, w_d = [along_z(piece) for piece in rest[:3]]

    in_ext = product(normed_one, w_a)
    in_b = product(normed_one, w_b)[:tok]
    in_a = in_ext[:tok]
    pre_ext = in_ext[:, :cw].astype(bf16)
    gate_z = in_b[:, HDIM:]
    slice_1 = lambda v, at, n: lax.dynamic_slice_in_dim(v, at, n, 1)
    taps = jnp.concatenate(
        [
            slice_1(conv_x, pi * xw, xw),
            slice_1(conv_bc, pi * bw, bw),
            slice_1(conv_bc, (n_p + pi) * bw, bw),
        ],
        axis=1,
    )
    ext = jnp.concatenate([pre_ext[tok + HALO - edge :], pre_ext[:tok]], axis=0)
    conv_in = convolve(ext, taps, ext_docs, tok)
    ssm = jax.nn.silu(conv_in).astype(bf16)
    head_slice = lambda v: lax.dynamic_slice_in_dim(v, pi * n_heads, n_heads, 0)
    my_bias, my_a, my_skip = head_slice(dt_bias), head_slice(a_log), head_slice(skip_gain)
    lanes = lambda v: jnp.pad(v, (0, 128 - n_heads))[None, :]
    dt_at = cw + 2 * kw
    dt_pre = jnp.pad(in_a[:, dt_at : dt_at + n_heads], ((0, 0), (0, 128 - n_heads))) + lanes(my_bias)
    neg_rate = lanes(-jnp.exp(my_a))
    skip_full = jnp.repeat(my_skip, MHDIM)[None, :]
    pair_ids = pi * hk + jnp.arange(hk)
    cos_k, sin_k = rope_tables(positions, pair_ids)
    k0, k1 = in_a[:, cw : cw + hk], in_a[:, cw + hk : cw + kw]
    key_own = jnp.concatenate([k0 * cos_k - k1 * sin_k, k1 * cos_k + k0 * sin_k], axis=1)
    val_own = in_a[:, cw + kw : cw + 2 * kw]
    kv_own = jnp.concatenate([key_own, val_own], axis=1).astype(bf16)
    kv_own = jnp.concatenate([kv_own[: tok // 2], kv_own[tok // 2 :]], axis=1)
    bc_all, kvz, g_ffn, w_e = gather_bc(
        ssm, xw // 128, n_p, kv_own, nz, grad_own, rest[3]
    )
    cos_q, sin_q = rope_tables(positions, jnp.arange(HDIM // 2))
    cos_q, sin_q = cos_q.reshape(tok, n_p, hk), sin_q.reshape(tok, n_p, hk)

    def rope_q(v, sign):
        v = v.reshape(tok, n_p, 2, hk)
        a, b = v[:, :, 0], v[:, :, 1]
        return jnp.stack(
            [a * cos_q - sign * b * sin_q, b * cos_q + sign * a * sin_q], axis=2
        ).reshape(tok, HDIM)

    queries = rope_q(in_b[:, :HDIM], 1.0).astype(bf16)

    base_arr = jnp.reshape(base, (1,)).astype(jnp.int32)
    y_local, span_starts, local_state, dev_decay, decay_full, c_mat = ssd_forward(
        base_arr, doc_starts, ssm, bc_all, dt_pre, neg_rate, skip_full
    )
    rate = jnp.broadcast_to(dev_decay[tok - 1 :], (8, 128))
    in_state, kv, rates, w_e = carry_step(local_state, rate, kvz, n_p, w_e)

    attn_f32, lse, keys, values = attend(base_arr, doc_starts, queries, kv)
    attn_low = attn_f32.astype(bf16)
    y_flat = y_local + product_nt(c_mat, in_state.astype(bf16)) * decay_full
    silu_z = jax.nn.silu(gate_z)
    gated = (y_flat * silu_z).astype(bf16)
    mixed = jnp.concatenate([gated, attn_low], axis=1)

    mid_own, normed_two, w_e = mid_step(mixed, w_c, hidden_own, gain_ffn, w_e)
    w_e = w_e.reshape(width, -1)
    gu = product(normed_two, w_d)
    ffw = gu.shape[1] // 2
    gate_val, up_val = gu[:, :ffw], gu[:, ffw:]
    silu_gate = jax.nn.silu(gate_val)
    activated = (silu_gate * up_val).astype(bf16)
    grad_e = product_t(g_ffn, activated).astype(bf16)
    g_ffn, grad_e = lax.optimization_barrier((g_ffn, grad_e))
    d_act = product(g_ffn, w_e)
    d_gu = jnp.concatenate(
        [d_act * up_val * silu_slope(gate_val), d_act * silu_gate], axis=1
    ).astype(bf16)
    grad_d = product_t(normed_two, d_gu).astype(bf16)
    d_gu, grad_d = lax.optimization_barrier((d_gu, grad_d))

    def scattered(grad):
        return lax.psum_scatter(grad, "z", scatter_dimension=0, tiled=True)

    def by_owner(grad):
        return grad.reshape(n_p, rows, grad.shape[1])

    ge = scattered(grad_e)
    gd = scattered(grad_d)
    d_mid_own, grad_gain_ffn, g_mid = two_step(d_gu, w_d, mid_own, grad_own, gain_ffn)
    g_mid, ge = lax.optimization_barrier((g_mid, ge))

    d_mixed = product(g_mid, w_c)
    grad_c = product_t(g_mid, mixed).astype(bf16)
    gc = scattered(grad_c)
    d_gated = d_mixed[:, :xw]
    d_attn = d_mixed[:, xw:].astype(bf16)
    d_y_flat = d_gated * silu_z
    d_z = (d_gated * y_flat * silu_slope(gate_z)).astype(bf16)
    d_in_local = product_t((d_y_flat * decay_full).astype(bf16), c_mat)
    d_in_local, d_attn = lax.optimization_barrier((d_in_local, d_attn))
    rates = jnp.repeat(rates[:, 0, :n_heads], MHDIM, axis=1)[:, :, None]
    state_grad = carry_back(d_in_local, rates)
    d_query, d_kv = attend_back(
        base_arr, doc_starts, queries, d_attn, attn_f32, lse, keys, values, kv.shape
    )
    d_q_pre = rope_q(d_query, -1.0).astype(bf16)
    d_b = jnp.concatenate([d_q_pre, d_z], axis=1)
    d_b, state_grad = lax.optimization_barrier((d_b, state_grad))
    more = lambda v: jnp.pad(v, ((0, HALO), (0, 0)))
    grad_b = product_t(normed_one, more(d_b)).astype(bf16)
    gb = scattered(grad_b)
    d_kv_parts = [lax.dynamic_index_in_dim(d_kv, pi, 0, keepdims=False)]
    for d in range(1, n_p):
        part = lax.dynamic_index_in_dim(d_kv, jnp.bitwise_xor(pi, d), 0, keepdims=False)
        d_kv_parts.append(lax.ppermute(part, "p", [(i, i ^ d) for i in range(n_p)]))

    start_decay = jnp.concatenate([jnp.ones((1, 128), f32), dev_decay[SPAN - 1 :: SPAN][:-1]])
    d_y_flat, gd = lax.optimization_barrier((d_y_flat, gd))
    d_xs, d_bc, d_dt, sums, skip_sums = ssd_backward(
        base_arr, doc_starts, ssm, bc_all, dt_pre, d_y_flat, span_starts,
        start_decay[:, None, :], neg_rate, skip_full, in_state, state_grad,
    )
    d_bc, d_kv_parts = lax.optimization_barrier((d_bc, d_kv_parts))
    d_kv = sum(part.astype(f32) for part in d_kv_parts).astype(bf16)
    slope = silu_slope(conv_in)
    d_bc, d_kv_own, du_next, ge, gd = reduce_bc(
        d_bc, d_kv, d_xs[:8], slope[:8], (by_owner(ge), by_owner(gd))
    )
    d_kv_own = jnp.concatenate([d_kv_own[:, : 2 * kw], d_kv_own[:, 2 * kw :]], axis=0)
    dk0, dk1 = d_kv_own[:, :hk], d_kv_own[:, hk:kw]
    d_kv_low = jnp.concatenate(
        [dk0 * cos_k + dk1 * sin_k, dk1 * cos_k - dk0 * sin_k, d_kv_own[:, kw:]], axis=1
    ).astype(bf16)
    du = jnp.concatenate([d_xs, d_bc], axis=1) * slope
    du = jnp.concatenate([du, du_next[:edge]], axis=0)
    d_pre, grad_taps = convolve_back(du, ext, taps, ext_docs, tok)
    d_pre = d_pre.astype(bf16)
    d_last = jnp.concatenate(
        [d_kv_low, d_dt[:, :n_heads].astype(bf16), jnp.zeros((tok, tail_w), bf16)], axis=1
    )
    d_a = jnp.concatenate([d_pre, d_last], axis=1)
    grad_a = product_t(normed_one, more(d_a)).astype(bf16)
    ga = scattered(grad_a)
    once = jnp.where(ci == 0, d_pre[:, xw:], jnp.zeros((), bf16))
    d_a_once = jnp.concatenate([d_pre[:, :xw], once, d_last], axis=1)
    d_a_once, grad_a, gc, gb = lax.optimization_barrier((d_a_once, grad_a, gc, gb))
    grad_in, block_out, grad_gain_mix, gc, gb = one_step(
        d_a_once, w_a, d_b, w_b, hidden_own, d_mid_own, gain_mix, activated, w_e, mid_own,
        (by_owner(gc), by_owner(gb)),
    )

    flat = jnp.concatenate(
        [
            grad_gain_mix.reshape(-1, 128),
            grad_gain_ffn.reshape(-1, 128),
            grad_taps.reshape(-1, 128),
            sums[:2],
            jnp.pad(jnp.sum(skip_sums.reshape(n_heads, MHDIM), axis=1), (0, 128 - n_heads))[None],
        ]
    )
    flat = jnp.pad(flat, ((0, -flat.shape[0] % 8), (0, 0)))
    summed, ga = sums_step(flat, nz, n_p, (by_owner(ga),))
    g_rows = width // 128
    t_rows = grad_taps.size // 128
    si = zi * n_p + pi
    gains_sum = jnp.sum(summed[:, :, : 2 * g_rows], axis=(0, 1)).reshape(2, width)
    gains_sum = lax.dynamic_slice_in_dim(gains_sum, si * rows, rows, 1)
    mine = lax.dynamic_index_in_dim(summed, ci, 0, keepdims=False)
    s_taps = mine[:, 2 * g_rows : 2 * g_rows + t_rows].reshape(n_p, edge + 1, cw).transpose(1, 0, 2)
    s_heads = mine[:, 2 * g_rows + t_rows : 2 * g_rows + t_rows + 3, :n_heads]
    s_heads = s_heads.transpose(1, 0, 2).reshape(3, n_p * n_heads)
    s_x = s_taps[:, :, :xw].reshape(edge + 1, n_p * xw)
    s_bc = summed[0][:, 2 * g_rows : 2 * g_rows + t_rows].reshape(n_p, edge + 1, cw)
    s_bc = s_bc[:, :, xw:].reshape(n_p, edge + 1, 2, bw).transpose(1, 2, 0, 3)
    s_bc = s_bc.reshape(edge + 1, 2 * n_p * bw)

    (
        g_x, g_bc, g_k, g_v, g_dt, g_q, g_z, g_mout, g_aout, g_gate, g_up, g_down, block_out,
        grad_in,
    ) = unpack((ga, gb, gc, gd, ge, block_out, grad_in), weights + (block_out, grad_in))
    return (
        block_out,
        grad_in,
        gains_sum[0],
        gains_sum[1],
        g_z,
        g_x,
        g_bc,
        g_dt,
        s_x,
        s_bc,
        s_heads[0],
        s_heads[1],
        s_heads[2],
        g_mout,
        g_q,
        g_k,
        g_v,
        g_aout,
        g_gate,
        g_up,
        g_down,
    )


def solution(mesh):
    seq, head = mesh.shape["seq"], mesh.shape["head"]
    plane = math.gcd(seq, 4)
    grid = Mesh(mesh.devices.reshape(seq // plane, plane, head), ("z", "p", "head"))
    s = ("z", "p")
    h = "head"
    placed = (
        P(s, None), P(s, None), P(), P(s), P(s), P(s, h), P(s, h), P(s, None), P(s, h),
        P(None, h), P(), P(h), P(h), P(h), P(h, s), P(s, h), P(s, h), P(s, h), P(h, s),
        P(s, h), P(s, h), P(h, s),
    )
    given = (
        P(s, None), P(s, None), P(s), P(s), P(s, h), P(s, h), P(s, None), P(s, h),
        P(None, h), P(), P(h), P(h), P(h), P(h, s), P(s, h), P(s, h), P(s, h), P(h, s),
        P(s, h), P(s, h), P(h, s),
    )
    return jax.shard_map(shards, mesh=grid, in_specs=placed, out_specs=given, check_vma=False)
```

```python
import functools
import math

import jax
import jax.numpy as jnp
from jax import lax
from jax.experimental import pallas as pl
from jax.experimental.pallas import tpu as pltpu
from jax.sharding import Mesh
from jax.sharding import PartitionSpec as P

MHDIM = 64
NSTATE = 256
HDIM = 128
SPAN = 128

eps_norm = 1e-05
rope_base = 100000000000.0
neg_large = -1e30
top_prec = lax.Precision.HIGHEST
bf16 = jnp.bfloat16
f32 = jnp.float32
MESH = pl.DeviceIdType.MESH
VMEM_LIMIT = 56 * 1024 * 1024


def doc_ids(positions, doc_starts):
    return jnp.sum((doc_starts[None, :] <= positions[:, None]).astype(jnp.int32), axis=1) - 1


def product(left, right):
    return jnp.dot(left, right, preferred_element_type=f32)


def product_t(left, right):
    return lax.dot_general(left, right, (((0,), (0,)), ((), ())), preferred_element_type=f32)


def product_nt(left, right):
    return lax.dot_general(left, right, (((1,), (1,)), ((), ())), preferred_element_type=f32)


def silu_slope(values):
    sigma_val = jax.nn.sigmoid(values)
    return sigma_val * (1.0 + values * (1.0 - sigma_val))


def convolve(extended, weights, ext_docs, tok_count):
    edge_rows = weights.shape[0] - 1
    here = ext_docs[edge_rows : edge_rows + tok_count]
    summed = jnp.zeros((tok_count, extended.shape[1]), f32)
    for tap_index in range(weights.shape[0]):
        begin_row = edge_rows - tap_index
        same_doc = (ext_docs[begin_row : begin_row + tok_count] == here)[:, None]
        rows = extended[begin_row : begin_row + tok_count].astype(f32)
        summed = summed + jnp.where(same_doc, rows, 0.0) * weights[tap_index][None, :]
    return summed


def convolve_back(d_conv, extended, weights, ext_docs, tok_count):
    edge_rows = weights.shape[0] - 1
    here = ext_docs[edge_rows : edge_rows + tok_count]
    d_rows = jnp.zeros((tok_count, d_conv.shape[1]), f32)
    tap_grads = []
    for tap_index in range(weights.shape[0]):
        begin_row = edge_rows - tap_index
        before = (ext_docs[begin_row : begin_row + tok_count] == here)[:, None]
        rows = extended[begin_row : begin_row + tok_count].astype(f32)
        tap_grads.append(jnp.sum(jnp.where(before, d_conv[:tok_count] * rows, 0.0), axis=0))
        last = edge_rows + tap_index
        after = (ext_docs[last : last + tok_count] == here)[:, None]
        ahead = d_conv[tap_index : tap_index + tok_count]
        d_rows = d_rows + jnp.where(after, ahead, 0.0) * weights[tap_index][None, :]
    return (d_rows, jnp.stack(tap_grads))


def tri_dot(a, b, dims=((1,), (0,))):
    return lax.dot_general(a, b, (dims, ((), ())), precision=top_prec, preferred_element_type=f32)


def dot_nn(a, b):
    return lax.dot_general(a, b, (((1,), (0,)), ((), ())), preferred_element_type=f32)


def dot_nt(a, b):
    return lax.dot_general(a, b, (((1,), (1,)), ((), ())), preferred_element_type=f32)


def dot_tn(a, b):
    return lax.dot_general(a, b, (((0,), (0,)), ((), ())), preferred_element_type=f32)


def iota2(shape, dim):
    return lax.broadcasted_iota(jnp.int32, shape, dim)


def docs_of(pos, starts_ref):
    count = jnp.where(starts_ref[0] <= pos, 1, 0)
    for i in range(1, starts_ref.shape[0]):
        count = count + jnp.where(starts_ref[i] <= pos, 1, 0)
    return count - 1


def softplus(v):
    return jnp.maximum(v, 0.0) + jnp.log(1.0 + jnp.exp(-jnp.abs(v)))


def head_maps(xw):
    lane_head = (iota2((128, xw), 1) // MHDIM == iota2((128, xw), 0)).astype(f32)
    row_head = (iota2((xw, 128), 0) // MHDIM == iota2((xw, 128), 1)).astype(f32)
    return lane_head, row_head


def span_setup(k, base_ref, starts_ref, dtp, nega):
    first = base_ref[0] + k * SPAN
    t_idx, s_idx = iota2((SPAN, SPAN), 0), iota2((SPAN, SPAN), 1)
    docs_t = docs_of(first + t_idx, starts_ref)
    docs_s = docs_of(first + s_idx, starts_ref)
    linked = (docs_t == docs_s) & (t_idx >= s_idx)
    dt = softplus(dtp)
    la = nega * dt
    tri = (t_idx >= s_idx).astype(f32)
    cum = tri_dot(tri, la)
    before = docs_of(first - 1, starts_ref)
    last_doc = docs_of(first + SPAN - 1, starts_ref)
    carried = jnp.where(docs_t == before, jnp.exp(cum), 0.0)
    cum_last = cum[SPAN - 1 : SPAN, :]
    tail = jnp.where(docs_t == last_doc, jnp.exp(cum_last - cum), 0.0)
    return docs_t, linked, dt, la, tri, cum, carried, tail


def split_bc(bc_ref):
    parts = [bc_ref[q] for q in range(bc_ref.shape[0])]
    half = parts[0].shape[1] // 2
    return (
        jnp.concatenate([part[:, :half] for part in parts], axis=1),
        jnp.concatenate([part[:, half:] for part in parts], axis=1),
    )


def ssd_forward_kernel(
    n_heads, base_ref, starts_ref, x_ref, bc_ref, dtp_ref, nega_ref, skip_ref,
    y_ref, span_ref, final_ref, decay_ref, wide_ref, c_out, state, running,
):
    k = pl.program_id(0)
    xw = n_heads * MHDIM

    @pl.when(k == 0)
    def _():
        state[...] = jnp.zeros_like(state)
        running[...] = jnp.zeros_like(running)

    docs_t, linked, dt, la, tri, cum, carried, tail = span_setup(
        k, base_ref, starts_ref, dtp_ref[...], nega_ref[...]
    )
    lane_head, row_head = head_maps(xw)
    prev_doc = docs_of(base_ref[0] - 1, starts_ref)
    since = jnp.where(docs_t == prev_doc, jnp.exp(running[0:1, :] + cum), 0.0)
    decay_ref[...] = since
    wide_ref[...] = tri_dot(since, lane_head)
    running[...] = running[...] + cum[SPAN - 1 : SPAN, :]
    start = state[...]
    span_ref[0] = start
    x, (b, c) = x_ref[...], split_bc(bc_ref)
    c_out[...] = c
    inner = dot_nt(c, b)
    cum_t, dt_t = cum.T, dt.T
    lane = iota2((SPAN, 128), 1)
    pieces = []
    for pair in range(n_heads // 2):
        xp = x[:, pair * 128 : pair * 128 + 128]
        got = []
        for h in (2 * pair, 2 * pair + 1):
            gap = jnp.where(linked, cum[:, h : h + 1] - cum_t[h : h + 1, :], neg_large)
            w = jnp.exp(gap) * inner * dt_t[h : h + 1, :]
            got.append(dot_nn(w.astype(bf16), xp))
        pieces.append(jnp.where(lane < MHDIM, got[0], got[1]))
    y = jnp.concatenate(pieces, axis=1)
    y = y + dot_nt(c, start.astype(bf16)) * tri_dot(carried, lane_head)
    xf = x.astype(f32)
    y_ref[...] = y + skip_ref[...] * xf
    xt = (xf * tri_dot(tail * dt, lane_head)).astype(bf16)
    keep = jnp.sum(row_head * carried[SPAN - 1 : SPAN, :], axis=1, keepdims=True)
    new = dot_tn(xt, b) + keep * start
    state[...] = new
    final_ref[...] = new


def ssd_forward(base, doc_starts, x, bc, dtp, nega, skip):
    tok, xw, n_p = x.shape[0], skip.shape[1], bc.shape[0]
    n_heads, nspan = xw // MHDIM, tok // SPAN
    row = lambda n: pl.BlockSpec((SPAN, n), lambda i: (i, 0))
    whole = lambda *s: pl.BlockSpec(s, lambda i: (0,) * len(s))
    smem = pl.BlockSpec(memory_space=pltpu.SMEM)
    return pl.pallas_call(
        functools.partial(ssd_forward_kernel, n_heads),
        grid=(nspan,),
        in_specs=[
            smem, smem, row(xw), pl.BlockSpec((n_p, SPAN, 128), lambda i: (0, i, 0)), row(128),
            whole(1, 128), whole(1, xw),
        ],
        out_specs=[
            row(xw),
            pl.BlockSpec((1, xw, NSTATE), lambda i: (i, 0, 0)),
            whole(xw, NSTATE),
            row(128),
            row(xw),
            row(NSTATE),
        ],
        out_shape=[
            jax.ShapeDtypeStruct((tok, xw), f32),
            jax.ShapeDtypeStruct((nspan, xw, NSTATE), f32),
            jax.ShapeDtypeStruct((xw, NSTATE), f32),
            jax.ShapeDtypeStruct((tok, 128), f32),
            jax.ShapeDtypeStruct((tok, xw), f32),
            jax.ShapeDtypeStruct((tok, NSTATE), bf16),
        ],
        scratch_shapes=[pltpu.VMEM((xw, NSTATE), f32), pltpu.VMEM((8, 128), f32)],
        compiler_params=pltpu.CompilerParams(vmem_limit_bytes=VMEM_LIMIT),
        cost_estimate=pl.CostEstimate(
            flops=2 * tok * xw * NSTATE * 3, bytes_accessed=40_000_000, transcendentals=0
        ),
        name="ssd_forward",
    )(base, doc_starts, x, bc, dtp, nega, skip)


def ssd_backward_kernel(
    n_heads, base_ref, starts_ref, x_ref, bc_ref, dtp_ref, dy_ref, span_ref, decay_ref,
    nega_ref, skip_ref, in_ref, grad_ref,
    dx_ref, dbc_ref, ddt_ref, sums_ref, gskip_ref, gstate,
):
    step = pl.program_id(0)
    k = pl.num_programs(0) - 1 - step
    xw = n_heads * MHDIM

    @pl.when(step == 0)
    def _():
        gstate[...] = grad_ref[...]
        sums_ref[...] = jnp.zeros_like(sums_ref)
        gskip_ref[...] = jnp.zeros_like(gskip_ref)

    nega = nega_ref[...]
    docs_t, linked, dt, la, tri, cum, carried, tail = span_setup(
        k, base_ref, starts_ref, dtp_ref[...], nega
    )
    lane_head, row_head = head_maps(xw)
    begin = jnp.sum(row_head * decay_ref[0], axis=1, keepdims=True)
    start = span_ref[0] + begin * in_ref[...]
    start_low = start.astype(bf16)
    g = gstate[...]
    g_low = g.astype(bf16)
    x, (b, c), dy = x_ref[...], split_bc(bc_ref), dy_ref[...]
    dy_low = dy.astype(bf16)
    xf = x.astype(f32)
    inner = dot_nt(c, b)
    cum_t, dt_t = cum.T, dt.T
    lane = iota2((SPAN, 128), 1)
    row8 = iota2((SPAN, 128), 0)
    d_inner = jnp.zeros((SPAN, SPAN), f32)
    r_cols = jnp.zeros((SPAN, 128), f32)
    k_rows = jnp.zeros((SPAN, 128), f32)
    u_pieces = []
    for pair in range(n_heads // 2):
        xp = x[:, pair * 128 : pair * 128 + 128]
        dyp = dy_low[:, pair * 128 : pair * 128 + 128]
        got = []
        for j, h in enumerate((2 * pair, 2 * pair + 1)):
            mine = (lane < MHDIM) if j == 0 else (lane >= MHDIM)
            gap = jnp.where(linked, cum[:, h : h + 1] - cum_t[h : h + 1, :], neg_large)
            e = jnp.exp(gap)
            m = e * inner
            dyx = dot_nt(dyp, jnp.where(mine, xp, jnp.zeros_like(xp)))
            ed = dyx * dt_t[h : h + 1, :]
            d_inner = d_inner + e * ed
            pairs = m * ed
            r_cols = jnp.where(lane == h, jnp.sum(pairs, axis=1, keepdims=True), r_cols)
            k_rows = jnp.where(row8 == h, jnp.sum(pairs, axis=0, keepdims=True), k_rows)
            got.append(dot_tn(m.astype(bf16), dyp))
        u_pieces.append(jnp.where(lane < MHDIM, got[0], got[1]))
    u = jnp.concatenate(u_pieces, axis=1)
    dye = dy * tri_dot(carried, lane_head)
    dye_low = dye.astype(bf16)
    di_low = d_inner.astype(bf16)
    r_state = tri_dot(dye * dot_nt(c, start_low), row_head)
    u_state = dot_nt(b, g_low) * tri_dot(tail, lane_head)
    u = u + u_state
    dt_full = tri_dot(dt, lane_head)
    k_state = dt * tri_dot(xf * u_state, row_head)
    d_dt = tri_dot(xf * u, row_head)
    tail_x = (xf * tri_dot(tail * dt, lane_head)).astype(bf16)
    dx_ref[...] = dt_full * u + skip_ref[...] * dy
    d_b = dot_nn(tail_x, g_low) + dot_tn(di_low, c)
    d_c = dot_nn(dye_low, start_low) + dot_nn(di_low, b)
    bw = 64
    for q in range(dbc_ref.shape[0]):
        cut = slice(q * bw, q * bw + bw)
        dbc_ref[q] = jnp.concatenate([d_b[:, cut], d_c[:, cut]], axis=1)
    gs = jnp.sum(g * start, axis=1, keepdims=True)
    gs_row = jnp.sum(row_head * gs, axis=0, keepdims=True)
    last = jnp.sum(k_state, axis=0, keepdims=True) + carried[SPAN - 1 : SPAN, :] * gs_row
    d_cum = r_cols - k_rows.T + r_state - k_state + jnp.where(row8 == SPAN - 1, last, 0.0)
    d_la = tri_dot(tri, d_cum, ((0,), (0,)))
    live = lane < n_heads
    dtp = dtp_ref[...]
    d_in = jnp.where(live, (d_dt + nega * d_la) * jax.nn.sigmoid(dtp), 0.0)
    ddt_ref[...] = d_in
    sum_a = jnp.sum(jnp.where(live, d_la * la, 0.0), axis=0, keepdims=True)
    sum_b = jnp.sum(d_in, axis=0, keepdims=True)
    pick = iota2((8, 128), 0)
    sums_ref[...] += jnp.where(pick == 0, sum_a, jnp.where(pick == 1, sum_b, 0.0))
    gskip_ref[...] += jnp.sum(dy * xf, axis=0, keepdims=True)
    keep = jnp.sum(row_head * carried[SPAN - 1 : SPAN, :], axis=1, keepdims=True)
    gstate[...] = keep * g + dot_tn(dye_low, c)


def ssd_backward(
    base, doc_starts, x, bc, dtp, dy, span_starts, start_decay, nega, skip, in_state, grad_state
):
    tok, xw, n_p = x.shape[0], skip.shape[1], bc.shape[0]
    wide = pl.BlockSpec((n_p, SPAN, 128), lambda i: (0, nspan - 1 - i, 0))
    n_heads, nspan = xw // MHDIM, tok // SPAN
    row = lambda n: pl.BlockSpec((SPAN, n), lambda i: (nspan - 1 - i, 0))
    whole = lambda *s: pl.BlockSpec(s, lambda i: (0,) * len(s))
    smem = pl.BlockSpec(memory_space=pltpu.SMEM)
    return pl.pallas_call(
        functools.partial(ssd_backward_kernel, n_heads),
        grid=(nspan,),
        in_specs=[
            smem, smem, row(xw), wide, row(128), row(xw),
            pl.BlockSpec((1, xw, NSTATE), lambda i: (nspan - 1 - i, 0, 0)),
            pl.BlockSpec((1, 1, 128), lambda i: (nspan - 1 - i, 0, 0)),
            whole(1, 128), whole(1, xw), whole(xw, NSTATE), whole(xw, NSTATE),
        ],
        out_specs=[row(xw), wide, row(128), whole(8, 128), whole(1, xw)],
        out_shape=[
            jax.ShapeDtypeStruct((tok, xw), f32),
            jax.ShapeDtypeStruct((n_p, tok, 128), f32),
            jax.ShapeDtypeStruct((tok, 128), f32),
            jax.ShapeDtypeStruct((8, 128), f32),
            jax.ShapeDtypeStruct((1, xw), f32),
        ],
        scratch_shapes=[pltpu.VMEM((xw, NSTATE), f32)],
        compiler_params=pltpu.CompilerParams(vmem_limit_bytes=VMEM_LIMIT),
        cost_estimate=pl.CostEstimate(
            flops=2 * tok * xw * NSTATE * 8, bytes_accessed=80_000_000, transcendentals=0
        ),
        name="ssd_backward",
    )(base, doc_starts, x, bc, dtp, dy, span_starts, start_decay, nega, skip, in_state, grad_state)


QB = 512
KB = 512


def sight(base_ref, starts_ref, q_first):
    q_pos = base_ref[0] + q_first + iota2((QB, 1), 0)
    low = jnp.zeros((QB, 1), jnp.int32)
    for i in range(starts_ref.shape[0]):
        low = jnp.where(starts_ref[i] <= q_pos, starts_ref[i], low)
    return jnp.broadcast_to(low, (QB, KB)), jnp.broadcast_to(q_pos, (QB, KB))


def seen(low, high, k_first):
    k_pos = k_first + iota2((QB, KB), 1)
    return (k_pos >= low) & (k_pos <= high)


def attend_kernel(scale, base_ref, starts_ref, q_ref, kv_ref, o_ref, lse_ref, k_ref, v_ref):
    i = pl.program_id(0)

    @pl.when(i == 0)
    def _():
        n_p, nz, rows, _ = kv_ref.shape
        kw = HDIM // n_p

        @pl.loop(0, nz)
        def _(z):
            parts = [kv_ref[q, z] for q in range(n_p)]
            for t in range(2):
                at = pl.ds(pl.multiple_of((2 * z + t) * rows, rows), rows)
                lo = 2 * kw * t
                k_ref[at, :] = jnp.concatenate([v[:, lo : lo + kw] for v in parts], axis=1)
                v_ref[at, :] = jnp.concatenate([v[:, lo + kw : lo + 2 * kw] for v in parts], axis=1)

    q = q_ref[...]
    low, high = sight(base_ref, starts_ref, i * QB)
    blocks = (base_ref[0] + (i + 1) * QB + KB - 1) // KB

    def turn(j, carry):
        m, l, acc = carry
        at = pl.ds(pl.multiple_of(j * KB, KB), KB)
        s = dot_nt(q, k_ref[at, :]) * scale
        s = jnp.where(seen(low, high, j * KB), s, neg_large)
        m_new = jnp.maximum(m, jnp.max(s, axis=1, keepdims=True))
        w = jnp.exp(s - m_new)
        r = jnp.exp(m - m_new)
        l = l * r + jnp.sum(w, axis=1, keepdims=True)
        return m_new, l, acc * r + dot_nn(w.astype(bf16), v_ref[at, :])

    m, l, acc = lax.fori_loop(
        0,
        blocks,
        turn,
        (jnp.full((QB, 1), 0.1 * neg_large, f32), jnp.zeros((QB, 1), f32), jnp.zeros((QB, HDIM), f32)),
    )
    o_ref[...] = acc / l
    lse_ref[...] = jnp.broadcast_to(m + jnp.log(l), (QB, 128))


def attend(base, doc_starts, q, kv):
    tok = q.shape[0]
    keys = kv.shape[1] * kv.shape[2] * 2
    row = pl.BlockSpec((QB, HDIM), lambda i: (i, 0))
    whole = lambda s: pl.BlockSpec(s, lambda i: (0,) * len(s))
    smem = pl.BlockSpec(memory_space=pltpu.SMEM)
    return pl.pallas_call(
        functools.partial(attend_kernel, HDIM ** (-0.5)),
        grid=(tok // QB,),
        in_specs=[smem, smem, row, whole(kv.shape)],
        out_specs=[row, row, whole((keys, HDIM)), whole((keys, HDIM))],
        out_shape=[jax.ShapeDtypeStruct((tok, HDIM), f32)] * 2
        + [jax.ShapeDtypeStruct((keys, HDIM), bf16)] * 2,
        compiler_params=pltpu.CompilerParams(vmem_limit_bytes=VMEM_LIMIT),
        cost_estimate=pl.CostEstimate(
            flops=4 * tok * keys * HDIM, bytes_accessed=30_000_000, transcendentals=0
        ),
        name="attend",
    )(base, doc_starts, q, kv)


def attend_back_kernel(
    scale, base_ref, starts_ref, q_ref, do_ref, o_ref, lse_ref, k_ref, v_ref,
    dq_ref, dkv_ref, dk_ref, dv_ref,
):
    i = pl.program_id(0)

    @pl.when(i == 0)
    def _():
        dk_ref[...] = jnp.zeros_like(dk_ref)
        dv_ref[...] = jnp.zeros_like(dv_ref)

    q, do = q_ref[...], do_ref[...]
    delta = jnp.sum(do.astype(f32) * o_ref[...], axis=1, keepdims=True)
    lse = lse_ref[:, 0:1]
    low, high = sight(base_ref, starts_ref, i * QB)
    blocks = (base_ref[0] + (i + 1) * QB + KB - 1) // KB

    def turn(j, dq):
        at = pl.ds(pl.multiple_of(j * KB, KB), KB)
        k, v = k_ref[at, :], v_ref[at, :]
        visible = seen(low, high, j * KB)
        s = dot_nt(q, k) * scale
        p = jnp.exp(jnp.where(visible, s - lse, neg_large))
        ds = (p * (dot_nt(do, v) - delta)).astype(bf16)
        dv_ref[at, :] += dot_tn(p.astype(bf16), do)
        dk_ref[at, :] += dot_tn(ds, q) * scale
        return dq + dot_nn(ds, k)

    dq_ref[...] = lax.fori_loop(0, blocks, turn, jnp.zeros((QB, HDIM), f32)) * scale

    @pl.when(i == pl.num_programs(0) - 1)
    def _():
        n_p, nz, rows, _ = dkv_ref.shape
        kw = HDIM // n_p

        @pl.loop(0, nz)
        def _(z):
            got = []
            for t in range(2):
                at = pl.ds(pl.multiple_of((2 * z + t) * rows, rows), rows)
                got += [dk_ref[at, :].astype(bf16), dv_ref[at, :].astype(bf16)]
            for q in range(n_p):
                cut = slice(q * kw, q * kw + kw)
                dkv_ref[q, z] = jnp.concatenate([v[:, cut] for v in got], axis=1)


def attend_back(base, doc_starts, q, do, o, lse, k, v, packed):
    tok = q.shape[0]
    row = pl.BlockSpec((QB, HDIM), lambda i: (i, 0))
    whole = lambda s: pl.BlockSpec(s, lambda i: (0,) * len(s))
    smem = pl.BlockSpec(memory_space=pltpu.SMEM)
    return pl.pallas_call(
        functools.partial(attend_back_kernel, HDIM ** (-0.5)),
        grid=(tok // QB,),
        in_specs=[smem, smem, row, row, row, row, whole(k.shape), whole(k.shape)],
        out_specs=[row, whole(packed)],
        out_shape=[
            jax.ShapeDtypeStruct((tok, HDIM), f32),
            jax.ShapeDtypeStruct(packed, bf16),
        ],
        scratch_shapes=[pltpu.VMEM(k.shape, f32), pltpu.VMEM(k.shape, f32)],
        compiler_params=pltpu.CompilerParams(vmem_limit_bytes=VMEM_LIMIT),
        cost_estimate=pl.CostEstimate(
            flops=10 * tok * k.shape[0] * HDIM, bytes_accessed=40_000_000, transcendentals=0
        ),
        name="attend_back",
    )(base, doc_starts, q, do, o, lse, k, v)


def one_at(shape, source, where=True):
    lane = iota2(shape, 1)
    return ((iota2(shape, 0) == source(lane)) & where).astype(bf16)


def eye(n):
    return one_at((n, n), lambda lane: lane)


def q_order(kw):
    hk = kw // 2
    return one_at(
        (HDIM, HDIM), lambda l: ((l % kw) // hk) * (HDIM // 2) + (l // kw) * hk + l % hk
    )


def bc_order(p, bw, n_p):
    return one_at((2 * n_p * bw, 2 * bw), lambda l: (l // bw) * (n_p * bw) + p * bw + l % bw)


def last_order(p, kw, n_heads, dt_rows):
    hk = kw // 2
    lane = iota2((HDIM, 128), 1)
    lane_dt = iota2((dt_rows, 128), 1)
    key = one_at((HDIM, 128), lambda l: (l // hk) * (HDIM // 2) + p * hk + l % hk, lane < kw)
    value = one_at((HDIM, 128), lambda l: p * kw + l - kw, (lane >= kw) & (lane < 2 * kw))
    step = one_at(
        (dt_rows, 128),
        lambda l: p * n_heads + l - 2 * kw,
        (lane_dt >= 2 * kw) & (lane_dt < 2 * kw + n_heads),
    )
    return key, value, step


def pack_kernel(
    x_ref, bc_ref, k_ref, v_ref, dt_ref, q_ref, z_ref, mout_ref, aout_ref, gate_ref, up_ref,
    down_ref, a_ref, b_ref, c_ref, d_ref, e_ref,
):
    n_p = a_ref.shape[0]
    xw, bw, kw = x_ref.shape[1] // n_p, bc_ref.shape[1] // (2 * n_p), HDIM // n_p
    n_heads, ff, aw = dt_ref.shape[1] // n_p, gate_ref.shape[1] // n_p, q_ref.shape[1] // n_p
    bc, key, value = bc_ref[...].astype(bf16), k_ref[...].astype(bf16), v_ref[...].astype(bf16)
    step = dt_ref[...].astype(bf16)
    order = q_order(kw)
    for p in range(n_p):
        cut = lambda ref, n: ref[:, p * n : p * n + n].astype(bf16)
        flip = lambda ref, n: dot_tn(ref[p * n : p * n + n, :].astype(bf16), eye(n)).astype(bf16)
        a_ref[p, :, :xw] = cut(x_ref, xw)
        a_ref[p, :, xw : xw + 2 * bw] = dot_nn(bc, bc_order(p, bw, n_p)).astype(bf16)
        s_key, s_value, s_step = last_order(p, kw, n_heads, dt_ref.shape[1])
        a_ref[p, :, xw + 2 * bw :] = (
            dot_nn(key, s_key) + dot_nn(value, s_value) + dot_nn(step, s_step)
        ).astype(bf16)
        b_ref[p, :, :HDIM] = dot_nn(cut(q_ref, aw), order).astype(bf16)
        b_ref[p, :, HDIM:] = cut(z_ref, xw)
        c_ref[p, :, :xw] = flip(mout_ref, xw)
        c_ref[p, :, xw:] = flip(aout_ref, aw)
        d_ref[p, :, :ff] = cut(gate_ref, ff)
        d_ref[p, :, ff:] = cut(up_ref, ff)
        e_ref[p] = flip(down_ref, ff)


def pack(n_p, *weights):
    x, bc, k, v, dt, q, z, mout, aout, gate, up, down = weights
    rows = x.shape[0]
    ff, xw = gate.shape[1] // n_p, x.shape[1] // n_p
    widths = (xw + bc.shape[1] // n_p + 128, HDIM + xw, xw + HDIM, 2 * ff, ff)
    vm = pl.BlockSpec(memory_space=pltpu.VMEM)
    return pl.pallas_call(
        pack_kernel,
        in_specs=[vm] * 12,
        out_specs=[vm] * 5,
        out_shape=[jax.ShapeDtypeStruct((n_p, rows, w), bf16) for w in widths],
        compiler_params=pltpu.CompilerParams(vmem_limit_bytes=VMEM_LIMIT),
        cost_estimate=pl.CostEstimate(flops=0, bytes_accessed=10_000_000, transcendentals=0),
        name="pack",
    )(*weights)


def unpack_kernel(
    a_ref, b_ref, c_ref, d_ref, e_ref, row_ref, grow_ref,
    x_ref, bc_ref, k_ref, v_ref, dt_ref, q_ref, z_ref, mout_ref, aout_ref, gate_ref, up_ref,
    down_ref, row_out, grow_out,
):
    row_out[...] = row_ref[...]
    grow_out[...] = grow_ref[...]
    n_p, rows = a_ref.shape[0], a_ref.shape[1]
    xw, bw, kw = x_ref.shape[1] // n_p, bc_ref.shape[1] // (2 * n_p), HDIM // n_p
    n_heads, ff, aw = dt_ref.shape[1] // n_p, gate_ref.shape[1] // n_p, q_ref.shape[1] // n_p
    order, turn = q_order(kw), eye(rows)
    bc, key = jnp.zeros(bc_ref.shape, f32), jnp.zeros(k_ref.shape, f32)
    value, step = jnp.zeros(v_ref.shape, f32), jnp.zeros(dt_ref.shape, f32)
    for p in range(n_p):
        cut = lambda n: slice(p * n, p * n + n)
        x_ref[:, cut(xw)] = a_ref[p, :, :xw].astype(f32)
        bc = bc + dot_nt(a_ref[p, :, xw : xw + 2 * bw], bc_order(p, bw, n_p))
        last = a_ref[p, :, xw + 2 * bw :]
        s_key, s_value, s_step = last_order(p, kw, n_heads, dt_ref.shape[1])
        key, value = key + dot_nt(last, s_key), value + dot_nt(last, s_value)
        step = step + dot_nt(last, s_step)
        q_ref[:, cut(aw)] = dot_nt(b_ref[p, :, :HDIM], order)
        z_ref[:, cut(xw)] = b_ref[p, :, HDIM:].astype(f32)
        mout_ref[cut(xw), :] = dot_tn(c_ref[p, :, :xw], turn)
        aout_ref[cut(aw), :] = dot_tn(c_ref[p, :, xw:], turn)
        gate_ref[:, cut(ff)] = d_ref[p, :, :ff].astype(f32)
        up_ref[:, cut(ff)] = d_ref[p, :, ff:].astype(f32)
        down_ref[cut(ff), :] = dot_tn(e_ref[p], turn)
    bc_ref[...] = bc
    k_ref[...], v_ref[...], dt_ref[...] = key, value, step


def unpack(pieces, like):
    vm = pl.BlockSpec(memory_space=pltpu.VMEM)
    return pl.pallas_call(
        unpack_kernel,
        in_specs=[vm] * 7,
        out_specs=[vm] * 14,
        out_shape=[jax.ShapeDtypeStruct(w.shape, f32) for w in like],
        compiler_params=pltpu.CompilerParams(vmem_limit_bytes=VMEM_LIMIT),
        cost_estimate=pl.CostEstimate(flops=0, bytes_accessed=10_000_000, transcendentals=0),
        name="unpack",
    )(*pieces)


def ffn_kernel(x_ref, w_ref, g_ref, gu_ref, act_ref, grad_ref, total):
    i = pl.program_id(0)
    ff = act_ref.shape[1]
    gu = dot_nn(x_ref[...], w_ref[...])
    gu_ref[...] = gu
    gate = gu[:, :ff]
    act = (gate * jax.nn.sigmoid(gate) * gu[:, ff:]).astype(bf16)
    act_ref[...] = act
    part = dot_tn(g_ref[...], act)

    @pl.when(i == 0)
    def _():
        total[...] = part

    @pl.when(i > 0)
    def _():
        total[...] += part

    @pl.when(i == pl.num_programs(0) - 1)
    def _():
        grad_ref[...] = total[...].astype(bf16)


def ffn_forward(x, w, g):
    tok, width = x.shape
    ff, block = w.shape[1] // 2, 256
    row = lambda n: pl.BlockSpec((block, n), lambda i: (i, 0))
    whole = lambda *s: pl.BlockSpec(s, lambda i: (0,) * len(s))
    return pl.pallas_call(
        ffn_kernel,
        grid=(tok // block,),
        in_specs=[row(width), whole(*w.shape), row(width)],
        out_specs=[row(2 * ff), row(ff), whole(width, ff)],
        out_shape=[
            jax.ShapeDtypeStruct((tok, 2 * ff), f32),
            jax.ShapeDtypeStruct((tok, ff), bf16),
            jax.ShapeDtypeStruct((width, ff), bf16),
        ],
        scratch_shapes=[pltpu.VMEM((width, ff), f32)],
        compiler_params=pltpu.CompilerParams(vmem_limit_bytes=VMEM_LIMIT),
        cost_estimate=pl.CostEstimate(
            flops=6 * tok * width * ff, bytes_accessed=25_000_000, transcendentals=0
        ),
        name="ffn_forward",
    )(x, w, g)


def at_rows(first, count):
    return pl.ds(pl.multiple_of(first, count), count)


def place():
    return lax.axis_index("z"), lax.axis_index("p"), lax.axis_index("head")


def hop(p, d):
    x, y = lax.rem(p, 2), p // 2
    return lax.rem(y + d // 2, 2) * 2 + lax.rem(x + d % 2, 2)


def chip(z, p, c):
    return (z, p, c)


def meet(others):
    barrier = pltpu.get_barrier_semaphore()
    for other in others:
        pl.semaphore_signal(barrier, inc=1, device_id=other, device_id_type=MESH)
    pl.semaphore_wait(barrier, len(others))


def send(src, dst, send_sem, recv_sem, to):
    copy = pltpu.make_async_remote_copy(
        src_ref=src, dst_ref=dst, send_sem=send_sem, recv_sem=recv_sem,
        device_id=to, device_id_type=MESH,
    )
    copy.start()
    return copy


HOPS = (3, 1, 2)


def z_chain(ref, up_sems, down_sems, since=0):
    z, p, c = place()
    nz = ref.shape[0]

    def block_up(k):
        at = ref.at[z - k]
        return pltpu.make_async_remote_copy(
            src_ref=at, dst_ref=at, send_sem=up_sems.at[0, k], recv_sem=up_sems.at[1, k],
            device_id=chip(z + 1, p, c), device_id_type=MESH,
        )

    def block_down(k):
        at = ref.at[z + k]
        return pltpu.make_async_remote_copy(
            src_ref=at, dst_ref=at, send_sem=down_sems.at[0, k], recv_sem=down_sems.at[1, k],
            device_id=chip(z - 1, p, c), device_id_type=MESH,
        )

    def got_up(k):
        at = ref.at[z - k]
        pltpu.make_async_remote_copy(
            src_ref=at, dst_ref=at, send_sem=up_sems.at[0, k - 1], recv_sem=up_sems.at[1, k - 1],
            device_id=chip(z - 1, p, c), device_id_type=MESH,
        ).wait_recv()

    def got_down(k):
        at = ref.at[z + k]
        pltpu.make_async_remote_copy(
            src_ref=at, dst_ref=at, send_sem=down_sems.at[0, k - 1],
            recv_sem=down_sems.at[1, k - 1],
            device_id=chip(z + 1, p, c), device_id_type=MESH,
        ).wait_recv()

    def stage(k):
        if k > since:

            @pl.when(z - k >= 0)
            def _():
                got_up(k)

        @pl.when((z - k >= 0) & (z + 1 < nz))
        def _():
            block_up(k).start()

        if k > since:

            @pl.when(z + k < nz)
            def _():
                got_down(k)

        @pl.when((z + k < nz) & (z > 0))
        def _():
            block_down(k).start()

    def done():
        for k in range(since, nz):

            @pl.when((z - k >= 0) & (z + 1 < nz))
            def _():
                block_up(k).wait_send()

            @pl.when((z + k < nz) & (z > 0))
            def _():
                block_down(k).wait_send()

    return stage, done


def z_hop(ref, k, sems):
    z, p, c = place()
    nz = ref.shape[0]

    def move(slot, i, to):
        return pltpu.make_async_remote_copy(
            src_ref=ref.at[slot], dst_ref=ref.at[slot], send_sem=sems.at[0, i],
            recv_sem=sems.at[1, i], device_id=chip(to, p, c), device_id_type=MESH,
        )

    goes_up, goes_down = (z - k >= 0) & (z + 1 < nz), (z + k < nz) & (z > 0)

    @pl.when(goes_up)
    def _():
        move(z - k, 0, z + 1).start()

    @pl.when(goes_down)
    def _():
        move(z + k, 1, z - 1).start()

    def end():
        @pl.when(z - k - 1 >= 0)
        def _():
            move(z - k - 1, 0, z - 1).wait_recv()

        @pl.when(z + k + 1 < nz)
        def _():
            move(z + k + 1, 1, z + 1).wait_recv()

        @pl.when(goes_up)
        def _():
            move(z - k, 0, z + 1).wait_send()

        @pl.when(goes_down)
        def _():
            move(z + k, 1, z - 1).wait_send()

    return end


def share(block, part, far_sems, near_sems, own_sems=None):
    z, p, c = place()
    other = chip(z, p, 1 - c)
    x, y, far = hop(p, 1), hop(p, 2), hop(p, 3)

    def far_send(ref, i, q):
        return send(ref, ref, far_sems.at[0, i], far_sems.at[1, i], chip(z, q, c))

    def near_send(q, i):
        return send(block(q), block(q), near_sems.at[0, i], near_sems.at[1, i], other)

    out = [far_send(block(p), 0, x), far_send(block(p), 1, y)]
    near = []
    if own_sems is not None:
        near.append(send(block(p), block(p), own_sems.at[0], own_sems.at[1], other))

    def middle():
        out[0].wait_recv()
        out.append(far_send(part(x, 0), 2, y))
        out[1].wait_recv()
        out.append(far_send(part(y, 1), 3, x))
        if near_sems is not None:
            near.append(near_send(x, 0))
            near.append(near_send(y, 1))

    def end():
        out[2].wait_recv()
        out[3].wait_recv()
        if near_sems is not None:
            near.append(near_send(far, 2))
        for copy in out:
            copy.wait_send()
        for copy in near:
            copy.wait()

    return middle, end


def share_rows(full_ref, half, own_sems, far_sems, near_sems):
    z, p, c = place()
    rows = lambda q: (q * 2 + c) * half
    return share(
        lambda q: full_ref.at[at_rows(rows(q), half), :],
        lambda q, i: full_ref.at[at_rows(rows(q) + i * (half // 2), half // 2), :],
        far_sems, near_sems, own_sems,
    )


def reduce_blocks(pairs, part, keep, sib_out, sib_in, out, relay, came, near_sems, far_sems):
    z, p, c = place()
    other = chip(z, p, 1 - c)
    half, width = keep.shape[1], keep.shape[2]
    tile, quarter = part.shape[1], half // 2
    x, y = chip(z, hop(p, 1), c), chip(z, hop(p, 2), c)
    first, second = at_rows(0, quarter), at_rows(quarter, quarter)
    near, far = [], []

    def far_send(src, dst, i, to):
        far.append(send(src, dst, far_sems.at[0, i], far_sems.at[1, i], to))

    def total_of(i, rows, extra=None):
        @pl.loop(0, quarter // 16)
        def _(r):
            at = at_rows(rows + r * 16, 16)
            total = keep[i, at, :] + sib_in[i, at, :].astype(f32)
            if extra is not None:
                total = total + relay[extra, at_rows(r * 16, 16), :].astype(f32)
            out[i, at, :] = total.astype(bf16)

    def pass_on(i):
        near[i].wait_recv()
        if i == 0:
            total_of(0, 0)
            far_send(out.at[0, first, :], relay.at[0], 0, x)
            total_of(0, quarter)
            far_send(out.at[0, second, :], relay.at[1], 1, y)
        if i == 1:
            total_of(1, 0)
            far_send(out.at[1, first, :], came.at[0, first, :], 2, x)
        if i == 2:
            total_of(2, quarter)
            far_send(out.at[2, second, :], came.at[1, second, :], 3, y)

    for i, d in enumerate((3, 1, 2, 0)):
        rows = at_rows(hop(p, d) * (2 * half), 2 * half)

        @pl.loop(0, width // tile)
        def _(n):
            cols = at_rows(n * tile, tile)
            total = dot_nt(pairs[0][0][rows, :], pairs[0][1][cols, :])
            for left, right in pairs[1:]:
                total = total + dot_nt(left[rows, :], right[cols, :])
            part[...] = total
            keep[i, :, cols] = part[at_rows(c * half, half), :]
            sib_out[i, :, cols] = part[at_rows((1 - c) * half, half), :].astype(bf16)

        near.append(
            send(sib_out.at[i], sib_in.at[i], near_sems.at[0, i], near_sems.at[1, i], other)
        )
        if i:
            pass_on(i - 1)

    def middle():
        far[1].wait_recv()
        total_of(1, quarter, 1)
        far_send(out.at[1, second, :], came.at[0, second, :], 4, x)
        far[0].wait_recv()
        total_of(2, 0, 0)
        far_send(out.at[2, first, :], came.at[1, first, :], 5, y)

    def finish():
        near[3].wait_recv()
        for copy in far[2:]:
            copy.wait_recv()

    def total_rows(at):
        total = keep[3, at, :] + sib_in[3, at, :].astype(f32)
        return total + came[0, at, :].astype(f32) + came[1, at, :].astype(f32)

    def done():
        for copy in near + far:
            copy.wait_send()

    return total_rows, middle, finish, done


def greet():
    z, p, c = place()
    meet([chip(z, p, 1 - c)] + [chip(z, hop(p, d), c) for d in HOPS])


def rms(rows):
    return lax.rsqrt(jnp.mean(rows * rows, axis=1, keepdims=True) + eps_norm)


def mid_kernel(
    left, right, resid, gain, e_given, mid_ref, full_ref, e_ref,
    part, keep, sib_out, sib_in, out, relay, came, n_sems, f_sems, own_sems, far_sems, near_sems,
    up_sems, down_sems,
):
    z, p, c = place()
    nz = e_ref.shape[0]
    meet(
        [chip(z, p, 1 - c)]
        + [chip(z, hop(p, d), c) for d in HOPS]
        + [chip(lax.rem(z + d, nz), p, c) for d in (1, nz - 1)]
    )
    stage, chain_done = z_chain(e_ref, up_sems, down_sems, 2)
    stage(2)
    half = keep.shape[1]
    total_rows, middle, finish, done = reduce_blocks(
        [(left, right)], part, keep, sib_out, sib_in, out, relay, came, n_sems, f_sems
    )
    middle()
    finish()
    g = gain[...]

    @pl.loop(0, half // 16)
    def _(r):
        at = at_rows(r * 16, 16)
        mid = resid[at, :] + total_rows(at)
        mid_ref[at, :] = mid
        full_ref[at_rows((p * 2 + c) * half + r * 16, 16), :] = (mid * rms(mid) * g).astype(bf16)

    share_middle, share_end = share_rows(full_ref, half, own_sems, far_sems, near_sems)
    share_middle()
    for k in range(3, nz):
        stage(k)
    done()
    share_end()
    chain_done()


def two_kernel(
    left, right, mid_own, grad_own, gain, dmid_ref, ggain_ref, full_ref,
    part, keep, sib_out, sib_in, out, relay, came, n_sems, f_sems, own_sems, far_sems, near_sems,
):
    greet()
    z, p, c = place()
    half = keep.shape[1]
    total_rows, middle, finish, done = reduce_blocks(
        [(left, right)], part, keep, sib_out, sib_in, out, relay, came, n_sems, f_sems
    )
    middle()
    finish()
    g = gain[...]
    ggain_ref[...] = jnp.zeros_like(ggain_ref)

    @pl.loop(0, half // 16)
    def _(r):
        at = at_rows(r * 16, 16)
        d_two, mid = total_rows(at), mid_own[at, :]
        scale = rms(mid)
        w = d_two * g
        d_mid = grad_own[at, :] + scale * w - mid * (scale * scale * scale) * jnp.mean(
            w * mid, axis=1, keepdims=True
        )
        ggain_ref[...] += jnp.sum(d_two * mid * scale, axis=0, keepdims=True)
        dmid_ref[at, :] = d_mid
        full_ref[at_rows((p * 2 + c) * half + r * 16, 16), :] = d_mid.astype(bf16)

    share_middle, share_end = share_rows(full_ref, half, own_sems, far_sems, near_sems)
    share_middle()
    done()
    share_end()


def one_kernel(
    n, left_a, right_a, left_b, right_b, hidden_own, dmid_own, gain, act, w_act, mid_own, rest,
    *refs
):
    ins, (grad_ref, block_ref, sums_ref), outs = refs[:n], refs[n : n + 3], refs[n + 3 : 2 * n + 3]
    first, second = refs[2 * n + 3 : 2 * n + 12], refs[2 * n + 12 : 2 * n + 21]
    own_sems, ggain_ref, flat, flat_came, z_sems, p_sems, c_sems, w_sems, loc_sems = refs[
        2 * n + 21 :
    ]
    z, p, c = place()
    nz = flat_came.shape[0] + 1
    ups = [chip(lax.rem(z + d, nz), p, c) for d in range(1, nz)]
    meet([chip(z, p, 1 - c)] + [chip(z, hop(p, d), c) for d in HOPS] + ups)
    half = hidden_own.shape[0]
    total_rows, middle, finish, done = reduce_blocks(
        [(left_a, right_a), (left_b, right_b)], *first
    )
    middle()
    total_out, middle_out, finish_out, done_out = reduce_blocks([(act, w_act)], *second)
    moved = swap_begin(ins, outs, w_sems, loc_sems)
    g = gain[...]
    ggain_ref[...] = jnp.zeros_like(ggain_ref)
    middle_out()
    finish()

    @pl.loop(0, half // 16)
    def _(r):
        at = at_rows(r * 16, 16)
        d_one, hid = total_rows(at), hidden_own[at, :]
        scale = rms(hid)
        w = d_one * g
        d_in = dmid_own[at, :] + scale * w - hid * (scale * scale * scale) * jnp.mean(
            w * hid, axis=1, keepdims=True
        )
        ggain_ref[...] += jnp.sum(d_one * hid * scale, axis=0, keepdims=True)
        grad_ref[at_rows(c * half + r * 16, 16), :] = d_in

    mine = at_rows(c * half, half)
    other = chip(z, p, 1 - c)
    copies = [
        send(grad_ref.at[mine, :], grad_ref.at[mine, :], own_sems.at[0, 0], own_sems.at[1, 0], other)
    ]
    g_rows = ggain_ref.shape[1] // 128
    for i in range(g_rows):
        flat[i : i + 1, :] = ggain_ref[:, i * 128 : i * 128 + 128]
    flat[g_rows:, :] = rest[...]
    up = [
        send(flat, flat_came.at[d], z_sems.at[0, d], z_sems.at[1, d], ups[d])
        for d in range(nz - 1)
    ]
    total = flat[...]
    for d in range(nz - 1):
        up[d].wait_recv()
        total = total + flat_came[d]
    sums_ref[c, p] = total
    around = [
        send(
            sums_ref.at[c, p], sums_ref.at[c, p], p_sems.at[0, i], p_sems.at[1, i],
            chip(z, hop(p, d), c),
        )
        for i, d in enumerate(HOPS)
    ]
    finish_out()

    @pl.loop(0, half // 16)
    def _(r):
        at = at_rows(r * 16, 16)
        block_ref[at_rows(c * half + r * 16, 16), :] = mid_own[at, :] + total_out(at)

    copies.append(
        send(block_ref.at[mine, :], block_ref.at[mine, :], own_sems.at[0, 1], own_sems.at[1, 1], other)
    )
    for copy in around:
        copy.wait_recv()
    copies.append(send(sums_ref.at[c], sums_ref.at[c], c_sems.at[0], c_sems.at[1], other))
    done()
    done_out()
    for copy in up + around:
        copy.wait_send()
    for copy in copies + moved:
        copy.wait()


VM = pl.BlockSpec(memory_space=pltpu.VMEM)
ANYWHERE = pl.BlockSpec(memory_space=pl.ANY)


def swap_begin(ins, outs, sems, loc_sems):
    z, p, c = place()
    copies = []
    for j, (src, dst) in enumerate(zip(ins, outs)):
        for i, d in enumerate(HOPS):
            q = hop(p, d)
            copies.append(
                send(src.at[q], dst.at[p], sems.at[0, j, i], sems.at[1, j, i], chip(z, q, c))
            )
        local = pltpu.make_async_copy(src.at[p], dst.at[p], loc_sems.at[j])
        local.start()
        copies.append(local)
    return copies


def swap_sems(n):
    return [pltpu.SemaphoreType.DMA((2, n, 3)), pltpu.SemaphoreType.DMA((n,))]


def reduce_scratch(half, width):
    return [
        pltpu.VMEM((2 * half, 512), f32),
        pltpu.VMEM((4, half, width), f32),
        pltpu.VMEM((4, half, width), bf16),
        pltpu.VMEM((4, half, width), bf16),
        pltpu.VMEM((3, half, width), bf16),
        pltpu.VMEM((2, half // 2, width), bf16),
        pltpu.VMEM((2, half, width), bf16),
        pltpu.SemaphoreType.DMA((2, 4)),
        pltpu.SemaphoreType.DMA((2, 6)),
    ]


SHARE_SEMS = [
    pltpu.SemaphoreType.DMA((2,)),
    pltpu.SemaphoreType.DMA((2, 4)),
    pltpu.SemaphoreType.DMA((2, 3)),
]


def plane_call(kernel, name, number, args, shapes, scratch, nbytes=150_000_000, moved=()):
    n = len(moved)
    if n:
        kernel = functools.partial(kernel, n)
        scratch = scratch + swap_sems(n)
    return pl.pallas_call(
        kernel,
        in_specs=[VM] * (len(args) + n),
        out_specs=[VM] * len(shapes) + [ANYWHERE] * n,
        out_shape=[jax.ShapeDtypeStruct(s, t) for s, t in shapes]
        + [jax.ShapeDtypeStruct(m.shape, m.dtype) for m in moved],
        scratch_shapes=scratch,
        compiler_params=pltpu.CompilerParams(
            collective_id=number, has_side_effects=True, vmem_limit_bytes=VMEM_LIMIT
        ),
        cost_estimate=pl.CostEstimate(flops=0, bytes_accessed=nbytes, transcendentals=0),
        name=name,
    )(*args, *moved)


def mid_step(mixed, w, resid_own, gain, piece):
    tok, width = mixed.shape[0], w.shape[0]
    half, nz = resid_own.shape[0], piece.shape[0]
    return pl.pallas_call(
        mid_kernel,
        in_specs=[VM] * 4 + [ANYWHERE],
        out_specs=[VM] * 2 + [ANYWHERE],
        out_shape=[
            jax.ShapeDtypeStruct((half, width), f32),
            jax.ShapeDtypeStruct((tok, width), bf16),
            jax.ShapeDtypeStruct(piece.shape, bf16),
        ],
        scratch_shapes=reduce_scratch(half, width)
        + SHARE_SEMS
        + [pltpu.SemaphoreType.DMA((2, nz))] * 2,
        input_output_aliases={4: 2},
        compiler_params=pltpu.CompilerParams(
            collective_id=1, has_side_effects=True, vmem_limit_bytes=VMEM_LIMIT
        ),
        cost_estimate=pl.CostEstimate(flops=0, bytes_accessed=150_000_000, transcendentals=0),
        name="mid_step",
    )(mixed, w, resid_own, gain, piece)


def two_step(d_gu, w, mid_own, grad_own, gain):
    tok, width = d_gu.shape[0], w.shape[0]
    half = mid_own.shape[0]
    return plane_call(
        two_kernel, "two_step", 2, (d_gu, w, mid_own, grad_own, gain),
        [((half, width), f32), ((1, width), f32), ((tok, width), bf16)],
        reduce_scratch(half, width) + SHARE_SEMS,
    )


def one_step(
    d_a, w_a, d_b, w_b, hidden_own, dmid_own, gain, act, w_act, mid_own, rest, nz, n_p, moved
):
    width = w_a.shape[0]
    half = hidden_own.shape[0]
    flat = (width // 128 + rest.shape[0], 128)
    dma = pltpu.SemaphoreType.DMA
    return plane_call(
        one_kernel, "one_step", 3,
        (d_a, w_a, d_b, w_b, hidden_own, dmid_own, gain, act, w_act, mid_own, rest),
        [((2 * half, width), f32), ((2 * half, width), f32), ((2, n_p) + flat, f32)],
        reduce_scratch(half, width)
        + reduce_scratch(half, width)
        + [
            dma((2, 2)), pltpu.VMEM((1, width), f32), pltpu.VMEM(flat, f32),
            pltpu.VMEM((nz - 1,) + flat, f32), dma((2, nz - 1)), dma((2, 3)), dma((2,)),
        ],
        moved=moved,
    )


HALO = 16


def open_kernel(n, *refs):
    hid, gains_ref, a_ref = refs[:3]
    w_refs = refs[3 : 3 + n]
    gain_out, full_ref, a_out = refs[3 + n : 6 + n]
    w_outs = refs[6 + n : 6 + 2 * n]
    (
        g_vec, gz_sems, gp_sems, a_sems, up_sems, down_sems, own_sems, far_sems, near_sems,
        w_sems, loc_sems, halo_sems,
    ) = refs[6 + 2 * n :]
    z, p, c = place()
    nz, half, rows = a_out.shape[0], hid.shape[0], a_ref.shape[1]
    tok = full_ref.shape[0] - HALO
    ups = [chip(lax.rem(z + d, nz), p, c) for d in range(1, nz)]
    flat = [chip(z, hop(p, d), c) for d in HOPS]
    meet(ups + flat + [chip(z, p, 1 - c)])
    gain_out[p, z] = gains_ref[...]
    gz = [
        send(gain_out.at[p, z], gain_out.at[p, z], gz_sems.at[0, d], gz_sems.at[1, d], ups[d])
        for d in range(nz - 1)
    ]
    to_plane = []
    for i, d in enumerate(HOPS):
        to_plane.append(
            send(a_ref.at[hop(p, d)], a_out.at[z, p], a_sems.at[0, i], a_sems.at[1, i], flat[i])
        )
    local = [pltpu.make_async_copy(a_ref.at[p], a_out.at[z, p], loc_sems.at[n])]
    for j in range(n):
        local.append(pltpu.make_async_copy(w_refs[j].at[p], w_outs[j].at[p], loc_sems.at[j]))
    for copy in local:
        copy.start()

    for copy in gz:
        copy.wait_recv()
    gp = [
        send(gain_out.at[p], gain_out.at[p], gp_sems.at[0, i], gp_sems.at[1, i], flat[i])
        for i in range(3)
    ]
    stage, chain_done = z_chain(a_out, up_sems, down_sems)
    for copy in to_plane:
        copy.wait_recv()
    local[0].wait()
    stage(0)
    for copy in gp:
        copy.wait_recv()
    for i in range(nz):
        for j in range(gain_out.shape[0]):
            first = (i * gain_out.shape[0] + j) * rows
            g_vec[:, first : first + rows] = gain_out[j, i][:, :rows]
    g = g_vec[0:1, :]

    @pl.loop(0, half // 16)
    def _(r):
        rows_in = hid[at_rows(r * 16, 16), :]
        full_ref[at_rows((p * 2 + c) * half + r * 16, 16), :] = (
            rows_in * rms(rows_in) * g
        ).astype(bf16)

    share_middle, share_end = share_rows(full_ref, half, own_sems, far_sems, near_sems)

    share_middle()
    if nz > 2:
        stage(1)
    moved = []
    for j in range(n):
        for i, d in enumerate(HOPS):
            moved.append(
                send(
                    w_refs[j].at[hop(p, d)], w_outs[j].at[p], w_sems.at[0, j, i],
                    w_sems.at[1, j, i], flat[i],
                )
            )
    share_end()
    halo_from = full_ref.at[at_rows(tok - HALO, HALO), :]
    halo_to = full_ref.at[at_rows(tok, HALO), :]

    def halo(to):
        return pltpu.make_async_remote_copy(
            src_ref=halo_from, dst_ref=halo_to, send_sem=halo_sems.at[0],
            recv_sem=halo_sems.at[1], device_id=to, device_id_type=MESH,
        )

    @pl.when(z + 1 < nz)
    def _():
        halo(chip(z + 1, p, c)).start()

    @pl.when(z == 0)
    def _():
        full_ref[at_rows(tok, HALO), :] = jnp.zeros((HALO, full_ref.shape[1]), bf16)

    for k in range(2, nz):
        stage(k)

    @pl.when(z > 0)
    def _():
        halo(chip(z - 1, p, c)).wait_recv()

    @pl.when(z + 1 < nz)
    def _():
        halo(chip(z + 1, p, c)).wait_send()

    chain_done()
    for copy in moved + local[1:]:
        copy.wait()
    for copy in gz + gp + to_plane:
        copy.wait_send()


def open_step(hid, gains, piece, rest, tok, nz):
    width, n, n_p = hid.shape[1], len(rest), piece.shape[0]
    anywhere = pl.BlockSpec(memory_space=pl.ANY)
    dma = pltpu.SemaphoreType.DMA
    return pl.pallas_call(
        functools.partial(open_kernel, n),
        in_specs=[VM] * (n + 3),
        out_specs=[VM, VM] + [anywhere] * (n + 1),
        out_shape=[
            jax.ShapeDtypeStruct((n_p, nz) + gains.shape, f32),
            jax.ShapeDtypeStruct((tok + HALO, width), bf16),
            jax.ShapeDtypeStruct((nz,) + piece.shape, bf16),
        ]
        + [jax.ShapeDtypeStruct(r.shape, bf16) for r in rest],
        scratch_shapes=[
            pltpu.VMEM((8, width), f32), dma((2, nz - 1)), dma((2, 3)), dma((2, 3)), dma((2, nz)),
            dma((2, nz)),
        ]
        + SHARE_SEMS
        + [dma((2, n, 3)), dma((n + 1,)), dma((2,))],
        compiler_params=pltpu.CompilerParams(
            collective_id=4, has_side_effects=True, vmem_limit_bytes=VMEM_LIMIT
        ),
        cost_estimate=pl.CostEstimate(flops=0, bytes_accessed=250_000_000, transcendentals=0),
        name="open_step",
    )(hid, gains, piece, *rest)


def gather_bc_kernel(
    x_ref, kv_ref, grad_ref, e_ref, full_ref, kvz_ref, g_ref, e_out,
    far_sems, near_sems, z_sems, e_sems, loc_sems, own_g, far_g, near_g,
):
    z, p, c = place()
    nz = kvz_ref.shape[0]
    other = chip(z, p, 1 - c)
    meet(
        [other]
        + [chip(z, hop(p, d), c) for d in HOPS]
        + [chip(lax.rem(z + d, nz), p, c) for d in range(1, nz)]
    )
    local = pltpu.make_async_copy(e_ref, e_out.at[z], loc_sems.at[0])
    local.start()
    kvz_ref[z] = kv_ref[...]

    def up(d):
        return pltpu.make_async_remote_copy(
            src_ref=kv_ref, dst_ref=kvz_ref.at[z], send_sem=z_sems.at[0, d - 1],
            recv_sem=z_sems.at[1, d - 1], device_id=chip(z + d, p, c), device_id_type=MESH,
        )

    for d in range(1, nz):

        @pl.when(z + d < nz)
        def _():
            up(d).start()

    half = x_ref.shape[0] // 2
    full_ref[p] = x_ref[...]
    bc_middle, bc_end = share(
        lambda q: full_ref.at[q, at_rows(c * half, half), :],
        lambda q, i: full_ref.at[q, at_rows(c * half + i * (half // 2), half // 2), :],
        far_sems, near_sems,
    )
    local.wait()
    e_end = z_hop(e_out, 0, e_sems)
    bc_middle()
    g_half = grad_ref.shape[0]
    g_ref[at_rows((p * 2 + c) * g_half, g_half), :] = grad_ref[...].astype(bf16)
    g_middle, g_end = share_rows(g_ref, g_half, own_g, far_g, near_g)
    bc_end()
    g_middle()
    for d in range(1, nz):

        @pl.when(z - d >= 0)
        def _():
            pltpu.make_async_remote_copy(
                src_ref=kv_ref, dst_ref=kvz_ref.at[z - d], send_sem=z_sems.at[0, d - 1],
                recv_sem=z_sems.at[1, d - 1], device_id=chip(z - d, p, c), device_id_type=MESH,
            ).wait_recv()

        @pl.when(z + d < nz)
        def _():
            kvz_ref[z + d] = jnp.zeros(kv_ref.shape, kv_ref.dtype)
            up(d).wait_send()

    g_end()
    e_end()


def gather_bc(x, at, n_p, kv, nz, grad, piece):
    tok = x.shape[0]
    dma = pltpu.SemaphoreType.DMA
    whole = lambda s: pl.BlockSpec(s, lambda i: (0,) * len(s))
    return pl.pallas_call(
        gather_bc_kernel,
        grid=(1,),
        in_specs=[
            pl.BlockSpec((tok, 128), lambda i: (0, at)), whole(kv.shape), whole(grad.shape),
            whole(piece.shape),
        ],
        out_specs=[
            whole((n_p, tok, 128)), whole((nz,) + kv.shape), whole((tok, grad.shape[1])),
            ANYWHERE,
        ],
        out_shape=[
            jax.ShapeDtypeStruct((n_p, tok, 128), bf16),
            jax.ShapeDtypeStruct((nz,) + kv.shape, bf16),
            jax.ShapeDtypeStruct((tok, grad.shape[1]), bf16),
            jax.ShapeDtypeStruct((nz,) + piece.shape, bf16),
        ],
        scratch_shapes=[dma((2, 4)), dma((2, 3)), dma((2, nz - 1)), dma((2, 2)), dma((1,))]
        + SHARE_SEMS,
        compiler_params=pltpu.CompilerParams(
            collective_id=5, has_side_effects=True, vmem_limit_bytes=VMEM_LIMIT
        ),
        cost_estimate=pl.CostEstimate(flops=0, bytes_accessed=40_000_000, transcendentals=0),
        name="gather_bc",
    )(x, kv, grad, piece)


def carry_kernel(
    state_ref, rate_ref, kvz_ref, e_given, in_ref, kv_ref, rates_ref, e_ref,
    low, came, factor, s_sems, r_sems, p_sems, e_sems,
):
    z, p, c = place()
    nz = kvz_ref.shape[0]
    ups = [chip(lax.rem(z + d, nz), p, c) for d in range(1, nz)]
    meet([chip(z, hop(p, d), c) for d in (1, 2)] + ups)
    low[...] = state_ref[...].astype(bf16)
    rates_ref[z] = rate_ref[...]
    rates = [
        send(rates_ref.at[z], rates_ref.at[z], r_sems.at[0, d], r_sems.at[1, d], ups[d])
        for d in range(nz - 1)
    ]

    def up(d):
        return pltpu.make_async_remote_copy(
            src_ref=low, dst_ref=came.at[d - 1], send_sem=s_sems.at[0, d - 1],
            recv_sem=s_sems.at[1, d - 1], device_id=chip(z + d, p, c), device_id_type=MESH,
        )

    for d in range(1, nz):

        @pl.when(z + d < nz)
        def _():
            up(d).start()

    e_end = z_hop(e_ref, 1, e_sems)
    kv_ref[p] = kvz_ref[...]
    kv_middle, kv_end = share(
        lambda q: kv_ref.at[q],
        lambda q, i: kv_ref.at[q, pl.ds(i * (nz // 2), nz // 2)],
        p_sems, None,
    )
    in_ref[...] = jnp.zeros_like(in_ref)
    factor[...] = jnp.ones_like(factor)
    lane_head, row_head = head_maps(state_ref.shape[0])
    kv_middle()
    for copy in rates:
        copy.wait_recv()
    for d in range(1, nz):

        @pl.when(z - d >= 0)
        def _():
            pltpu.make_async_remote_copy(
                src_ref=low, dst_ref=came.at[d - 1], send_sem=s_sems.at[0, d - 1],
                recv_sem=s_sems.at[1, d - 1], device_id=chip(z - d, p, c), device_id_type=MESH,
            ).wait_recv()
            scale = jnp.sum(row_head * factor[0:1, :], axis=1, keepdims=True)
            in_ref[...] += scale * came[d - 1].astype(f32)
            factor[...] = factor[...] * rates_ref[z - d]

        @pl.when(z + d < nz)
        def _():
            up(d).wait_send()

    kv_end()
    e_end()
    for copy in rates:
        copy.wait_send()


def carry_step(state, rate, kvz, n_p, piece):
    nz = kvz.shape[0]
    dma = pltpu.SemaphoreType.DMA
    return pl.pallas_call(
        carry_kernel,
        in_specs=[VM] * 3 + [ANYWHERE],
        out_specs=[VM] * 3 + [ANYWHERE],
        out_shape=[
            jax.ShapeDtypeStruct(state.shape, f32),
            jax.ShapeDtypeStruct((n_p,) + kvz.shape, bf16),
            jax.ShapeDtypeStruct((nz,) + rate.shape, f32),
            jax.ShapeDtypeStruct(piece.shape, bf16),
        ],
        scratch_shapes=[
            pltpu.VMEM(state.shape, bf16),
            pltpu.VMEM((nz - 1,) + state.shape, bf16),
            pltpu.VMEM(rate.shape, f32),
            dma((2, nz - 1)), dma((2, nz - 1)), dma((2, 4)), dma((2, 2)),
        ],
        input_output_aliases={3: 3},
        compiler_params=pltpu.CompilerParams(
            collective_id=8, has_side_effects=True, vmem_limit_bytes=VMEM_LIMIT
        ),
        cost_estimate=pl.CostEstimate(flops=0, bytes_accessed=80_000_000, transcendentals=0),
        name="carry_step",
    )(state, rate, kvz, piece)


def reduce_bc_kernel(n, x_ref, dkv_ref, dx_ref, slope_ref, *refs):
    ins, (out_ref, own_ref, next_ref), outs = refs[:n], refs[n : n + 3], refs[n + 3 : 2 * n + 3]
    (
        sib_out, sib_in, out, came, z_came, first, n_sems, f_sems, own_sems, z_sems, h_sems,
        w_sems, loc_sems,
    ) = refs[2 * n + 3 :]
    z, p, c = place()
    nz = dkv_ref.shape[0]
    half = x_ref.shape[1] // 2
    xw = dx_ref.shape[1]
    other = chip(z, p, 1 - c)
    meet(
        [other]
        + [chip(z, hop(p, d), c) for d in HOPS]
        + [chip(lax.rem(z + d, nz), p, c) for d in range(1, nz)]
    )

    def down(d):
        return pltpu.make_async_remote_copy(
            src_ref=dkv_ref.at[z - d], dst_ref=z_came.at[d - 1], send_sem=z_sems.at[0, d - 1],
            recv_sem=z_sems.at[1, d - 1], device_id=chip(z - d, p, c), device_id_type=MESH,
        )

    for d in range(1, nz):

        @pl.when(z - d >= 0)
        def _():
            down(d).start()

    near, far = [], []
    order = HOPS + (0,)
    for i, d in enumerate(order):
        q = hop(p, d)
        sib_out[i] = x_ref[q, at_rows((1 - c) * half, half), :].astype(bf16)
        near.append(
            send(sib_out.at[i], sib_in.at[i], n_sems.at[0, i], n_sems.at[1, i], other)
        )
    for i, d in enumerate(HOPS):
        q = hop(p, d)
        near[i].wait_recv()
        out[i] = (x_ref[q, at_rows(c * half, half), :] + sib_in[i].astype(f32)).astype(bf16)
        far.append(
            send(out.at[i], came.at[i], f_sems.at[0, i], f_sems.at[1, i], chip(z, q, c))
        )
    moved = swap_begin(ins, outs, w_sems, loc_sems)
    near[3].wait_recv()
    total = x_ref[p, at_rows(c * half, half), :] + sib_in[3].astype(f32)
    for i in (1, 2, 0):
        far[i].wait_recv()
        total = total + came[i].astype(f32)
    mine = out_ref.at[at_rows(c * half, half), :]
    out_ref[at_rows(c * half, half), :] = total
    copy = send(mine, mine, own_sems.at[0], own_sems.at[1], other)
    copy.wait()
    first[:, :xw] = dx_ref[...] * slope_ref[:, :xw]
    first[:, xw:] = out_ref[0:8, :] * slope_ref[:, xw:]

    def edge(to):
        return pltpu.make_async_remote_copy(
            src_ref=first, dst_ref=next_ref, send_sem=h_sems.at[0], recv_sem=h_sems.at[1],
            device_id=to, device_id_type=MESH,
        )

    @pl.when(z > 0)
    def _():
        edge(chip(z - 1, p, c)).start()

    own_ref[...] = dkv_ref[z].astype(f32)
    for d in range(1, nz):

        @pl.when(z + d < nz)
        def _():
            pltpu.make_async_remote_copy(
                src_ref=dkv_ref.at[z], dst_ref=z_came.at[d - 1], send_sem=z_sems.at[0, d - 1],
                recv_sem=z_sems.at[1, d - 1], device_id=chip(z + d, p, c), device_id_type=MESH,
            ).wait_recv()
            own_ref[...] += z_came[d - 1].astype(f32)

        @pl.when(z - d >= 0)
        def _():
            down(d).wait_send()

    @pl.when(z + 1 == nz)
    def _():
        next_ref[...] = jnp.zeros_like(next_ref)

    @pl.when(z + 1 < nz)
    def _():
        edge(chip(z + 1, p, c)).wait_recv()

    @pl.when(z > 0)
    def _():
        edge(chip(z - 1, p, c)).wait_send()

    for done in near + far:
        done.wait_send()
    for copy in moved:
        copy.wait()


def reduce_bc(x, dkv, dx, slope, moved):
    n_p, tok, _ = x.shape
    half, nz = tok // 2, dkv.shape[0]
    dma = pltpu.SemaphoreType.DMA
    return plane_call(
        reduce_bc_kernel, "reduce_bc", 7, (x, dkv, dx, slope),
        [((tok, 128), f32), (dkv.shape[1:], f32), (slope.shape, f32)],
        [
            pltpu.VMEM((4, half, 128), bf16),
            pltpu.VMEM((4, half, 128), bf16),
            pltpu.VMEM((3, half, 128), bf16),
            pltpu.VMEM((3, half, 128), bf16),
            pltpu.VMEM((nz - 1,) + dkv.shape[1:], bf16),
            pltpu.VMEM(slope.shape, f32),
            dma((2, 4)), dma((2, 3)), dma((2,)), dma((2, nz - 1)), dma((2,)),
        ],
        nbytes=100_000_000,
        moved=moved,
    )


def swap_kernel(n, *refs):
    ins, outs, sems = refs[:n], refs[n : 2 * n], refs[2 * n :]
    z, p, c = place()
    meet([chip(z, hop(p, d), c) for d in HOPS])
    for copy in swap_begin(ins, outs, *sems):
        copy.wait()


def swap_step(*moved):
    return plane_call(swap_kernel, "swap_step", 6, (), [], [], nbytes=20_000_000, moved=moved)


def rope_tables(positions, pairs):
    freqs = rope_base ** (-2.0 * pairs.astype(f32) / HDIM)
    angles = positions.astype(f32)[:, None] * freqs[None, :]
    return jnp.cos(angles), jnp.sin(angles)


def carry_back(state, rates):
    nz, zi = lax.axis_size("z"), lax.axis_index("z")
    low = state.astype(bf16)
    total, factor = None, None
    for d in range(1, nz):
        came = lax.ppermute(low, "z", [(i, i - d) for i in range(d, nz)]).astype(f32)
        total = came if total is None else total + factor * came
        rate = lax.dynamic_index_in_dim(rates, (zi + d) % nz, 0, keepdims=False)
        factor = rate if factor is None else factor * rate
    return total


def shards(
    hidden_in,
    grad_out,
    doc_starts,
    norm_mixer,
    norm_ffn,
    mamba_z,
    mamba_x,
    mamba_bc,
    mamba_dt,
    conv_x,
    conv_bc,
    a_log,
    dt_bias,
    skip_gain,
    mamba_out,
    attn_query,
    attn_key,
    attn_value,
    attn_out,
    ffn_gate,
    ffn_up,
    ffn_down,
):
    own = hidden_in.shape[0]
    width = hidden_in.shape[1]
    half = own // 2
    nz, n_p = lax.axis_size("z"), lax.axis_size("p")
    zi, pi, ci = lax.axis_index("z"), lax.axis_index("p"), lax.axis_index("head")
    tok = own * n_p
    base = zi * tok
    positions = base + jnp.arange(tok, dtype=jnp.int32)
    edge = conv_x.shape[0] - 1
    ext_docs = doc_ids(base - edge + jnp.arange(tok + 2 * edge, dtype=jnp.int32), doc_starts)
    rows = mamba_z.shape[0]
    n_heads = a_log.shape[0] // n_p
    xw = n_heads * MHDIM
    bw = mamba_bc.shape[1] // (2 * n_p)
    cw = xw + 2 * bw
    kw = HDIM // n_p
    hk = kw // 2
    tail_w = 128 - 2 * kw - n_heads

    weights = (
        mamba_x, mamba_bc, attn_key, attn_value, mamba_dt, attn_query, mamba_z, mamba_out, attn_out,
        ffn_gate, ffn_up, ffn_down,
    )
    piece_a, *rest = pack(n_p, *weights)

    def along_z(piece):
        piece = piece.reshape(n_p * rows, piece.shape[2])
        return lax.all_gather(piece, "z", axis=0, tiled=True)

    gains_own = jnp.pad(
        jnp.stack([norm_mixer, norm_ffn]).astype(bf16).astype(f32), ((0, 6), (0, 128 - rows))
    )
    my_half = lambda v: lax.dynamic_slice_in_dim(v, ci * half, half, 0)
    hidden_own, grad_own = my_half(hidden_in), my_half(grad_out)
    gains, normed_one, w_a, *rest = open_step(hidden_own, gains_own, piece_a, rest, tok, nz)
    w_a = w_a.reshape(nz * n_p * rows, w_a.shape[3])
    gains = gains.transpose(2, 1, 0, 3)[:, :, :, :rows].reshape(8, 1, width)
    gain_mix, gain_ffn = gains[0], gains[1]
    w_b, w_c, w_d = [along_z(piece) for piece in rest[:3]]

    in_ext = product(normed_one, w_a)
    in_b = product(normed_one, w_b)[:tok]
    in_a = in_ext[:tok]
    pre_ext = in_ext[:, :cw].astype(bf16)
    gate_z = in_b[:, HDIM:]
    slice_1 = lambda v, at, n: lax.dynamic_slice_in_dim(v, at, n, 1)
    taps = jnp.concatenate(
        [
            slice_1(conv_x, pi * xw, xw),
            slice_1(conv_bc, pi * bw, bw),
            slice_1(conv_bc, (n_p + pi) * bw, bw),
        ],
        axis=1,
    )
    ext = jnp.concatenate([pre_ext[tok + HALO - edge :], pre_ext[:tok]], axis=0)
    conv_in = convolve(ext, taps, ext_docs, tok)
    ssm = jax.nn.silu(conv_in).astype(bf16)
    head_slice = lambda v: lax.dynamic_slice_in_dim(v, pi * n_heads, n_heads, 0)
    my_bias, my_a, my_skip = head_slice(dt_bias), head_slice(a_log), head_slice(skip_gain)
    lanes = lambda v: jnp.pad(v, (0, 128 - n_heads))[None, :]
    dt_at = cw + 2 * kw
    dt_pre = jnp.pad(in_a[:, dt_at : dt_at + n_heads], ((0, 0), (0, 128 - n_heads))) + lanes(my_bias)
    neg_rate = lanes(-jnp.exp(my_a))
    skip_full = jnp.repeat(my_skip, MHDIM)[None, :]
    pair_ids = pi * hk + jnp.arange(hk)
    cos_k, sin_k = rope_tables(positions, pair_ids)
    k0, k1 = in_a[:, cw : cw + hk], in_a[:, cw + hk : cw + kw]
    key_own = jnp.concatenate([k0 * cos_k - k1 * sin_k, k1 * cos_k + k0 * sin_k], axis=1)
    val_own = in_a[:, cw + kw : cw + 2 * kw]
    kv_own = jnp.concatenate([key_own, val_own], axis=1).astype(bf16)
    kv_own = jnp.concatenate([kv_own[: tok // 2], kv_own[tok // 2 :]], axis=1)
    bc_all, kvz, g_ffn, w_e = gather_bc(
        ssm, xw // 128, n_p, kv_own, nz, grad_own, rest[3]
    )
    cos_q, sin_q = rope_tables(positions, jnp.arange(HDIM // 2))
    cos_q, sin_q = cos_q.reshape(tok, n_p, hk), sin_q.reshape(tok, n_p, hk)

    def rope_q(v, sign):
        v = v.reshape(tok, n_p, 2, hk)
        a, b = v[:, :, 0], v[:, :, 1]
        return jnp.stack(
            [a * cos_q - sign * b * sin_q, b * cos_q + sign * a * sin_q], axis=2
        ).reshape(tok, HDIM)

    queries = rope_q(in_b[:, :HDIM], 1.0).astype(bf16)

    base_arr = jnp.reshape(base, (1,)).astype(jnp.int32)
    y_local, span_starts, local_state, dev_decay, decay_full, c_mat = ssd_forward(
        base_arr, doc_starts, ssm, bc_all, dt_pre, neg_rate, skip_full
    )
    rate = jnp.broadcast_to(dev_decay[tok - 1 :], (8, 128))
    in_state, kv, rates, w_e = carry_step(local_state, rate, kvz, n_p, w_e)

    attn_f32, lse, keys, values = attend(base_arr, doc_starts, queries, kv)
    attn_low = attn_f32.astype(bf16)
    y_flat = y_local + product_nt(c_mat, in_state.astype(bf16)) * decay_full
    silu_z = jax.nn.silu(gate_z)
    gated = (y_flat * silu_z).astype(bf16)
    mixed = jnp.concatenate([gated, attn_low], axis=1)

    mid_own, normed_two, w_e = mid_step(mixed, w_c, hidden_own, gain_ffn, w_e)
    w_e = w_e.reshape(width, -1)
    gu, activated, grad_e = ffn_forward(normed_two, w_d, g_ffn)
    ffw = gu.shape[1] // 2
    gate_val, up_val = gu[:, :ffw], gu[:, ffw:]
    silu_gate = jax.nn.silu(gate_val)
    g_ffn, grad_e = lax.optimization_barrier((g_ffn, grad_e))
    d_act = product(g_ffn, w_e)
    d_gu = jnp.concatenate(
        [d_act * up_val * silu_slope(gate_val), d_act * silu_gate], axis=1
    ).astype(bf16)
    grad_d = product_t(normed_two, d_gu).astype(bf16)
    d_gu, grad_d = lax.optimization_barrier((d_gu, grad_d))

    def scattered(grad):
        return lax.psum_scatter(grad, "z", scatter_dimension=0, tiled=True)

    def by_owner(grad):
        return grad.reshape(n_p, rows, grad.shape[1])

    ge = scattered(grad_e)
    gd = scattered(grad_d)
    d_mid_own, grad_gain_ffn, g_mid = two_step(d_gu, w_d, mid_own, grad_own, gain_ffn)
    g_mid, ge = lax.optimization_barrier((g_mid, ge))

    d_mixed = product(g_mid, w_c)
    grad_c = product_t(g_mid, mixed).astype(bf16)
    gc = scattered(grad_c)
    d_gated = d_mixed[:, :xw]
    d_attn = d_mixed[:, xw:].astype(bf16)
    d_y_flat = d_gated * silu_z
    d_z = (d_gated * y_flat * silu_slope(gate_z)).astype(bf16)
    d_in_local = product_t((d_y_flat * decay_full).astype(bf16), c_mat)
    d_in_local, d_attn = lax.optimization_barrier((d_in_local, d_attn))
    rates = jnp.repeat(rates[:, 0, :n_heads], MHDIM, axis=1)[:, :, None]
    state_grad = carry_back(d_in_local, rates)
    d_query, d_kv = attend_back(
        base_arr, doc_starts, queries, d_attn, attn_f32, lse, keys, values, kv.shape
    )
    d_q_pre = rope_q(d_query, -1.0).astype(bf16)
    d_b = jnp.concatenate([d_q_pre, d_z], axis=1)
    d_b, state_grad = lax.optimization_barrier((d_b, state_grad))
    more = lambda v: jnp.pad(v, ((0, HALO), (0, 0)))
    grad_b = product_t(normed_one, more(d_b)).astype(bf16)
    gb = scattered(grad_b)
    d_kv_parts = [lax.dynamic_index_in_dim(d_kv, pi, 0, keepdims=False)]
    for d in range(1, n_p):
        part = lax.dynamic_index_in_dim(d_kv, jnp.bitwise_xor(pi, d), 0, keepdims=False)
        d_kv_parts.append(lax.ppermute(part, "p", [(i, i ^ d) for i in range(n_p)]))

    start_decay = jnp.concatenate([jnp.ones((1, 128), f32), dev_decay[SPAN - 1 :: SPAN][:-1]])
    d_y_flat, gd = lax.optimization_barrier((d_y_flat, gd))
    d_xs, d_bc, d_dt, sums, skip_sums = ssd_backward(
        base_arr, doc_starts, ssm, bc_all, dt_pre, d_y_flat, span_starts,
        start_decay[:, None, :], neg_rate, skip_full, in_state, state_grad,
    )
    d_bc, d_kv_parts = lax.optimization_barrier((d_bc, d_kv_parts))
    d_kv = sum(part.astype(f32) for part in d_kv_parts).astype(bf16)
    slope = silu_slope(conv_in)
    d_bc, d_kv_own, du_next, ge, gd = reduce_bc(
        d_bc, d_kv, d_xs[:8], slope[:8], (by_owner(ge), by_owner(gd))
    )
    d_kv_own = jnp.concatenate([d_kv_own[:, : 2 * kw], d_kv_own[:, 2 * kw :]], axis=0)
    dk0, dk1 = d_kv_own[:, :hk], d_kv_own[:, hk:kw]
    d_kv_low = jnp.concatenate(
        [dk0 * cos_k + dk1 * sin_k, dk1 * cos_k - dk0 * sin_k, d_kv_own[:, kw:]], axis=1
    ).astype(bf16)
    du = jnp.concatenate([d_xs, d_bc], axis=1) * slope
    du = jnp.concatenate([du, du_next[:edge]], axis=0)
    d_pre, grad_taps = convolve_back(du, ext, taps, ext_docs, tok)
    d_pre = d_pre.astype(bf16)
    d_last = jnp.concatenate(
        [d_kv_low, d_dt[:, :n_heads].astype(bf16), jnp.zeros((tok, tail_w), bf16)], axis=1
    )
    d_a = jnp.concatenate([d_pre, d_last], axis=1)
    grad_a = product_t(normed_one, more(d_a)).astype(bf16)
    ga = scattered(grad_a)
    once = jnp.where(ci == 0, d_pre[:, xw:], jnp.zeros((), bf16))
    d_a_once = jnp.concatenate([d_pre[:, :xw], once, d_last], axis=1)
    d_a_once, grad_a, gc = lax.optimization_barrier((d_a_once, grad_a, gc))
    rest = jnp.concatenate(
        [
            grad_gain_ffn.reshape(-1, 128),
            grad_taps.reshape(-1, 128),
            sums[:2],
            jnp.pad(jnp.sum(skip_sums.reshape(n_heads, MHDIM), axis=1), (0, 128 - n_heads))[None],
        ]
    )
    rest = jnp.pad(rest, ((0, -rest.shape[0] % 8), (0, 0)))
    grad_in, block_out, summed, gc = one_step(
        d_a_once, w_a, d_b, w_b, hidden_own, d_mid_own, gain_mix, activated, w_e, mid_own, rest,
        nz, n_p, (by_owner(gc),),
    )

    g_rows = width // 128
    t_rows = grad_taps.size // 128
    si = zi * n_p + pi
    gains_sum = jnp.sum(summed[:, :, : 2 * g_rows], axis=(0, 1)).reshape(2, width)
    gains_sum = lax.dynamic_slice_in_dim(gains_sum, si * rows, rows, 1)
    mine = lax.dynamic_index_in_dim(summed, ci, 0, keepdims=False)
    s_taps = mine[:, 2 * g_rows : 2 * g_rows + t_rows].reshape(n_p, edge + 1, cw).transpose(1, 0, 2)
    s_heads = mine[:, 2 * g_rows + t_rows : 2 * g_rows + t_rows + 3, :n_heads]
    s_heads = s_heads.transpose(1, 0, 2).reshape(3, n_p * n_heads)
    s_x = s_taps[:, :, :xw].reshape(edge + 1, n_p * xw)
    s_bc = summed[0][:, 2 * g_rows : 2 * g_rows + t_rows].reshape(n_p, edge + 1, cw)
    s_bc = s_bc[:, :, xw:].reshape(n_p, edge + 1, 2, bw).transpose(1, 2, 0, 3)
    s_bc = s_bc.reshape(edge + 1, 2 * n_p * bw)

    ga, gb = swap_step(by_owner(ga), by_owner(gb))
    (
        g_x, g_bc, g_k, g_v, g_dt, g_q, g_z, g_mout, g_aout, g_gate, g_up, g_down, block_out,
        grad_in,
    ) = unpack((ga, gb, gc, gd, ge, block_out, grad_in), weights + (block_out, grad_in))
    return (
        block_out,
        grad_in,
        gains_sum[0],
        gains_sum[1],
        g_z,
        g_x,
        g_bc,
        g_dt,
        s_x,
        s_bc,
        s_heads[0],
        s_heads[1],
        s_heads[2],
        g_mout,
        g_q,
        g_k,
        g_v,
        g_aout,
        g_gate,
        g_up,
        g_down,
    )


def solution(mesh):
    seq, head = mesh.shape["seq"], mesh.shape["head"]
    plane = math.gcd(seq, 4)
    grid = Mesh(mesh.devices.reshape(seq // plane, plane, head), ("z", "p", "head"))
    s = ("z", "p")
    h = "head"
    placed = (
        P(s, None), P(s, None), P(), P(s), P(s), P(s, h), P(s, h), P(s, None), P(s, h),
        P(None, h), P(), P(h), P(h), P(h), P(h, s), P(s, h), P(s, h), P(s, h), P(h, s),
        P(s, h), P(s, h), P(h, s),
    )
    given = (
        P(s, None), P(s, None), P(s), P(s), P(s, h), P(s, h), P(s, None), P(s, h),
        P(None, h), P(), P(h), P(h), P(h), P(h, s), P(s, h), P(s, h), P(s, h), P(h, s),
        P(s, h), P(s, h), P(h, s),
    )
    return jax.shard_map(shards, mesh=grid, in_specs=placed, out_specs=given, check_vma=False)
```

```python
import functools
import math

import jax
import jax.numpy as jnp
from jax import lax
from jax.experimental import pallas as pl
from jax.experimental.pallas import tpu as pltpu
from jax.sharding import Mesh
from jax.sharding import PartitionSpec as P

MHDIM = 64
NSTATE = 256
HDIM = 128
SPAN = 128

eps_norm = 1e-05
rope_base = 100000000000.0
neg_large = -1e30
top_prec = lax.Precision.HIGHEST
bf16 = jnp.bfloat16
f32 = jnp.float32
MESH = pl.DeviceIdType.MESH
VMEM_LIMIT = 56 * 1024 * 1024


def doc_ids(positions, doc_starts):
    return jnp.sum((doc_starts[None, :] <= positions[:, None]).astype(jnp.int32), axis=1) - 1


def product(left, right):
    return jnp.dot(left, right, preferred_element_type=f32)


def product_t(left, right):
    return lax.dot_general(left, right, (((0,), (0,)), ((), ())), preferred_element_type=f32)


def product_nt(left, right):
    return lax.dot_general(left, right, (((1,), (1,)), ((), ())), preferred_element_type=f32)


def silu_slope(values):
    sigma_val = jax.nn.sigmoid(values)
    return sigma_val * (1.0 + values * (1.0 - sigma_val))


def convolve(extended, weights, ext_docs, tok_count):
    edge_rows = weights.shape[0] - 1
    here = ext_docs[edge_rows : edge_rows + tok_count]
    summed = jnp.zeros((tok_count, extended.shape[1]), f32)
    for tap_index in range(weights.shape[0]):
        begin_row = edge_rows - tap_index
        same_doc = (ext_docs[begin_row : begin_row + tok_count] == here)[:, None]
        rows = extended[begin_row : begin_row + tok_count].astype(f32)
        summed = summed + jnp.where(same_doc, rows, 0.0) * weights[tap_index][None, :]
    return summed


def convolve_back(d_conv, extended, weights, ext_docs, tok_count):
    edge_rows = weights.shape[0] - 1
    here = ext_docs[edge_rows : edge_rows + tok_count]
    d_rows = jnp.zeros((tok_count, d_conv.shape[1]), f32)
    tap_grads = []
    for tap_index in range(weights.shape[0]):
        begin_row = edge_rows - tap_index
        before = (ext_docs[begin_row : begin_row + tok_count] == here)[:, None]
        rows = extended[begin_row : begin_row + tok_count].astype(f32)
        tap_grads.append(jnp.sum(jnp.where(before, d_conv[:tok_count] * rows, 0.0), axis=0))
        last = edge_rows + tap_index
        after = (ext_docs[last : last + tok_count] == here)[:, None]
        ahead = d_conv[tap_index : tap_index + tok_count]
        d_rows = d_rows + jnp.where(after, ahead, 0.0) * weights[tap_index][None, :]
    return (d_rows, jnp.stack(tap_grads))


def tri_dot(a, b, dims=((1,), (0,))):
    return lax.dot_general(a, b, (dims, ((), ())), precision=top_prec, preferred_element_type=f32)


def dot_nn(a, b):
    return lax.dot_general(a, b, (((1,), (0,)), ((), ())), preferred_element_type=f32)


def dot_nt(a, b):
    return lax.dot_general(a, b, (((1,), (1,)), ((), ())), preferred_element_type=f32)


def dot_tn(a, b):
    return lax.dot_general(a, b, (((0,), (0,)), ((), ())), preferred_element_type=f32)


def iota2(shape, dim):
    return lax.broadcasted_iota(jnp.int32, shape, dim)


def docs_of(pos, starts_ref):
    count = jnp.where(starts_ref[0] <= pos, 1, 0)
    for i in range(1, starts_ref.shape[0]):
        count = count + jnp.where(starts_ref[i] <= pos, 1, 0)
    return count - 1


def softplus(v):
    return jnp.maximum(v, 0.0) + jnp.log(1.0 + jnp.exp(-jnp.abs(v)))


def head_maps(xw):
    lane_head = (iota2((128, xw), 1) // MHDIM == iota2((128, xw), 0)).astype(f32)
    row_head = (iota2((xw, 128), 0) // MHDIM == iota2((xw, 128), 1)).astype(f32)
    return lane_head, row_head


def span_setup(k, base_ref, starts_ref, dtp, nega):
    first = base_ref[0] + k * SPAN
    t_idx, s_idx = iota2((SPAN, SPAN), 0), iota2((SPAN, SPAN), 1)
    docs_t = docs_of(first + t_idx, starts_ref)
    docs_s = docs_of(first + s_idx, starts_ref)
    linked = (docs_t == docs_s) & (t_idx >= s_idx)
    dt = softplus(dtp)
    la = nega * dt
    tri = (t_idx >= s_idx).astype(f32)
    cum = tri_dot(tri, la)
    before = docs_of(first - 1, starts_ref)
    last_doc = docs_of(first + SPAN - 1, starts_ref)
    carried = jnp.where(docs_t == before, jnp.exp(cum), 0.0)
    cum_last = cum[SPAN - 1 : SPAN, :]
    tail = jnp.where(docs_t == last_doc, jnp.exp(cum_last - cum), 0.0)
    return docs_t, linked, dt, la, tri, cum, carried, tail


def split_bc(bc_ref):
    parts = [bc_ref[q] for q in range(bc_ref.shape[0])]
    half = parts[0].shape[1] // 2
    return (
        jnp.concatenate([part[:, :half] for part in parts], axis=1),
        jnp.concatenate([part[:, half:] for part in parts], axis=1),
    )


def ssd_forward_kernel(
    n_heads, base_ref, starts_ref, x_ref, bc_ref, dtp_ref, nega_ref, skip_ref,
    y_ref, span_ref, final_ref, decay_ref, wide_ref, c_out, state, running,
):
    k = pl.program_id(0)
    xw = n_heads * MHDIM

    @pl.when(k == 0)
    def _():
        state[...] = jnp.zeros_like(state)
        running[...] = jnp.zeros_like(running)

    docs_t, linked, dt, la, tri, cum, carried, tail = span_setup(
        k, base_ref, starts_ref, dtp_ref[...], nega_ref[...]
    )
    lane_head, row_head = head_maps(xw)
    prev_doc = docs_of(base_ref[0] - 1, starts_ref)
    since = jnp.where(docs_t == prev_doc, jnp.exp(running[0:1, :] + cum), 0.0)
    decay_ref[...] = since
    wide_ref[...] = tri_dot(since, lane_head)
    running[...] = running[...] + cum[SPAN - 1 : SPAN, :]
    start = state[...]
    span_ref[0] = start
    x, (b, c) = x_ref[...], split_bc(bc_ref)
    c_out[...] = c
    inner = dot_nt(c, b)
    cum_t, dt_t = cum.T, dt.T
    lane = iota2((SPAN, 128), 1)
    pieces = []
    for pair in range(n_heads // 2):
        xp = x[:, pair * 128 : pair * 128 + 128]
        got = []
        for h in (2 * pair, 2 * pair + 1):
            gap = jnp.where(linked, cum[:, h : h + 1] - cum_t[h : h + 1, :], neg_large)
            w = jnp.exp(gap) * inner * dt_t[h : h + 1, :]
            got.append(dot_nn(w.astype(bf16), xp))
        pieces.append(jnp.where(lane < MHDIM, got[0], got[1]))
    y = jnp.concatenate(pieces, axis=1)
    y = y + dot_nt(c, start.astype(bf16)) * tri_dot(carried, lane_head)
    xf = x.astype(f32)
    y_ref[...] = y + skip_ref[...] * xf
    xt = (xf * tri_dot(tail * dt, lane_head)).astype(bf16)
    keep = jnp.sum(row_head * carried[SPAN - 1 : SPAN, :], axis=1, keepdims=True)
    new = dot_tn(xt, b) + keep * start
    state[...] = new
    final_ref[...] = new


def ssd_forward(base, doc_starts, x, bc, dtp, nega, skip):
    tok, xw, n_p = x.shape[0], skip.shape[1], bc.shape[0]
    n_heads, nspan = xw // MHDIM, tok // SPAN
    row = lambda n: pl.BlockSpec((SPAN, n), lambda i: (i, 0))
    whole = lambda *s: pl.BlockSpec(s, lambda i: (0,) * len(s))
    smem = pl.BlockSpec(memory_space=pltpu.SMEM)
    return pl.pallas_call(
        functools.partial(ssd_forward_kernel, n_heads),
        grid=(nspan,),
        in_specs=[
            smem, smem, row(xw), pl.BlockSpec((n_p, SPAN, 128), lambda i: (0, i, 0)), row(128),
            whole(1, 128), whole(1, xw),
        ],
        out_specs=[
            row(xw),
            pl.BlockSpec((1, xw, NSTATE), lambda i: (i, 0, 0)),
            whole(xw, NSTATE),
            row(128),
            row(xw),
            row(NSTATE),
        ],
        out_shape=[
            jax.ShapeDtypeStruct((tok, xw), f32),
            jax.ShapeDtypeStruct((nspan, xw, NSTATE), f32),
            jax.ShapeDtypeStruct((xw, NSTATE), f32),
            jax.ShapeDtypeStruct((tok, 128), f32),
            jax.ShapeDtypeStruct((tok, xw), f32),
            jax.ShapeDtypeStruct((tok, NSTATE), bf16),
        ],
        scratch_shapes=[pltpu.VMEM((xw, NSTATE), f32), pltpu.VMEM((8, 128), f32)],
        compiler_params=pltpu.CompilerParams(vmem_limit_bytes=VMEM_LIMIT),
        cost_estimate=pl.CostEstimate(
            flops=2 * tok * xw * NSTATE * 3, bytes_accessed=40_000_000, transcendentals=0
        ),
        name="ssd_forward",
    )(base, doc_starts, x, bc, dtp, nega, skip)


def ssd_backward_kernel(
    n_heads, base_ref, starts_ref, x_ref, bc_ref, dtp_ref, dy_ref, span_ref, decay_ref,
    nega_ref, skip_ref, in_ref, grad_ref,
    dx_ref, dbc_ref, ddt_ref, sums_ref, gskip_ref, gstate,
):
    step = pl.program_id(0)
    k = pl.num_programs(0) - 1 - step
    xw = n_heads * MHDIM

    @pl.when(step == 0)
    def _():
        gstate[...] = grad_ref[...]
        sums_ref[...] = jnp.zeros_like(sums_ref)
        gskip_ref[...] = jnp.zeros_like(gskip_ref)

    nega = nega_ref[...]
    docs_t, linked, dt, la, tri, cum, carried, tail = span_setup(
        k, base_ref, starts_ref, dtp_ref[...], nega
    )
    lane_head, row_head = head_maps(xw)
    begin = jnp.sum(row_head * decay_ref[0], axis=1, keepdims=True)
    start = span_ref[0] + begin * in_ref[...]
    start_low = start.astype(bf16)
    g = gstate[...]
    g_low = g.astype(bf16)
    x, (b, c), dy = x_ref[...], split_bc(bc_ref), dy_ref[...]
    dy_low = dy.astype(bf16)
    xf = x.astype(f32)
    inner = dot_nt(c, b)
    cum_t, dt_t = cum.T, dt.T
    lane = iota2((SPAN, 128), 1)
    row8 = iota2((SPAN, 128), 0)
    d_inner = jnp.zeros((SPAN, SPAN), f32)
    r_cols = jnp.zeros((SPAN, 128), f32)
    k_rows = jnp.zeros((SPAN, 128), f32)
    u_pieces = []
    for pair in range(n_heads // 2):
        xp = x[:, pair * 128 : pair * 128 + 128]
        dyp = dy_low[:, pair * 128 : pair * 128 + 128]
        got = []
        for j, h in enumerate((2 * pair, 2 * pair + 1)):
            mine = (lane < MHDIM) if j == 0 else (lane >= MHDIM)
            gap = jnp.where(linked, cum[:, h : h + 1] - cum_t[h : h + 1, :], neg_large)
            e = jnp.exp(gap)
            m = e * inner
            dyx = dot_nt(dyp, jnp.where(mine, xp, jnp.zeros_like(xp)))
            ed = dyx * dt_t[h : h + 1, :]
            d_inner = d_inner + e * ed
            pairs = m * ed
            r_cols = jnp.where(lane == h, jnp.sum(pairs, axis=1, keepdims=True), r_cols)
            k_rows = jnp.where(row8 == h, jnp.sum(pairs, axis=0, keepdims=True), k_rows)
            got.append(dot_tn(m.astype(bf16), dyp))
        u_pieces.append(jnp.where(lane < MHDIM, got[0], got[1]))
    u = jnp.concatenate(u_pieces, axis=1)
    dye = dy * tri_dot(carried, lane_head)
    dye_low = dye.astype(bf16)
    di_low = d_inner.astype(bf16)
    r_state = tri_dot(dye * dot_nt(c, start_low), row_head)
    u_state = dot_nt(b, g_low) * tri_dot(tail, lane_head)
    u = u + u_state
    dt_full = tri_dot(dt, lane_head)
    k_state = dt * tri_dot(xf * u_state, row_head)
    d_dt = tri_dot(xf * u, row_head)
    tail_x = (xf * tri_dot(tail * dt, lane_head)).astype(bf16)
    dx_ref[...] = dt_full * u + skip_ref[...] * dy
    d_b = dot_nn(tail_x, g_low) + dot_tn(di_low, c)
    d_c = dot_nn(dye_low, start_low) + dot_nn(di_low, b)
    bw = 64
    for q in range(dbc_ref.shape[0]):
        cut = slice(q * bw, q * bw + bw)
        dbc_ref[q] = jnp.concatenate([d_b[:, cut], d_c[:, cut]], axis=1)
    gs = jnp.sum(g * start, axis=1, keepdims=True)
    gs_row = jnp.sum(row_head * gs, axis=0, keepdims=True)
    last = jnp.sum(k_state, axis=0, keepdims=True) + carried[SPAN - 1 : SPAN, :] * gs_row
    d_cum = r_cols - k_rows.T + r_state - k_state + jnp.where(row8 == SPAN - 1, last, 0.0)
    d_la = tri_dot(tri, d_cum, ((0,), (0,)))
    live = lane < n_heads
    dtp = dtp_ref[...]
    d_in = jnp.where(live, (d_dt + nega * d_la) * jax.nn.sigmoid(dtp), 0.0)
    ddt_ref[...] = d_in
    sum_a = jnp.sum(jnp.where(live, d_la * la, 0.0), axis=0, keepdims=True)
    sum_b = jnp.sum(d_in, axis=0, keepdims=True)
    pick = iota2((8, 128), 0)
    sums_ref[...] += jnp.where(pick == 0, sum_a, jnp.where(pick == 1, sum_b, 0.0))
    gskip_ref[...] += jnp.sum(dy * xf, axis=0, keepdims=True)
    keep = jnp.sum(row_head * carried[SPAN - 1 : SPAN, :], axis=1, keepdims=True)
    gstate[...] = keep * g + dot_tn(dye_low, c)


def ssd_backward(
    base, doc_starts, x, bc, dtp, dy, span_starts, start_decay, nega, skip, in_state, grad_state
):
    tok, xw, n_p = x.shape[0], skip.shape[1], bc.shape[0]
    wide = pl.BlockSpec((n_p, SPAN, 128), lambda i: (0, nspan - 1 - i, 0))
    n_heads, nspan = xw // MHDIM, tok // SPAN
    row = lambda n: pl.BlockSpec((SPAN, n), lambda i: (nspan - 1 - i, 0))
    whole = lambda *s: pl.BlockSpec(s, lambda i: (0,) * len(s))
    smem = pl.BlockSpec(memory_space=pltpu.SMEM)
    return pl.pallas_call(
        functools.partial(ssd_backward_kernel, n_heads),
        grid=(nspan,),
        in_specs=[
            smem, smem, row(xw), wide, row(128), row(xw),
            pl.BlockSpec((1, xw, NSTATE), lambda i: (nspan - 1 - i, 0, 0)),
            pl.BlockSpec((1, 1, 128), lambda i: (nspan - 1 - i, 0, 0)),
            whole(1, 128), whole(1, xw), whole(xw, NSTATE), whole(xw, NSTATE),
        ],
        out_specs=[row(xw), wide, row(128), whole(8, 128), whole(1, xw)],
        out_shape=[
            jax.ShapeDtypeStruct((tok, xw), f32),
            jax.ShapeDtypeStruct((n_p, tok, 128), f32),
            jax.ShapeDtypeStruct((tok, 128), f32),
            jax.ShapeDtypeStruct((8, 128), f32),
            jax.ShapeDtypeStruct((1, xw), f32),
        ],
        scratch_shapes=[pltpu.VMEM((xw, NSTATE), f32)],
        compiler_params=pltpu.CompilerParams(vmem_limit_bytes=VMEM_LIMIT),
        cost_estimate=pl.CostEstimate(
            flops=2 * tok * xw * NSTATE * 8, bytes_accessed=80_000_000, transcendentals=0
        ),
        name="ssd_backward",
    )(base, doc_starts, x, bc, dtp, dy, span_starts, start_decay, nega, skip, in_state, grad_state)


QB = 512
KB = 512


def sight(base_ref, starts_ref, q_first):
    q_pos = base_ref[0] + q_first + iota2((QB, 1), 0)
    low = jnp.zeros((QB, 1), jnp.int32)
    for i in range(starts_ref.shape[0]):
        low = jnp.where(starts_ref[i] <= q_pos, starts_ref[i], low)
    return jnp.broadcast_to(low, (QB, KB)), jnp.broadcast_to(q_pos, (QB, KB))


def seen(low, high, k_first):
    k_pos = k_first + iota2((QB, KB), 1)
    return (k_pos >= low) & (k_pos <= high)


def attend_kernel(
    scale, base_ref, starts_ref, raw_ref, cos_ref, sin_ref, kv_ref,
    o_ref, lse_ref, k_ref, v_ref, q_ref,
):
    i = pl.program_id(0)

    @pl.when(i == 0)
    def _():
        n_p, nz, rows, _ = kv_ref.shape
        kw = HDIM // n_p

        @pl.loop(0, nz)
        def _(z):
            parts = [kv_ref[q, z] for q in range(n_p)]
            for t in range(2):
                at = pl.ds(pl.multiple_of((2 * z + t) * rows, rows), rows)
                lo = 2 * kw * t
                k_ref[at, :] = jnp.concatenate([v[:, lo : lo + kw] for v in parts], axis=1)
                v_ref[at, :] = jnp.concatenate([v[:, lo + kw : lo + 2 * kw] for v in parts], axis=1)

    raw = raw_ref[...]
    hk = HDIM // kv_ref.shape[0] // 2
    leading = iota2(raw.shape, 1) % (2 * hk) < hk
    partner = jnp.where(leading, pltpu.roll(raw, HDIM - hk, 1), pltpu.roll(raw, hk, 1))
    q = (raw * cos_ref[...] + partner * sin_ref[...]).astype(bf16)
    q_ref[...] = q
    low, high = sight(base_ref, starts_ref, i * QB)
    blocks = (base_ref[0] + (i + 1) * QB + KB - 1) // KB

    def turn(j, carry):
        m, l, acc = carry
        at = pl.ds(pl.multiple_of(j * KB, KB), KB)
        s = dot_nt(q, k_ref[at, :]) * scale
        s = jnp.where(seen(low, high, j * KB), s, neg_large)
        m_new = jnp.maximum(m, jnp.max(s, axis=1, keepdims=True))
        w = jnp.exp(s - m_new)
        r = jnp.exp(m - m_new)
        l = l * r + jnp.sum(w, axis=1, keepdims=True)
        return m_new, l, acc * r + dot_nn(w.astype(bf16), v_ref[at, :])

    m, l, acc = lax.fori_loop(
        0,
        blocks,
        turn,
        (jnp.full((QB, 1), 0.1 * neg_large, f32), jnp.zeros((QB, 1), f32), jnp.zeros((QB, HDIM), f32)),
    )
    o_ref[...] = acc / l
    lse_ref[...] = jnp.broadcast_to(m + jnp.log(l), (QB, 128))


def attend(base, doc_starts, raw, cosine, sine, kv):
    tok = cosine.shape[0]
    keys = kv.shape[1] * kv.shape[2] * 2
    row = pl.BlockSpec((QB, HDIM), lambda i: (i, 0))
    whole = lambda s: pl.BlockSpec(s, lambda i: (0,) * len(s))
    smem = pl.BlockSpec(memory_space=pltpu.SMEM)
    return pl.pallas_call(
        functools.partial(attend_kernel, HDIM ** (-0.5)),
        grid=(tok // QB,),
        in_specs=[smem, smem, row, row, row, whole(kv.shape)],
        out_specs=[row, row, whole((keys, HDIM)), whole((keys, HDIM)), row],
        out_shape=[jax.ShapeDtypeStruct((tok, HDIM), f32)] * 2
        + [jax.ShapeDtypeStruct((keys, HDIM), bf16)] * 2
        + [jax.ShapeDtypeStruct((tok, HDIM), bf16)],
        compiler_params=pltpu.CompilerParams(vmem_limit_bytes=VMEM_LIMIT),
        cost_estimate=pl.CostEstimate(
            flops=4 * tok * keys * HDIM, bytes_accessed=30_000_000, transcendentals=0
        ),
        name="attend",
    )(base, doc_starts, raw, cosine, sine, kv)


def attend_back_kernel(
    scale, base_ref, starts_ref, q_ref, do_ref, o_ref, lse_ref, k_ref, v_ref,
    dq_ref, dkv_ref, dk_ref, dv_ref,
):
    i = pl.program_id(0)

    @pl.when(i == 0)
    def _():
        dk_ref[...] = jnp.zeros_like(dk_ref)
        dv_ref[...] = jnp.zeros_like(dv_ref)

    q, do = q_ref[...], do_ref[...]
    delta = jnp.sum(do.astype(f32) * o_ref[...], axis=1, keepdims=True)
    lse = lse_ref[:, 0:1]
    low, high = sight(base_ref, starts_ref, i * QB)
    blocks = (base_ref[0] + (i + 1) * QB + KB - 1) // KB

    def turn(j, dq):
        at = pl.ds(pl.multiple_of(j * KB, KB), KB)
        k, v = k_ref[at, :], v_ref[at, :]
        visible = seen(low, high, j * KB)
        s = dot_nt(q, k) * scale
        p = jnp.exp(jnp.where(visible, s - lse, neg_large))
        ds = (p * (dot_nt(do, v) - delta)).astype(bf16)
        dv_ref[at, :] += dot_tn(p.astype(bf16), do)
        dk_ref[at, :] += dot_tn(ds, q) * scale
        return dq + dot_nn(ds, k)

    dq_ref[...] = lax.fori_loop(0, blocks, turn, jnp.zeros((QB, HDIM), f32)) * scale

    @pl.when(i == pl.num_programs(0) - 1)
    def _():
        n_p, nz, rows, _ = dkv_ref.shape
        kw = HDIM // n_p

        @pl.loop(0, nz)
        def _(z):
            got = []
            for t in range(2):
                at = pl.ds(pl.multiple_of((2 * z + t) * rows, rows), rows)
                got += [dk_ref[at, :].astype(bf16), dv_ref[at, :].astype(bf16)]
            for q in range(n_p):
                cut = slice(q * kw, q * kw + kw)
                dkv_ref[q, z] = jnp.concatenate([v[:, cut] for v in got], axis=1)


def attend_back(base, doc_starts, q, do, o, lse, k, v, packed):
    tok = q.shape[0]
    row = pl.BlockSpec((QB, HDIM), lambda i: (i, 0))
    whole = lambda s: pl.BlockSpec(s, lambda i: (0,) * len(s))
    smem = pl.BlockSpec(memory_space=pltpu.SMEM)
    return pl.pallas_call(
        functools.partial(attend_back_kernel, HDIM ** (-0.5)),
        grid=(tok // QB,),
        in_specs=[smem, smem, row, row, row, row, whole(k.shape), whole(k.shape)],
        out_specs=[row, whole(packed)],
        out_shape=[
            jax.ShapeDtypeStruct((tok, HDIM), f32),
            jax.ShapeDtypeStruct(packed, bf16),
        ],
        scratch_shapes=[pltpu.VMEM(k.shape, f32), pltpu.VMEM(k.shape, f32)],
        compiler_params=pltpu.CompilerParams(vmem_limit_bytes=VMEM_LIMIT),
        cost_estimate=pl.CostEstimate(
            flops=10 * tok * k.shape[0] * HDIM, bytes_accessed=40_000_000, transcendentals=0
        ),
        name="attend_back",
    )(base, doc_starts, q, do, o, lse, k, v)


def one_at(shape, source, where=True):
    lane = iota2(shape, 1)
    return ((iota2(shape, 0) == source(lane)) & where).astype(bf16)


def eye(n):
    return one_at((n, n), lambda lane: lane)


def q_order(kw):
    hk = kw // 2
    return one_at(
        (HDIM, HDIM), lambda l: ((l % kw) // hk) * (HDIM // 2) + (l // kw) * hk + l % hk
    )


def bc_order(p, bw, n_p):
    return one_at((2 * n_p * bw, 2 * bw), lambda l: (l // bw) * (n_p * bw) + p * bw + l % bw)


def last_order(p, kw, n_heads, dt_rows):
    hk = kw // 2
    lane = iota2((HDIM, 128), 1)
    lane_dt = iota2((dt_rows, 128), 1)
    key = one_at((HDIM, 128), lambda l: (l // hk) * (HDIM // 2) + p * hk + l % hk, lane < kw)
    value = one_at((HDIM, 128), lambda l: p * kw + l - kw, (lane >= kw) & (lane < 2 * kw))
    step = one_at(
        (dt_rows, 128),
        lambda l: p * n_heads + l - 2 * kw,
        (lane_dt >= 2 * kw) & (lane_dt < 2 * kw + n_heads),
    )
    return key, value, step


def pack_kernel(
    x_ref, bc_ref, k_ref, v_ref, dt_ref, q_ref, z_ref, mout_ref, aout_ref, gate_ref, up_ref,
    down_ref, a_ref, b_ref, c_ref, d_ref, e_ref,
):
    n_p = a_ref.shape[0]
    xw, bw, kw = x_ref.shape[1] // n_p, bc_ref.shape[1] // (2 * n_p), HDIM // n_p
    n_heads, ff, aw = dt_ref.shape[1] // n_p, gate_ref.shape[1] // n_p, q_ref.shape[1] // n_p
    bc, key, value = bc_ref[...].astype(bf16), k_ref[...].astype(bf16), v_ref[...].astype(bf16)
    step = dt_ref[...].astype(bf16)
    order = q_order(kw)
    for p in range(n_p):
        cut = lambda ref, n: ref[:, p * n : p * n + n].astype(bf16)
        flip = lambda ref, n: dot_tn(ref[p * n : p * n + n, :].astype(bf16), eye(n)).astype(bf16)
        a_ref[p, :, :xw] = cut(x_ref, xw)
        a_ref[p, :, xw : xw + 2 * bw] = dot_nn(bc, bc_order(p, bw, n_p)).astype(bf16)
        s_key, s_value, s_step = last_order(p, kw, n_heads, dt_ref.shape[1])
        a_ref[p, :, xw + 2 * bw :] = (
            dot_nn(key, s_key) + dot_nn(value, s_value) + dot_nn(step, s_step)
        ).astype(bf16)
        b_ref[p, :, :HDIM] = dot_nn(cut(q_ref, aw), order).astype(bf16)
        b_ref[p, :, HDIM:] = cut(z_ref, xw)
        c_ref[p, :, :xw] = flip(mout_ref, xw)
        c_ref[p, :, xw:] = flip(aout_ref, aw)
        d_ref[p, :, :ff] = cut(gate_ref, ff)
        d_ref[p, :, ff:] = cut(up_ref, ff)
        e_ref[p] = flip(down_ref, ff)


def pack(n_p, *weights):
    x, bc, k, v, dt, q, z, mout, aout, gate, up, down = weights
    rows = x.shape[0]
    ff, xw = gate.shape[1] // n_p, x.shape[1] // n_p
    widths = (xw + bc.shape[1] // n_p + 128, HDIM + xw, xw + HDIM, 2 * ff, ff)
    vm = pl.BlockSpec(memory_space=pltpu.VMEM)
    return pl.pallas_call(
        pack_kernel,
        in_specs=[vm] * 12,
        out_specs=[vm] * 5,
        out_shape=[jax.ShapeDtypeStruct((n_p, rows, w), bf16) for w in widths],
        compiler_params=pltpu.CompilerParams(vmem_limit_bytes=VMEM_LIMIT),
        cost_estimate=pl.CostEstimate(flops=0, bytes_accessed=10_000_000, transcendentals=0),
        name="pack",
    )(*weights)


def unpack_kernel(
    a_ref, b_ref, c_ref, d_ref, e_ref, row_ref, grow_ref,
    x_ref, bc_ref, k_ref, v_ref, dt_ref, q_ref, z_ref, mout_ref, aout_ref, gate_ref, up_ref,
    down_ref, row_out, grow_out,
):
    row_out[...] = row_ref[...]
    grow_out[...] = grow_ref[...]
    n_p, rows = a_ref.shape[0], a_ref.shape[1]
    xw, bw, kw = x_ref.shape[1] // n_p, bc_ref.shape[1] // (2 * n_p), HDIM // n_p
    n_heads, ff, aw = dt_ref.shape[1] // n_p, gate_ref.shape[1] // n_p, q_ref.shape[1] // n_p
    order, turn = q_order(kw), eye(rows)
    bc, key = jnp.zeros(bc_ref.shape, f32), jnp.zeros(k_ref.shape, f32)
    value, step = jnp.zeros(v_ref.shape, f32), jnp.zeros(dt_ref.shape, f32)
    for p in range(n_p):
        cut = lambda n: slice(p * n, p * n + n)
        x_ref[:, cut(xw)] = a_ref[p, :, :xw].astype(f32)
        bc = bc + dot_nt(a_ref[p, :, xw : xw + 2 * bw], bc_order(p, bw, n_p))
        last = a_ref[p, :, xw + 2 * bw :]
        s_key, s_value, s_step = last_order(p, kw, n_heads, dt_ref.shape[1])
        key, value = key + dot_nt(last, s_key), value + dot_nt(last, s_value)
        step = step + dot_nt(last, s_step)
        q_ref[:, cut(aw)] = dot_nt(b_ref[p, :, :HDIM], order)
        z_ref[:, cut(xw)] = b_ref[p, :, HDIM:].astype(f32)
        mout_ref[cut(xw), :] = dot_tn(c_ref[p, :, :xw], turn)
        aout_ref[cut(aw), :] = dot_tn(c_ref[p, :, xw:], turn)
        gate_ref[:, cut(ff)] = d_ref[p, :, :ff].astype(f32)
        up_ref[:, cut(ff)] = d_ref[p, :, ff:].astype(f32)
        down_ref[cut(ff), :] = dot_tn(e_ref[p], turn)
    bc_ref[...] = bc
    k_ref[...], v_ref[...], dt_ref[...] = key, value, step


def unpack(pieces, like):
    vm = pl.BlockSpec(memory_space=pltpu.VMEM)
    return pl.pallas_call(
        unpack_kernel,
        in_specs=[vm] * 7,
        out_specs=[vm] * 14,
        out_shape=[jax.ShapeDtypeStruct(w.shape, f32) for w in like],
        compiler_params=pltpu.CompilerParams(vmem_limit_bytes=VMEM_LIMIT),
        cost_estimate=pl.CostEstimate(flops=0, bytes_accessed=10_000_000, transcendentals=0),
        name="unpack",
    )(*pieces)


def ffn_kernel(x_ref, w_ref, g_ref, gu_ref, act_ref, grad_ref, total):
    i = pl.program_id(0)
    ff = act_ref.shape[1]
    gu = dot_nn(x_ref[...], w_ref[...])
    gu_ref[...] = gu
    gate = gu[:, :ff]
    act = (gate * jax.nn.sigmoid(gate) * gu[:, ff:]).astype(bf16)
    act_ref[...] = act
    part = dot_tn(g_ref[...], act)

    @pl.when(i == 0)
    def _():
        total[...] = part

    @pl.when(i > 0)
    def _():
        total[...] += part

    @pl.when(i == pl.num_programs(0) - 1)
    def _():
        grad_ref[...] = total[...].astype(bf16)


def ffn_forward(x, w, g):
    tok, width = x.shape
    ff, block = w.shape[1] // 2, 256
    row = lambda n: pl.BlockSpec((block, n), lambda i: (i, 0))
    whole = lambda *s: pl.BlockSpec(s, lambda i: (0,) * len(s))
    return pl.pallas_call(
        ffn_kernel,
        grid=(tok // block,),
        in_specs=[row(width), whole(*w.shape), row(width)],
        out_specs=[row(2 * ff), row(ff), whole(width, ff)],
        out_shape=[
            jax.ShapeDtypeStruct((tok, 2 * ff), f32),
            jax.ShapeDtypeStruct((tok, ff), bf16),
            jax.ShapeDtypeStruct((width, ff), bf16),
        ],
        scratch_shapes=[pltpu.VMEM((width, ff), f32)],
        compiler_params=pltpu.CompilerParams(vmem_limit_bytes=VMEM_LIMIT),
        cost_estimate=pl.CostEstimate(
            flops=6 * tok * width * ff, bytes_accessed=25_000_000, transcendentals=0
        ),
        name="ffn_forward",
    )(x, w, g)


def at_rows(first, count):
    return pl.ds(pl.multiple_of(first, count), count)


def place():
    return lax.axis_index("z"), lax.axis_index("p"), lax.axis_index("head")


def hop(p, d):
    x, y = lax.rem(p, 2), p // 2
    return lax.rem(y + d // 2, 2) * 2 + lax.rem(x + d % 2, 2)


def chip(z, p, c):
    return (z, p, c)


def meet(others):
    barrier = pltpu.get_barrier_semaphore()
    for other in others:
        pl.semaphore_signal(barrier, inc=1, device_id=other, device_id_type=MESH)
    pl.semaphore_wait(barrier, len(others))


def send(src, dst, send_sem, recv_sem, to):
    copy = pltpu.make_async_remote_copy(
        src_ref=src, dst_ref=dst, send_sem=send_sem, recv_sem=recv_sem,
        device_id=to, device_id_type=MESH,
    )
    copy.start()
    return copy


HOPS = (3, 1, 2)


def z_chain(ref, up_sems, down_sems, since=0):
    z, p, c = place()
    nz = ref.shape[0]

    def block_up(k):
        at = ref.at[z - k]
        return pltpu.make_async_remote_copy(
            src_ref=at, dst_ref=at, send_sem=up_sems.at[0, k], recv_sem=up_sems.at[1, k],
            device_id=chip(z + 1, p, c), device_id_type=MESH,
        )

    def block_down(k):
        at = ref.at[z + k]
        return pltpu.make_async_remote_copy(
            src_ref=at, dst_ref=at, send_sem=down_sems.at[0, k], recv_sem=down_sems.at[1, k],
            device_id=chip(z - 1, p, c), device_id_type=MESH,
        )

    def got_up(k):
        at = ref.at[z - k]
        pltpu.make_async_remote_copy(
            src_ref=at, dst_ref=at, send_sem=up_sems.at[0, k - 1], recv_sem=up_sems.at[1, k - 1],
            device_id=chip(z - 1, p, c), device_id_type=MESH,
        ).wait_recv()

    def got_down(k):
        at = ref.at[z + k]
        pltpu.make_async_remote_copy(
            src_ref=at, dst_ref=at, send_sem=down_sems.at[0, k - 1],
            recv_sem=down_sems.at[1, k - 1],
            device_id=chip(z + 1, p, c), device_id_type=MESH,
        ).wait_recv()

    def stage(k):
        if k > since:

            @pl.when(z - k >= 0)
            def _():
                got_up(k)

        @pl.when((z - k >= 0) & (z + 1 < nz))
        def _():
            block_up(k).start()

        if k > since:

            @pl.when(z + k < nz)
            def _():
                got_down(k)

        @pl.when((z + k < nz) & (z > 0))
        def _():
            block_down(k).start()

    def done():
        for k in range(since, nz):

            @pl.when((z - k >= 0) & (z + 1 < nz))
            def _():
                block_up(k).wait_send()

            @pl.when((z + k < nz) & (z > 0))
            def _():
                block_down(k).wait_send()

    return stage, done


def z_hop(ref, k, sems):
    z, p, c = place()
    nz = ref.shape[0]

    def move(slot, i, to):
        return pltpu.make_async_remote_copy(
            src_ref=ref.at[slot], dst_ref=ref.at[slot], send_sem=sems.at[0, i],
            recv_sem=sems.at[1, i], device_id=chip(to, p, c), device_id_type=MESH,
        )

    goes_up, goes_down = (z - k >= 0) & (z + 1 < nz), (z + k < nz) & (z > 0)

    @pl.when(goes_up)
    def _():
        move(z - k, 0, z + 1).start()

    @pl.when(goes_down)
    def _():
        move(z + k, 1, z - 1).start()

    def end():
        @pl.when(z - k - 1 >= 0)
        def _():
            move(z - k - 1, 0, z - 1).wait_recv()

        @pl.when(z + k + 1 < nz)
        def _():
            move(z + k + 1, 1, z + 1).wait_recv()

        @pl.when(goes_up)
        def _():
            move(z - k, 0, z + 1).wait_send()

        @pl.when(goes_down)
        def _():
            move(z + k, 1, z - 1).wait_send()

    return end


def share(block, part, far_sems, near_sems, own_sems=None):
    z, p, c = place()
    other = chip(z, p, 1 - c)
    x, y, far = hop(p, 1), hop(p, 2), hop(p, 3)

    def far_send(ref, i, q):
        return send(ref, ref, far_sems.at[0, i], far_sems.at[1, i], chip(z, q, c))

    def near_send(q, i):
        return send(block(q), block(q), near_sems.at[0, i], near_sems.at[1, i], other)

    out = [far_send(block(p), 0, x), far_send(block(p), 1, y)]
    near = []
    if own_sems is not None:
        near.append(send(block(p), block(p), own_sems.at[0], own_sems.at[1], other))

    def middle():
        out[0].wait_recv()
        out.append(far_send(part(x, 0), 2, y))
        out[1].wait_recv()
        out.append(far_send(part(y, 1), 3, x))
        if near_sems is not None:
            near.append(near_send(x, 0))
            near.append(near_send(y, 1))

    def end():
        out[2].wait_recv()
        out[3].wait_recv()
        if near_sems is not None:
            near.append(near_send(far, 2))
        for copy in out:
            copy.wait_send()
        for copy in near:
            copy.wait()

    return middle, end


def share_rows(full_ref, half, own_sems, far_sems, near_sems):
    z, p, c = place()
    rows = lambda q: (q * 2 + c) * half
    return share(
        lambda q: full_ref.at[at_rows(rows(q), half), :],
        lambda q, i: full_ref.at[at_rows(rows(q) + i * (half // 2), half // 2), :],
        far_sems, near_sems, own_sems,
    )


def reduce_blocks(pairs, part, keep, sib_out, sib_in, out, relay, came, near_sems, far_sems):
    z, p, c = place()
    other = chip(z, p, 1 - c)
    half, width = keep.shape[1], keep.shape[2]
    tile, quarter = part.shape[1], half // 2
    x, y = chip(z, hop(p, 1), c), chip(z, hop(p, 2), c)
    first, second = at_rows(0, quarter), at_rows(quarter, quarter)
    near, far = [], []

    def far_send(src, dst, i, to):
        far.append(send(src, dst, far_sems.at[0, i], far_sems.at[1, i], to))

    def total_of(i, rows, extra=None):
        @pl.loop(0, quarter // 16)
        def _(r):
            at = at_rows(rows + r * 16, 16)
            total = keep[i, at, :] + sib_in[i, at, :].astype(f32)
            if extra is not None:
                total = total + relay[extra, at_rows(r * 16, 16), :].astype(f32)
            out[i, at, :] = total.astype(bf16)

    def pass_on(i):
        near[i].wait_recv()
        if i == 0:
            total_of(0, 0)
            far_send(out.at[0, first, :], relay.at[0], 0, x)
            total_of(0, quarter)
            far_send(out.at[0, second, :], relay.at[1], 1, y)
        if i == 1:
            total_of(1, 0)
            far_send(out.at[1, first, :], came.at[0, first, :], 2, x)
        if i == 2:
            total_of(2, quarter)
            far_send(out.at[2, second, :], came.at[1, second, :], 3, y)

    for i, d in enumerate((3, 1, 2, 0)):
        rows = at_rows(hop(p, d) * (2 * half), 2 * half)

        @pl.loop(0, width // tile)
        def _(n):
            cols = at_rows(n * tile, tile)
            total = dot_nt(pairs[0][0][rows, :], pairs[0][1][cols, :])
            for left, right in pairs[1:]:
                total = total + dot_nt(left[rows, :], right[cols, :])
            part[...] = total
            keep[i, :, cols] = part[at_rows(c * half, half), :]
            sib_out[i, :, cols] = part[at_rows((1 - c) * half, half), :].astype(bf16)

        near.append(
            send(sib_out.at[i], sib_in.at[i], near_sems.at[0, i], near_sems.at[1, i], other)
        )
        if i:
            pass_on(i - 1)

    def middle():
        far[1].wait_recv()
        total_of(1, quarter, 1)
        far_send(out.at[1, second, :], came.at[0, second, :], 4, x)
        far[0].wait_recv()
        total_of(2, 0, 0)
        far_send(out.at[2, first, :], came.at[1, first, :], 5, y)

    def finish():
        near[3].wait_recv()
        for copy in far[2:]:
            copy.wait_recv()

    def total_rows(at):
        total = keep[3, at, :] + sib_in[3, at, :].astype(f32)
        return total + came[0, at, :].astype(f32) + came[1, at, :].astype(f32)

    def done():
        for copy in near + far:
            copy.wait_send()

    return total_rows, middle, finish, done


def greet():
    z, p, c = place()
    meet([chip(z, p, 1 - c)] + [chip(z, hop(p, d), c) for d in HOPS])


def rms(rows):
    return lax.rsqrt(jnp.mean(rows * rows, axis=1, keepdims=True) + eps_norm)


def mid_kernel(
    left, right, resid, gain, e_given, mid_ref, full_ref, e_ref,
    part, keep, sib_out, sib_in, out, relay, came, n_sems, f_sems, own_sems, far_sems, near_sems,
    up_sems, down_sems,
):
    z, p, c = place()
    nz = e_ref.shape[0]
    meet(
        [chip(z, p, 1 - c)]
        + [chip(z, hop(p, d), c) for d in HOPS]
        + [chip(lax.rem(z + d, nz), p, c) for d in (1, nz - 1)]
    )
    stage, chain_done = z_chain(e_ref, up_sems, down_sems, 2)
    stage(2)
    half = keep.shape[1]
    total_rows, middle, finish, done = reduce_blocks(
        [(left, right)], part, keep, sib_out, sib_in, out, relay, came, n_sems, f_sems
    )
    middle()
    finish()
    g = gain[...]

    @pl.loop(0, half // 16)
    def _(r):
        at = at_rows(r * 16, 16)
        mid = resid[at, :] + total_rows(at)
        mid_ref[at, :] = mid
        full_ref[at_rows((p * 2 + c) * half + r * 16, 16), :] = (mid * rms(mid) * g).astype(bf16)

    share_middle, share_end = share_rows(full_ref, half, own_sems, far_sems, near_sems)
    share_middle()
    for k in range(3, nz):
        stage(k)
    done()
    share_end()
    chain_done()


def two_kernel(
    left, right, mid_own, grad_own, gain, dmid_ref, ggain_ref, full_ref,
    part, keep, sib_out, sib_in, out, relay, came, n_sems, f_sems, own_sems, far_sems, near_sems,
):
    greet()
    z, p, c = place()
    half = keep.shape[1]
    total_rows, middle, finish, done = reduce_blocks(
        [(left, right)], part, keep, sib_out, sib_in, out, relay, came, n_sems, f_sems
    )
    middle()
    finish()
    g = gain[...]
    ggain_ref[...] = jnp.zeros_like(ggain_ref)

    @pl.loop(0, half // 16)
    def _(r):
        at = at_rows(r * 16, 16)
        d_two, mid = total_rows(at), mid_own[at, :]
        scale = rms(mid)
        w = d_two * g
        d_mid = grad_own[at, :] + scale * w - mid * (scale * scale * scale) * jnp.mean(
            w * mid, axis=1, keepdims=True
        )
        ggain_ref[...] += jnp.sum(d_two * mid * scale, axis=0, keepdims=True)
        dmid_ref[at, :] = d_mid
        full_ref[at_rows((p * 2 + c) * half + r * 16, 16), :] = d_mid.astype(bf16)

    share_middle, share_end = share_rows(full_ref, half, own_sems, far_sems, near_sems)
    share_middle()
    done()
    share_end()


def one_kernel(
    n, left_a, right_a, left_b, right_b, hidden_own, dmid_own, gain, act, w_act, mid_own, rest,
    *refs
):
    ins, (grad_ref, block_ref, sums_ref), outs = refs[:n], refs[n : n + 3], refs[n + 3 : 2 * n + 3]
    first, second = refs[2 * n + 3 : 2 * n + 12], refs[2 * n + 12 : 2 * n + 21]
    own_sems, ggain_ref, flat, flat_came, z_sems, p_sems, c_sems, w_sems, loc_sems = refs[
        2 * n + 21 :
    ]
    z, p, c = place()
    nz = flat_came.shape[0] + 1
    ups = [chip(lax.rem(z + d, nz), p, c) for d in range(1, nz)]
    meet([chip(z, p, 1 - c)] + [chip(z, hop(p, d), c) for d in HOPS] + ups)
    half = hidden_own.shape[0]
    total_rows, middle, finish, done = reduce_blocks(
        [(left_a, right_a), (left_b, right_b)], *first
    )
    middle()
    total_out, middle_out, finish_out, done_out = reduce_blocks([(act, w_act)], *second)
    moved = swap_begin(ins, outs, w_sems, loc_sems)
    g = gain[...]
    ggain_ref[...] = jnp.zeros_like(ggain_ref)
    middle_out()
    finish()

    @pl.loop(0, half // 16)
    def _(r):
        at = at_rows(r * 16, 16)
        d_one, hid = total_rows(at), hidden_own[at, :]
        scale = rms(hid)
        w = d_one * g
        d_in = dmid_own[at, :] + scale * w - hid * (scale * scale * scale) * jnp.mean(
            w * hid, axis=1, keepdims=True
        )
        ggain_ref[...] += jnp.sum(d_one * hid * scale, axis=0, keepdims=True)
        grad_ref[at_rows(c * half + r * 16, 16), :] = d_in

    mine = at_rows(c * half, half)
    other = chip(z, p, 1 - c)
    copies = [
        send(grad_ref.at[mine, :], grad_ref.at[mine, :], own_sems.at[0, 0], own_sems.at[1, 0], other)
    ]
    g_rows = ggain_ref.shape[1] // 128
    for i in range(g_rows):
        flat[i : i + 1, :] = ggain_ref[:, i * 128 : i * 128 + 128]
    flat[g_rows:, :] = rest[...]
    up = [
        send(flat, flat_came.at[d], z_sems.at[0, d], z_sems.at[1, d], ups[d])
        for d in range(nz - 1)
    ]
    total = flat[...]
    for d in range(nz - 1):
        up[d].wait_recv()
        total = total + flat_came[d]
    sums_ref[c, p] = total
    around = [
        send(
            sums_ref.at[c, p], sums_ref.at[c, p], p_sems.at[0, i], p_sems.at[1, i],
            chip(z, hop(p, d), c),
        )
        for i, d in enumerate(HOPS)
    ]
    finish_out()

    @pl.loop(0, half // 16)
    def _(r):
        at = at_rows(r * 16, 16)
        block_ref[at_rows(c * half + r * 16, 16), :] = mid_own[at, :] + total_out(at)

    copies.append(
        send(block_ref.at[mine, :], block_ref.at[mine, :], own_sems.at[0, 1], own_sems.at[1, 1], other)
    )
    for copy in around:
        copy.wait_recv()
    copies.append(send(sums_ref.at[c], sums_ref.at[c], c_sems.at[0], c_sems.at[1], other))
    done()
    done_out()
    for copy in up + around:
        copy.wait_send()
    for copy in copies + moved:
        copy.wait()


VM = pl.BlockSpec(memory_space=pltpu.VMEM)
ANYWHERE = pl.BlockSpec(memory_space=pl.ANY)


def swap_begin(ins, outs, sems, loc_sems):
    z, p, c = place()
    copies = []
    for j, (src, dst) in enumerate(zip(ins, outs)):
        for i, d in enumerate(HOPS):
            q = hop(p, d)
            copies.append(
                send(src.at[q], dst.at[p], sems.at[0, j, i], sems.at[1, j, i], chip(z, q, c))
            )
        local = pltpu.make_async_copy(src.at[p], dst.at[p], loc_sems.at[j])
        local.start()
        copies.append(local)
    return copies


def swap_sems(n):
    return [pltpu.SemaphoreType.DMA((2, n, 3)), pltpu.SemaphoreType.DMA((n,))]


def reduce_scratch(half, width):
    return [
        pltpu.VMEM((2 * half, 512), f32),
        pltpu.VMEM((4, half, width), f32),
        pltpu.VMEM((4, half, width), bf16),
        pltpu.VMEM((4, half, width), bf16),
        pltpu.VMEM((3, half, width), bf16),
        pltpu.VMEM((2, half // 2, width), bf16),
        pltpu.VMEM((2, half, width), bf16),
        pltpu.SemaphoreType.DMA((2, 4)),
        pltpu.SemaphoreType.DMA((2, 6)),
    ]


SHARE_SEMS = [
    pltpu.SemaphoreType.DMA((2,)),
    pltpu.SemaphoreType.DMA((2, 4)),
    pltpu.SemaphoreType.DMA((2, 3)),
]


def plane_call(kernel, name, number, args, shapes, scratch, nbytes=150_000_000, moved=()):
    n = len(moved)
    if n:
        kernel = functools.partial(kernel, n)
        scratch = scratch + swap_sems(n)
    return pl.pallas_call(
        kernel,
        in_specs=[VM] * (len(args) + n),
        out_specs=[VM] * len(shapes) + [ANYWHERE] * n,
        out_shape=[jax.ShapeDtypeStruct(s, t) for s, t in shapes]
        + [jax.ShapeDtypeStruct(m.shape, m.dtype) for m in moved],
        scratch_shapes=scratch,
        compiler_params=pltpu.CompilerParams(
            collective_id=number, has_side_effects=True, vmem_limit_bytes=VMEM_LIMIT
        ),
        cost_estimate=pl.CostEstimate(flops=0, bytes_accessed=nbytes, transcendentals=0),
        name=name,
    )(*args, *moved)


def mid_step(mixed, w, resid_own, gain, piece):
    tok, width = mixed.shape[0], w.shape[0]
    half, nz = resid_own.shape[0], piece.shape[0]
    return pl.pallas_call(
        mid_kernel,
        in_specs=[VM] * 4 + [ANYWHERE],
        out_specs=[VM] * 2 + [ANYWHERE],
        out_shape=[
            jax.ShapeDtypeStruct((half, width), f32),
            jax.ShapeDtypeStruct((tok, width), bf16),
            jax.ShapeDtypeStruct(piece.shape, bf16),
        ],
        scratch_shapes=reduce_scratch(half, width)
        + SHARE_SEMS
        + [pltpu.SemaphoreType.DMA((2, nz))] * 2,
        input_output_aliases={4: 2},
        compiler_params=pltpu.CompilerParams(
            collective_id=1, has_side_effects=True, vmem_limit_bytes=VMEM_LIMIT
        ),
        cost_estimate=pl.CostEstimate(flops=0, bytes_accessed=150_000_000, transcendentals=0),
        name="mid_step",
    )(mixed, w, resid_own, gain, piece)


def two_step(d_gu, w, mid_own, grad_own, gain):
    tok, width = d_gu.shape[0], w.shape[0]
    half = mid_own.shape[0]
    return plane_call(
        two_kernel, "two_step", 2, (d_gu, w, mid_own, grad_own, gain),
        [((half, width), f32), ((1, width), f32), ((tok, width), bf16)],
        reduce_scratch(half, width) + SHARE_SEMS,
    )


def one_step(
    d_a, w_a, d_b, w_b, hidden_own, dmid_own, gain, act, w_act, mid_own, rest, nz, n_p, moved
):
    width = w_a.shape[0]
    half = hidden_own.shape[0]
    flat = (width // 128 + rest.shape[0], 128)
    dma = pltpu.SemaphoreType.DMA
    return plane_call(
        one_kernel, "one_step", 3,
        (d_a, w_a, d_b, w_b, hidden_own, dmid_own, gain, act, w_act, mid_own, rest),
        [((2 * half, width), f32), ((2 * half, width), f32), ((2, n_p) + flat, f32)],
        reduce_scratch(half, width)
        + reduce_scratch(half, width)
        + [
            dma((2, 2)), pltpu.VMEM((1, width), f32), pltpu.VMEM(flat, f32),
            pltpu.VMEM((nz - 1,) + flat, f32), dma((2, nz - 1)), dma((2, 3)), dma((2,)),
        ],
        moved=moved,
    )


HALO = 16


def open_kernel(n, *refs):
    hid, gains_ref, a_ref = refs[:3]
    w_refs = refs[3 : 3 + n]
    gain_out, full_ref, a_out = refs[3 + n : 6 + n]
    w_outs = refs[6 + n : 6 + 2 * n]
    (
        g_vec, gz_sems, gp_sems, a_sems, up_sems, down_sems, own_sems, far_sems, near_sems,
        w_sems, loc_sems, halo_sems,
    ) = refs[6 + 2 * n :]
    z, p, c = place()
    nz, half, rows = a_out.shape[0], hid.shape[0], a_ref.shape[1]
    tok = full_ref.shape[0] - HALO
    ups = [chip(lax.rem(z + d, nz), p, c) for d in range(1, nz)]
    flat = [chip(z, hop(p, d), c) for d in HOPS]
    meet(ups + flat + [chip(z, p, 1 - c)])
    gain_out[p, z] = gains_ref[...]
    gz = [
        send(gain_out.at[p, z], gain_out.at[p, z], gz_sems.at[0, d], gz_sems.at[1, d], ups[d])
        for d in range(nz - 1)
    ]
    to_plane = []
    for i, d in enumerate(HOPS):
        to_plane.append(
            send(a_ref.at[hop(p, d)], a_out.at[z, p], a_sems.at[0, i], a_sems.at[1, i], flat[i])
        )
    local = [pltpu.make_async_copy(a_ref.at[p], a_out.at[z, p], loc_sems.at[n])]
    for j in range(n):
        local.append(pltpu.make_async_copy(w_refs[j].at[p], w_outs[j].at[p], loc_sems.at[j]))
    for copy in local:
        copy.start()

    for copy in gz:
        copy.wait_recv()
    gp = [
        send(gain_out.at[p], gain_out.at[p], gp_sems.at[0, i], gp_sems.at[1, i], flat[i])
        for i in range(3)
    ]
    stage, chain_done = z_chain(a_out, up_sems, down_sems)
    for copy in to_plane:
        copy.wait_recv()
    local[0].wait()
    stage(0)
    for copy in gp:
        copy.wait_recv()
    for i in range(nz):
        for j in range(gain_out.shape[0]):
            first = (i * gain_out.shape[0] + j) * rows
            g_vec[:, first : first + rows] = gain_out[j, i][:, :rows]
    g = g_vec[0:1, :]

    @pl.loop(0, half // 16)
    def _(r):
        rows_in = hid[at_rows(r * 16, 16), :]
        full_ref[at_rows((p * 2 + c) * half + r * 16, 16), :] = (
            rows_in * rms(rows_in) * g
        ).astype(bf16)

    share_middle, share_end = share_rows(full_ref, half, own_sems, far_sems, near_sems)

    share_middle()
    if nz > 2:
        stage(1)
    moved = []
    for j in range(n):
        for i, d in enumerate(HOPS):
            moved.append(
                send(
                    w_refs[j].at[hop(p, d)], w_outs[j].at[p], w_sems.at[0, j, i],
                    w_sems.at[1, j, i], flat[i],
                )
            )
    share_end()
    halo_from = full_ref.at[at_rows(tok - HALO, HALO), :]
    halo_to = full_ref.at[at_rows(tok, HALO), :]

    def halo(to):
        return pltpu.make_async_remote_copy(
            src_ref=halo_from, dst_ref=halo_to, send_sem=halo_sems.at[0],
            recv_sem=halo_sems.at[1], device_id=to, device_id_type=MESH,
        )

    @pl.when(z + 1 < nz)
    def _():
        halo(chip(z + 1, p, c)).start()

    @pl.when(z == 0)
    def _():
        full_ref[at_rows(tok, HALO), :] = jnp.zeros((HALO, full_ref.shape[1]), bf16)

    for k in range(2, nz):
        stage(k)

    @pl.when(z > 0)
    def _():
        halo(chip(z - 1, p, c)).wait_recv()

    @pl.when(z + 1 < nz)
    def _():
        halo(chip(z + 1, p, c)).wait_send()

    chain_done()
    for copy in moved + local[1:]:
        copy.wait()
    for copy in gz + gp + to_plane:
        copy.wait_send()


def open_step(hid, gains, piece, rest, tok, nz):
    width, n, n_p = hid.shape[1], len(rest), piece.shape[0]
    anywhere = pl.BlockSpec(memory_space=pl.ANY)
    dma = pltpu.SemaphoreType.DMA
    return pl.pallas_call(
        functools.partial(open_kernel, n),
        in_specs=[VM] * (n + 3),
        out_specs=[VM, VM] + [anywhere] * (n + 1),
        out_shape=[
            jax.ShapeDtypeStruct((n_p, nz) + gains.shape, f32),
            jax.ShapeDtypeStruct((tok + HALO, width), bf16),
            jax.ShapeDtypeStruct((nz,) + piece.shape, bf16),
        ]
        + [jax.ShapeDtypeStruct(r.shape, bf16) for r in rest],
        scratch_shapes=[
            pltpu.VMEM((8, width), f32), dma((2, nz - 1)), dma((2, 3)), dma((2, 3)), dma((2, nz)),
            dma((2, nz)),
        ]
        + SHARE_SEMS
        + [dma((2, n, 3)), dma((n + 1,)), dma((2,))],
        compiler_params=pltpu.CompilerParams(
            collective_id=4, has_side_effects=True, vmem_limit_bytes=VMEM_LIMIT
        ),
        cost_estimate=pl.CostEstimate(flops=0, bytes_accessed=250_000_000, transcendentals=0),
        name="open_step",
    )(hid, gains, piece, *rest)


def gather_bc_kernel(
    x_ref, kv_ref, grad_ref, e_ref, full_ref, kvz_ref, g_ref, e_out,
    far_sems, near_sems, z_sems, e_sems, loc_sems, own_g, far_g, near_g,
):
    z, p, c = place()
    nz = kvz_ref.shape[0]
    other = chip(z, p, 1 - c)
    meet(
        [other]
        + [chip(z, hop(p, d), c) for d in HOPS]
        + [chip(lax.rem(z + d, nz), p, c) for d in range(1, nz)]
    )
    local = pltpu.make_async_copy(e_ref, e_out.at[z], loc_sems.at[0])
    local.start()
    kvz_ref[z] = kv_ref[...]

    def up(d):
        return pltpu.make_async_remote_copy(
            src_ref=kv_ref, dst_ref=kvz_ref.at[z], send_sem=z_sems.at[0, d - 1],
            recv_sem=z_sems.at[1, d - 1], device_id=chip(z + d, p, c), device_id_type=MESH,
        )

    for d in range(1, nz):

        @pl.when(z + d < nz)
        def _():
            up(d).start()

    half = x_ref.shape[0] // 2
    full_ref[p] = x_ref[...]
    bc_middle, bc_end = share(
        lambda q: full_ref.at[q, at_rows(c * half, half), :],
        lambda q, i: full_ref.at[q, at_rows(c * half + i * (half // 2), half // 2), :],
        far_sems, near_sems,
    )
    local.wait()
    e_end = z_hop(e_out, 0, e_sems)
    bc_middle()
    g_half = grad_ref.shape[0]
    g_ref[at_rows((p * 2 + c) * g_half, g_half), :] = grad_ref[...].astype(bf16)
    g_middle, g_end = share_rows(g_ref, g_half, own_g, far_g, near_g)
    bc_end()
    g_middle()
    for d in range(1, nz):

        @pl.when(z - d >= 0)
        def _():
            pltpu.make_async_remote_copy(
                src_ref=kv_ref, dst_ref=kvz_ref.at[z - d], send_sem=z_sems.at[0, d - 1],
                recv_sem=z_sems.at[1, d - 1], device_id=chip(z - d, p, c), device_id_type=MESH,
            ).wait_recv()

        @pl.when(z + d < nz)
        def _():
            kvz_ref[z + d] = jnp.zeros(kv_ref.shape, kv_ref.dtype)
            up(d).wait_send()

    g_end()
    e_end()


def gather_bc(x, at, n_p, kv, nz, grad, piece):
    tok = x.shape[0]
    dma = pltpu.SemaphoreType.DMA
    whole = lambda s: pl.BlockSpec(s, lambda i: (0,) * len(s))
    return pl.pallas_call(
        gather_bc_kernel,
        grid=(1,),
        in_specs=[
            pl.BlockSpec((tok, 128), lambda i: (0, at)), whole(kv.shape), whole(grad.shape),
            whole(piece.shape),
        ],
        out_specs=[
            whole((n_p, tok, 128)), whole((nz,) + kv.shape), whole((tok, grad.shape[1])),
            ANYWHERE,
        ],
        out_shape=[
            jax.ShapeDtypeStruct((n_p, tok, 128), bf16),
            jax.ShapeDtypeStruct((nz,) + kv.shape, bf16),
            jax.ShapeDtypeStruct((tok, grad.shape[1]), bf16),
            jax.ShapeDtypeStruct((nz,) + piece.shape, bf16),
        ],
        scratch_shapes=[dma((2, 4)), dma((2, 3)), dma((2, nz - 1)), dma((2, 2)), dma((1,))]
        + SHARE_SEMS,
        compiler_params=pltpu.CompilerParams(
            collective_id=5, has_side_effects=True, vmem_limit_bytes=VMEM_LIMIT
        ),
        cost_estimate=pl.CostEstimate(flops=0, bytes_accessed=40_000_000, transcendentals=0),
        name="gather_bc",
    )(x, kv, grad, piece)


def carry_kernel(
    state_ref, rate_ref, kvz_ref, e_given, in_ref, kv_ref, rates_ref, e_ref,
    low, came, factor, s_sems, r_sems, p_sems, e_sems,
):
    z, p, c = place()
    nz = kvz_ref.shape[0]
    ups = [chip(lax.rem(z + d, nz), p, c) for d in range(1, nz)]
    meet([chip(z, hop(p, d), c) for d in (1, 2)] + ups)
    low[...] = state_ref[...].astype(bf16)
    rates_ref[z] = rate_ref[...]
    rates = [
        send(rates_ref.at[z], rates_ref.at[z], r_sems.at[0, d], r_sems.at[1, d], ups[d])
        for d in range(nz - 1)
    ]

    def up(d):
        return pltpu.make_async_remote_copy(
            src_ref=low, dst_ref=came.at[d - 1], send_sem=s_sems.at[0, d - 1],
            recv_sem=s_sems.at[1, d - 1], device_id=chip(z + d, p, c), device_id_type=MESH,
        )

    for d in range(1, nz):

        @pl.when(z + d < nz)
        def _():
            up(d).start()

    e_end = z_hop(e_ref, 1, e_sems)
    kv_ref[p] = kvz_ref[...]
    kv_middle, kv_end = share(
        lambda q: kv_ref.at[q],
        lambda q, i: kv_ref.at[q, pl.ds(i * (nz // 2), nz // 2)],
        p_sems, None,
    )
    in_ref[...] = jnp.zeros_like(in_ref)
    factor[...] = jnp.ones_like(factor)
    lane_head, row_head = head_maps(state_ref.shape[0])
    kv_middle()
    for copy in rates:
        copy.wait_recv()
    for d in range(1, nz):

        @pl.when(z - d >= 0)
        def _():
            pltpu.make_async_remote_copy(
                src_ref=low, dst_ref=came.at[d - 1], send_sem=s_sems.at[0, d - 1],
                recv_sem=s_sems.at[1, d - 1], device_id=chip(z - d, p, c), device_id_type=MESH,
            ).wait_recv()
            scale = jnp.sum(row_head * factor[0:1, :], axis=1, keepdims=True)
            in_ref[...] += scale * came[d - 1].astype(f32)
            factor[...] = factor[...] * rates_ref[z - d]

        @pl.when(z + d < nz)
        def _():
            up(d).wait_send()

    kv_end()
    e_end()
    for copy in rates:
        copy.wait_send()


def carry_step(state, rate, kvz, n_p, piece):
    nz = kvz.shape[0]
    dma = pltpu.SemaphoreType.DMA
    return pl.pallas_call(
        carry_kernel,
        in_specs=[VM] * 3 + [ANYWHERE],
        out_specs=[VM] * 3 + [ANYWHERE],
        out_shape=[
            jax.ShapeDtypeStruct(state.shape, f32),
            jax.ShapeDtypeStruct((n_p,) + kvz.shape, bf16),
            jax.ShapeDtypeStruct((nz,) + rate.shape, f32),
            jax.ShapeDtypeStruct(piece.shape, bf16),
        ],
        scratch_shapes=[
            pltpu.VMEM(state.shape, bf16),
            pltpu.VMEM((nz - 1,) + state.shape, bf16),
            pltpu.VMEM(rate.shape, f32),
            dma((2, nz - 1)), dma((2, nz - 1)), dma((2, 4)), dma((2, 2)),
        ],
        input_output_aliases={3: 3},
        compiler_params=pltpu.CompilerParams(
            collective_id=8, has_side_effects=True, vmem_limit_bytes=VMEM_LIMIT
        ),
        cost_estimate=pl.CostEstimate(flops=0, bytes_accessed=80_000_000, transcendentals=0),
        name="carry_step",
    )(state, rate, kvz, piece)


def reduce_bc_kernel(n, x_ref, dkv_ref, dx_ref, slope_ref, *refs):
    ins, (out_ref, own_ref, next_ref), outs = refs[:n], refs[n : n + 3], refs[n + 3 : 2 * n + 3]
    (
        sib_out, sib_in, out, came, z_came, first, n_sems, f_sems, own_sems, z_sems, h_sems,
        w_sems, loc_sems,
    ) = refs[2 * n + 3 :]
    z, p, c = place()
    nz = dkv_ref.shape[0]
    half = x_ref.shape[1] // 2
    xw = dx_ref.shape[1]
    other = chip(z, p, 1 - c)
    meet(
        [other]
        + [chip(z, hop(p, d), c) for d in HOPS]
        + [chip(lax.rem(z + d, nz), p, c) for d in range(1, nz)]
    )

    def down(d):
        return pltpu.make_async_remote_copy(
            src_ref=dkv_ref.at[z - d], dst_ref=z_came.at[d - 1], send_sem=z_sems.at[0, d - 1],
            recv_sem=z_sems.at[1, d - 1], device_id=chip(z - d, p, c), device_id_type=MESH,
        )

    for d in range(1, nz):

        @pl.when(z - d >= 0)
        def _():
            down(d).start()

    near, far = [], []
    order = HOPS + (0,)
    for i, d in enumerate(order):
        q = hop(p, d)
        sib_out[i] = x_ref[q, at_rows((1 - c) * half, half), :].astype(bf16)
        near.append(
            send(sib_out.at[i], sib_in.at[i], n_sems.at[0, i], n_sems.at[1, i], other)
        )
    for i, d in enumerate(HOPS):
        q = hop(p, d)
        near[i].wait_recv()
        out[i] = (x_ref[q, at_rows(c * half, half), :] + sib_in[i].astype(f32)).astype(bf16)
        far.append(
            send(out.at[i], came.at[i], f_sems.at[0, i], f_sems.at[1, i], chip(z, q, c))
        )
    moved = swap_begin(ins, outs, w_sems, loc_sems)
    near[3].wait_recv()
    total = x_ref[p, at_rows(c * half, half), :] + sib_in[3].astype(f32)
    for i in (1, 2, 0):
        far[i].wait_recv()
        total = total + came[i].astype(f32)
    mine = out_ref.at[at_rows(c * half, half), :]
    out_ref[at_rows(c * half, half), :] = total
    copy = send(mine, mine, own_sems.at[0], own_sems.at[1], other)
    copy.wait()
    first[:, :xw] = dx_ref[...] * slope_ref[:, :xw]
    first[:, xw:] = out_ref[0:8, :] * slope_ref[:, xw:]

    def edge(to):
        return pltpu.make_async_remote_copy(
            src_ref=first, dst_ref=next_ref, send_sem=h_sems.at[0], recv_sem=h_sems.at[1],
            device_id=to, device_id_type=MESH,
        )

    @pl.when(z > 0)
    def _():
        edge(chip(z - 1, p, c)).start()

    own_ref[...] = dkv_ref[z].astype(f32)
    for d in range(1, nz):

        @pl.when(z + d < nz)
        def _():
            pltpu.make_async_remote_copy(
                src_ref=dkv_ref.at[z], dst_ref=z_came.at[d - 1], send_sem=z_sems.at[0, d - 1],
                recv_sem=z_sems.at[1, d - 1], device_id=chip(z + d, p, c), device_id_type=MESH,
            ).wait_recv()
            own_ref[...] += z_came[d - 1].astype(f32)

        @pl.when(z - d >= 0)
        def _():
            down(d).wait_send()

    @pl.when(z + 1 == nz)
    def _():
        next_ref[...] = jnp.zeros_like(next_ref)

    @pl.when(z + 1 < nz)
    def _():
        edge(chip(z + 1, p, c)).wait_recv()

    @pl.when(z > 0)
    def _():
        edge(chip(z - 1, p, c)).wait_send()

    for done in near + far:
        done.wait_send()
    for copy in moved:
        copy.wait()


def reduce_bc(x, dkv, dx, slope, moved):
    n_p, tok, _ = x.shape
    half, nz = tok // 2, dkv.shape[0]
    dma = pltpu.SemaphoreType.DMA
    return plane_call(
        reduce_bc_kernel, "reduce_bc", 7, (x, dkv, dx, slope),
        [((tok, 128), f32), (dkv.shape[1:], f32), (slope.shape, f32)],
        [
            pltpu.VMEM((4, half, 128), bf16),
            pltpu.VMEM((4, half, 128), bf16),
            pltpu.VMEM((3, half, 128), bf16),
            pltpu.VMEM((3, half, 128), bf16),
            pltpu.VMEM((nz - 1,) + dkv.shape[1:], bf16),
            pltpu.VMEM(slope.shape, f32),
            dma((2, 4)), dma((2, 3)), dma((2,)), dma((2, nz - 1)), dma((2,)),
        ],
        nbytes=100_000_000,
        moved=moved,
    )


def swap_kernel(n, *refs):
    ins, outs, sems = refs[:n], refs[n : 2 * n], refs[2 * n :]
    z, p, c = place()
    meet([chip(z, hop(p, d), c) for d in HOPS])
    for copy in swap_begin(ins, outs, *sems):
        copy.wait()


def swap_step(*moved):
    return plane_call(swap_kernel, "swap_step", 6, (), [], [], nbytes=20_000_000, moved=moved)


def rope_tables(positions, pairs):
    freqs = rope_base ** (-2.0 * pairs.astype(f32) / HDIM)
    angles = positions.astype(f32)[:, None] * freqs[None, :]
    return jnp.cos(angles), jnp.sin(angles)


def carry_back(state, rates):
    nz, zi = lax.axis_size("z"), lax.axis_index("z")
    low = state.astype(bf16)
    total, factor = None, None
    for d in range(1, nz):
        came = lax.ppermute(low, "z", [(i, i - d) for i in range(d, nz)]).astype(f32)
        total = came if total is None else total + factor * came
        rate = lax.dynamic_index_in_dim(rates, (zi + d) % nz, 0, keepdims=False)
        factor = rate if factor is None else factor * rate
    return total


def shards(
    hidden_in,
    grad_out,
    doc_starts,
    norm_mixer,
    norm_ffn,
    mamba_z,
    mamba_x,
    mamba_bc,
    mamba_dt,
    conv_x,
    conv_bc,
    a_log,
    dt_bias,
    skip_gain,
    mamba_out,
    attn_query,
    attn_key,
    attn_value,
    attn_out,
    ffn_gate,
    ffn_up,
    ffn_down,
):
    own = hidden_in.shape[0]
    width = hidden_in.shape[1]
    half = own // 2
    nz, n_p = lax.axis_size("z"), lax.axis_size("p")
    zi, pi, ci = lax.axis_index("z"), lax.axis_index("p"), lax.axis_index("head")
    tok = own * n_p
    base = zi * tok
    positions = base + jnp.arange(tok, dtype=jnp.int32)
    edge = conv_x.shape[0] - 1
    ext_docs = doc_ids(base - edge + jnp.arange(tok + 2 * edge, dtype=jnp.int32), doc_starts)
    rows = mamba_z.shape[0]
    n_heads = a_log.shape[0] // n_p
    xw = n_heads * MHDIM
    bw = mamba_bc.shape[1] // (2 * n_p)
    cw = xw + 2 * bw
    kw = HDIM // n_p
    hk = kw // 2
    tail_w = 128 - 2 * kw - n_heads

    weights = (
        mamba_x, mamba_bc, attn_key, attn_value, mamba_dt, attn_query, mamba_z, mamba_out, attn_out,
        ffn_gate, ffn_up, ffn_down,
    )
    piece_a, *rest = pack(n_p, *weights)

    def along_z(piece):
        piece = piece.reshape(n_p * rows, piece.shape[2])
        return lax.all_gather(piece, "z", axis=0, tiled=True)

    gains_own = jnp.pad(
        jnp.stack([norm_mixer, norm_ffn]).astype(bf16).astype(f32), ((0, 6), (0, 128 - rows))
    )
    my_half = lambda v: lax.dynamic_slice_in_dim(v, ci * half, half, 0)
    hidden_own, grad_own = my_half(hidden_in), my_half(grad_out)
    gains, normed_one, w_a, *rest = open_step(hidden_own, gains_own, piece_a, rest, tok, nz)
    w_a = w_a.reshape(nz * n_p * rows, w_a.shape[3])
    gains = gains.transpose(2, 1, 0, 3)[:, :, :, :rows].reshape(8, 1, width)
    gain_mix, gain_ffn = gains[0], gains[1]
    w_b, w_c, w_d = [along_z(piece) for piece in rest[:3]]

    in_ext = product(normed_one, w_a)
    in_b_ext = product(normed_one, w_b)
    in_b = in_b_ext[:tok]
    in_a = in_ext[:tok]
    pre_ext = in_ext[:, :cw].astype(bf16)
    gate_z = in_b[:, HDIM:]
    slice_1 = lambda v, at, n: lax.dynamic_slice_in_dim(v, at, n, 1)
    taps = jnp.concatenate(
        [
            slice_1(conv_x, pi * xw, xw),
            slice_1(conv_bc, pi * bw, bw),
            slice_1(conv_bc, (n_p + pi) * bw, bw),
        ],
        axis=1,
    )
    ext = jnp.concatenate([pre_ext[tok + HALO - edge :], pre_ext[:tok]], axis=0)
    conv_in = convolve(ext, taps, ext_docs, tok)
    ssm = jax.nn.silu(conv_in).astype(bf16)
    head_slice = lambda v: lax.dynamic_slice_in_dim(v, pi * n_heads, n_heads, 0)
    my_bias, my_a, my_skip = head_slice(dt_bias), head_slice(a_log), head_slice(skip_gain)
    lanes = lambda v: jnp.pad(v, (0, 128 - n_heads))[None, :]
    dt_at = cw + 2 * kw
    dt_pre = jnp.pad(in_a[:, dt_at : dt_at + n_heads], ((0, 0), (0, 128 - n_heads))) + lanes(my_bias)
    neg_rate = lanes(-jnp.exp(my_a))
    skip_full = jnp.repeat(my_skip, MHDIM)[None, :]
    pair_ids = pi * hk + jnp.arange(hk)
    cos_k, sin_k = rope_tables(positions, pair_ids)
    k0, k1 = in_a[:, cw : cw + hk], in_a[:, cw + hk : cw + kw]
    key_own = jnp.concatenate([k0 * cos_k - k1 * sin_k, k1 * cos_k + k0 * sin_k], axis=1)
    val_own = in_a[:, cw + kw : cw + 2 * kw]
    kv_own = jnp.concatenate([key_own, val_own], axis=1).astype(bf16)
    kv_own = jnp.concatenate([kv_own[: tok // 2], kv_own[tok // 2 :]], axis=1)
    bc_all, kvz, g_ffn, w_e = gather_bc(
        ssm, xw // 128, n_p, kv_own, nz, grad_own, rest[3]
    )
    cos_q, sin_q = rope_tables(positions, jnp.arange(HDIM // 2))
    cos_q, sin_q = cos_q.reshape(tok, n_p, hk), sin_q.reshape(tok, n_p, hk)

    def rope_q(v, sign):
        v = v.reshape(tok, n_p, 2, hk)
        a, b = v[:, :, 0], v[:, :, 1]
        return jnp.stack(
            [a * cos_q - sign * b * sin_q, b * cos_q + sign * a * sin_q], axis=2
        ).reshape(tok, HDIM)

    lane = jnp.arange(HDIM)
    cos_w, sin_w = rope_tables(positions, (lane // kw) * hk + lane % hk)
    sin_w = jnp.where(lane % kw < hk, -1.0, 1.0)[None, :] * sin_w

    base_arr = jnp.reshape(base, (1,)).astype(jnp.int32)
    y_local, span_starts, local_state, dev_decay, decay_full, c_mat = ssd_forward(
        base_arr, doc_starts, ssm, bc_all, dt_pre, neg_rate, skip_full
    )
    rate = jnp.broadcast_to(dev_decay[tok - 1 :], (8, 128))
    in_state, kv, rates, w_e = carry_step(local_state, rate, kvz, n_p, w_e)

    attn_f32, lse, keys, values, queries = attend(
        base_arr, doc_starts, in_b_ext, cos_w, sin_w, kv
    )
    attn_low = attn_f32.astype(bf16)
    y_flat = y_local + product_nt(c_mat, in_state.astype(bf16)) * decay_full
    silu_z = jax.nn.silu(gate_z)
    gated = (y_flat * silu_z).astype(bf16)
    mixed = jnp.concatenate([gated, attn_low], axis=1)

    mid_own, normed_two, w_e = mid_step(mixed, w_c, hidden_own, gain_ffn, w_e)
    w_e = w_e.reshape(width, -1)
    gu, activated, grad_e = ffn_forward(normed_two, w_d, g_ffn)
    ffw = gu.shape[1] // 2
    gate_val, up_val = gu[:, :ffw], gu[:, ffw:]
    silu_gate = jax.nn.silu(gate_val)
    g_ffn, grad_e = lax.optimization_barrier((g_ffn, grad_e))
    d_act = product(g_ffn, w_e)
    d_gu = jnp.concatenate(
        [d_act * up_val * silu_slope(gate_val), d_act * silu_gate], axis=1
    ).astype(bf16)
    grad_d = product_t(normed_two, d_gu).astype(bf16)
    d_gu, grad_d = lax.optimization_barrier((d_gu, grad_d))

    def scattered(grad):
        return lax.psum_scatter(grad, "z", scatter_dimension=0, tiled=True)

    def by_owner(grad):
        return grad.reshape(n_p, rows, grad.shape[1])

    ge = scattered(grad_e)
    gd = scattered(grad_d)
    d_mid_own, grad_gain_ffn, g_mid = two_step(d_gu, w_d, mid_own, grad_own, gain_ffn)
    g_mid, ge = lax.optimization_barrier((g_mid, ge))

    d_mixed = product(g_mid, w_c)
    grad_c = product_t(g_mid, mixed).astype(bf16)
    gc = scattered(grad_c)
    d_gated = d_mixed[:, :xw]
    d_attn = d_mixed[:, xw:].astype(bf16)
    d_y_flat = d_gated * silu_z
    d_z = (d_gated * y_flat * silu_slope(gate_z)).astype(bf16)
    d_in_local = product_t((d_y_flat * decay_full).astype(bf16), c_mat)
    d_in_local, d_attn = lax.optimization_barrier((d_in_local, d_attn))
    rates = jnp.repeat(rates[:, 0, :n_heads], MHDIM, axis=1)[:, :, None]
    state_grad = carry_back(d_in_local, rates)
    d_query, d_kv = attend_back(
        base_arr, doc_starts, queries, d_attn, attn_f32, lse, keys, values, kv.shape
    )
    d_q_pre = rope_q(d_query, -1.0).astype(bf16)
    d_b = jnp.concatenate([d_q_pre, d_z], axis=1)
    d_b, state_grad = lax.optimization_barrier((d_b, state_grad))
    more = lambda v: jnp.pad(v, ((0, HALO), (0, 0)))
    grad_b = product_t(normed_one, more(d_b)).astype(bf16)
    gb = scattered(grad_b)
    d_kv_parts = [lax.dynamic_index_in_dim(d_kv, pi, 0, keepdims=False)]
    for d in range(1, n_p):
        part = lax.dynamic_index_in_dim(d_kv, jnp.bitwise_xor(pi, d), 0, keepdims=False)
        d_kv_parts.append(lax.ppermute(part, "p", [(i, i ^ d) for i in range(n_p)]))

    start_decay = jnp.concatenate([jnp.ones((1, 128), f32), dev_decay[SPAN - 1 :: SPAN][:-1]])
    d_y_flat, gd = lax.optimization_barrier((d_y_flat, gd))
    d_xs, d_bc, d_dt, sums, skip_sums = ssd_backward(
        base_arr, doc_starts, ssm, bc_all, dt_pre, d_y_flat, span_starts,
        start_decay[:, None, :], neg_rate, skip_full, in_state, state_grad,
    )
    d_bc, d_kv_parts = lax.optimization_barrier((d_bc, d_kv_parts))
    d_kv = sum(part.astype(f32) for part in d_kv_parts).astype(bf16)
    slope = silu_slope(conv_in)
    d_bc, d_kv_own, du_next, ge, gd = reduce_bc(
        d_bc, d_kv, d_xs[:8], slope[:8], (by_owner(ge), by_owner(gd))
    )
    d_kv_own = jnp.concatenate([d_kv_own[:, : 2 * kw], d_kv_own[:, 2 * kw :]], axis=0)
    dk0, dk1 = d_kv_own[:, :hk], d_kv_own[:, hk:kw]
    d_kv_low = jnp.concatenate(
        [dk0 * cos_k + dk1 * sin_k, dk1 * cos_k - dk0 * sin_k, d_kv_own[:, kw:]], axis=1
    ).astype(bf16)
    du = jnp.concatenate([d_xs, d_bc], axis=1) * slope
    du = jnp.concatenate([du, du_next[:edge]], axis=0)
    d_pre, grad_taps = convolve_back(du, ext, taps, ext_docs, tok)
    d_pre = d_pre.astype(bf16)
    d_last = jnp.concatenate(
        [d_kv_low, d_dt[:, :n_heads].astype(bf16), jnp.zeros((tok, tail_w), bf16)], axis=1
    )
    d_a = jnp.concatenate([d_pre, d_last], axis=1)
    grad_a = product_t(normed_one, more(d_a)).astype(bf16)
    ga = scattered(grad_a)
    once = jnp.where(ci == 0, d_pre[:, xw:], jnp.zeros((), bf16))
    d_a_once = jnp.concatenate([d_pre[:, :xw], once, d_last], axis=1)
    d_a_once, grad_a, gc = lax.optimization_barrier((d_a_once, grad_a, gc))
    rest = jnp.concatenate(
        [
            grad_gain_ffn.reshape(-1, 128),
            grad_taps.reshape(-1, 128),
            sums[:2],
            jnp.pad(jnp.sum(skip_sums.reshape(n_heads, MHDIM), axis=1), (0, 128 - n_heads))[None],
        ]
    )
    rest = jnp.pad(rest, ((0, -rest.shape[0] % 8), (0, 0)))
    grad_in, block_out, summed, gc = one_step(
        d_a_once, w_a, d_b, w_b, hidden_own, d_mid_own, gain_mix, activated, w_e, mid_own, rest,
        nz, n_p, (by_owner(gc),),
    )

    g_rows = width // 128
    t_rows = grad_taps.size // 128
    si = zi * n_p + pi
    gains_sum = jnp.sum(summed[:, :, : 2 * g_rows], axis=(0, 1)).reshape(2, width)
    gains_sum = lax.dynamic_slice_in_dim(gains_sum, si * rows, rows, 1)
    mine = lax.dynamic_index_in_dim(summed, ci, 0, keepdims=False)
    s_taps = mine[:, 2 * g_rows : 2 * g_rows + t_rows].reshape(n_p, edge + 1, cw).transpose(1, 0, 2)
    s_heads = mine[:, 2 * g_rows + t_rows : 2 * g_rows + t_rows + 3, :n_heads]
    s_heads = s_heads.transpose(1, 0, 2).reshape(3, n_p * n_heads)
    s_x = s_taps[:, :, :xw].reshape(edge + 1, n_p * xw)
    s_bc = summed[0][:, 2 * g_rows : 2 * g_rows + t_rows].reshape(n_p, edge + 1, cw)
    s_bc = s_bc[:, :, xw:].reshape(n_p, edge + 1, 2, bw).transpose(1, 2, 0, 3)
    s_bc = s_bc.reshape(edge + 1, 2 * n_p * bw)

    ga, gb = swap_step(by_owner(ga), by_owner(gb))
    (
        g_x, g_bc, g_k, g_v, g_dt, g_q, g_z, g_mout, g_aout, g_gate, g_up, g_down, block_out,
        grad_in,
    ) = unpack((ga, gb, gc, gd, ge, block_out, grad_in), weights + (block_out, grad_in))
    return (
        block_out,
        grad_in,
        gains_sum[0],
        gains_sum[1],
        g_z,
        g_x,
        g_bc,
        g_dt,
        s_x,
        s_bc,
        s_heads[0],
        s_heads[1],
        s_heads[2],
        g_mout,
        g_q,
        g_k,
        g_v,
        g_aout,
        g_gate,
        g_up,
        g_down,
    )


def solution(mesh):
    seq, head = mesh.shape["seq"], mesh.shape["head"]
    plane = math.gcd(seq, 4)
    grid = Mesh(mesh.devices.reshape(seq // plane, plane, head), ("z", "p", "head"))
    s = ("z", "p")
    h = "head"
    placed = (
        P(s, None), P(s, None), P(), P(s), P(s), P(s, h), P(s, h), P(s, None), P(s, h),
        P(None, h), P(), P(h), P(h), P(h), P(h, s), P(s, h), P(s, h), P(s, h), P(h, s),
        P(s, h), P(s, h), P(h, s),
    )
    given = (
        P(s, None), P(s, None), P(s), P(s), P(s, h), P(s, h), P(s, None), P(s, h),
        P(None, h), P(), P(h), P(h), P(h), P(h, s), P(s, h), P(s, h), P(s, h), P(h, s),
        P(s, h), P(s, h), P(h, s),
    )
    return jax.shard_map(shards, mesh=grid, in_specs=placed, out_specs=given, check_vma=False)
```
